32 devices in a mesh: dp: 8 (over z, y), tensor: 4 (over x, core).
Axes of the slice: x: 2, y: 2, z: 4, core: 2. Of those that a mesh axis runs over, the one named last changes fastest.
Arguments:
- queries: bfloat16 [4096, 4096], P('dp', 'tensor'), may hold values from -20 to 20
- cotangent: bfloat16 [4096, 4096], P('dp', 'tensor'), may hold values from -6 to 6
- table: bfloat16 [128, 128, 896], P('dp'), may hold values from -6 to 6
- key_weight: bfloat16 [896, 4096], P(None, 'tensor'), may hold values from -0.1875 to 0.1875
- value_weight: bfloat16 [896, 4096], P(None, 'tensor'), may hold values from -0.1875 to 0.1875
- owners: int32 [64, 2], P('dp'), may hold values from 0 to 7, all different within a row; in each aligned block of 8 rows (0 to 7, 8 to 15, ...) at most 4 rows name the same one
- slots: int32 [64, 2], P('dp'), may hold values from 0 to 15
Outputs:
- attended: bfloat16 [4096, 4096], P('dp', 'tensor')
- d_query: bfloat16 [4096, 4096], P('dp', 'tensor')
- d_table: float32 [128, 128, 896], P('dp', 'tensor')
The draws below stay inside these ranges and needn't reach their ends.
Inputs may be any that keep to these rules, and one draw needn't show every extreme that they name: `owners`: in each aligned block of 8 rows (the spans of one dp index) no value occurs more than 4 times, and in some block one value occurs exactly 4 times; the two entries of a row differ.
All inputs are finite; a program needn't handle non-finite values.
Results may differ from the reference program's by a relative error of at most 0.0055.
The reference program's roundings to bfloat16 on the way (of `neighbours`, `keys`, `weights`, `dscores` and `d_keys`) count: a program that leaves them out, or rounds other values in their place, can miss the bound.
Values may be sent and summed in bfloat16 or wider, within the bound.
No kernel may reach another device: no remote copies, remote signals or barrier semaphores. Data moves between devices by JAX's collectives and lax.ppermute only.
A program may use at most 128 MiB of HBM per device.

```python
import math
import jax
import jax.numpy as jnp
import numpy as np
from jax import lax

ENC = 896
HEADS = 32
HD = 128
SPAN = 64
NLEN = 128
CH_DEV = 8
SLABS_DEV = 16
CAP = 4
SPANS = 64
TOKENS = 4096
SLABS = 128
N_DP = 8


def draw_queries(key, part):
    key = jax.random.fold_in(key, 11)
    first_key = jax.random.fold_in(key, 0)
    entries = jnp.clip(jax.random.normal(first_key, (TOKENS, HEADS * HD), jnp.float32), -5.0, 5.0)
    return entries.astype(jnp.bfloat16)


def plant(values, own_key, smallest, largest):
    dims = values.shape
    spot = [jax.random.randint(jax.random.fold_in(own_key, axis), (), 0, dims[axis]) for axis in range(len(dims))]
    values = values.at[tuple(spot)].set(smallest)
    longest = dims.index(max(dims))
    spot[longest] = (spot[longest] + 1) % dims[longest]
    return values.at[tuple(spot)].set(largest)


def block_levels(stream_key, shape, cuts, smallest, largest):
    loudness, own = 1.0, jax.random.fold_in(stream_key, 6)
    for position, parts in cuts:
        steps = jnp.exp(jax.random.uniform(jax.random.fold_in(own, position), (parts,), jnp.float32, smallest / len(cuts), largest / len(cuts)))
        loudness = loudness * jnp.repeat(steps, shape[position] // parts).reshape([-1 if axis == position else 1 for axis in range(len(shape))])
    return loudness


def assign_block(rng, own, number, rows, count, top, bound, skew):
    order = jax.random.permutation(rng, count)
    heavy_load, usual = load_shares(count, rows * top, bound, skew, True), load_shares(count, rows * top, bound, skew, False)
    places = jnp.arange(count)

    def named(tallies, turn):
        used = int((tallies > 0).sum())
        fixed = max(1, used // 4)
        passed = fixed + (places - fixed + turn * (used - fixed)) % max(1, count - fixed)
        return jnp.zeros((count,), jnp.int32).at[order[jnp.where(places < fixed, places, passed)]].set(jnp.asarray(tallies, jnp.int32))

    tallies = jnp.where(number % 4 == 0, named(heavy_load, number // 4), named(usual, number - number // 4 - 1))
    mixed = jax.random.permutation(jax.random.fold_in(own, 3), count)
    giver, taker = mixed[0:count // 2 * 2:2], mixed[1:count // 2 * 2:2]
    room = jnp.minimum(tallies[giver] - 1, bound - tallies[taker]) // 2
    room = jnp.where((giver == order[0]) | (taker == order[0]) | (tallies[taker] == 0), 0, jnp.maximum(room, 0))
    passed = jax.random.randint(jax.random.fold_in(own, 4), (count // 2,), 0, 1 << 20) % (room + 1)
    tallies = tallies.at[giver].add(-passed).at[taker].add(passed)
    members = jnp.searchsorted(jnp.cumsum(tallies), jnp.arange(rows * top), side="right").astype(jnp.int32)
    table = members.reshape(top, rows).T
    table = table[jax.random.permutation(jax.random.fold_in(own, 1), rows)]
    turn = jax.random.randint(jax.random.fold_in(own, 2), (rows, 1), 0, top)
    return jnp.take_along_axis(table, (jnp.arange(top)[None, :] + turn) % top, axis=1)


def load_shares(count, total, limit, skew, full):
    portions = [(1 << 20) // math.isqrt(standing ** skew) + 1 for standing in range(1, count + 1)]
    largest = limit if full else min(limit, max(-(-total // count), total * portions[0] // sum(portions)))
    least = 1 if total - largest >= count - 1 else 0
    counts, spare = [largest] + [least] * (count - 1), total - largest - least * (count - 1)
    while spare > 0:
        free = [i for i in range(1, count) if counts[i] < largest] or [i for i in range(1, count) if counts[i] < limit]
        whole, budget = sum([portions[i] for i in free]), spare
        for i in free:
            extra = min(limit - counts[i], max(1, budget * portions[i] // whole), spare)
            counts[i] = counts[i] + extra
            spare = spare - extra
    return np.array(counts)


def bell_draw(stream_key, extent, scale, reach, pieces=(), kind=jnp.bfloat16):
    gain = block_levels(stream_key, extent, pieces, -0.22, 0.18) if pieces else 1.0
    values = jax.random.normal(stream_key, extent, jnp.float32) * scale * gain
    return jnp.minimum(jnp.maximum(values, -reach), reach).astype(kind)


def setup_inputs(seed: int = 0) -> dict:
    splits = jax.random.split(jax.random.key(seed), 8)
    queries = draw_queries(jax.random.fold_in(splits[7], 71), 0)
    cotangent = bell_draw(splits[1], (TOKENS, HEADS * HD), 1.0, 6.0, ((0, 8), (1, 4)))
    table = bell_draw(splits[2], (SLABS, NLEN, ENC), 1.0, 6.0, ((0, 8),))
    key_weight = bell_draw(splits[3], (ENC, HEADS * HD), ENC ** -0.5, 0.1875, ((1, 4),))
    value_weight = bell_draw(splits[4], (ENC, HEADS * HD), ENC ** -0.5, 0.1875, ((1, 4),))
    owners_keys = jax.random.split(jax.random.fold_in(splits[5], 1), SPANS // CH_DEV)
    owners_turns = jax.random.permutation(jax.random.fold_in(splits[5], 3), SPANS // CH_DEV)
    owners = jax.vmap(lambda own, number: assign_block(jax.random.fold_in(splits[5], 2), own, number, CH_DEV, N_DP, 2, CAP, 2))(owners_keys, owners_turns).reshape((SPANS, 2))
    slots = plant(jax.random.randint(splits[6], (SPANS, 2), 0, SLABS_DEV), jax.random.fold_in(splits[6], 1), 0, SLABS_DEV - 1).astype(jnp.int32)
    return {"queries": queries, "cotangent": cotangent, "table": table, "key_weight": key_weight, "value_weight": value_weight, "owners": owners, "slots": slots}


def reference(queries, cotangent, table, key_weight, value_weight, owners, slots):
    slab_ids = (owners * SLABS_DEV + slots).astype(jnp.int32)
    kv_width = HEADS * HD
    score_scale = 1.0 / math.sqrt(HD)
    query_spans = queries.reshape(SPANS, SPAN, kv_width)
    grad_spans = cotangent.reshape(SPANS, SPAN, kv_width)

    def per_span(inputs):
        query_rows, grad_rows, span_ids = inputs
        neighbours = table[span_ids].reshape(2 * NLEN, ENC)
        keys = jnp.dot(neighbours, key_weight, preferred_element_type=jnp.float32).astype(jnp.bfloat16)
        values = jnp.dot(neighbours, value_weight, preferred_element_type=jnp.float32).astype(jnp.bfloat16)
        query_f = query_rows.astype(jnp.float32).reshape(SPAN, HEADS, HD)
        grad_f = grad_rows.astype(jnp.float32).reshape(SPAN, HEADS, HD)
        keys_f = keys.astype(jnp.float32).reshape(2 * NLEN, HEADS, HD)
        values_f = values.astype(jnp.float32).reshape(2 * NLEN, HEADS, HD)
        scores = jnp.einsum('qhd,khd->hqk', query_f, keys_f) * score_scale
        attn_probs = jax.nn.softmax(scores, axis=-1)
        weights = attn_probs.astype(jnp.bfloat16).astype(jnp.float32)
        attended = jnp.einsum('hqk,khd->qhd', weights, values_f).astype(jnp.bfloat16).reshape(SPAN, kv_width)
        d_weights = jnp.einsum('qhd,khd->hqk', grad_f, values_f)
        row_sums = lax.optimization_barrier(jnp.sum(d_weights * attn_probs, axis=-1, keepdims=True))
        dscores = (attn_probs * (d_weights - row_sums) * score_scale).astype(jnp.bfloat16).astype(jnp.float32)
        d_query = jnp.einsum('hqk,khd->qhd', dscores, keys_f).astype(jnp.bfloat16).reshape(SPAN, kv_width)
        d_keys = jnp.einsum('hqk,qhd->khd', dscores, query_f).astype(jnp.bfloat16).reshape(2 * NLEN, kv_width)
        d_values = jnp.einsum('hqk,qhd->khd', weights, grad_f).astype(jnp.bfloat16).reshape(2 * NLEN, kv_width)
        d_neigh = jnp.dot(d_keys, key_weight.T, preferred_element_type=jnp.float32)
        d_neigh = d_neigh + jnp.dot(d_values, value_weight.T, preferred_element_type=jnp.float32)
        return (attended, d_query, d_neigh.reshape(2, NLEN, ENC))
    attended, d_query, d_neigh = lax.map(per_span, (query_spans, grad_spans, slab_ids))
    d_table = jnp.zeros((SLABS, NLEN, ENC), jnp.float32).at[slab_ids.reshape(-1)].add(d_neigh.reshape(-1, NLEN, ENC))
    return (attended.reshape(TOKENS, kv_width), d_query.reshape(TOKENS, kv_width), d_table)
```

```python
import functools
import math

import jax
import jax.numpy as jnp
from jax import lax
from jax.experimental import pallas as pl
from jax.experimental.pallas import tpu as pltpu
from jax.sharding import PartitionSpec as P

HD = 128
SPAN = 64
SUB = 16
LANES = 128
VMEM_LIMIT = 56 * 1024 * 1024
F32 = jnp.float32
BF16 = jnp.bfloat16

ANY = pl.BlockSpec(memory_space=pl.ANY)
SMEM = pl.BlockSpec(memory_space=pltpu.SMEM)
VMEM = pl.BlockSpec(memory_space=pltpu.VMEM)


def params():
    return pltpu.CompilerParams(vmem_limit_bytes=VMEM_LIMIT)


def cost(flops, nbytes):
    return pl.CostEstimate(flops=int(flops), bytes_accessed=int(nbytes), transcendentals=0)


def pack_body(n_chunks, share, asked, first, table, *rest):
    outs, sem = rest[:n_chunks], rest[n_chunks]
    n = asked.shape[0]
    base = first[0]

    def each(act):
        for s in range(n):
            slab = asked[s]

            @pl.when(slab >= 0)
            def _():
                for c in range(n_chunks):
                    row = pl.multiple_of(base + c * SUB, SUB)
                    act(
                        pltpu.make_async_copy(
                            table.at[slab, pl.ds(row, SUB)], outs[c].at[s], sem.at[c, s]
                        )
                    )

    each(lambda copy: copy.start())
    each(lambda copy: copy.wait())


def pack(asked, first, table, n_chunks):
    n = asked.shape[0]
    enc = table.shape[2]
    return pl.pallas_call(
        functools.partial(pack_body, n_chunks, None),
        out_shape=[jax.ShapeDtypeStruct((n, SUB, enc), table.dtype)] * n_chunks,
        in_specs=[SMEM, SMEM, ANY],
        out_specs=[ANY] * n_chunks,
        scratch_shapes=[pltpu.SemaphoreType.DMA((n_chunks, n))],
        compiler_params=params(),
        cost_estimate=cost(0, 4 * n_chunks * n * SUB * enc),
        name="pack_rows",
    )(asked, first, table)


def compact_body(position, arrived, out, sem):
    n = position.shape[0]
    copies = [
        pltpu.make_async_copy(arrived.at[position[r]], out.at[r], sem.at[r]) for r in range(n)
    ]
    for copy in copies:
        copy.start()
    for copy in copies:
        copy.wait()


def compact(position, arrived):
    n = position.shape[0]
    shape = (n,) + arrived.shape[1:]
    return pl.pallas_call(
        compact_body,
        out_shape=jax.ShapeDtypeStruct(shape, arrived.dtype),
        in_specs=[SMEM, ANY],
        out_specs=ANY,
        scratch_shapes=[pltpu.SemaphoreType.DMA((n,))],
        compiler_params=params(),
        cost_estimate=cost(0, 4 * math.prod(shape)),
        name="compact_rows",
    )(position, arrived)


def project_body(n_in, *refs):
    w, out = refs[n_in], refs[n_in + 1]
    for i in range(n_in):
        n, sub, enc = refs[i].shape
        rows = refs[i][...].reshape(n * sub, enc)
        res = jnp.dot(rows, w[...], preferred_element_type=F32)
        out[i] = res.astype(BF16).reshape(n, sub, res.shape[1])


def project(pieces, w_kv):
    n_in = len(pieces)
    n, sub, enc = pieces[0].shape
    width = w_kv.shape[1]
    step = width // 4
    return pl.pallas_call(
        functools.partial(project_body, n_in),
        out_shape=jax.ShapeDtypeStruct((n_in, n, sub, width), BF16),
        grid=(4,),
        in_specs=[pl.BlockSpec((n, sub, enc), lambda i: (0, 0, 0))] * n_in
        + [pl.BlockSpec((enc, step), lambda i: (0, i))],
        out_specs=pl.BlockSpec((n_in, n, sub, step), lambda i: (0, 0, 0, i)),
        compiler_params=params(),
        cost_estimate=cost(
            2 * n_in * n * sub * enc * width, 2 * (n_in * n * sub * (enc + width) + enc * width)
        ),
        name="project",
    )(*pieces, w_kv)


def attend_body(groups, n_x, n_chunks, *refs):
    n_kv = n_chunks * len(groups)
    kvs = refs[:n_kv]
    q_ref, g_ref = refs[n_kv : n_kv + 2]
    att_ref, dq_ref = refs[n_kv + 2 : n_kv + 4]
    own_refs = refs[n_kv + 4 : n_kv + 4 + n_chunks]
    core_refs = refs[n_kv + 4 + n_chunks :]
    width = q_ref.shape[1]
    scale = 1.0 / math.sqrt(HD)

    def keys_of(col):
        cols = pl.ds(col, HD)
        parts = []
        for ref in kvs:
            block = ref[:, :, :, cols]
            parts.append(block.reshape(-1, HD))
        return jnp.concatenate(parts, axis=0)

    def put(col, grad):
        at = 0
        for c in range(n_chunks):
            for group in groups:
                for kind, d in group:
                    ref = (own_refs if kind == 0 else core_refs)[c]
                    ref[d, :, :, pl.ds(col, HD)] = grad[at : at + 2 * SUB].reshape(2, SUB, HD)
                    at += 2 * SUB

    last = (((1,), (1,)), ((), ()))
    first = (((0,), (0,)), ((), ()))
    for h in range(width // HD):
        cols = pl.ds(h * HD, HD)
        q, g = q_ref[:, cols], g_ref[:, cols]
        k, v = keys_of(h * HD), keys_of(width + h * HD)
        s = lax.dot_general(q, k, last, preferred_element_type=F32) * scale
        e = jnp.exp(s - jnp.max(s, axis=1, keepdims=True))
        p = e / jnp.sum(e, axis=1, keepdims=True)
        w = p.astype(BF16)
        att_ref[:, cols] = jnp.dot(w, v, preferred_element_type=F32).astype(BF16)
        dw = lax.dot_general(g, v, last, preferred_element_type=F32)
        rs = jnp.sum(dw * p, axis=1, keepdims=True)
        ds = (p * (dw - rs) * scale).astype(BF16)
        dq_ref[:, cols] = jnp.dot(ds, k, preferred_element_type=F32).astype(BF16)
        put(h * HD, lax.dot_general(ds, q, first, preferred_element_type=F32).astype(BF16))
        put(width + h * HD, lax.dot_general(w, g, first, preferred_element_type=F32).astype(BF16))


def attend(kvs, groups, n_x, n_chunks, queries, cotangent):
    tokens, width = queries.shape
    spans = tokens // SPAN
    n = kvs[0].shape[1]
    rows = pl.BlockSpec((SPAN, width), lambda i: (i, 0))

    def kv_block(pieces):
        return pl.BlockSpec((pieces, 2, SUB, 2 * width), lambda i: (0, i, 0, 0))

    keys = n_chunks * 2 * n_x * 2 * SUB
    out = pl.pallas_call(
        functools.partial(attend_body, groups, n_x, n_chunks),
        out_shape=[jax.ShapeDtypeStruct((tokens, width), BF16)] * 2
        + [jax.ShapeDtypeStruct((n_x, n, SUB, 2 * width), BF16)] * (2 * n_chunks),
        grid=(spans,),
        in_specs=[kv_block(kv.shape[0]) for kv in kvs] + [rows, rows],
        out_specs=[rows, rows] + [kv_block(n_x)] * (2 * n_chunks),
        compiler_params=params(),
        cost_estimate=cost(12 * tokens * width * keys, 8 * tokens * width + 8 * spans * keys * 2 * width),
        name="attend",
    )(*kvs, queries, cotangent)
    return out[0], out[1], out[2 : 2 + n_chunks], out[2 + n_chunks :]


def encode(x, axes):
    top = jnp.maximum(jnp.max(jnp.abs(x), axis=axes, keepdims=True), 1e-30)
    power = jnp.floor(jnp.log2(top)) + 1.0
    code = jnp.clip(jnp.round(x * jnp.exp2(15.0 - power)), -32767.0, 32767.0)
    return code.astype(jnp.int32).astype(jnp.int16), power


def partial_grad(d_ref, w_ref, acc):
    k = pl.program_id(0)
    n_x, n, sub, step = d_ref.shape
    part = lax.dot_general(
        d_ref[...].reshape(n_x * n * sub, step),
        w_ref[...],
        (((1,), (1,)), ((), ())),
        preferred_element_type=F32,
    )

    @pl.when(k == 0)
    def _():
        acc[...] = part

    @pl.when(k > 0)
    def _():
        acc[...] += part


def core_grad_body(d_ref, w_ref, out, acc):
    partial_grad(d_ref, w_ref, acc)

    @pl.when(pl.program_id(0) == pl.num_programs(0) - 1)
    def _():
        out[...] = acc[...].reshape(out.shape)


def own_grad_body(n_x, d_ref, w_ref, got, own, *rest):
    codes, acc = rest[:-1], rest[-1]
    partial_grad(d_ref, w_ref, acc)
    n, sub, enc = own.shape
    rows = n * sub

    @pl.when(pl.program_id(0) == pl.num_programs(0) - 1)
    def _():
        own[...] = acc[:rows].reshape(own.shape) + got[0]
        for d in range(1, n_x):
            full = acc[d * rows : (d + 1) * rows].reshape(n, sub, enc) + got[d]
            code, power = encode(full, (1, 2))
            out = codes[d - 1]
            for e in range(enc // LANES):
                out[e] = code[:, :, e * LANES : (e + 1) * LANES]
            note = jnp.broadcast_to(power.reshape(n, 1, 1), (n, sub, LANES))
            out[enc // LANES] = note.astype(jnp.int32).astype(jnp.int16)


def core_grad(d_kv, w_kv):
    n_x, n, sub, width = d_kv.shape
    enc = w_kv.shape[0]
    step = width // 4
    return pl.pallas_call(
        core_grad_body,
        out_shape=jax.ShapeDtypeStruct((n_x, n, sub, enc), F32),
        grid=(4,),
        in_specs=[
            pl.BlockSpec((n_x, n, sub, step), lambda i: (0, 0, 0, i)),
            pl.BlockSpec((enc, step), lambda i: (0, i)),
        ],
        out_specs=pl.BlockSpec((n_x, n, sub, enc), lambda i: (0, 0, 0, 0)),
        scratch_shapes=[pltpu.VMEM((n_x * n * sub, enc), F32)],
        compiler_params=params(),
        cost_estimate=cost(2 * n_x * n * sub * enc * width, 2 * (enc + n_x * n * sub) * width),
        name="core_grad",
    )(d_kv, w_kv)


def own_grad(d_kv, w_kv, got):
    n_x, n, sub, width = d_kv.shape
    enc = w_kv.shape[0]
    step = width // 4
    code = (enc // LANES + 1, n, sub, LANES)
    out = pl.pallas_call(
        functools.partial(own_grad_body, n_x),
        out_shape=[jax.ShapeDtypeStruct((n, sub, enc), F32)]
        + [jax.ShapeDtypeStruct(code, jnp.int16)] * (n_x - 1),
        grid=(4,),
        in_specs=[
            pl.BlockSpec((n_x, n, sub, step), lambda i: (0, 0, 0, i)),
            pl.BlockSpec((enc, step), lambda i: (0, i)),
            pl.BlockSpec((n_x, n, sub, enc), lambda i: (0, 0, 0, 0)),
        ],
        out_specs=[pl.BlockSpec((n, sub, enc), lambda i: (0, 0, 0))]
        + [pl.BlockSpec(code, lambda i: (0, 0, 0, 0))] * (n_x - 1),
        scratch_shapes=[pltpu.VMEM((n_x * n * sub, enc), F32)],
        compiler_params=params(),
        cost_estimate=cost(2 * n_x * n * sub * enc * width, 2 * (enc + n_x * n * sub) * width),
        name="own_grad",
    )(d_kv, w_kv, got)
    return out[0], out[1:]


def send_body(cap, position, own, *rest):
    codes, out, notes = rest[:-2], rest[-2], rest[-1]
    n, sub, enc = own.shape
    tiles = enc // LANES
    row = lax.broadcasted_iota(jnp.int32, (SUB, LANES), 0) // (SUB // cap)
    notes[...] = jnp.zeros_like(notes)
    for r in range(n):
        total = own[r]
        for code in codes:
            power = code[tiles, r].astype(F32)
            unit = jnp.exp2(power - 15.0)
            total = total + jnp.concatenate(
                [code[e, r].astype(F32) * unit for e in range(tiles)], axis=1
            )
        coded, power = encode(total, (0, 1))
        p = position[r]
        dest, slot = p // cap, p % cap
        for e in range(tiles):
            out[dest, slot * tiles + e] = coded[:, e * LANES : (e + 1) * LANES]
        mark = jnp.broadcast_to(power, (SUB, LANES)).astype(jnp.int32)
        notes[dest] = jnp.where(row == slot, mark, notes[dest])
    for d in range(out.shape[0]):
        out[d, cap * tiles] = notes[d].astype(jnp.int16)


def send_codes(position, own, codes, n_dp, cap):
    n, sub, enc = own.shape
    shape = (n_dp, cap * (enc // LANES) + 1, SUB, LANES)
    return pl.pallas_call(
        functools.partial(send_body, cap),
        out_shape=jax.ShapeDtypeStruct(shape, jnp.int16),
        in_specs=[SMEM, VMEM] + [VMEM] * len(codes),
        out_specs=VMEM,
        scratch_shapes=[pltpu.VMEM((n_dp, SUB, LANES), jnp.int32)],
        compiler_params=params(),
        cost_estimate=cost(10 * n * sub * enc, 6 * n * sub * enc + 2 * math.prod(shape)),
        name="send_codes",
    )(position, own, *codes)


def gather_body(cap, n_chunks, asked, *rest):
    arrived, out = rest[:n_chunks], rest[n_chunks]
    tiles = out.shape[2] // LANES
    out[...] = jnp.zeros_like(out)
    n_dp = arrived[0].shape[0]
    for d in range(n_dp):
        for s in range(cap):
            slab = asked[d * cap + s]

            @pl.when(slab >= 0)
            def _():
                for c in range(n_chunks):
                    ref = arrived[c]
                    note = ref[d, cap * tiles].astype(F32)
                    at = s * (SUB // cap)
                    unit = jnp.exp2(note[at : at + 1] - 15.0)
                    for e in range(tiles):
                        value = ref[d, s * tiles + e].astype(F32) * unit
                        out[slab, pl.ds(c * SUB, SUB), pl.ds(e * LANES, LANES)] += value


def gather_grads(asked, arrived, n_slabs, enc, cap):
    n_chunks = len(arrived)
    shape = (n_slabs, n_chunks * SUB, enc)
    return pl.pallas_call(
        functools.partial(gather_body, cap, n_chunks),
        out_shape=jax.ShapeDtypeStruct(shape, F32),
        in_specs=[SMEM] + [VMEM] * n_chunks,
        out_specs=VMEM,
        compiler_params=params(),
        cost_estimate=cost(0, 8 * math.prod(shape)),
        name="gather_grads",
    )(asked, *arrived)


def on_device(queries, cotangent, table, key_weight, value_weight, owners, slots):
    n_dp = lax.axis_size("dp")
    n_tp = lax.axis_size("tensor")
    n_x = n_tp // 2
    spans = owners.shape[0]
    n_requests = 2 * spans
    n_slabs, n_tokens, enc = table.shape
    cap = max(2, (4 * spans + n_dp - 1) // n_dp)
    share = n_tokens // n_tp
    n_chunks = share // SUB

    def over_core(x):
        return lax.ppermute(x, "tensor", [(t, t ^ 1) for t in range(n_tp)])

    def over_x(x, d):
        return lax.ppermute(x, "tensor", [(t, (t + 2 * d) % n_tp) for t in range(n_tp)])

    def over_dp(x):
        return lax.all_to_all(x, "dp", split_axis=0, concat_axis=0, tiled=True)

    owner_flat = owners.reshape(n_requests)
    slot_flat = slots.reshape(n_requests)
    onehot = (owner_flat[:, None] == jnp.arange(n_dp, dtype=jnp.int32)[None, :]).astype(jnp.int32)
    within = jnp.sum((jnp.cumsum(onehot, axis=0) - onehot) * onehot, axis=1)
    position = owner_flat * cap + within
    wanted = jnp.full((n_dp * cap,), -1, jnp.int32).at[position].set(slot_flat)
    asked = over_dp(wanted.reshape(n_dp, cap)).reshape(-1)

    first = (lax.axis_index("tensor") * share).astype(jnp.int32).reshape(1)
    w_kv = jnp.concatenate([key_weight, value_weight], axis=1)
    groups = [[(0, 0), (1, 0)], [(0, d) for d in range(1, n_x)] + [(1, d) for d in range(1, n_x)]]

    kvs = []
    for sent in pack(asked, first, table, n_chunks):
        mine = compact(position, over_dp(sent))
        near = [mine, over_core(mine)]
        far = [over_x(mine, d) for d in range(1, n_x)]
        far = far + [over_core(x) for x in far]
        kvs += [project(near, w_kv), project(far, w_kv)]

    attended, d_query, d_own, d_core = attend(kvs, groups, n_x, n_chunks, queries, cotangent)

    got = [over_core(core_grad(d, w_kv)) for d in d_core]
    arrived = []
    for c in range(n_chunks):
        own, codes = own_grad(d_own[c], w_kv, got[c])
        codes = [over_x(code, n_x - d) for d, code in enumerate(codes, 1)]
        arrived.append(over_dp(send_codes(position, own, codes, n_dp, cap)))
    d_table = gather_grads(asked, arrived, n_slabs, enc, cap)
    return (attended, d_query, d_table)


def solution(mesh):
    in_specs = (
        P("dp", "tensor"),
        P("dp", "tensor"),
        P("dp", None, None),
        P(None, "tensor"),
        P(None, "tensor"),
        P("dp", None),
        P("dp", None),
    )
    out_specs = (P("dp", "tensor"), P("dp", "tensor"), P("dp", "tensor", None))
    return jax.shard_map(
        on_device, mesh=mesh, in_specs=in_specs, out_specs=out_specs, check_vma=False
    )
```

```python
import functools
import math

import jax
import jax.numpy as jnp
from jax import lax
from jax.experimental import pallas as pl
from jax.experimental.pallas import tpu as pltpu
from jax.sharding import PartitionSpec as P

HD = 128
SPAN = 64
SUB = 16
LANES = 128
VMEM_LIMIT = 56 * 1024 * 1024
F32 = jnp.float32
BF16 = jnp.bfloat16

ANY = pl.BlockSpec(memory_space=pl.ANY)
SMEM = pl.BlockSpec(memory_space=pltpu.SMEM)
VMEM = pl.BlockSpec(memory_space=pltpu.VMEM)


def params():
    return pltpu.CompilerParams(vmem_limit_bytes=VMEM_LIMIT)


def cost(flops, nbytes):
    return pl.CostEstimate(flops=int(flops), bytes_accessed=int(nbytes), transcendentals=0)


def pack_body(n_chunks, asked, first, table, *rest):
    outs, sem = rest[:n_chunks], rest[n_chunks]
    n = asked.shape[0]
    base = first[0]

    def each(act):
        for c in range(n_chunks):
            row = pl.multiple_of(base + c * SUB, SUB)
            for s in range(n):
                slab = asked[s]

                @pl.when(slab >= 0)
                def _():
                    act(
                        pltpu.make_async_copy(
                            table.at[slab, pl.ds(row, SUB)], outs[c].at[s], sem.at[c, s]
                        )
                    )

    each(lambda copy: copy.start())
    each(lambda copy: copy.wait())


def pack(asked, first, table, n_chunks):
    n = asked.shape[0]
    enc = table.shape[2]
    return pl.pallas_call(
        functools.partial(pack_body, n_chunks),
        out_shape=[jax.ShapeDtypeStruct((n, SUB, enc), table.dtype)] * n_chunks,
        in_specs=[SMEM, SMEM, ANY],
        out_specs=[VMEM] * n_chunks,
        scratch_shapes=[pltpu.SemaphoreType.DMA((n_chunks, n))],
        compiler_params=params(),
        cost_estimate=cost(0, 4 * n_chunks * n * SUB * enc),
        name="pack_rows",
    )(asked, first, table)


def compact_body(position, arrived, out, sem):
    n = position.shape[0]
    copies = [
        pltpu.make_async_copy(arrived.at[position[r]], out.at[r], sem.at[r]) for r in range(n)
    ]
    for copy in copies:
        copy.start()
    for copy in copies:
        copy.wait()


def compact(position, arrived):
    n = position.shape[0]
    shape = (n,) + arrived.shape[1:]
    return pl.pallas_call(
        compact_body,
        out_shape=jax.ShapeDtypeStruct(shape, arrived.dtype),
        in_specs=[SMEM, ANY],
        out_specs=VMEM,
        scratch_shapes=[pltpu.SemaphoreType.DMA((n,))],
        compiler_params=params(),
        cost_estimate=cost(0, 4 * math.prod(shape)),
        name="compact_rows",
    )(position, arrived)


def project_body(n_in, *refs):
    w, out = refs[n_in], refs[n_in + 1]
    n, sub, enc = refs[0].shape
    rows = jnp.concatenate([ref[...].reshape(n * sub, enc) for ref in refs[:n_in]], axis=0)
    res = jnp.dot(rows, w[...], preferred_element_type=F32)
    out[...] = res.astype(BF16).reshape(out.shape)


def project(pieces, w_kv):
    n_in = len(pieces)
    n, sub, enc = pieces[0].shape
    width = w_kv.shape[1]
    step = width // 4
    return pl.pallas_call(
        functools.partial(project_body, n_in),
        out_shape=jax.ShapeDtypeStruct((n_in, n, sub, width), BF16),
        grid=(4,),
        in_specs=[pl.BlockSpec((n, sub, enc), lambda i: (0, 0, 0))] * n_in
        + [pl.BlockSpec((enc, step), lambda i: (0, i))],
        out_specs=pl.BlockSpec((n_in, n, sub, step), lambda i: (0, 0, 0, i)),
        compiler_params=params(),
        cost_estimate=cost(
            2 * n_in * n * sub * enc * width, 2 * (n_in * n * sub * (enc + width) + enc * width)
        ),
        name="project",
    )(*pieces, w_kv)


def attend_body(places, n_kv, *refs):
    kvs = refs[:n_kv]
    q_ref, g_ref, att_ref, dq_ref = refs[n_kv : n_kv + 4]
    grads = refs[n_kv + 4 :]
    width = q_ref.shape[1]
    scale = 1.0 / math.sqrt(HD)
    heads = width // HD
    group = min(4, heads)

    def keys_of(col):
        parts = [ref[:, :, :, pl.ds(col, HD)].reshape(-1, HD) for ref in kvs]
        return jnp.concatenate(parts, axis=0)

    def put(col, grad):
        for at, (ref, i) in enumerate(places):
            block = grad[at * 2 * SUB : (at + 1) * 2 * SUB]
            grads[ref][i, :, :, pl.ds(col, HD)] = block.reshape(2, SUB, HD)

    last = (((1,), (1,)), ((), ()))
    first = (((0,), (0,)), ((), ()))

    def dot(a, b, dims=(((1,), (0,)), ((), ()))):
        return lax.dot_general(a, b, dims, preferred_element_type=F32)

    for h0 in range(0, heads, group):
        hs = range(h0, h0 + group)
        q = [q_ref[:, pl.ds(h * HD, HD)] for h in hs]
        g = [g_ref[:, pl.ds(h * HD, HD)] for h in hs]
        k = [keys_of(h * HD) for h in hs]
        v = [keys_of(width + h * HD) for h in hs]
        s = jnp.concatenate([dot(a, b, last) for a, b in zip(q, k)], axis=0) * scale
        dw = jnp.concatenate([dot(a, b, last) for a, b in zip(g, v)], axis=0)
        e = jnp.exp(s - jnp.max(s, axis=1, keepdims=True))
        p = e * (1.0 / jnp.sum(e, axis=1, keepdims=True))
        rs = jnp.sum(dw * p, axis=1, keepdims=True)
        w = p.astype(BF16)
        ds = (p * (dw - rs) * scale).astype(BF16)
        ws = [w[i * SPAN : (i + 1) * SPAN] for i in range(group)]
        dss = [ds[i * SPAN : (i + 1) * SPAN] for i in range(group)]
        att = [dot(a, b).astype(BF16) for a, b in zip(ws, v)]
        dq = [dot(a, b).astype(BF16) for a, b in zip(dss, k)]
        dk = [dot(a, b, first).astype(BF16) for a, b in zip(dss, q)]
        dv = [dot(a, b, first).astype(BF16) for a, b in zip(ws, g)]
        for i, h in enumerate(hs):
            att_ref[:, pl.ds(h * HD, HD)] = att[i]
            dq_ref[:, pl.ds(h * HD, HD)] = dq[i]
            put(h * HD, dk[i])
            put(width + h * HD, dv[i])


def attend(kvs, places, sizes, queries, cotangent):
    tokens, width = queries.shape
    spans = tokens // SPAN
    n = kvs[0].shape[1]
    rows = pl.BlockSpec((SPAN, width), lambda i: (i, 0))

    def kv_block(pieces):
        return pl.BlockSpec((pieces, 2, SUB, 2 * width), lambda i: (0, i, 0, 0))

    keys = len(places) * 2 * SUB
    out = pl.pallas_call(
        functools.partial(attend_body, places, len(kvs)),
        out_shape=[jax.ShapeDtypeStruct((tokens, width), BF16)] * 2
        + [jax.ShapeDtypeStruct((size, n, SUB, 2 * width), BF16) for size in sizes],
        grid=(spans,),
        in_specs=[kv_block(kv.shape[0]) for kv in kvs] + [rows, rows],
        out_specs=[rows, rows] + [kv_block(size) for size in sizes],
        compiler_params=params(),
        cost_estimate=cost(12 * tokens * width * keys, 8 * tokens * width + 8 * spans * keys * 2 * width),
        name="attend",
    )(*kvs, queries, cotangent)
    return out[0], out[1], out[2:]


def encode(x, axes):
    top = jnp.maximum(jnp.max(jnp.abs(x), axis=axes, keepdims=True), 1e-30)
    power = jnp.floor(jnp.log2(top)) + 1.0
    code = jnp.clip(jnp.round(x * jnp.exp2(15.0 - power)), -32767.0, 32767.0)
    return code.astype(jnp.int32).astype(jnp.int16), power


def grad_body(kind, *refs):
    d_ref, w_ref = refs[:2]
    acc = refs[-1]
    k = pl.program_id(0)
    pieces, n, sub, step = d_ref.shape
    rows = d_ref[...].reshape(pieces * n * sub, step)
    part = jnp.dot(rows, w_ref[...], preferred_element_type=F32)

    @pl.when(k == 0)
    def _():
        acc[...] = part

    @pl.when(k > 0)
    def _():
        acc[...] += part

    @pl.when(k == pl.num_programs(0) - 1)
    def _():
        full = acc[...].reshape(pieces, n, sub, acc.shape[1])
        if kind == "plain":
            refs[2][...] = full
        elif kind == "add":
            refs[3][...] = full + refs[2][...]
        else:
            for i in range(pieces):
                code, power = encode(full[i] + refs[2][i], (1, 2))
                out = refs[3 + i]
                tiles = out.shape[0] - 1
                for e in range(tiles):
                    out[e] = code[:, :, e * LANES : (e + 1) * LANES]
                note = jnp.broadcast_to(power.reshape(n, 1, 1), (n, sub, LANES))
                out[tiles] = note.astype(jnp.int32).astype(jnp.int16)


def grad(kind, d_kv, w_t, got=None):
    pieces, n, sub, width = d_kv.shape
    enc = w_t.shape[1]
    step = width // 4
    full = (pieces, n, sub, enc)
    whole = pl.BlockSpec(full, lambda i: (0, 0, 0, 0))
    if kind == "code":
        code = (enc // LANES + 1, n, sub, LANES)
        out_shape = [jax.ShapeDtypeStruct(code, jnp.int16)] * pieces
        out_specs = [pl.BlockSpec(code, lambda i: (0, 0, 0, 0))] * pieces
    else:
        out_shape, out_specs = jax.ShapeDtypeStruct(full, F32), whole
    return pl.pallas_call(
        functools.partial(grad_body, kind),
        out_shape=out_shape,
        grid=(4,),
        in_specs=[
            pl.BlockSpec((pieces, n, sub, step), lambda i: (0, 0, 0, i)),
            pl.BlockSpec((step, enc), lambda i: (i, 0)),
        ]
        + [whole] * (got is not None),
        out_specs=out_specs,
        scratch_shapes=[pltpu.VMEM((pieces * n * sub, enc), F32)],
        compiler_params=params(),
        cost_estimate=cost(2 * pieces * n * sub * enc * width, 2 * (enc + pieces * n * sub) * width),
        name="grad_" + kind,
    )(d_kv, w_t, *([] if got is None else [got]))


def send_body(cap, chunk, position, own, *rest):
    codes, out, notes = rest[:-2], rest[-2], rest[-1]
    n, sub, enc = own.shape[1:]
    tiles = enc // LANES
    row = lax.broadcasted_iota(jnp.int32, (SUB, LANES), 0) // (SUB // cap)
    notes[...] = jnp.zeros_like(notes)
    for r in range(n):
        total = own[chunk, r]
        for code in codes:
            power = code[tiles, r].astype(F32)
            unit = jnp.exp2(power - 15.0)
            total = total + jnp.concatenate(
                [code[e, r].astype(F32) * unit for e in range(tiles)], axis=1
            )
        coded, power = encode(total, (0, 1))
        p = position[r]
        dest, slot = p // cap, p % cap
        for e in range(tiles):
            out[dest, slot * tiles + e] = coded[:, e * LANES : (e + 1) * LANES]
        mark = jnp.broadcast_to(power, (SUB, LANES)).astype(jnp.int32)
        notes[dest] = jnp.where(row == slot, mark, notes[dest])
    for d in range(out.shape[0]):
        out[d, cap * tiles] = notes[d].astype(jnp.int16)


def send_codes(chunk, position, own, codes, n_dp, cap):
    n, sub, enc = own.shape[1:]
    shape = (n_dp, cap * (enc // LANES) + 1, SUB, LANES)
    return pl.pallas_call(
        functools.partial(send_body, cap, chunk),
        out_shape=jax.ShapeDtypeStruct(shape, jnp.int16),
        in_specs=[SMEM, VMEM] + [VMEM] * len(codes),
        out_specs=VMEM,
        scratch_shapes=[pltpu.VMEM((n_dp, SUB, LANES), jnp.int32)],
        compiler_params=params(),
        cost_estimate=cost(10 * n * sub * enc, 6 * n * sub * enc + 2 * math.prod(shape)),
        name="send_codes",
    )(position, own, *codes)


def gather_body(cap, n_chunks, asked, *rest):
    arrived, out = rest[:n_chunks], rest[n_chunks]
    tiles = out.shape[2] // LANES
    out[...] = jnp.zeros_like(out)
    n_dp = arrived[0].shape[0]
    for d in range(n_dp):
        for s in range(cap):
            slab = asked[d * cap + s]

            @pl.when(slab >= 0)
            def _():
                for c in range(n_chunks):
                    ref = arrived[c]
                    note = ref[d, cap * tiles].astype(F32)
                    at = s * (SUB // cap)
                    unit = jnp.exp2(note[at : at + 1] - 15.0)
                    for e in range(tiles):
                        value = ref[d, s * tiles + e].astype(F32) * unit
                        out[slab, pl.ds(c * SUB, SUB), pl.ds(e * LANES, LANES)] += value


def gather_grads(asked, arrived, n_slabs, enc, cap):
    n_chunks = len(arrived)
    shape = (n_slabs, n_chunks * SUB, enc)
    return pl.pallas_call(
        functools.partial(gather_body, cap, n_chunks),
        out_shape=jax.ShapeDtypeStruct(shape, F32),
        in_specs=[SMEM] + [VMEM] * n_chunks,
        out_specs=VMEM,
        compiler_params=params(),
        cost_estimate=cost(0, 8 * math.prod(shape)),
        name="gather_grads",
    )(asked, *arrived)


def on_device(queries, cotangent, table, key_weight, value_weight, owners, slots):
    n_dp = lax.axis_size("dp")
    n_tp = lax.axis_size("tensor")
    n_x = n_tp // 2
    spans = owners.shape[0]
    n_requests = 2 * spans
    n_slabs, n_tokens, enc = table.shape
    cap = max(2, (4 * spans + n_dp - 1) // n_dp)
    share = n_tokens // n_tp
    n_chunks = share // SUB

    def over_core(x):
        return lax.ppermute(x, "tensor", [(t, t ^ 1) for t in range(n_tp)])

    def over_x(x, d):
        return lax.ppermute(x, "tensor", [(t, (t + 2 * d) % n_tp) for t in range(n_tp)])

    def over_dp(x):
        return lax.all_to_all(x, "dp", split_axis=0, concat_axis=0, tiled=True)

    owner_flat = owners.reshape(n_requests)
    slot_flat = slots.reshape(n_requests)
    onehot = (owner_flat[:, None] == jnp.arange(n_dp, dtype=jnp.int32)[None, :]).astype(jnp.int32)
    within = jnp.sum((jnp.cumsum(onehot, axis=0) - onehot) * onehot, axis=1)
    position = owner_flat * cap + within
    wanted = jnp.full((n_dp * cap,), -1, jnp.int32).at[position].set(slot_flat)
    asked = over_dp(wanted.reshape(n_dp, cap)).reshape(-1)

    first = (lax.axis_index("tensor") * share).astype(jnp.int32).reshape(1)
    w_kv = jnp.concatenate([key_weight, value_weight], axis=1)
    w_t = w_kv.T

    def place(c, kind, d):
        return (kind, c) if d == 0 else (2 + kind, c * (n_x - 1) + d - 1)

    kvs, places = [], []
    for c, sent in enumerate(pack(asked, first, table, n_chunks)):
        mine = compact(position, over_dp(sent))
        near = [mine, over_core(mine)]
        far = [over_x(mine, d) for d in range(1, n_x)]
        far = far + [over_core(x) for x in far]
        near_at = [place(c, kind, 0) for kind in range(2)]
        far_at = [place(c, kind, d) for kind in range(2) for d in range(1, n_x)]
        if c < n_chunks - 1:
            kvs.append(project(near + far, w_kv))
        else:
            kvs += [project(near, w_kv), project(far, w_kv)]
        places += near_at + far_at

    sizes = [n_chunks, n_chunks, n_chunks * (n_x - 1), n_chunks * (n_x - 1)]
    attended, d_query, grads = attend(kvs, places, sizes, queries, cotangent)
    own_near, core_near, own_far, core_far = grads

    far_got = over_core(grad("plain", core_far, w_t))
    near_got = over_core(grad("plain", core_near, w_t))
    codes = grad("code", own_far, w_t, far_got)
    own = grad("add", own_near, w_t, near_got)
    arrived = []
    for c in range(n_chunks):
        got = [over_x(codes[c * (n_x - 1) + d - 1], n_x - d) for d in range(1, n_x)]
        arrived.append(over_dp(send_codes(c, position, own, got, n_dp, cap)))
    d_table = gather_grads(asked, arrived, n_slabs, enc, cap)
    return (attended, d_query, d_table)


def solution(mesh):
    in_specs = (
        P("dp", "tensor"),
        P("dp", "tensor"),
        P("dp", None, None),
        P(None, "tensor"),
        P(None, "tensor"),
        P("dp", None),
        P("dp", None),
    )
    out_specs = (P("dp", "tensor"), P("dp", "tensor"), P("dp", "tensor", None))
    return jax.shard_map(
        on_device, mesh=mesh, in_specs=in_specs, out_specs=out_specs, check_vma=False
    )
```

```python
import functools
import math

import jax
import jax.numpy as jnp
from jax import lax
from jax.experimental import pallas as pl
from jax.experimental.pallas import tpu as pltpu
from jax.sharding import PartitionSpec as P

HD = 128
SPAN = 64
SUB = 16
LANES = 128
VMEM_LIMIT = 56 * 1024 * 1024
F32 = jnp.float32
BF16 = jnp.bfloat16

ANY = pl.BlockSpec(memory_space=pl.ANY)
SMEM = pl.BlockSpec(memory_space=pltpu.SMEM)
VMEM = pl.BlockSpec(memory_space=pltpu.VMEM)


def params():
    return pltpu.CompilerParams(vmem_limit_bytes=VMEM_LIMIT)


def cost(flops, nbytes):
    return pl.CostEstimate(flops=int(flops), bytes_accessed=int(nbytes), transcendentals=0)


def ask_body(cap, owners, slots, position, wanted, count):
    spans, two = owners.shape
    for i in range(wanted.shape[0]):
        wanted[i] = -1
    for i in range(wanted.shape[0] // cap):
        count[i] = 0
    for r in range(spans * two):
        owner = owners[r // two, r % two]
        at = owner * cap + count[owner]
        count[owner] = count[owner] + 1
        position[r] = at
        wanted[at] = slots[r // two, r % two]


def ask(owners, slots, n_dp, cap):
    return pl.pallas_call(
        functools.partial(ask_body, cap),
        out_shape=[
            jax.ShapeDtypeStruct((owners.size,), jnp.int32),
            jax.ShapeDtypeStruct((n_dp * cap,), jnp.int32),
        ],
        in_specs=[SMEM, SMEM],
        out_specs=[SMEM, SMEM],
        scratch_shapes=[pltpu.SMEM((n_dp,), jnp.int32)],
        name="ask",
    )(owners, slots)


def pack_body(n_chunks, asked, first, table, *rest):
    outs, sem = rest[:n_chunks], rest[n_chunks]
    n = asked.shape[0]
    base = first[0]

    def each(act):
        for c in range(n_chunks):
            row = pl.multiple_of(base + c * SUB, SUB)
            for s in range(n):
                slab = asked[s]

                @pl.when(slab >= 0)
                def _():
                    act(
                        pltpu.make_async_copy(
                            table.at[slab, pl.ds(row, SUB)], outs[c].at[s], sem.at[c, s]
                        )
                    )

    each(lambda copy: copy.start())
    each(lambda copy: copy.wait())


def pack(asked, first, table, n_chunks):
    n = asked.shape[0]
    enc = table.shape[2]
    return pl.pallas_call(
        functools.partial(pack_body, n_chunks),
        out_shape=[jax.ShapeDtypeStruct((n, SUB, enc), table.dtype)] * n_chunks,
        in_specs=[SMEM, SMEM, ANY],
        out_specs=[VMEM] * n_chunks,
        scratch_shapes=[pltpu.SemaphoreType.DMA((n_chunks, n))],
        compiler_params=params(),
        cost_estimate=cost(0, 4 * n_chunks * n * SUB * enc),
        name="pack_rows",
    )(asked, first, table)


def compact_body(position, arrived, out, sem):
    n = position.shape[0]
    copies = [
        pltpu.make_async_copy(arrived.at[position[r]], out.at[r], sem.at[r]) for r in range(n)
    ]
    for copy in copies:
        copy.start()
    for copy in copies:
        copy.wait()


def compact(position, arrived):
    n = position.shape[0]
    shape = (n,) + arrived.shape[1:]
    return pl.pallas_call(
        compact_body,
        out_shape=jax.ShapeDtypeStruct(shape, arrived.dtype),
        in_specs=[SMEM, ANY],
        out_specs=VMEM,
        scratch_shapes=[pltpu.SemaphoreType.DMA((n,))],
        compiler_params=params(),
        cost_estimate=cost(0, 4 * math.prod(shape)),
        name="compact_rows",
    )(position, arrived)


def weight_specs(rows, step, first=0):
    return [
        pl.BlockSpec((rows, step), lambda i: (first, jnp.minimum(i, 1))),
        pl.BlockSpec((rows, step), lambda i: (first, jnp.maximum(i - 2, 0))),
    ]


def project_body(n_in, *refs):
    wk, wv, out = refs[n_in : n_in + 3]
    n, sub, enc = refs[0].shape
    w = jnp.where(pl.program_id(0) < 2, wk[...], wv[...])
    rows = jnp.concatenate([ref[...].reshape(n * sub, enc) for ref in refs[:n_in]], axis=0)
    res = jnp.dot(rows, w, preferred_element_type=F32)
    out[...] = res.astype(BF16).reshape(out.shape)


def project(pieces, wk, wv):
    n_in = len(pieces)
    n, sub, enc = pieces[0].shape
    width = 2 * wk.shape[1]
    step = width // 4
    return pl.pallas_call(
        functools.partial(project_body, n_in),
        out_shape=jax.ShapeDtypeStruct((n_in, n, sub, width), BF16),
        grid=(4,),
        in_specs=[pl.BlockSpec((n, sub, enc), lambda i: (0, 0, 0))] * n_in
        + weight_specs(enc, step),
        out_specs=pl.BlockSpec((n_in, n, sub, step), lambda i: (0, 0, 0, i)),
        compiler_params=params(),
        cost_estimate=cost(
            2 * n_in * n * sub * enc * width, 2 * (n_in * n * sub * (enc + width) + enc * width)
        ),
        name="project",
    )(*pieces, wk, wv)


def attend_body(places, n_kv, *refs):
    kvs = refs[:n_kv]
    q_ref, g_ref, att_ref, dq_ref = refs[n_kv : n_kv + 4]
    grads = refs[n_kv + 4 :]
    width = q_ref.shape[1]
    scale = 1.0 / math.sqrt(HD)
    heads = width // HD
    group = min(4, heads)

    def keys_of(col):
        parts = [ref[:, :, :, pl.ds(col, HD)].reshape(-1, HD) for ref in kvs]
        return jnp.concatenate(parts, axis=0)

    def put(col, grad):
        for at, (ref, i) in enumerate(places):
            block = grad[at * 2 * SUB : (at + 1) * 2 * SUB]
            grads[ref][i, :, :, pl.ds(col, HD)] = block.reshape(2, SUB, HD)

    last = (((1,), (1,)), ((), ()))
    first = (((0,), (0,)), ((), ()))

    def dot(a, b, dims=(((1,), (0,)), ((), ()))):
        return lax.dot_general(a, b, dims, preferred_element_type=F32)

    for h0 in range(0, heads, group):
        hs = range(h0, h0 + group)
        q = [q_ref[:, pl.ds(h * HD, HD)] for h in hs]
        g = [g_ref[:, pl.ds(h * HD, HD)] for h in hs]
        k = [keys_of(h * HD) for h in hs]
        v = [keys_of(width + h * HD) for h in hs]
        s = jnp.concatenate([dot(a, b, last) for a, b in zip(q, k)], axis=0) * scale
        dw = jnp.concatenate([dot(a, b, last) for a, b in zip(g, v)], axis=0)
        e = jnp.exp(s - jnp.max(s, axis=1, keepdims=True))
        p = e * (1.0 / jnp.sum(e, axis=1, keepdims=True))
        rs = jnp.sum(dw * p, axis=1, keepdims=True)
        w = p.astype(BF16)
        ds = (p * (dw - rs) * scale).astype(BF16)
        ws = [w[i * SPAN : (i + 1) * SPAN] for i in range(group)]
        dss = [ds[i * SPAN : (i + 1) * SPAN] for i in range(group)]
        att = [dot(a, b).astype(BF16) for a, b in zip(ws, v)]
        dq = [dot(a, b).astype(BF16) for a, b in zip(dss, k)]
        dk = [dot(a, b, first).astype(BF16) for a, b in zip(dss, q)]
        dv = [dot(a, b, first).astype(BF16) for a, b in zip(ws, g)]
        for i, h in enumerate(hs):
            att_ref[:, pl.ds(h * HD, HD)] = att[i]
            dq_ref[:, pl.ds(h * HD, HD)] = dq[i]
            put(h * HD, dk[i])
            put(width + h * HD, dv[i])


def attend(kvs, places, sizes, queries, cotangent):
    tokens, width = queries.shape
    spans = tokens // SPAN
    n = kvs[0].shape[1]
    rows = pl.BlockSpec((SPAN, width), lambda i: (i, 0))

    def kv_block(pieces):
        return pl.BlockSpec((pieces, 2, SUB, 2 * width), lambda i: (0, i, 0, 0))

    keys = len(places) * 2 * SUB
    out = pl.pallas_call(
        functools.partial(attend_body, places, len(kvs)),
        out_shape=[jax.ShapeDtypeStruct((tokens, width), BF16)] * 2
        + [jax.ShapeDtypeStruct((size, n, SUB, 2 * width), BF16) for size in sizes],
        grid=(spans,),
        in_specs=[kv_block(kv.shape[0]) for kv in kvs] + [rows, rows],
        out_specs=[rows, rows] + [kv_block(size) for size in sizes],
        compiler_params=params(),
        cost_estimate=cost(12 * tokens * width * keys, 8 * tokens * width + 8 * spans * keys * 2 * width),
        name="attend",
    )(*kvs, queries, cotangent)
    return out[0], out[1], out[2:]


def encode(x, axes):
    top = jnp.maximum(jnp.max(jnp.abs(x), axis=axes, keepdims=True), 1e-30)
    power = jnp.floor(jnp.log2(top)) + 1.0
    code = jnp.clip(jnp.round(x * jnp.exp2(15.0 - power)), -32767.0, 32767.0)
    return code.astype(jnp.int32).astype(jnp.int16), power


def grad_step(d_ref, wk, wv, acc):
    i = pl.program_id(0)
    pieces, n, sub, step = d_ref.shape
    w = jnp.where(i < 2, wk[...], wv[...])
    rows = d_ref[...].reshape(pieces * n * sub, step)
    part = lax.dot_general(rows, w, (((1,), (1,)), ((), ())), preferred_element_type=F32)

    @pl.when(i == 0)
    def _():
        acc[...] = part

    @pl.when(i > 0)
    def _():
        acc[...] += part


def core_grad_body(near, d_ref, wk, wv, near_out, far_out, acc):
    grad_step(d_ref, wk, wv, acc)

    @pl.when(pl.program_id(0) == pl.num_programs(0) - 1)
    def _():
        full = acc[...].reshape(d_ref.shape[:3] + acc.shape[1:])
        near_out[...] = full[:near]
        far_out[...] = full[near:]


def own_grad_body(near, d_ref, wk, wv, near_got, far_got, near_out, *rest):
    codes, acc = rest[:-1], rest[-1]
    grad_step(d_ref, wk, wv, acc)

    @pl.when(pl.program_id(0) == pl.num_programs(0) - 1)
    def _():
        full = acc[...].reshape(d_ref.shape[:3] + acc.shape[1:])
        near_out[...] = full[:near] + near_got[...]
        for i in range(far_got.shape[0]):
            out, c = codes[i // near], i % near
            tiles, n = out.shape[1] - 1, out.shape[2]
            code, power = encode(full[near + i] + far_got[i], (1, 2))
            for e in range(tiles):
                out[c, e] = code[:, :, e * LANES : (e + 1) * LANES]
            note = jnp.broadcast_to(power.reshape(n, 1, 1), out.shape[2:])
            out[c, tiles] = note.astype(jnp.int32).astype(jnp.int16)


def grads_of(d_kv, wk, wv, near, cols, got=None):
    pieces, n, sub, width = d_kv.shape
    far = pieces - near
    first, count = cols
    step = width // 4
    tiles = count // LANES
    near_shape, far_shape = (near, n, sub, count), (far, n, sub, count)

    def whole(shape):
        return pl.BlockSpec(shape, lambda i: (0,) * len(shape))

    if got is None:
        body, outs = core_grad_body, [(near_shape, F32), (far_shape, F32)]
    else:
        body = own_grad_body
        outs = [(near_shape, F32)] + [((near, tiles + 1, n, sub, LANES), jnp.int16)] * (far // near)
    out = pl.pallas_call(
        functools.partial(body, near),
        out_shape=[jax.ShapeDtypeStruct(*o) for o in outs],
        grid=(4,),
        in_specs=[pl.BlockSpec((pieces, n, sub, step), lambda i: (0, 0, 0, i))]
        + weight_specs(count, step)
        + ([] if got is None else [whole(near_shape), whole(far_shape)]),
        out_specs=[whole(shape) for shape, _ in outs],
        scratch_shapes=[pltpu.VMEM((pieces * n * sub, count), F32)],
        compiler_params=params(),
        cost_estimate=cost(2 * pieces * n * sub * count * width, 2 * (count + pieces * n * sub) * width),
        name="core_grads" if got is None else "own_grads",
    )(
        d_kv,
        wk[first : first + count],
        wv[first : first + count],
        *([] if got is None else got),
    )
    return out[0], out[1:]


def send_body(cap, position, own, *rest):
    codes, out, notes = rest[:-2], rest[-2], rest[-1]
    n_chunks, n, sub, count = own.shape
    tiles = count // LANES
    row = lax.broadcasted_iota(jnp.int32, (SUB, LANES), 0)
    notes[...] = jnp.zeros_like(notes)
    for r in range(n):
        p = position[r]
        dest, slot = p // cap, p % cap
        for c in range(n_chunks):
            total = own[c, r]
            for code in codes:
                unit = jnp.exp2(code[c, tiles, r].astype(F32) - 15.0)
                total = total + jnp.concatenate(
                    [code[c, e, r].astype(F32) * unit for e in range(tiles)], axis=1
                )
            coded, power = encode(total, (0, 1))
            mine = slot * n_chunks + c
            for e in range(tiles):
                out[dest, mine * tiles + e] = coded[:, e * LANES : (e + 1) * LANES]
            mark = jnp.broadcast_to(power, (SUB, LANES)).astype(jnp.int32)
            notes[dest] = jnp.where(row == mine, mark, notes[dest])
    for d in range(out.shape[0]):
        out[d, cap * n_chunks * tiles] = notes[d].astype(jnp.int16)


def send_codes(position, own, codes, n_dp, cap):
    n_chunks, n, sub, count = own.shape
    shape = (n_dp, cap * n_chunks * (count // LANES) + 1, SUB, LANES)
    return pl.pallas_call(
        functools.partial(send_body, cap),
        out_shape=jax.ShapeDtypeStruct(shape, jnp.int16),
        in_specs=[SMEM, VMEM] + [VMEM] * len(codes),
        out_specs=VMEM,
        scratch_shapes=[pltpu.VMEM((n_dp, SUB, LANES), jnp.int32)],
        compiler_params=params(),
        cost_estimate=cost(10 * own.size, 6 * own.size + 2 * math.prod(shape)),
        name="send_codes",
    )(position, own, *codes)


def gather_body(cap, n_chunks, first, asked, arrived, *rest):
    out, total, sem = rest[-3:]
    count = total.shape[2]
    tiles = count // LANES
    total[...] = jnp.zeros_like(total)
    for d in range(arrived.shape[0]):
        for s in range(cap):
            slab = asked[d * cap + s]

            @pl.when(slab >= 0)
            def _():
                note = arrived[d, cap * n_chunks * tiles].astype(F32)
                for c in range(n_chunks):
                    at = s * n_chunks + c
                    unit = jnp.exp2(note[at : at + 1] - 15.0)
                    for e in range(tiles):
                        value = arrived[d, at * tiles + e].astype(F32) * unit
                        total[slab, pl.ds(c * SUB, SUB), pl.ds(e * LANES, LANES)] += value

    copy = pltpu.make_async_copy(total, out.at[:, :, pl.ds(first, count)], sem)
    copy.start()
    copy.wait()


def gather_grads(asked, arrived, n_slabs, n_chunks, enc, cap, cols, before):
    first, count = cols
    rows = n_chunks * SUB
    return pl.pallas_call(
        functools.partial(gather_body, cap, n_chunks, first),
        out_shape=jax.ShapeDtypeStruct((n_slabs, rows, enc), F32),
        in_specs=[SMEM, VMEM] + [ANY] * (before is not None),
        out_specs=ANY,
        scratch_shapes=[pltpu.VMEM((n_slabs, rows, count), F32), pltpu.SemaphoreType.DMA],
        input_output_aliases={} if before is None else {2: 0},
        compiler_params=params(),
        cost_estimate=cost(0, 8 * n_slabs * rows * count),
        name="gather_grads",
    )(asked, arrived, *([] if before is None else [before]))


def on_device(queries, cotangent, table, key_weight, value_weight, owners, slots):
    n_dp = lax.axis_size("dp")
    n_tp = lax.axis_size("tensor")
    n_x = n_tp // 2
    spans = owners.shape[0]
    n_requests = 2 * spans
    n_slabs, n_tokens, enc = table.shape
    cap = max(2, (4 * spans + n_dp - 1) // n_dp)
    share = n_tokens // n_tp
    n_chunks = share // SUB

    def over_core(x):
        return lax.ppermute(x, "tensor", [(t, t ^ 1) for t in range(n_tp)])

    def over_x(x, d):
        return lax.ppermute(x, "tensor", [(t, (t + 2 * d) % n_tp) for t in range(n_tp)])

    def over_dp(x):
        return lax.all_to_all(x, "dp", split_axis=0, concat_axis=0, tiled=True)

    position, wanted = ask(owners, slots, n_dp, cap)
    asked = over_dp(wanted.reshape(n_dp, cap)).reshape(-1)

    first = (lax.axis_index("tensor") * share).astype(jnp.int32).reshape(1)

    def place(c, kind, d):
        return (kind, c if d == 0 else n_chunks * d + c)

    kvs, places = [], []
    for c, sent in enumerate(pack(asked, first, table, n_chunks)):
        got = over_dp(sent)
        if kvs:
            got, kvs = lax.optimization_barrier((got, kvs))
        mine = compact(position, got)
        near = [mine, over_core(mine)]
        far = [over_x(mine, d) for d in range(1, n_x)]
        far = far + [over_core(x) for x in far]
        near_at = [place(c, kind, 0) for kind in range(2)]
        far_at = [place(c, kind, d) for kind in range(2) for d in range(1, n_x)]
        if c < n_chunks - 1:
            kvs = kvs + [project(near + far, key_weight, value_weight)]
        else:
            kvs = kvs + [project(x, key_weight, value_weight) for x in (near, far)]
        places += near_at + far_at

    sizes = [n_chunks * n_x, n_chunks * n_x]
    attended, d_query, (d_own, d_core) = attend(kvs, places, sizes, queries, cotangent)

    lead = 2 * LANES
    d_table = None
    for cols in ((0, lead), (lead, enc - lead)):
        grads = grads_of(d_core, key_weight, value_weight, n_chunks, cols)
        got = over_core(grads[0]), over_core(grads[1][0])
        own, codes = grads_of(d_own, key_weight, value_weight, n_chunks, cols, got)
        codes = [over_x(code, n_x - d) for d, code in enumerate(codes, 1)]
        arrived = over_dp(send_codes(position, own, codes, n_dp, cap))
        d_table = gather_grads(asked, arrived, n_slabs, n_chunks, enc, cap, cols, d_table)
    return (attended, d_query, d_table)


def solution(mesh):
    in_specs = (
        P("dp", "tensor"),
        P("dp", "tensor"),
        P("dp", None, None),
        P(None, "tensor"),
        P(None, "tensor"),
        P("dp", None),
        P("dp", None),
    )
    out_specs = (P("dp", "tensor"), P("dp", "tensor"), P("dp", "tensor", None))
    return jax.shard_map(
        on_device, mesh=mesh, in_specs=in_specs, out_specs=out_specs, check_vma=False
    )
```

```python
import functools
import math

import jax
import jax.numpy as jnp
from jax import lax
from jax.experimental import pallas as pl
from jax.experimental.pallas import tpu as pltpu
from jax.sharding import PartitionSpec as P

HD = 128
SPAN = 64
SUB = 16
LANES = 128
VMEM_LIMIT = 28 * 1024 * 1024
F32 = jnp.float32
BF16 = jnp.bfloat16

ANY = pl.BlockSpec(memory_space=pl.ANY)
SMEM = pl.BlockSpec(memory_space=pltpu.SMEM)
VMEM = pl.BlockSpec(memory_space=pltpu.VMEM)


def params():
    return pltpu.CompilerParams(vmem_limit_bytes=VMEM_LIMIT)


def cost(flops, nbytes):
    return pl.CostEstimate(flops=int(flops), bytes_accessed=int(nbytes), transcendentals=0)


def ask_body(cap, me, owners, slots, wanted, request, count):
    n_dp = wanted.shape[0] // cap
    for i in range(n_dp * cap):
        wanted[i] = -1
        request[i] = -1
    for d in range(n_dp):
        count[d] = 0
    for r in range(owners.size):
        d = owners[r % 2, r // 2] - me[0]
        d = jnp.where(d < 0, d + n_dp, d)
        j = count[d]
        count[d] = j + 1
        wanted[d * cap + j] = slots[r % 2, r // 2]
        request[d * cap + j] = r


def ask(me, owners, slots, n_dp, cap):
    shape = jax.ShapeDtypeStruct((n_dp * cap,), jnp.int32)
    return pl.pallas_call(
        functools.partial(ask_body, cap),
        out_shape=[shape, shape],
        in_specs=[SMEM, SMEM, SMEM],
        out_specs=[SMEM, SMEM],
        scratch_shapes=[pltpu.SMEM((n_dp,), jnp.int32)],
        name="ask",
    )(me, owners.T, slots.T)


def pack_body(n_dp, n_chunks, *refs):
    asked, (first, table), rest = refs[:n_dp], refs[n_dp : n_dp + 2], refs[n_dp + 2 :]
    outs, sem = rest[:-1], rest[-1]
    cap = outs[0].shape[0]

    def each(act):
        for c in range(n_chunks):
            row = pl.multiple_of(first[0] + c * SUB, SUB)
            for d in range(n_dp):
                for j in range(cap):
                    slab = asked[d][d * cap + j]

                    @pl.when(slab >= 0)
                    def _():
                        act(
                            pltpu.make_async_copy(
                                table.at[slab, pl.ds(row, SUB)],
                                outs[c * n_dp + d].at[j],
                                sem.at[c, d * cap + j],
                            )
                        )

    each(lambda copy: copy.start())
    each(lambda copy: copy.wait())


def pack(asked, first, table, n_chunks, cap):
    n_dp = len(asked)
    enc = table.shape[2]
    return pl.pallas_call(
        functools.partial(pack_body, n_dp, n_chunks),
        out_shape=[jax.ShapeDtypeStruct((cap, SUB, enc), table.dtype)] * (n_chunks * n_dp),
        in_specs=[SMEM] * n_dp + [SMEM, ANY],
        out_specs=[VMEM] * (n_chunks * n_dp),
        scratch_shapes=[pltpu.SemaphoreType.DMA((n_chunks, n_dp * cap))],
        compiler_params=params(),
        cost_estimate=cost(0, 4 * n_chunks * n_dp * cap * SUB * enc),
        name="pack_rows",
    )(*asked, first, table)


def compact_body(n_dp, request, *refs):
    arrived, out, sem = refs[:n_dp], refs[n_dp], refs[n_dp + 1]
    cap = arrived[0].shape[0]

    def each(act):
        for d in range(n_dp):
            for j in range(cap):
                r = request[d * cap + j]

                @pl.when(r >= 0)
                def _():
                    act(pltpu.make_async_copy(arrived[d].at[j], out.at[r], sem.at[d * cap + j]))

    each(lambda copy: copy.start())
    each(lambda copy: copy.wait())


def compact(request, arrived, n):
    shape = (n,) + arrived[0].shape[1:]
    return pl.pallas_call(
        functools.partial(compact_body, len(arrived)),
        out_shape=jax.ShapeDtypeStruct(shape, arrived[0].dtype),
        in_specs=[SMEM] + [ANY] * len(arrived),
        out_specs=VMEM,
        scratch_shapes=[pltpu.SemaphoreType.DMA((request.shape[0],))],
        compiler_params=params(),
        cost_estimate=cost(0, 4 * math.prod(shape)),
        name="compact_rows",
    )(request, *arrived)


def weight_specs(rows, step):
    return [
        pl.BlockSpec((rows, step), lambda i: (0, jnp.minimum(i, 1))),
        pl.BlockSpec((rows, step), lambda i: (0, jnp.maximum(i - 2, 0))),
    ]


def with_weight(wk, wv, act):
    @pl.when(pl.program_id(0) < 2)
    def _():
        act(wk)

    @pl.when(pl.program_id(0) >= 2)
    def _():
        act(wv)


def project_body(n_in, *refs):
    wk, wv, out = refs[n_in : n_in + 3]
    n, sub, enc = refs[0].shape
    rows = jnp.concatenate([ref[...].reshape(n * sub, enc) for ref in refs[:n_in]], axis=0)

    def act(w):
        res = jnp.dot(rows, w[...], preferred_element_type=F32)
        out[...] = res.astype(BF16).reshape(out.shape)

    with_weight(wk, wv, act)


def project(pieces, wk, wv):
    n_in = len(pieces)
    n, sub, enc = pieces[0].shape
    width = 2 * wk.shape[1]
    step = width // 4
    return pl.pallas_call(
        functools.partial(project_body, n_in),
        out_shape=jax.ShapeDtypeStruct((n_in, n, sub, width), BF16),
        grid=(4,),
        in_specs=[pl.BlockSpec((n, sub, enc), lambda i: (0, 0, 0))] * n_in
        + weight_specs(enc, step),
        out_specs=pl.BlockSpec((n_in, n, sub, step), lambda i: (0, 0, 0, i)),
        compiler_params=params(),
        cost_estimate=cost(
            2 * n_in * n * sub * enc * width, 2 * (n_in * n * sub * (enc + width) + enc * width)
        ),
        name="project",
    )(*pieces, wk, wv)


def attend_body(places, n_kv, *refs):
    kvs = refs[:n_kv]
    q_ref, g_ref, att_ref, dq_ref = refs[n_kv : n_kv + 4]
    grads = refs[n_kv + 4 :]
    width = q_ref.shape[1]
    scale = 1.0 / math.sqrt(HD)
    heads = width // HD
    group = min(4, heads)

    def keys_of(col):
        parts = [ref[:, :, :, pl.ds(col, HD)].reshape(-1, HD) for ref in kvs]
        return jnp.concatenate(parts, axis=0)

    def put(col, grad):
        for at, (ref, i) in enumerate(places):
            block = grad[at * 2 * SUB : (at + 1) * 2 * SUB]
            grads[ref][i, :, :, pl.ds(col, HD)] = block.reshape(2, SUB, HD)

    last = (((1,), (1,)), ((), ()))
    first = (((0,), (0,)), ((), ()))

    def dot(a, b, dims=(((1,), (0,)), ((), ()))):
        return lax.dot_general(a, b, dims, preferred_element_type=F32)

    for h0 in range(0, heads, group):
        hs = range(h0, h0 + group)
        q = [q_ref[:, pl.ds(h * HD, HD)] for h in hs]
        g = [g_ref[:, pl.ds(h * HD, HD)] for h in hs]
        k = [keys_of(h * HD) for h in hs]
        v = [keys_of(width + h * HD) for h in hs]
        s = jnp.concatenate([dot(a, b, last) for a, b in zip(q, k)], axis=0) * scale
        dw = jnp.concatenate([dot(a, b, last) for a, b in zip(g, v)], axis=0)
        e = jnp.exp(s - jnp.max(s, axis=1, keepdims=True))
        p = e * (1.0 / jnp.sum(e, axis=1, keepdims=True))
        rs = jnp.sum(dw * p, axis=1, keepdims=True)
        w = p.astype(BF16)
        ds = (p * (dw - rs) * scale).astype(BF16)
        ws = [w[i * SPAN : (i + 1) * SPAN] for i in range(group)]
        dss = [ds[i * SPAN : (i + 1) * SPAN] for i in range(group)]
        att = [dot(a, b).astype(BF16) for a, b in zip(ws, v)]
        dq = [dot(a, b).astype(BF16) for a, b in zip(dss, k)]
        dk = [dot(a, b, first).astype(BF16) for a, b in zip(dss, q)]
        dv = [dot(a, b, first).astype(BF16) for a, b in zip(ws, g)]
        for i, h in enumerate(hs):
            att_ref[:, pl.ds(h * HD, HD)] = att[i]
            dq_ref[:, pl.ds(h * HD, HD)] = dq[i]
            put(h * HD, dk[i])
            put(width + h * HD, dv[i])


def attend(kvs, places, sizes, queries, cotangent):
    tokens, width = queries.shape
    spans = tokens // SPAN
    n = kvs[0].shape[1]
    rows = pl.BlockSpec((SPAN, width), lambda i: (i, 0))

    def kv_block(pieces):
        return pl.BlockSpec((pieces, 2, SUB, 2 * width), lambda i: (0, i, 0, 0))

    keys = len(places) * 2 * SUB
    out = pl.pallas_call(
        functools.partial(attend_body, places, len(kvs)),
        out_shape=[jax.ShapeDtypeStruct((tokens, width), BF16)] * 2
        + [jax.ShapeDtypeStruct((size, n, SUB, 2 * width), BF16) for size in sizes],
        grid=(spans,),
        in_specs=[kv_block(kv.shape[0]) for kv in kvs] + [rows, rows],
        out_specs=[rows, rows] + [kv_block(size) for size in sizes],
        compiler_params=params(),
        cost_estimate=cost(12 * tokens * width * keys, 8 * tokens * width + 8 * spans * keys * 2 * width),
        name="attend",
    )(*kvs, queries, cotangent)
    return out[0], out[1], out[2:]


def encode(x, axes):
    top = jnp.maximum(jnp.max(jnp.abs(x), axis=axes, keepdims=True), 1e-30)
    power = jnp.floor(jnp.log2(top)) + 1.0
    code = jnp.clip(jnp.round(x * jnp.exp2(15.0 - power)), -32767.0, 32767.0)
    return code.astype(jnp.int32).astype(jnp.int16), power


def grad_step(first, d_ref, wk, wv, acc):
    i = pl.program_id(0)
    pieces, n, sub, step = d_ref.shape
    rows = d_ref[...].reshape(pieces * n * sub, step)

    def act(w):
        w = w[first : first + acc.shape[1], :]
        part = lax.dot_general(rows, w, (((1,), (1,)), ((), ())), preferred_element_type=F32)

        @pl.when(i == 0)
        def _():
            acc[...] = part

        @pl.when(i > 0)
        def _():
            acc[...] += part

    with_weight(wk, wv, act)


def core_grad_body(near, first, d_ref, wk, wv, near_out, far_out, acc):
    grad_step(first, d_ref, wk, wv, acc)

    @pl.when(pl.program_id(0) == pl.num_programs(0) - 1)
    def _():
        full = acc[...].reshape(d_ref.shape[:3] + acc.shape[1:])
        near_out[...] = full[:near]
        far_out[...] = full[near:]


def own_grad_body(near, first, d_ref, wk, wv, near_got, far_got, near_out, *rest):
    codes, acc = rest[:-1], rest[-1]
    grad_step(first, d_ref, wk, wv, acc)

    @pl.when(pl.program_id(0) == pl.num_programs(0) - 1)
    def _():
        full = acc[...].reshape(d_ref.shape[:3] + acc.shape[1:])
        near_out[...] = full[:near] + near_got[...]
        n = d_ref.shape[1]
        tiles = acc.shape[1] // LANES
        row = lax.broadcasted_iota(jnp.int32, (SUB, LANES), 0)
        for i in range(far_got.shape[0]):
            out, c = codes[i // near], i % near
            code, power = encode(full[near + i] + far_got[i], (1, 2))
            for e in range(tiles):
                out[c, e * n : (e + 1) * n] = code[:, :, e * LANES : (e + 1) * LANES]
            note = jnp.zeros((SUB, LANES), F32)
            for r in range(n):
                note = jnp.where(row == r, power[r], note)
            out[c, tiles * n] = note.astype(jnp.int32).astype(jnp.int16)


def grads_of(d_kv, wk, wv, near, cols, got=None):
    pieces, n, sub, width = d_kv.shape
    far = pieces - near
    first, count = cols
    step = width // 4
    tiles = count // LANES
    near_shape, far_shape = (near, n, sub, count), (far, n, sub, count)

    def whole(shape):
        return pl.BlockSpec(shape, lambda i: (0,) * len(shape))

    if got is None:
        body, outs = core_grad_body, [(near_shape, F32), (far_shape, F32)]
    else:
        body = own_grad_body
        outs = [(near_shape, F32)] + [((near, tiles * n + 1, sub, LANES), jnp.int16)] * (far // near)
    out = pl.pallas_call(
        functools.partial(body, near, first),
        out_shape=[jax.ShapeDtypeStruct(*o) for o in outs],
        grid=(4,),
        in_specs=[pl.BlockSpec((pieces, n, sub, step), lambda i: (0, 0, 0, i))]
        + weight_specs(wk.shape[0], step)
        + ([] if got is None else [whole(near_shape), whole(far_shape)]),
        out_specs=[whole(shape) for shape, _ in outs],
        scratch_shapes=[pltpu.VMEM((pieces * n * sub, count), F32)],
        compiler_params=params(),
        cost_estimate=cost(2 * pieces * n * sub * count * width, 2 * (count + pieces * n * sub) * width),
        name="core_grads" if got is None else "own_grads",
    )(
        d_kv,
        wk,
        wv,
        *([] if got is None else got),
    )
    return out[0], out[1:]


def send_body(n_dp, request, own, *rest):
    codes, outs, (stage, powers) = rest[: -n_dp - 2], rest[-n_dp - 2 : -2], rest[-2:]
    n_chunks, n, sub, count = own.shape
    tiles = count // LANES
    cap = request.shape[0] // n_dp
    for c in range(n_chunks):
        for r in range(n):
            total = own[c, r]
            for code in codes:
                unit = jnp.exp2(code[c, tiles * n].astype(F32)[r : r + 1] - 15.0)
                total = total + jnp.concatenate(
                    [code[c, e * n + r].astype(F32) * unit for e in range(tiles)], axis=1
                )
            coded, power = encode(total, (0, 1))
            for e in range(tiles):
                stage[r, c * tiles + e] = coded[:, e * LANES : (e + 1) * LANES]
            powers[r, c] = jnp.broadcast_to(power, (SUB, LANES))
    row = lax.broadcasted_iota(jnp.int32, (SUB, LANES), 0)
    for d in range(n_dp):
        note = jnp.zeros((SUB, LANES), F32)
        for j in range(cap):
            r = request[d * cap + j]

            @pl.when(r >= 0)
            def _():
                outs[d][pl.ds(j * n_chunks * tiles, n_chunks * tiles)] = stage[r]

            for c in range(n_chunks):
                note = jnp.where(row == j * n_chunks + c, powers[jnp.maximum(r, 0), c], note)
        outs[d][cap * n_chunks * tiles] = note.astype(jnp.int32).astype(jnp.int16)


def send_codes(request, own, codes, n_dp):
    n_chunks, n, sub, count = own.shape
    tiles = count // LANES
    cap = request.shape[0] // n_dp
    shape = (cap * n_chunks * tiles + 1, SUB, LANES)
    return pl.pallas_call(
        functools.partial(send_body, n_dp),
        out_shape=[jax.ShapeDtypeStruct(shape, jnp.int16)] * n_dp,
        in_specs=[SMEM, VMEM] + [VMEM] * len(codes),
        out_specs=[VMEM] * n_dp,
        scratch_shapes=[
            pltpu.VMEM((n, n_chunks * tiles, SUB, LANES), jnp.int16),
            pltpu.VMEM((n, n_chunks, SUB, LANES), F32),
        ],
        compiler_params=params(),
        cost_estimate=cost(10 * own.size, 6 * own.size + 2 * n_dp * math.prod(shape)),
        name="send_codes",
    )(request, own, *codes)


def gather_body(n_dp, n_chunks, first, *refs):
    asked, arrived = refs[:n_dp], refs[n_dp : 2 * n_dp]
    out, total, sem = refs[-3:]
    count = total.shape[2]
    tiles = count // LANES
    cap = asked[0].shape[0] // n_dp
    total[...] = jnp.zeros_like(total)
    for d in range(n_dp):
        for j in range(cap):
            slab = asked[d][d * cap + j]

            @pl.when(slab >= 0)
            def _():
                note = arrived[d][cap * n_chunks * tiles].astype(F32)
                for c in range(n_chunks):
                    at = j * n_chunks + c
                    unit = jnp.exp2(note[at : at + 1] - 15.0)
                    for e in range(tiles):
                        value = arrived[d][at * tiles + e].astype(F32) * unit
                        total[slab, pl.ds(c * SUB, SUB), pl.ds(e * LANES, LANES)] += value

    copy = pltpu.make_async_copy(total, out.at[:, :, pl.ds(first, count)], sem)
    copy.start()
    copy.wait()


def gather_grads(asked, arrived, n_slabs, n_chunks, enc, cols, before):
    first, count = cols
    n_dp = len(asked)
    rows = n_chunks * SUB
    return pl.pallas_call(
        functools.partial(gather_body, n_dp, n_chunks, first),
        out_shape=jax.ShapeDtypeStruct((n_slabs, rows, enc), F32),
        in_specs=[SMEM] * n_dp + [VMEM] * n_dp + [ANY] * (before is not None),
        out_specs=ANY,
        scratch_shapes=[pltpu.VMEM((n_slabs, rows, count), F32), pltpu.SemaphoreType.DMA],
        input_output_aliases={} if before is None else {2 * n_dp: 0},
        compiler_params=params(),
        cost_estimate=cost(0, 8 * n_slabs * rows * count),
        name="gather_grads",
    )(*asked, *arrived, *([] if before is None else [before]))


def on_device(queries, cotangent, table, key_weight, value_weight, owners, slots):
    n_dp = lax.axis_size("dp")
    n_tp = lax.axis_size("tensor")
    n_x = n_tp // 2
    spans = owners.shape[0]
    n_requests = 2 * spans
    n_slabs, n_tokens, enc = table.shape
    cap = max(2, (4 * spans + n_dp - 1) // n_dp)
    share = n_tokens // n_tp
    n_chunks = share // SUB

    def over_core(x):
        return lax.ppermute(x, "tensor", [(t, t ^ 1) for t in range(n_tp)])

    def over_x(x, d):
        return lax.ppermute(x, "tensor", [(t, (t + 2 * d) % n_tp) for t in range(n_tp)])

    def over_dp(x, d):
        return lax.ppermute(x, "dp", [(i, (i + d) % n_dp) for i in range(n_dp)])

    def to_all(xs, sign):
        return [xs[0]] + [over_dp(xs[d], sign * d) for d in range(1, n_dp)]

    me = lax.axis_index("dp").astype(jnp.int32).reshape(1)
    wanted, request = ask(me, owners, slots, n_dp, cap)
    asked = to_all([wanted] * n_dp, 1)
    first = (lax.axis_index("tensor") * share).astype(jnp.int32).reshape(1)

    def place(c, kind, d):
        return (kind, c if d == 0 else n_chunks * d + c)

    kvs, places = [], []
    packed = pack(asked, first, table, n_chunks, cap)
    for c in range(n_chunks):
        arrived = to_all(packed[c * n_dp : (c + 1) * n_dp], -1)
        if kvs:
            arrived, kvs = lax.optimization_barrier((arrived, kvs))
        mine = compact(request, arrived, n_requests)
        near = [mine, over_core(mine)]
        far = [over_x(mine, d) for d in range(1, n_x)]
        near_at = [place(c, kind, 0) for kind in range(2)]
        far_at = [place(c, kind, d) for kind in range(2) for d in range(1, n_x)]
        if c < n_chunks - 1:
            far = far + [over_core(x) for x in far]
            kvs = kvs + [project(near + far, key_weight, value_weight)]
        else:
            near = project(near, key_weight, value_weight)
            near, far = lax.optimization_barrier((near, far))
            far = far + [over_core(x) for x in far]
            kvs = kvs + [near, project(far, key_weight, value_weight)]
        places += near_at + far_at

    sizes = [n_chunks * n_x, n_chunks * n_x]
    attended, d_query, (d_own, d_core) = attend(kvs, places, sizes, queries, cotangent)

    lead = 3 * LANES
    d_table = None
    for cols in ((0, lead), (lead, enc - lead)):
        grads = grads_of(d_core, key_weight, value_weight, n_chunks, cols)
        got = over_core(grads[0]), over_core(grads[1][0])
        own, codes = grads_of(d_own, key_weight, value_weight, n_chunks, cols, got)
        if d_table is None:
            codes, d_core = lax.optimization_barrier((codes, d_core))
        codes = [over_x(code, n_x - d) for d, code in enumerate(codes, 1)]
        arrived = to_all(send_codes(request, own, codes, n_dp), 1)
        d_table = gather_grads(asked, arrived, n_slabs, n_chunks, enc, cols, d_table)
    return (attended, d_query, d_table)


def solution(mesh):
    in_specs = (
        P("dp", "tensor"),
        P("dp", "tensor"),
        P("dp", None, None),
        P(None, "tensor"),
        P(None, "tensor"),
        P("dp", None),
        P("dp", None),
    )
    out_specs = (P("dp", "tensor"), P("dp", "tensor"), P("dp", "tensor", None))
    return jax.shard_map(
        on_device, mesh=mesh, in_specs=in_specs, out_specs=out_specs, check_vma=False
    )
```

```python
import functools
import math

import jax
import jax.numpy as jnp
from jax import lax
from jax.experimental import pallas as pl
from jax.experimental.pallas import tpu as pltpu
from jax.sharding import PartitionSpec as P

HD = 128
SPAN = 64
SUB = 16
LANES = 128
VMEM_LIMIT = 28 * 1024 * 1024
F32 = jnp.float32
BF16 = jnp.bfloat16

ANY = pl.BlockSpec(memory_space=pl.ANY)
SMEM = pl.BlockSpec(memory_space=pltpu.SMEM)
VMEM = pl.BlockSpec(memory_space=pltpu.VMEM)


def params():
    return pltpu.CompilerParams(vmem_limit_bytes=VMEM_LIMIT)


def cost(flops, nbytes):
    return pl.CostEstimate(flops=int(flops), bytes_accessed=int(nbytes), transcendentals=0)


def ask_body(cap, me, owners, slots, wanted, request, count):
    n_dp = wanted.shape[0] // cap
    for i in range(n_dp * cap):
        wanted[i] = -1
        request[i] = -1
    for d in range(n_dp):
        count[d] = 0
    for r in range(owners.size):
        d = owners[r % 2, r // 2] - me[0]
        d = jnp.where(d < 0, d + n_dp, d)
        j = count[d]
        count[d] = j + 1
        wanted[d * cap + j] = slots[r % 2, r // 2]
        request[d * cap + j] = r


def ask(me, owners, slots, n_dp, cap):
    shape = jax.ShapeDtypeStruct((n_dp * cap,), jnp.int32)
    return pl.pallas_call(
        functools.partial(ask_body, cap),
        out_shape=[shape, shape],
        in_specs=[SMEM, SMEM, SMEM],
        out_specs=[SMEM, SMEM],
        scratch_shapes=[pltpu.SMEM((n_dp,), jnp.int32)],
        name="ask",
    )(me, owners.T, slots.T)


def asked_of(asked, me, d, j):
    n_dp = asked.shape[0]
    asker = me[0] - d
    asker = jnp.where(asker < 0, asker + n_dp, asker)
    return asked[asker, d * (asked.shape[1] // n_dp) + j]


def pack_body(n_dp, n_chunks, me, asked, first, table, *rest):
    outs, sem = rest[:-1], rest[-1]
    cap = outs[0].shape[0]

    def each(act):
        for c in range(n_chunks):
            row = pl.multiple_of(first[0] + c * SUB, SUB)
            for d in range(n_dp):
                for j in range(cap):
                    slab = asked_of(asked, me, d, j)

                    @pl.when(slab >= 0)
                    def _():
                        act(
                            pltpu.make_async_copy(
                                table.at[slab, pl.ds(row, SUB)],
                                outs[c * n_dp + d].at[j],
                                sem.at[c, d * cap + j],
                            )
                        )

    each(lambda copy: copy.start())
    each(lambda copy: copy.wait())


def pack(me, asked, first, table, n_chunks, cap):
    n_dp = asked.shape[0]
    enc = table.shape[2]
    return pl.pallas_call(
        functools.partial(pack_body, n_dp, n_chunks),
        out_shape=[jax.ShapeDtypeStruct((cap, SUB, enc), table.dtype)] * (n_chunks * n_dp),
        in_specs=[SMEM, SMEM, SMEM, ANY],
        out_specs=[VMEM] * (n_chunks * n_dp),
        scratch_shapes=[pltpu.SemaphoreType.DMA((n_chunks, n_dp * cap))],
        compiler_params=params(),
        cost_estimate=cost(0, 4 * n_chunks * n_dp * cap * SUB * enc),
        name="pack_rows",
    )(me, asked, first, table)


def compact_body(n_dp, request, *refs):
    arrived, out, sem = refs[:n_dp], refs[n_dp], refs[n_dp + 1]
    cap = arrived[0].shape[0]

    def each(act):
        for d in range(n_dp):
            for j in range(cap):
                r = request[d * cap + j]

                @pl.when(r >= 0)
                def _():
                    act(pltpu.make_async_copy(arrived[d].at[j], out.at[r], sem.at[d * cap + j]))

    each(lambda copy: copy.start())
    each(lambda copy: copy.wait())


def compact(request, arrived, n):
    shape = (n,) + arrived[0].shape[1:]
    return pl.pallas_call(
        functools.partial(compact_body, len(arrived)),
        out_shape=jax.ShapeDtypeStruct(shape, arrived[0].dtype),
        in_specs=[SMEM] + [ANY] * len(arrived),
        out_specs=VMEM,
        scratch_shapes=[pltpu.SemaphoreType.DMA((request.shape[0],))],
        compiler_params=params(),
        cost_estimate=cost(0, 4 * math.prod(shape)),
        name="compact_rows",
    )(request, *arrived)


def weight_specs(rows, step):
    return [
        pl.BlockSpec((rows, step), lambda i: (0, jnp.minimum(i, 1))),
        pl.BlockSpec((rows, step), lambda i: (0, jnp.maximum(i - 2, 0))),
    ]


def with_weight(wk, wv, act):
    @pl.when(pl.program_id(0) < 2)
    def _():
        act(wk)

    @pl.when(pl.program_id(0) >= 2)
    def _():
        act(wv)


def project_body(n_in, *refs):
    wk, wv, out = refs[n_in : n_in + 3]
    n, sub, enc = refs[0].shape
    rows = jnp.concatenate([ref[...].reshape(n * sub, enc) for ref in refs[:n_in]], axis=0)

    def act(w):
        res = jnp.dot(rows, w[...], preferred_element_type=F32)
        out[...] = res.astype(BF16).reshape(out.shape)

    with_weight(wk, wv, act)


def project(pieces, wk, wv):
    n_in = len(pieces)
    n, sub, enc = pieces[0].shape
    width = 2 * wk.shape[1]
    step = width // 4
    return pl.pallas_call(
        functools.partial(project_body, n_in),
        out_shape=jax.ShapeDtypeStruct((n_in, n, sub, width), BF16),
        grid=(4,),
        in_specs=[pl.BlockSpec((n, sub, enc), lambda i: (0, 0, 0))] * n_in
        + weight_specs(enc, step),
        out_specs=pl.BlockSpec((n_in, n, sub, step), lambda i: (0, 0, 0, i)),
        compiler_params=params(),
        cost_estimate=cost(
            2 * n_in * n * sub * enc * width, 2 * (n_in * n * sub * (enc + width) + enc * width)
        ),
        name="project",
    )(*pieces, wk, wv)


def attend_body(places, n_kv, *refs):
    kvs = refs[:n_kv]
    q_ref, g_ref, att_ref, dq_ref = refs[n_kv : n_kv + 4]
    grads = refs[n_kv + 4 :]
    width = q_ref.shape[1]
    scale = 1.0 / math.sqrt(HD)
    heads = width // HD
    group = min(4, heads)

    def keys_of(col):
        parts = [ref[:, :, :, pl.ds(col, HD)].reshape(-1, HD) for ref in kvs]
        return jnp.concatenate(parts, axis=0)

    def put(col, grad):
        for at, (ref, i) in enumerate(places):
            block = grad[at * 2 * SUB : (at + 1) * 2 * SUB]
            grads[ref][i, :, :, pl.ds(col, HD)] = block.reshape(2, SUB, HD)

    last = (((1,), (1,)), ((), ()))
    first = (((0,), (0,)), ((), ()))

    def dot(a, b, dims=(((1,), (0,)), ((), ()))):
        return lax.dot_general(a, b, dims, preferred_element_type=F32)

    for h0 in range(0, heads, group):
        hs = range(h0, h0 + group)
        q = [q_ref[:, pl.ds(h * HD, HD)] for h in hs]
        g = [g_ref[:, pl.ds(h * HD, HD)] for h in hs]
        k = [keys_of(h * HD) for h in hs]
        v = [keys_of(width + h * HD) for h in hs]
        s = jnp.concatenate([dot(a, b, last) for a, b in zip(q, k)], axis=0) * scale
        dw = jnp.concatenate([dot(a, b, last) for a, b in zip(g, v)], axis=0)
        e = jnp.exp(s - jnp.max(s, axis=1, keepdims=True))
        p = e * (1.0 / jnp.sum(e, axis=1, keepdims=True))
        rs = jnp.sum(dw * p, axis=1, keepdims=True)
        w = p.astype(BF16)
        ds = (p * (dw - rs) * scale).astype(BF16)
        ws = [w[i * SPAN : (i + 1) * SPAN] for i in range(group)]
        dss = [ds[i * SPAN : (i + 1) * SPAN] for i in range(group)]
        att = [dot(a, b).astype(BF16) for a, b in zip(ws, v)]
        dq = [dot(a, b).astype(BF16) for a, b in zip(dss, k)]
        dk = [dot(a, b, first).astype(BF16) for a, b in zip(dss, q)]
        dv = [dot(a, b, first).astype(BF16) for a, b in zip(ws, g)]
        for i, h in enumerate(hs):
            att_ref[:, pl.ds(h * HD, HD)] = att[i]
            dq_ref[:, pl.ds(h * HD, HD)] = dq[i]
            put(h * HD, dk[i])
            put(width + h * HD, dv[i])


def attend(kvs, places, sizes, queries, cotangent):
    tokens, width = queries.shape
    spans = tokens // SPAN
    n = kvs[0].shape[1]
    rows = pl.BlockSpec((SPAN, width), lambda i: (i, 0))

    def kv_block(pieces):
        return pl.BlockSpec((pieces, 2, SUB, 2 * width), lambda i: (0, i, 0, 0))

    keys = len(places) * 2 * SUB
    out = pl.pallas_call(
        functools.partial(attend_body, places, len(kvs)),
        out_shape=[jax.ShapeDtypeStruct((tokens, width), BF16)] * 2
        + [jax.ShapeDtypeStruct((size, n, SUB, 2 * width), BF16) for size in sizes],
        grid=(spans,),
        in_specs=[kv_block(kv.shape[0]) for kv in kvs] + [rows, rows],
        out_specs=[rows, rows] + [kv_block(size) for size in sizes],
        compiler_params=params(),
        cost_estimate=cost(12 * tokens * width * keys, 8 * tokens * width + 8 * spans * keys * 2 * width),
        name="attend",
    )(*kvs, queries, cotangent)
    return out[0], out[1], out[2:]


def encode(x, axes):
    top = jnp.maximum(jnp.max(jnp.abs(x), axis=axes, keepdims=True), 1e-30)
    power = jnp.floor(jnp.log2(top)) + 1.0
    code = jnp.clip(jnp.round(x * jnp.exp2(15.0 - power)), -32767.0, 32767.0)
    return code.astype(jnp.int32).astype(jnp.int16), power


def grad_step(first, d_ref, wk, wv, acc):
    i = pl.program_id(0)
    pieces, n, sub, step = d_ref.shape
    rows = d_ref[...].reshape(pieces * n * sub, step)

    def act(w):
        w = w[first : first + acc.shape[1], :]
        part = lax.dot_general(rows, w, (((1,), (1,)), ((), ())), preferred_element_type=F32)

        @pl.when(i == 0)
        def _():
            acc[...] = part

        @pl.when(i > 0)
        def _():
            acc[...] += part

    with_weight(wk, wv, act)


def core_grad_body(near, first, d_ref, wk, wv, near_out, far_out, acc):
    grad_step(first, d_ref, wk, wv, acc)

    @pl.when(pl.program_id(0) == pl.num_programs(0) - 1)
    def _():
        full = acc[...].reshape(d_ref.shape[:3] + acc.shape[1:])
        near_out[...] = full[:near]
        far_out[...] = full[near:]


def own_grad_body(near, first, d_ref, wk, wv, near_got, far_got, near_out, *rest):
    codes, acc = rest[:-1], rest[-1]
    grad_step(first, d_ref, wk, wv, acc)

    @pl.when(pl.program_id(0) == pl.num_programs(0) - 1)
    def _():
        full = acc[...].reshape(d_ref.shape[:3] + acc.shape[1:])
        near_out[...] = full[:near] + near_got[...]
        n = d_ref.shape[1]
        tiles = acc.shape[1] // LANES
        row = lax.broadcasted_iota(jnp.int32, (SUB, LANES), 0)
        for i in range(far_got.shape[0]):
            out, c = codes[i // near], i % near
            code, power = encode(full[near + i] + far_got[i], (1, 2))
            for e in range(tiles):
                out[c, e * n : (e + 1) * n] = code[:, :, e * LANES : (e + 1) * LANES]
            note = jnp.zeros((SUB, LANES), F32)
            for r in range(n):
                note = jnp.where(row == r, power[r], note)
            out[c, tiles * n] = note.astype(jnp.int32).astype(jnp.int16)


def grads_of(d_kv, wk, wv, near, cols, got=None):
    pieces, n, sub, width = d_kv.shape
    far = pieces - near
    first, count = cols
    step = width // 4
    tiles = count // LANES
    near_shape, far_shape = (near, n, sub, count), (far, n, sub, count)

    def whole(shape):
        return pl.BlockSpec(shape, lambda i: (0,) * len(shape))

    if got is None:
        body, outs = core_grad_body, [(near_shape, F32), (far_shape, F32)]
    else:
        body = own_grad_body
        outs = [(near_shape, F32)] + [((near, tiles * n + 1, sub, LANES), jnp.int16)] * (far // near)
    out = pl.pallas_call(
        functools.partial(body, near, first),
        out_shape=[jax.ShapeDtypeStruct(*o) for o in outs],
        grid=(4,),
        in_specs=[pl.BlockSpec((pieces, n, sub, step), lambda i: (0, 0, 0, i))]
        + weight_specs(wk.shape[0], step)
        + ([] if got is None else [whole(near_shape), whole(far_shape)]),
        out_specs=[whole(shape) for shape, _ in outs],
        scratch_shapes=[pltpu.VMEM((pieces * n * sub, count), F32)],
        compiler_params=params(),
        cost_estimate=cost(2 * pieces * n * sub * count * width, 2 * (count + pieces * n * sub) * width),
        name="core_grads" if got is None else "own_grads",
    )(
        d_kv,
        wk,
        wv,
        *([] if got is None else got),
    )
    return out[0], out[1:]


def send_body(n_dp, request, own, *rest):
    codes, outs, (stage, powers) = rest[: -n_dp - 2], rest[-n_dp - 2 : -2], rest[-2:]
    n_chunks, n, sub, count = own.shape
    tiles = count // LANES
    cap = request.shape[0] // n_dp
    for c in range(n_chunks):
        for r in range(n):
            total = own[c, r]
            for code in codes:
                unit = jnp.exp2(code[c, tiles * n].astype(F32)[r : r + 1] - 15.0)
                total = total + jnp.concatenate(
                    [code[c, e * n + r].astype(F32) * unit for e in range(tiles)], axis=1
                )
            coded, power = encode(total, (0, 1))
            for e in range(tiles):
                stage[r, c * tiles + e] = coded[:, e * LANES : (e + 1) * LANES]
            powers[r, c] = jnp.broadcast_to(power, (SUB, LANES))
    row = lax.broadcasted_iota(jnp.int32, (SUB, LANES), 0)
    for d in range(n_dp):
        note = jnp.zeros((SUB, LANES), F32)
        for j in range(cap):
            r = request[d * cap + j]

            @pl.when(r >= 0)
            def _():
                outs[d][pl.ds(j * n_chunks * tiles, n_chunks * tiles)] = stage[r]

            for c in range(n_chunks):
                note = jnp.where(row == j * n_chunks + c, powers[jnp.maximum(r, 0), c], note)
        outs[d][cap * n_chunks * tiles] = note.astype(jnp.int32).astype(jnp.int16)


def send_codes(request, own, codes, n_dp):
    n_chunks, n, sub, count = own.shape
    tiles = count // LANES
    cap = request.shape[0] // n_dp
    shape = (cap * n_chunks * tiles + 1, SUB, LANES)
    return pl.pallas_call(
        functools.partial(send_body, n_dp),
        out_shape=[jax.ShapeDtypeStruct(shape, jnp.int16)] * n_dp,
        in_specs=[SMEM, VMEM] + [VMEM] * len(codes),
        out_specs=[VMEM] * n_dp,
        scratch_shapes=[
            pltpu.VMEM((n, n_chunks * tiles, SUB, LANES), jnp.int16),
            pltpu.VMEM((n, n_chunks, SUB, LANES), F32),
        ],
        compiler_params=params(),
        cost_estimate=cost(10 * own.size, 6 * own.size + 2 * n_dp * math.prod(shape)),
        name="send_codes",
    )(request, own, *codes)


def gather_body(n_dp, n_chunks, first, me, asked, *refs):
    arrived = refs[:n_dp]
    out, total, sem = refs[-3:]
    count = total.shape[2]
    tiles = count // LANES
    cap = asked.shape[1] // n_dp
    total[...] = jnp.zeros_like(total)
    for d in range(n_dp):
        for j in range(cap):
            slab = asked_of(asked, me, d, j)

            @pl.when(slab >= 0)
            def _():
                note = arrived[d][cap * n_chunks * tiles].astype(F32)
                for c in range(n_chunks):
                    at = j * n_chunks + c
                    unit = jnp.exp2(note[at : at + 1] - 15.0)
                    for e in range(tiles):
                        value = arrived[d][at * tiles + e].astype(F32) * unit
                        total[slab, pl.ds(c * SUB, SUB), pl.ds(e * LANES, LANES)] += value

    copy = pltpu.make_async_copy(total, out.at[:, :, pl.ds(first, count)], sem)
    copy.start()
    copy.wait()


def gather_grads(me, asked, arrived, n_slabs, n_chunks, enc, cols, before):
    first, count = cols
    n_dp = asked.shape[0]
    rows = n_chunks * SUB
    return pl.pallas_call(
        functools.partial(gather_body, n_dp, n_chunks, first),
        out_shape=jax.ShapeDtypeStruct((n_slabs, rows, enc), F32),
        in_specs=[SMEM, SMEM] + [VMEM] * n_dp + [ANY] * (before is not None),
        out_specs=ANY,
        scratch_shapes=[pltpu.VMEM((n_slabs, rows, count), F32), pltpu.SemaphoreType.DMA],
        input_output_aliases={} if before is None else {2 + n_dp: 0},
        compiler_params=params(),
        cost_estimate=cost(0, 8 * n_slabs * rows * count),
        name="gather_grads",
    )(me, asked, *arrived, *([] if before is None else [before]))


def on_device(queries, cotangent, table, key_weight, value_weight, owners, slots):
    n_dp = lax.axis_size("dp")
    n_tp = lax.axis_size("tensor")
    n_x = n_tp // 2
    spans = owners.shape[0]
    n_requests = 2 * spans
    n_slabs, n_tokens, enc = table.shape
    cap = max(2, (4 * spans + n_dp - 1) // n_dp)
    share = n_tokens // n_tp
    n_chunks = share // SUB

    def over_core(x):
        return lax.ppermute(x, "tensor", [(t, t ^ 1) for t in range(n_tp)])

    def over_x(x, d):
        return lax.ppermute(x, "tensor", [(t, (t + 2 * d) % n_tp) for t in range(n_tp)])

    def over_dp(x, d):
        return lax.ppermute(x, "dp", [(i, (i + d) % n_dp) for i in range(n_dp)])

    farthest_first = sorted(range(1, n_dp), key=lambda d: -min(d, n_dp - d))

    def to_all(xs, sign, distances=farthest_first):
        got = {d: over_dp(xs[d], sign * d) for d in distances}
        return got

    me = lax.axis_index("dp").astype(jnp.int32).reshape(1)
    wanted, request = ask(me, owners, slots, n_dp, cap)
    asked = lax.all_gather(wanted, "dp")
    first = (lax.axis_index("tensor") * share).astype(jnp.int32).reshape(1)

    def place(c, kind, d):
        return (kind, c if d == 0 else n_chunks * d + c)

    kvs, places = [], []
    packed = pack(me, asked, first, table, n_chunks, cap)
    early = {}
    for c in range(n_chunks):
        sent = packed[c * n_dp : (c + 1) * n_dp]
        rest = [d for d in farthest_first if d not in early]
        arrived = [sent[0]] + [None] * (n_dp - 1)
        for d, x in {**early, **to_all(sent, -1, rest)}.items():
            arrived[d] = x
        if kvs:
            arrived, kvs = lax.optimization_barrier((arrived, kvs))
        mine = compact(request, arrived, n_requests)
        near = [mine, over_core(mine)]
        far = [over_x(mine, d) for d in range(1, n_x)]
        near_at = [place(c, kind, 0) for kind in range(2)]
        far_at = [place(c, kind, d) for kind in range(2) for d in range(1, n_x)]
        if c < n_chunks - 1:
            early = to_all(packed[(c + 1) * n_dp : (c + 2) * n_dp], -1, farthest_first[:3])
            early, far = lax.optimization_barrier((early, far))
            far = far + [over_core(x) for x in far]
            kvs = kvs + [project(near + far, key_weight, value_weight)]
        else:
            near = project(near, key_weight, value_weight)
            near, far = lax.optimization_barrier((near, far))
            far = far + [over_core(x) for x in far]
            kvs = kvs + [near, project(far, key_weight, value_weight)]
        places += near_at + far_at

    sizes = [n_chunks * n_x, n_chunks * n_x]
    attended, d_query, (d_own, d_core) = attend(kvs, places, sizes, queries, cotangent)

    lead = 3 * LANES
    parts = ((0, lead), (lead, enc - lead))
    d_table, got, before = None, [], None
    for cols in parts:
        near, (far,) = grads_of(d_core, key_weight, value_weight, n_chunks, cols)
        if got:
            got, near = lax.optimization_barrier((got, near))
        got = got + [(over_core(near), over_core(far))]
    for cols, sums in zip(parts, got):
        own, codes = grads_of(d_own, key_weight, value_weight, n_chunks, cols, sums)
        if before is not None:
            codes, before = lax.optimization_barrier((codes, before))
        codes = before = [over_x(code, n_x - d) for d, code in enumerate(codes, 1)]
        sent = send_codes(request, own, codes, n_dp)
        came = to_all(sent, 1)
        arrived = [sent[0]] + [came[d] for d in range(1, n_dp)]
        d_table = gather_grads(me, asked, arrived, n_slabs, n_chunks, enc, cols, d_table)
    return (attended, d_query, d_table)


def solution(mesh):
    in_specs = (
        P("dp", "tensor"),
        P("dp", "tensor"),
        P("dp", None, None),
        P(None, "tensor"),
        P(None, "tensor"),
        P("dp", None),
        P("dp", None),
    )
    out_specs = (P("dp", "tensor"), P("dp", "tensor"), P("dp", "tensor", None))
    return jax.shard_map(
        on_device, mesh=mesh, in_specs=in_specs, out_specs=out_specs, check_vma=False
    )
```

```python
import functools
import math

import jax
import jax.numpy as jnp
from jax import lax
from jax.experimental import pallas as pl
from jax.experimental.pallas import tpu as pltpu
from jax.sharding import PartitionSpec as P

HD = 128
SPAN = 64
SUB = 16
LANES = 128
VMEM_LIMIT = 28 * 1024 * 1024
VMEM_MORE = 40 * 1024 * 1024
VMEM_ALL = 60 * 1024 * 1024
F32 = jnp.float32
BF16 = jnp.bfloat16

ANY = pl.BlockSpec(memory_space=pl.ANY)
SMEM = pl.BlockSpec(memory_space=pltpu.SMEM)
VMEM = pl.BlockSpec(memory_space=pltpu.VMEM)


def params(limit=VMEM_LIMIT):
    return pltpu.CompilerParams(vmem_limit_bytes=limit)


def cost(flops, nbytes):
    return pl.CostEstimate(flops=int(flops), bytes_accessed=int(nbytes), transcendentals=0)


def ask_body(cap, owners, slots, me_out, wanted, request, count):
    n_dp = wanted.shape[0]
    me = lax.axis_index("dp")
    me_out[0] = me
    for i in range(n_dp * cap):
        request[i] = -1
        for asker in range(n_dp):
            wanted[asker, i] = 0
    for d in range(n_dp):
        count[d] = 0
    for r in range(owners.size):
        d = owners[r % 2, r // 2] - me
        d = jnp.where(d < 0, d + n_dp, d)
        j = count[d]
        count[d] = j + 1
        wanted[me, d * cap + j] = slots[r % 2, r // 2] + 1
        request[d * cap + j] = r


def ask(owners, slots, n_dp, cap):
    return pl.pallas_call(
        functools.partial(ask_body, cap),
        out_shape=[
            jax.ShapeDtypeStruct((1,), jnp.int32),
            jax.ShapeDtypeStruct((n_dp, n_dp * cap), jnp.int32),
            jax.ShapeDtypeStruct((n_dp * cap,), jnp.int32),
        ],
        in_specs=[SMEM, SMEM],
        out_specs=[SMEM, SMEM, SMEM],
        scratch_shapes=[pltpu.SMEM((n_dp,), jnp.int32)],
        name="ask",
    )(owners.T, slots.T)


def asked_of(asked, me, d, j):
    n_dp = asked.shape[0]
    asker = me[0] - d
    asker = jnp.where(asker < 0, asker + n_dp, asker)
    return asked[asker, d * (asked.shape[1] // n_dp) + j] - 1


def pack_body(n_dp, n_chunks, me, asked, table, *rest):
    outs, sem = rest[:-1], rest[-1]
    cap = outs[0].shape[0]
    first = lax.axis_index("tensor") * (n_chunks * SUB)

    def each(act):
        for c in range(n_chunks):
            row = pl.multiple_of(first + c * SUB, SUB)
            for d in range(n_dp):
                for j in range(cap):
                    slab = asked_of(asked, me, d, j)

                    @pl.when(slab >= 0)
                    def _():
                        act(
                            pltpu.make_async_copy(
                                table.at[slab, pl.ds(row, SUB)],
                                outs[c * n_dp + d].at[j],
                                sem.at[c, d * cap + j],
                            )
                        )

    each(lambda copy: copy.start())
    each(lambda copy: copy.wait())


def pack(me, asked, table, n_chunks, cap):
    n_dp = asked.shape[0]
    enc = table.shape[2]
    return pl.pallas_call(
        functools.partial(pack_body, n_dp, n_chunks),
        out_shape=[jax.ShapeDtypeStruct((cap, SUB, enc), table.dtype)] * (n_chunks * n_dp),
        in_specs=[SMEM, SMEM, ANY],
        out_specs=[VMEM] * (n_chunks * n_dp),
        scratch_shapes=[pltpu.SemaphoreType.DMA((n_chunks, n_dp * cap))],
        compiler_params=params(VMEM_ALL),
        cost_estimate=cost(0, 4 * n_chunks * n_dp * cap * SUB * enc),
        name="pack_rows",
    )(me, asked, table)


def compact_body(n_dp, request, *refs):
    arrived, out, sem = refs[:n_dp], refs[n_dp], refs[n_dp + 1]
    cap = arrived[0].shape[0]

    def each(act):
        for d in range(n_dp):
            for j in range(cap):
                r = request[d * cap + j]

                @pl.when(r >= 0)
                def _():
                    act(pltpu.make_async_copy(arrived[d].at[j], out.at[r], sem.at[d * cap + j]))

    each(lambda copy: copy.start())
    each(lambda copy: copy.wait())


def compact(request, arrived, n):
    shape = (n,) + arrived[0].shape[1:]
    return pl.pallas_call(
        functools.partial(compact_body, len(arrived)),
        out_shape=jax.ShapeDtypeStruct(shape, arrived[0].dtype),
        in_specs=[SMEM] + [ANY] * len(arrived),
        out_specs=VMEM,
        scratch_shapes=[pltpu.SemaphoreType.DMA((request.shape[0],))],
        compiler_params=params(),
        cost_estimate=cost(0, 4 * math.prod(shape)),
        name="compact_rows",
    )(request, *arrived)


def weight_specs(rows, step):
    return [
        pl.BlockSpec((rows, step), lambda i: (0, jnp.minimum(i, 1))),
        pl.BlockSpec((rows, step), lambda i: (0, jnp.maximum(i - 2, 0))),
    ]


def with_weight(wk, wv, act):
    @pl.when(pl.program_id(0) < 2)
    def _():
        act(wk)

    @pl.when(pl.program_id(0) >= 2)
    def _():
        act(wv)


def project_body(n_in, *refs):
    wk, wv, out = refs[n_in : n_in + 3]
    n, sub, enc = refs[0].shape
    rows = jnp.concatenate([ref[...].reshape(n * sub, enc) for ref in refs[:n_in]], axis=0)

    def act(w):
        res = jnp.dot(rows, w[...], preferred_element_type=F32)
        out[...] = res.astype(BF16).reshape(out.shape)

    with_weight(wk, wv, act)


def project(pieces, wk, wv):
    n_in = len(pieces)
    n, sub, enc = pieces[0].shape
    width = 2 * wk.shape[1]
    step = width // 4
    return pl.pallas_call(
        functools.partial(project_body, n_in),
        out_shape=jax.ShapeDtypeStruct((n_in, n, sub, width), BF16),
        grid=(4,),
        in_specs=[pl.BlockSpec((n, sub, enc), lambda i: (0, 0, 0))] * n_in
        + weight_specs(enc, step),
        out_specs=pl.BlockSpec((n_in, n, sub, step), lambda i: (0, 0, 0, i)),
        compiler_params=params(),
        cost_estimate=cost(
            2 * n_in * n * sub * enc * width, 2 * (n_in * n * sub * (enc + width) + enc * width)
        ),
        name="project",
    )(*pieces, wk, wv)


def attend_body(places, n_kv, n_late, near, *refs):
    kvs, late = refs[:n_kv], refs[n_kv : n_kv + n_late]
    wk, wv, q_ref, g_ref, att_ref, dq_ref = refs[n_kv + n_late : n_kv + n_late + 6]
    *grads, near_out, far_out, own_out, late_kv, own_all, core_all = refs[n_kv + n_late + 6 :]
    step = pl.program_id(0)
    width = q_ref.shape[1]
    enc = wk.shape[0]
    scale = 1.0 / math.sqrt(HD)
    heads = width // HD
    group = min(4, heads)
    last = (((1,), (1,)), ((), ()))
    first = (((0,), (0,)), ((), ()))

    def dot(a, b, dims=(((1,), (0,)), ((), ()))):
        return lax.dot_general(a, b, dims, preferred_element_type=F32)

    @pl.when(step == 0)
    def _():
        rows = jnp.concatenate([ref[...].reshape(-1, enc) for ref in late], axis=0)
        shape = late_kv.shape[:3] + (width,)
        late_kv[:, :, :, :width] = dot(rows, wk[...]).astype(BF16).reshape(shape)
        late_kv[:, :, :, width:] = dot(rows, wv[...]).astype(BF16).reshape(shape)

    mine = pl.ds(2 * step, 2)

    def rows_of(col):
        cols = pl.ds(col, HD)
        parts = [ref[:, :, :, cols].reshape(-1, HD) for ref in kvs]
        parts.append(late_kv[:, mine, :, cols].reshape(-1, HD))
        return jnp.concatenate(parts, axis=0)

    def put(col, grad):
        cols = pl.ds(col, HD)
        for at, (kind, i) in enumerate(places):
            block = grad[at * 2 * SUB : (at + 1) * 2 * SUB].reshape(2, SUB, HD)
            grads[kind][i, :, :, cols] = block
            (own_all, core_all)[kind][i, mine, :, cols] = block

    zero = jnp.zeros((SPAN, HD), BF16)
    for h0 in range(0, heads, group):
        hs = range(h0, h0 + group)
        qg, kv = [], []
        for h in hs:
            cols = pl.ds(h * HD, HD)
            top = jnp.concatenate([q_ref[:, cols], zero], axis=1)
            low = jnp.concatenate([zero, g_ref[:, cols]], axis=1)
            qg.append(jnp.concatenate([top, low], axis=0))
            kv.append(jnp.concatenate([rows_of(h * HD), rows_of(width + h * HD)], axis=1))
        both = [dot(a, b, last) for a, b in zip(qg, kv)]
        s = jnp.concatenate([x[:SPAN] for x in both], axis=0) * scale
        dw = jnp.concatenate([x[SPAN:] for x in both], axis=0)
        e = jnp.exp(s - jnp.max(s, axis=1, keepdims=True))
        p = e * (1.0 / jnp.sum(e, axis=1, keepdims=True))
        rs = jnp.sum(dw * p, axis=1, keepdims=True)
        w = p.astype(BF16)
        ds = (p * (dw - rs) * scale).astype(BF16)
        span = [slice(i * SPAN, (i + 1) * SPAN) for i in range(group)]
        dsw = [jnp.concatenate([ds[i], w[i]], axis=0) for i in span]
        out = [dot(a, b).astype(BF16) for a, b in zip(dsw, kv)]
        back = [dot(a, b, first).astype(BF16) for a, b in zip(dsw, qg)]
        for i, h in enumerate(hs):
            dq_ref[:, pl.ds(h * HD, HD)] = out[i][:SPAN, :HD]
            att_ref[:, pl.ds(h * HD, HD)] = out[i][SPAN:, HD:]
            put(h * HD, back[i][:, :HD])
            put(width + h * HD, back[i][:, HD:])

    @pl.when(step == pl.num_programs(0) - 1)
    def _():
        count = own_out.shape[-1]
        for ref, outs in ((core_all, (near_out, far_out)), (own_all, (own_out,))):
            rows = ref[...].reshape(-1, 2 * width)
            res = dot(rows[:, :width], wk[:count, :], last) + dot(rows[:, width:], wv[:count, :], last)
            res = res.reshape(ref.shape[:3] + (count,))
            if len(outs) == 1:
                outs[0][...] = res
            else:
                outs[0][...] = res[:near]
                outs[1][...] = res[near:]


def attend(kvs, late, wk, wv, places, near, count, queries, cotangent):
    tokens, width = queries.shape
    spans = tokens // SPAN
    n = kvs[0].shape[1]
    enc = wk.shape[0]
    pieces = len(places) // 2
    rows = pl.BlockSpec((SPAN, width), lambda i: (i, 0))

    def kv_block(pieces):
        return pl.BlockSpec((pieces, 2, SUB, 2 * width), lambda i: (0, i, 0, 0))

    def whole(shape):
        return pl.BlockSpec(shape, lambda i: (0,) * len(shape))

    keys = len(places) * 2 * SUB
    parts = [(near, n, SUB, count), (pieces - near, n, SUB, count), (pieces, n, SUB, count)]
    every = (pieces, n, SUB, 2 * width)
    return pl.pallas_call(
        functools.partial(attend_body, places, len(kvs), len(late), near),
        out_shape=[jax.ShapeDtypeStruct((tokens, width), BF16)] * 2
        + [jax.ShapeDtypeStruct(every, BF16)] * 2
        + [jax.ShapeDtypeStruct(part, F32) for part in parts],
        grid=(spans,),
        in_specs=[kv_block(kv.shape[0]) for kv in kvs]
        + [whole(x.shape) for x in late]
        + [whole(wk.shape), whole(wv.shape), rows, rows],
        out_specs=[rows, rows] + [kv_block(pieces)] * 2 + [whole(part) for part in parts],
        scratch_shapes=[
            pltpu.VMEM((len(late), n, SUB, 2 * width), BF16),
            pltpu.VMEM(every, BF16),
            pltpu.VMEM(every, BF16),
        ],
        compiler_params=params(VMEM_MORE),
        cost_estimate=cost(
            16 * tokens * width * keys + 4 * n * SUB * width * (len(late) * enc + 2 * pieces * count),
            8 * tokens * width + 8 * spans * keys * 2 * width,
        ),
        name="attend",
    )(*kvs, *late, wk, wv, queries, cotangent)


def encode(x, axes):
    top = jnp.maximum(jnp.max(jnp.abs(x), axis=axes, keepdims=True), 1e-30)
    power = jnp.floor(jnp.log2(top)) + 1.0
    code = jnp.clip(jnp.round(x * jnp.exp2(15.0 - power)), -32767.0, 32767.0)
    return code.astype(jnp.int32).astype(jnp.int16), power


def grad_step(first, d_ref, wk, wv, acc):
    i = pl.program_id(0)
    pieces, n, sub, step = d_ref.shape
    rows = d_ref[...].reshape(pieces * n * sub, step)

    def act(w):
        w = w[first : first + acc.shape[1], :]
        part = lax.dot_general(rows, w, (((1,), (1,)), ((), ())), preferred_element_type=F32)

        @pl.when(i == 0)
        def _():
            acc[...] = part

        @pl.when(i > 0)
        def _():
            acc[...] += part

    with_weight(wk, wv, act)


def core_grad_body(near, first, d_ref, wk, wv, near_out, far_out, acc):
    grad_step(first, d_ref, wk, wv, acc)

    @pl.when(pl.program_id(0) == pl.num_programs(0) - 1)
    def _():
        full = acc[...].reshape(d_ref.shape[:3] + acc.shape[1:])
        near_out[...] = full[:near]
        far_out[...] = full[near:]


def put_codes(far, codes):
    pieces, n, sub, count = far.shape
    near = codes[0].shape[0]
    tiles = count // LANES
    row = lax.broadcasted_iota(jnp.int32, (SUB, LANES), 0)
    for i in range(pieces):
        out, c = codes[i // near], i % near
        code, power = encode(far[i], (1, 2))
        for e in range(tiles):
            out[c, e * n : (e + 1) * n] = code[:, :, e * LANES : (e + 1) * LANES]
        note = jnp.zeros((SUB, LANES), F32)
        for r in range(n):
            note = jnp.where(row == r, power[r], note)
        out[c, tiles * n] = note.astype(jnp.int32).astype(jnp.int16)


def far_codes_body(mine, got, *codes):
    put_codes(mine[...] + got[...], codes)


def far_codes(own, got, near):
    far, n, sub, count = got.shape
    shape = (near, count // LANES * n + 1, sub, LANES)
    return pl.pallas_call(
        far_codes_body,
        out_shape=[jax.ShapeDtypeStruct(shape, jnp.int16)] * (far // near),
        grid=(1,),
        in_specs=[
            pl.BlockSpec((pl.Element(far), pl.Element(n), pl.Element(sub), pl.Element(count)), lambda i: (near, 0, 0, 0)),
            pl.BlockSpec(got.shape, lambda i: (0, 0, 0, 0)),
        ],
        out_specs=[pl.BlockSpec(shape, lambda i: (0, 0, 0, 0))] * (far // near),
        compiler_params=params(),
        cost_estimate=cost(8 * got.size, 10 * got.size),
        name="far_codes",
    )(own, got)


def own_grad_body(near, first, d_ref, wk, wv, far_got, near_out, *rest):
    codes, acc = rest[:-1], rest[-1]
    grad_step(first, d_ref, wk, wv, acc)

    @pl.when(pl.program_id(0) == pl.num_programs(0) - 1)
    def _():
        full = acc[...].reshape(d_ref.shape[:3] + acc.shape[1:])
        near_out[...] = full[:near]
        put_codes(full[near:] + far_got[...], codes)


def grads_of(d_kv, wk, wv, near, cols, got=None):
    pieces, n, sub, width = d_kv.shape
    far = pieces - near
    first, count = cols
    step = width // 4
    tiles = count // LANES
    near_shape, far_shape = (near, n, sub, count), (far, n, sub, count)

    def whole(shape):
        return pl.BlockSpec(shape, lambda i: (0,) * len(shape))

    if got is None:
        body, outs = core_grad_body, [(near_shape, F32), (far_shape, F32)]
    else:
        body = own_grad_body
        outs = [(near_shape, F32)] + [((near, tiles * n + 1, sub, LANES), jnp.int16)] * (far // near)
    out = pl.pallas_call(
        functools.partial(body, near, first),
        out_shape=[jax.ShapeDtypeStruct(*o) for o in outs],
        grid=(4,),
        in_specs=[pl.BlockSpec((pieces, n, sub, step), lambda i: (0, 0, 0, i))]
        + weight_specs(wk.shape[0], step)
        + ([] if got is None else [whole(far_shape)]),
        out_specs=[whole(shape) for shape, _ in outs],
        scratch_shapes=[pltpu.VMEM((pieces * n * sub, count), F32)],
        compiler_params=params(),
        cost_estimate=cost(2 * pieces * n * sub * count * width, 2 * (count + pieces * n * sub) * width),
        name="core_grads" if got is None else "own_grads",
    )(
        d_kv,
        wk,
        wv,
        *([] if got is None else [got]),
    )
    return out[0], out[1:]


def send_body(n_dp, request, own, got, *rest):
    codes, outs, (stage, powers) = rest[: -n_dp - 2], rest[-n_dp - 2 : -2], rest[-2:]
    n_chunks, n, sub, count = got.shape
    tiles = count // LANES
    cap = request.shape[0] // n_dp
    for c in range(n_chunks):
        for r in range(n):
            total = own[c, r] + got[c, r]
            for code in codes:
                unit = jnp.exp2(code[c, tiles * n].astype(F32)[r : r + 1] - 15.0)
                total = total + jnp.concatenate(
                    [code[c, e * n + r].astype(F32) * unit for e in range(tiles)], axis=1
                )
            coded, power = encode(total, (0, 1))
            for e in range(tiles):
                stage[r, c * tiles + e] = coded[:, e * LANES : (e + 1) * LANES]
            powers[r, c] = jnp.broadcast_to(power, (SUB, LANES))
    row = lax.broadcasted_iota(jnp.int32, (SUB, LANES), 0)
    for d in range(n_dp):
        note = jnp.zeros((SUB, LANES), F32)
        for j in range(cap):
            r = request[d * cap + j]

            @pl.when(r >= 0)
            def _():
                outs[d][pl.ds(j * n_chunks * tiles, n_chunks * tiles)] = stage[r]

            for c in range(n_chunks):
                note = jnp.where(row == j * n_chunks + c, powers[jnp.maximum(r, 0), c], note)
        outs[d][cap * n_chunks * tiles] = note.astype(jnp.int32).astype(jnp.int16)


def send_codes(request, own, got, codes, n_dp):
    n_chunks, n, sub, count = got.shape
    block = pl.BlockSpec(got.shape, lambda i: (0, 0, 0, 0))
    tiles = count // LANES
    cap = request.shape[0] // n_dp
    shape = (cap * n_chunks * tiles + 1, SUB, LANES)
    return pl.pallas_call(
        functools.partial(send_body, n_dp),
        out_shape=[jax.ShapeDtypeStruct(shape, jnp.int16)] * n_dp,
        grid=(1,),
        in_specs=[SMEM, block, block] + [VMEM] * len(codes),
        out_specs=[VMEM] * n_dp,
        scratch_shapes=[
            pltpu.VMEM((n, n_chunks * tiles, SUB, LANES), jnp.int16),
            pltpu.VMEM((n, n_chunks, SUB, LANES), F32),
        ],
        compiler_params=params(),
        cost_estimate=cost(10 * got.size, 6 * got.size + 2 * n_dp * math.prod(shape)),
        name="send_codes",
    )(request, own, got, *codes)


def gather_body(n_dp, n_chunks, first, me, asked, *refs):
    arrived = refs[:n_dp]
    out, total, sem = refs[-3:]
    count = total.shape[2]
    tiles = count // LANES
    cap = asked.shape[1] // n_dp
    total[...] = jnp.zeros_like(total)
    for d in range(n_dp):
        for j in range(cap):
            slab = asked_of(asked, me, d, j)

            @pl.when(slab >= 0)
            def _():
                note = arrived[d][cap * n_chunks * tiles].astype(F32)
                for c in range(n_chunks):
                    at = j * n_chunks + c
                    unit = jnp.exp2(note[at : at + 1] - 15.0)
                    for e in range(tiles):
                        value = arrived[d][at * tiles + e].astype(F32) * unit
                        total[slab, pl.ds(c * SUB, SUB), pl.ds(e * LANES, LANES)] += value

    copy = pltpu.make_async_copy(total, out.at[:, :, pl.ds(first, count)], sem)
    copy.start()
    copy.wait()


def gather_grads(me, asked, arrived, n_slabs, n_chunks, enc, cols, before):
    first, count = cols
    n_dp = asked.shape[0]
    rows = n_chunks * SUB
    return pl.pallas_call(
        functools.partial(gather_body, n_dp, n_chunks, first),
        out_shape=jax.ShapeDtypeStruct((n_slabs, rows, enc), F32),
        in_specs=[SMEM, SMEM] + [VMEM] * n_dp + [ANY] * (before is not None),
        out_specs=ANY,
        scratch_shapes=[pltpu.VMEM((n_slabs, rows, count), F32), pltpu.SemaphoreType.DMA],
        input_output_aliases={} if before is None else {2 + n_dp: 0},
        compiler_params=params(),
        cost_estimate=cost(0, 8 * n_slabs * rows * count),
        name="gather_grads",
    )(me, asked, *arrived, *([] if before is None else [before]))


def on_device(queries, cotangent, table, key_weight, value_weight, owners, slots):
    n_dp = lax.axis_size("dp")
    n_tp = lax.axis_size("tensor")
    n_x = n_tp // 2
    spans = owners.shape[0]
    n_requests = 2 * spans
    n_slabs, n_tokens, enc = table.shape
    cap = max(2, (4 * spans + n_dp - 1) // n_dp)
    share = n_tokens // n_tp
    n_chunks = share // SUB

    def over_core(x):
        return lax.ppermute(x, "tensor", [(t, t ^ 1) for t in range(n_tp)])

    def over_x(x, d):
        return lax.ppermute(x, "tensor", [(t, (t + 2 * d) % n_tp) for t in range(n_tp)])

    def over_dp(x, d):
        return lax.ppermute(x, "dp", [(i, (i + d) % n_dp) for i in range(n_dp)])

    farthest_first = sorted(range(1, n_dp), key=lambda d: -min(d, n_dp - d))

    def to_all(xs, sign, distances=farthest_first):
        got = {d: over_dp(xs[d], sign * d) for d in distances}
        return got

    me, wanted, request = ask(owners, slots, n_dp, cap)
    asked = lax.psum(wanted, "dp")

    def place(c, kind, d):
        return (kind, c if d == 0 else n_chunks * d + c)

    kvs, places = [], []
    packed = pack(me, asked, table, n_chunks, cap)
    early = {}
    for c in range(n_chunks):
        sent = packed[c * n_dp : (c + 1) * n_dp]
        rest = [d for d in farthest_first if d not in early]
        arrived = [sent[0]] + [None] * (n_dp - 1)
        for d, x in {**early, **to_all(sent, -1, rest)}.items():
            arrived[d] = x
        if kvs:
            arrived, kvs = lax.optimization_barrier((arrived, kvs))
        mine = compact(request, arrived, n_requests)
        near = [mine, over_core(mine)]
        far = [over_x(mine, d) for d in range(1, n_x)]
        near_at = [place(c, kind, 0) for kind in range(2)]
        far_at = [place(c, kind, d) for kind in range(2) for d in range(1, n_x)]
        if c < n_chunks - 1:
            early = to_all(packed[(c + 1) * n_dp : (c + 2) * n_dp], -1, farthest_first[:3])
            early, far = lax.optimization_barrier((early, far))
            far = far + [over_core(x) for x in far]
            kvs = kvs + [project(near + far, key_weight, value_weight)]
        else:
            near = project(near, key_weight, value_weight)
            near, far = lax.optimization_barrier((near, far))
            late = far + [over_core(x) for x in far]
            kvs = kvs + [near]
        places += near_at + far_at

    lead = 3 * LANES
    parts = ((0, lead), (lead, enc - lead))
    attended, d_query, d_own, d_core, near, far, own = attend(
        kvs, late, key_weight, value_weight, places, n_chunks, lead, queries, cotangent
    )
    near_got, far_got = over_core(near), over_core(far)
    near, (far,) = grads_of(d_core, key_weight, value_weight, n_chunks, parts[1])
    far_got, near = lax.optimization_barrier((far_got, near))
    sums = [(own, near_got, far_codes(own, far_got, n_chunks))]
    near_got, far_got = over_core(near), over_core(far)
    own, codes = grads_of(d_own, key_weight, value_weight, n_chunks, parts[1], far_got)
    sums.append((own, near_got, codes))

    d_table, before = None, None
    for cols, (own, got, codes) in zip(parts, sums):
        if before is not None:
            codes, before = lax.optimization_barrier((codes, before))
        codes = before = [over_x(code, n_x - d) for d, code in enumerate(codes, 1)]
        sent = send_codes(request, own, got, codes, n_dp)
        came = to_all(sent, 1)
        arrived = [sent[0]] + [came[d] for d in range(1, n_dp)]
        d_table = gather_grads(me, asked, arrived, n_slabs, n_chunks, enc, cols, d_table)
    return (attended, d_query, d_table)


def solution(mesh):
    in_specs = (
        P("dp", "tensor"),
        P("dp", "tensor"),
        P("dp", None, None),
        P(None, "tensor"),
        P(None, "tensor"),
        P("dp", None),
        P("dp", None),
    )
    out_specs = (P("dp", "tensor"), P("dp", "tensor"), P("dp", "tensor", None))
    return jax.shard_map(
        on_device, mesh=mesh, in_specs=in_specs, out_specs=out_specs, check_vma=False
    )
```

```python
import functools
import math

import jax
import jax.numpy as jnp
from jax import lax
from jax.experimental import pallas as pl
from jax.experimental.pallas import tpu as pltpu
from jax.sharding import PartitionSpec as P

HD = 128
SPAN = 64
SUB = 16
LANES = 128
VMEM_LIMIT = 28 * 1024 * 1024
VMEM_MORE = 40 * 1024 * 1024
VMEM_ALL = 60 * 1024 * 1024
F32 = jnp.float32
BF16 = jnp.bfloat16

ANY = pl.BlockSpec(memory_space=pl.ANY)
SMEM = pl.BlockSpec(memory_space=pltpu.SMEM)
VMEM = pl.BlockSpec(memory_space=pltpu.VMEM)


def params(limit=VMEM_LIMIT):
    return pltpu.CompilerParams(vmem_limit_bytes=limit)


def cost(flops, nbytes):
    return pl.CostEstimate(flops=int(flops), bytes_accessed=int(nbytes), transcendentals=0)


def ask_body(cap, owners, slots, me_out, wanted, request, count):
    n_dp = wanted.shape[0]
    me = lax.axis_index("dp")
    me_out[0] = me
    for i in range(n_dp * cap):
        request[i] = -1
        for asker in range(n_dp):
            wanted[asker, i] = 0
    for d in range(n_dp):
        count[d] = 0
    for r in range(owners.size):
        d = owners[r % 2, r // 2] - me
        d = jnp.where(d < 0, d + n_dp, d)
        j = count[d]
        count[d] = j + 1
        wanted[me, d * cap + j] = slots[r % 2, r // 2] + 1
        request[d * cap + j] = r


def ask(owners, slots, n_dp, cap):
    return pl.pallas_call(
        functools.partial(ask_body, cap),
        out_shape=[
            jax.ShapeDtypeStruct((1,), jnp.int32),
            jax.ShapeDtypeStruct((n_dp, n_dp * cap), jnp.int32),
            jax.ShapeDtypeStruct((n_dp * cap,), jnp.int32),
        ],
        in_specs=[SMEM, SMEM],
        out_specs=[SMEM, SMEM, SMEM],
        scratch_shapes=[pltpu.SMEM((n_dp,), jnp.int32)],
        name="ask",
    )(owners.T, slots.T)


def asked_of(asked, me, d, j):
    n_dp = asked.shape[0]
    asker = me[0] - d
    asker = jnp.where(asker < 0, asker + n_dp, asker)
    return asked[asker, d * (asked.shape[1] // n_dp) + j] - 1


def pack_body(n_dp, chunk, share, me, asked, table, *rest):
    outs, sem = rest[:-1], rest[-1]
    cap = outs[0].shape[0]
    row = pl.multiple_of(lax.axis_index("tensor") * share + chunk * SUB, SUB)

    def each(act):
        for d in range(n_dp):
            for j in range(cap):
                slab = asked_of(asked, me, d, j)

                @pl.when(slab >= 0)
                def _():
                    source = table.at[slab, pl.ds(row, SUB)]
                    act(pltpu.make_async_copy(source, outs[d].at[j], sem.at[d * cap + j]))

    each(lambda copy: copy.start())
    each(lambda copy: copy.wait())


def pack(me, asked, table, chunk, share, cap):
    n_dp = asked.shape[0]
    enc = table.shape[2]
    return pl.pallas_call(
        functools.partial(pack_body, n_dp, chunk, share),
        out_shape=[jax.ShapeDtypeStruct((cap, SUB, enc), table.dtype)] * n_dp,
        in_specs=[SMEM, SMEM, ANY],
        out_specs=[VMEM] * n_dp,
        scratch_shapes=[pltpu.SemaphoreType.DMA((n_dp * cap,))],
        compiler_params=params(VMEM_ALL),
        cost_estimate=cost(0, 4 * n_dp * cap * SUB * enc),
        name="pack_rows",
    )(me, asked, table)


def compact_body(n_dp, request, *refs):
    arrived, out, sem = refs[:n_dp], refs[n_dp], refs[n_dp + 1]
    cap = arrived[0].shape[0]

    def each(act):
        for d in range(n_dp):
            for j in range(cap):
                r = request[d * cap + j]

                @pl.when(r >= 0)
                def _():
                    act(pltpu.make_async_copy(arrived[d].at[j], out.at[r], sem.at[d * cap + j]))

    each(lambda copy: copy.start())
    each(lambda copy: copy.wait())


def compact(request, arrived, n):
    shape = (n,) + arrived[0].shape[1:]
    return pl.pallas_call(
        functools.partial(compact_body, len(arrived)),
        out_shape=jax.ShapeDtypeStruct(shape, arrived[0].dtype),
        in_specs=[SMEM] + [ANY] * len(arrived),
        out_specs=VMEM,
        scratch_shapes=[pltpu.SemaphoreType.DMA((request.shape[0],))],
        compiler_params=params(),
        cost_estimate=cost(0, 4 * math.prod(shape)),
        name="compact_rows",
    )(request, *arrived)


def weight_specs(rows, step):
    return [
        pl.BlockSpec((rows, step), lambda i: (0, jnp.minimum(i, 1))),
        pl.BlockSpec((rows, step), lambda i: (0, jnp.maximum(i - 2, 0))),
    ]


def with_weight(wk, wv, act):
    @pl.when(pl.program_id(0) < 2)
    def _():
        act(wk)

    @pl.when(pl.program_id(0) >= 2)
    def _():
        act(wv)


def project_body(n_in, *refs):
    wk, wv, out = refs[n_in : n_in + 3]
    n, sub, enc = refs[0].shape
    rows = jnp.concatenate([ref[...].reshape(n * sub, enc) for ref in refs[:n_in]], axis=0)

    def act(w):
        res = jnp.dot(rows, w[...], preferred_element_type=F32)
        out[...] = res.astype(BF16).reshape(out.shape)

    with_weight(wk, wv, act)


def project(pieces, wk, wv):
    n_in = len(pieces)
    n, sub, enc = pieces[0].shape
    width = 2 * wk.shape[1]
    step = width // 4
    return pl.pallas_call(
        functools.partial(project_body, n_in),
        out_shape=jax.ShapeDtypeStruct((n_in, n, sub, width), BF16),
        grid=(4,),
        in_specs=[pl.BlockSpec((n, sub, enc), lambda i: (0, 0, 0))] * n_in
        + weight_specs(enc, step),
        out_specs=pl.BlockSpec((n_in, n, sub, step), lambda i: (0, 0, 0, i)),
        compiler_params=params(),
        cost_estimate=cost(
            2 * n_in * n * sub * enc * width, 2 * (n_in * n * sub * (enc + width) + enc * width)
        ),
        name="project",
    )(*pieces, wk, wv)


def attend_body(places, n_kv, n_late, near, *refs):
    kvs, late = refs[:n_kv], refs[n_kv : n_kv + n_late]
    wk, wv, q_ref, g_ref, att_ref, dq_ref = refs[n_kv + n_late : n_kv + n_late + 6]
    *grads, near_out, far_out, own_out, late_kv, own_all, core_all = refs[n_kv + n_late + 6 :]
    step = pl.program_id(0)
    width = q_ref.shape[1]
    enc = wk.shape[0]
    scale = 1.0 / math.sqrt(HD)
    heads = width // HD
    group = min(8, heads)
    last = (((1,), (1,)), ((), ()))
    first = (((0,), (0,)), ((), ()))

    def dot(a, b, dims=(((1,), (0,)), ((), ()))):
        return lax.dot_general(a, b, dims, preferred_element_type=F32)

    @pl.when(step == 0)
    def _():
        rows = jnp.concatenate([ref[...].reshape(-1, enc) for ref in late], axis=0)
        shape = late_kv.shape[:3] + (width,)
        late_kv[:, :, :, :width] = dot(rows, wk[...]).astype(BF16).reshape(shape)
        late_kv[:, :, :, width:] = dot(rows, wv[...]).astype(BF16).reshape(shape)

    mine = pl.ds(2 * step, 2)

    def rows_of(col):
        cols = pl.ds(col, HD)
        parts = [ref[:, :, :, cols].reshape(-1, HD) for ref in kvs]
        parts.append(late_kv[:, mine, :, cols].reshape(-1, HD))
        return jnp.concatenate(parts, axis=0)

    def put(col, grad):
        cols = pl.ds(col, HD)
        for at, (kind, i) in enumerate(places):
            block = grad[at * 2 * SUB : (at + 1) * 2 * SUB].reshape(2, SUB, HD)
            grads[kind][i, :, :, cols] = block
            (own_all, core_all)[kind][i, mine, :, cols] = block

    zero = jnp.zeros((SPAN, HD), BF16)
    for h0 in range(0, heads, group):
        hs = range(h0, h0 + group)
        qg, kv = [], []
        for h in hs:
            cols = pl.ds(h * HD, HD)
            top = jnp.concatenate([q_ref[:, cols], zero], axis=1)
            low = jnp.concatenate([zero, g_ref[:, cols]], axis=1)
            qg.append(jnp.concatenate([top, low], axis=0))
            kv.append(jnp.concatenate([rows_of(h * HD), rows_of(width + h * HD)], axis=1))
        both = [dot(a, b, last) for a, b in zip(qg, kv)]
        s = jnp.concatenate([x[:SPAN] for x in both], axis=0) * scale
        dw = jnp.concatenate([x[SPAN:] for x in both], axis=0)
        e = jnp.exp(s - jnp.max(s, axis=1, keepdims=True))
        p = e * (1.0 / jnp.sum(e, axis=1, keepdims=True))
        rs = jnp.sum(dw * p, axis=1, keepdims=True)
        w = p.astype(BF16)
        ds = (p * (dw - rs) * scale).astype(BF16)
        span = [slice(i * SPAN, (i + 1) * SPAN) for i in range(group)]
        dsw = [jnp.concatenate([ds[i], w[i]], axis=0) for i in span]
        out = [dot(a, b).astype(BF16) for a, b in zip(dsw, kv)]
        back = [dot(a, b, first).astype(BF16) for a, b in zip(dsw, qg)]
        for i, h in enumerate(hs):
            dq_ref[:, pl.ds(h * HD, HD)] = out[i][:SPAN, :HD]
            att_ref[:, pl.ds(h * HD, HD)] = out[i][SPAN:, HD:]
            put(h * HD, back[i][:, :HD])
            put(width + h * HD, back[i][:, HD:])

    @pl.when(step == pl.num_programs(0) - 1)
    def _():
        count = own_out.shape[-1]
        for ref, outs in ((core_all, (near_out, far_out)), (own_all, (own_out,))):
            rows = ref[...].reshape(-1, 2 * width)
            res = dot(rows[:, :width], wk[:count, :], last) + dot(rows[:, width:], wv[:count, :], last)
            res = res.reshape(ref.shape[:3] + (count,))
            if len(outs) == 1:
                outs[0][...] = res
            else:
                outs[0][...] = res[:near]
                outs[1][...] = res[near:]


def attend(kvs, late, wk, wv, places, near, count, queries, cotangent):
    tokens, width = queries.shape
    spans = tokens // SPAN
    n = kvs[0].shape[1]
    enc = wk.shape[0]
    pieces = len(places) // 2
    rows = pl.BlockSpec((SPAN, width), lambda i: (i, 0))

    def kv_block(pieces):
        return pl.BlockSpec((pieces, 2, SUB, 2 * width), lambda i: (0, i, 0, 0))

    def whole(shape):
        return pl.BlockSpec(shape, lambda i: (0,) * len(shape))

    keys = len(places) * 2 * SUB
    parts = [(near, n, SUB, count), (pieces - near, n, SUB, count), (pieces, n, SUB, count)]
    every = (pieces, n, SUB, 2 * width)
    return pl.pallas_call(
        functools.partial(attend_body, places, len(kvs), len(late), near),
        out_shape=[jax.ShapeDtypeStruct((tokens, width), BF16)] * 2
        + [jax.ShapeDtypeStruct(every, BF16)] * 2
        + [jax.ShapeDtypeStruct(part, F32) for part in parts],
        grid=(spans,),
        in_specs=[kv_block(kv.shape[0]) for kv in kvs]
        + [whole(x.shape) for x in late]
        + [whole(wk.shape), whole(wv.shape), rows, rows],
        out_specs=[rows, rows] + [kv_block(pieces)] * 2 + [whole(part) for part in parts],
        scratch_shapes=[
            pltpu.VMEM((len(late), n, SUB, 2 * width), BF16),
            pltpu.VMEM(every, BF16),
            pltpu.VMEM(every, BF16),
        ],
        compiler_params=params(VMEM_MORE),
        cost_estimate=cost(
            16 * tokens * width * keys + 4 * n * SUB * width * (len(late) * enc + 2 * pieces * count),
            8 * tokens * width + 8 * spans * keys * 2 * width,
        ),
        name="attend",
    )(*kvs, *late, wk, wv, queries, cotangent)


def encode(x, axes):
    top = jnp.maximum(jnp.max(jnp.abs(x), axis=axes, keepdims=True), 1e-30)
    power = jnp.floor(jnp.log2(top)) + 1.0
    code = jnp.clip(jnp.round(x * jnp.exp2(15.0 - power)), -32767.0, 32767.0)
    return code.astype(jnp.int32).astype(jnp.int16), power


def grads_body(near, first, core_ref, own_ref, wk, wv, near_out, far_out, own_out, core_acc, own_acc):
    i = pl.program_id(0)

    def act(w):
        w = w[first : first + own_acc.shape[1], :]
        for ref, acc in ((core_ref, core_acc), (own_ref, own_acc)):
            rows = ref[...].reshape(acc.shape[0], -1)
            part = lax.dot_general(rows, w, (((1,), (1,)), ((), ())), preferred_element_type=F32)

            @pl.when(i == 0)
            def _():
                acc[...] = part

            @pl.when(i > 0)
            def _():
                acc[...] += part

    with_weight(wk, wv, act)

    @pl.when(i == pl.num_programs(0) - 1)
    def _():
        core = core_acc[...].reshape(core_ref.shape[:3] + core_acc.shape[1:])
        near_out[...] = core[:near]
        far_out[...] = core[near:]
        own_out[...] = own_acc[...].reshape(own_out.shape)


def grads_of(d_core, d_own, wk, wv, near, cols):
    pieces, n, sub, width = d_own.shape
    first, count = cols
    step = width // 4
    shapes = [(near, n, sub, count), (pieces - near, n, sub, count), (pieces, n, sub, count)]
    rows = pieces * n * sub
    return pl.pallas_call(
        functools.partial(grads_body, near, first),
        out_shape=[jax.ShapeDtypeStruct(shape, F32) for shape in shapes],
        grid=(4,),
        in_specs=[pl.BlockSpec((pieces, n, sub, step), lambda i: (0, 0, 0, i))] * 2
        + weight_specs(wk.shape[0], step),
        out_specs=[pl.BlockSpec(shape, lambda i: (0, 0, 0, 0)) for shape in shapes],
        scratch_shapes=[pltpu.VMEM((rows, count), F32)] * 2,
        compiler_params=params(VMEM_ALL),
        cost_estimate=cost(4 * rows * count * width, 2 * (count + 2 * rows) * width + 8 * rows * count),
        name="grads",
    )(d_core, d_own, wk, wv)


def put_codes(far, codes):
    pieces, n, sub, count = far.shape
    near = codes[0].shape[0]
    tiles = count // LANES
    row = lax.broadcasted_iota(jnp.int32, (SUB, LANES), 0)
    for i in range(pieces):
        out, c = codes[i // near], i % near
        code, power = encode(far[i], (1, 2))
        for e in range(tiles):
            out[c, e * n : (e + 1) * n] = code[:, :, e * LANES : (e + 1) * LANES]
        note = jnp.zeros((SUB, LANES), F32)
        for r in range(n):
            note = jnp.where(row == r, power[r], note)
        out[c, tiles * n] = note.astype(jnp.int32).astype(jnp.int16)


def far_codes_body(mine, got, *codes):
    put_codes(mine[...] + got[...], codes)


def far_codes(own, got, near):
    far, n, sub, count = got.shape
    shape = (near, count // LANES * n + 1, sub, LANES)
    return pl.pallas_call(
        far_codes_body,
        out_shape=[jax.ShapeDtypeStruct(shape, jnp.int16)] * (far // near),
        grid=(1,),
        in_specs=[
            pl.BlockSpec((pl.Element(far), pl.Element(n), pl.Element(sub), pl.Element(count)), lambda i: (near, 0, 0, 0)),
            pl.BlockSpec(got.shape, lambda i: (0, 0, 0, 0)),
        ],
        out_specs=[pl.BlockSpec(shape, lambda i: (0, 0, 0, 0))] * (far // near),
        compiler_params=params(),
        cost_estimate=cost(8 * got.size, 10 * got.size),
        name="far_codes",
    )(own, got)


def send_body(n_dp, request, own, got, *rest):
    codes, outs, (stage, powers) = rest[: -n_dp - 2], rest[-n_dp - 2 : -2], rest[-2:]
    n_chunks, n, sub, count = got.shape
    tiles = count // LANES
    cap = request.shape[0] // n_dp
    for c in range(n_chunks):
        for r in range(n):
            total = own[c, r] + got[c, r]
            for code in codes:
                unit = jnp.exp2(code[c, tiles * n].astype(F32)[r : r + 1] - 15.0)
                total = total + jnp.concatenate(
                    [code[c, e * n + r].astype(F32) * unit for e in range(tiles)], axis=1
                )
            coded, power = encode(total, (0, 1))
            for e in range(tiles):
                stage[r, c * tiles + e] = coded[:, e * LANES : (e + 1) * LANES]
            powers[r, c] = jnp.broadcast_to(power, (SUB, LANES))
    row = lax.broadcasted_iota(jnp.int32, (SUB, LANES), 0)
    for d in range(n_dp):
        note = jnp.zeros((SUB, LANES), F32)
        for j in range(cap):
            r = request[d * cap + j]

            @pl.when(r >= 0)
            def _():
                outs[d][pl.ds(j * n_chunks * tiles, n_chunks * tiles)] = stage[r]

            for c in range(n_chunks):
                note = jnp.where(row == j * n_chunks + c, powers[jnp.maximum(r, 0), c], note)
        outs[d][cap * n_chunks * tiles] = note.astype(jnp.int32).astype(jnp.int16)


def send_codes(request, own, got, codes, n_dp):
    n_chunks, n, sub, count = got.shape
    block = pl.BlockSpec(got.shape, lambda i: (0, 0, 0, 0))
    tiles = count // LANES
    cap = request.shape[0] // n_dp
    shape = (cap * n_chunks * tiles + 1, SUB, LANES)
    return pl.pallas_call(
        functools.partial(send_body, n_dp),
        out_shape=[jax.ShapeDtypeStruct(shape, jnp.int16)] * n_dp,
        grid=(1,),
        in_specs=[SMEM, block, block] + [VMEM] * len(codes),
        out_specs=[VMEM] * n_dp,
        scratch_shapes=[
            pltpu.VMEM((n, n_chunks * tiles, SUB, LANES), jnp.int16),
            pltpu.VMEM((n, n_chunks, SUB, LANES), F32),
        ],
        compiler_params=params(),
        cost_estimate=cost(10 * got.size, 6 * got.size + 2 * n_dp * math.prod(shape)),
        name="send_codes",
    )(request, own, got, *codes)


def gather_body(n_dp, n_chunks, first, me, asked, *refs):
    arrived = refs[:n_dp]
    out, total, sem = refs[-3:]
    count = total.shape[2]
    tiles = count // LANES
    cap = asked.shape[1] // n_dp
    total[...] = jnp.zeros_like(total)
    for d in range(n_dp):
        for j in range(cap):
            slab = asked_of(asked, me, d, j)

            @pl.when(slab >= 0)
            def _():
                note = arrived[d][cap * n_chunks * tiles].astype(F32)
                for c in range(n_chunks):
                    at = j * n_chunks + c
                    unit = jnp.exp2(note[at : at + 1] - 15.0)
                    for e in range(tiles):
                        value = arrived[d][at * tiles + e].astype(F32) * unit
                        total[slab, pl.ds(c * SUB, SUB), pl.ds(e * LANES, LANES)] += value

    copy = pltpu.make_async_copy(total, out.at[:, :, pl.ds(first, count)], sem)
    copy.start()
    copy.wait()


def gather_grads(me, asked, arrived, n_slabs, n_chunks, enc, cols, before):
    first, count = cols
    n_dp = asked.shape[0]
    rows = n_chunks * SUB
    return pl.pallas_call(
        functools.partial(gather_body, n_dp, n_chunks, first),
        out_shape=jax.ShapeDtypeStruct((n_slabs, rows, enc), F32),
        in_specs=[SMEM, SMEM] + [VMEM] * n_dp + [ANY] * (before is not None),
        out_specs=ANY,
        scratch_shapes=[pltpu.VMEM((n_slabs, rows, count), F32), pltpu.SemaphoreType.DMA],
        input_output_aliases={} if before is None else {2 + n_dp: 0},
        compiler_params=params(),
        cost_estimate=cost(0, 8 * n_slabs * rows * count),
        name="gather_grads",
    )(me, asked, *arrived, *([] if before is None else [before]))


def on_device(queries, cotangent, table, key_weight, value_weight, owners, slots):
    n_dp = lax.axis_size("dp")
    n_tp = lax.axis_size("tensor")
    n_x = n_tp // 2
    spans = owners.shape[0]
    n_requests = 2 * spans
    n_slabs, n_tokens, enc = table.shape
    cap = max(2, (4 * spans + n_dp - 1) // n_dp)
    share = n_tokens // n_tp
    n_chunks = share // SUB

    def over_core(x):
        return lax.ppermute(x, "tensor", [(t, t ^ 1) for t in range(n_tp)])

    def over_x(x, d):
        return lax.ppermute(x, "tensor", [(t, (t + 2 * d) % n_tp) for t in range(n_tp)])

    def over_dp(x, d):
        return lax.ppermute(x, "dp", [(i, (i + d) % n_dp) for i in range(n_dp)])

    farthest_first = sorted(range(1, n_dp), key=lambda d: -min(d, n_dp - d))

    def to_all(xs, sign, distances=farthest_first):
        got = {d: over_dp(xs[d], sign * d) for d in distances}
        return got

    me, wanted, request = ask(owners, slots, n_dp, cap)
    asked = lax.psum(wanted, "dp")

    def place(c, kind, d):
        return (kind, c if d == 0 else n_chunks * d + c)

    kvs, places = [], []
    early = {}
    sent = pack(me, asked, table, 0, share, cap)
    for c in range(n_chunks):
        rest = [d for d in farthest_first if d not in early]
        arrived = [sent[0]] + [None] * (n_dp - 1)
        for d, x in {**early, **to_all(sent, -1, rest)}.items():
            arrived[d] = x
        if c < n_chunks - 1:
            sent = pack(me, asked, table, c + 1, share, cap)
            early = to_all(sent, -1, farthest_first[:1])
            early, arrived = lax.optimization_barrier((early, arrived))
        if kvs:
            arrived, kvs = lax.optimization_barrier((arrived, kvs))
        mine = compact(request, arrived, n_requests)
        near = [mine, over_core(mine)]
        far = [over_x(mine, d) for d in range(1, n_x)]
        near_at = [place(c, kind, 0) for kind in range(2)]
        far_at = [place(c, kind, d) for kind in range(2) for d in range(1, n_x)]
        if c < n_chunks - 1:
            early = {**early, **to_all(sent, -1, farthest_first[1:4])}
            early, far = lax.optimization_barrier((early, far))
            far = far + [over_core(x) for x in far]
            kvs = kvs + [project(near + far, key_weight, value_weight)]
        else:
            near = project(near, key_weight, value_weight)
            near, far = lax.optimization_barrier((near, far))
            late = far + [over_core(x) for x in far]
            kvs = kvs + [near]
        places += near_at + far_at

    split = 3 * LANES
    parts = ((0, split), (split, enc - split))
    attended, d_query, d_own, d_core, near, far, own = attend(
        kvs, late, key_weight, value_weight, places, n_chunks, split, queries, cotangent
    )
    far_got = over_core(far)
    near_got = over_core(near)
    codes = far_codes(own, far_got, n_chunks)
    near_b, far_b, own_b = grads_of(d_core, d_own, key_weight, value_weight, n_chunks, parts[1])

    d_table = None
    for part in range(2):
        codes = [over_x(code, n_x - d) for d, code in enumerate(codes, 1)]
        sent = send_codes(request, own, near_got, codes, n_dp)
        if part == 0:
            sent, near_b, far_b = lax.optimization_barrier((sent, near_b, far_b))
        came = to_all(sent, 1)
        if part == 0:
            far_got = over_core(far_b)
            near_got = over_core(near_b)
            own = own_b
            lead = {d: came[d] for d in farthest_first[:2]}
            far_got, lead = lax.optimization_barrier((far_got, lead))
            came.update(lead)
            codes = far_codes(own, far_got, n_chunks)
        arrived = [sent[0]] + [came[d] for d in range(1, n_dp)]
        d_table = gather_grads(me, asked, arrived, n_slabs, n_chunks, enc, parts[part], d_table)
    return (attended, d_query, d_table)


def solution(mesh):
    in_specs = (
        P("dp", "tensor"),
        P("dp", "tensor"),
        P("dp", None, None),
        P(None, "tensor"),
        P(None, "tensor"),
        P("dp", None),
        P("dp", None),
    )
    out_specs = (P("dp", "tensor"), P("dp", "tensor"), P("dp", "tensor", None))
    return jax.shard_map(
        on_device, mesh=mesh, in_specs=in_specs, out_specs=out_specs, check_vma=False
    )
```

```python
import functools
import math

import jax
import jax.numpy as jnp
from jax import lax
from jax.experimental import pallas as pl
from jax.experimental.pallas import tpu as pltpu
from jax.sharding import PartitionSpec as P

HD = 128
SPAN = 64
SUB = 16
LANES = 128
VMEM_LIMIT = 28 * 1024 * 1024
VMEM_MORE = 40 * 1024 * 1024
VMEM_ALL = 60 * 1024 * 1024
F32 = jnp.float32
BF16 = jnp.bfloat16

ANY = pl.BlockSpec(memory_space=pl.ANY)
SMEM = pl.BlockSpec(memory_space=pltpu.SMEM)
VMEM = pl.BlockSpec(memory_space=pltpu.VMEM)


def params(limit=VMEM_LIMIT):
    return pltpu.CompilerParams(vmem_limit_bytes=limit)


def cost(flops, nbytes):
    return pl.CostEstimate(flops=int(flops), bytes_accessed=int(nbytes), transcendentals=0)


def ask_body(cap, owners, slots, me_out, wanted, request, count):
    n_dp = wanted.shape[0]
    me = lax.axis_index("dp")
    me_out[0] = me
    for i in range(n_dp * cap):
        request[i] = -1
        for asker in range(n_dp):
            wanted[asker, i] = 0
    for d in range(n_dp):
        count[d] = 0
    for r in range(owners.size):
        d = owners[r % 2, r // 2] - me
        d = jnp.where(d < 0, d + n_dp, d)
        j = count[d]
        count[d] = j + 1
        wanted[me, d * cap + j] = slots[r % 2, r // 2] + 1
        request[d * cap + j] = r


def ask(owners, slots, n_dp, cap):
    return pl.pallas_call(
        functools.partial(ask_body, cap),
        out_shape=[
            jax.ShapeDtypeStruct((1,), jnp.int32),
            jax.ShapeDtypeStruct((n_dp, n_dp * cap), jnp.int32),
            jax.ShapeDtypeStruct((n_dp * cap,), jnp.int32),
        ],
        in_specs=[SMEM, SMEM],
        out_specs=[SMEM, SMEM, SMEM],
        scratch_shapes=[pltpu.SMEM((n_dp,), jnp.int32)],
        name="ask",
    )(owners.T, slots.T)


def asked_of(asked, me, d, j):
    n_dp = asked.shape[0]
    asker = me[0] - d
    asker = jnp.where(asker < 0, asker + n_dp, asker)
    return asked[asker, d * (asked.shape[1] // n_dp) + j] - 1


def pack_body(n_dp, chunk, share, me, asked, table, *rest):
    outs, sem = rest[:-1], rest[-1]
    cap = outs[0].shape[0]
    row = pl.multiple_of(lax.axis_index("tensor") * share + chunk * SUB, SUB)

    def each(act):
        for d in range(n_dp):
            for j in range(cap):
                slab = asked_of(asked, me, d, j)

                @pl.when(slab >= 0)
                def _():
                    source = table.at[slab, pl.ds(row, SUB)]
                    act(pltpu.make_async_copy(source, outs[d].at[j], sem.at[d * cap + j]))

    each(lambda copy: copy.start())
    each(lambda copy: copy.wait())


def pack(me, asked, table, chunk, share, cap):
    n_dp = asked.shape[0]
    enc = table.shape[2]
    return pl.pallas_call(
        functools.partial(pack_body, n_dp, chunk, share),
        out_shape=[jax.ShapeDtypeStruct((cap, SUB, enc), table.dtype)] * n_dp,
        in_specs=[SMEM, SMEM, ANY],
        out_specs=[VMEM] * n_dp,
        scratch_shapes=[pltpu.SemaphoreType.DMA((n_dp * cap,))],
        compiler_params=params(VMEM_ALL),
        cost_estimate=cost(0, 4 * n_dp * cap * SUB * enc),
        name="pack_rows",
    )(me, asked, table)


def compact_body(n_dp, request, *refs):
    arrived, out, sem = refs[:n_dp], refs[n_dp], refs[n_dp + 1]
    cap = arrived[0].shape[0]

    def each(act):
        for d in range(n_dp):
            for j in range(cap):
                r = request[d * cap + j]

                @pl.when(r >= 0)
                def _():
                    act(pltpu.make_async_copy(arrived[d].at[j], out.at[r], sem.at[d * cap + j]))

    each(lambda copy: copy.start())
    each(lambda copy: copy.wait())


def compact(request, arrived, n):
    shape = (n,) + arrived[0].shape[1:]
    return pl.pallas_call(
        functools.partial(compact_body, len(arrived)),
        out_shape=jax.ShapeDtypeStruct(shape, arrived[0].dtype),
        in_specs=[SMEM] + [ANY] * len(arrived),
        out_specs=VMEM,
        scratch_shapes=[pltpu.SemaphoreType.DMA((request.shape[0],))],
        compiler_params=params(),
        cost_estimate=cost(0, 4 * math.prod(shape)),
        name="compact_rows",
    )(request, *arrived)


def weight_specs(rows, step):
    return [
        pl.BlockSpec((rows, step), lambda i: (0, jnp.minimum(i, 1))),
        pl.BlockSpec((rows, step), lambda i: (0, jnp.maximum(i - 2, 0))),
    ]


def with_weight(wk, wv, act):
    @pl.when(pl.program_id(0) < 2)
    def _():
        act(wk)

    @pl.when(pl.program_id(0) >= 2)
    def _():
        act(wv)


def project_body(n_in, *refs):
    wk, wv, out = refs[n_in : n_in + 3]
    n, sub, enc = refs[0].shape
    rows = jnp.concatenate([ref[...].reshape(n * sub, enc) for ref in refs[:n_in]], axis=0)

    def act(w):
        res = jnp.dot(rows, w[...], preferred_element_type=F32)
        out[...] = res.astype(BF16).reshape(out.shape)

    with_weight(wk, wv, act)


def project(pieces, wk, wv):
    n_in = len(pieces)
    n, sub, enc = pieces[0].shape
    width = 2 * wk.shape[1]
    step = width // 4
    return pl.pallas_call(
        functools.partial(project_body, n_in),
        out_shape=jax.ShapeDtypeStruct((n_in, n, sub, width), BF16),
        grid=(4,),
        in_specs=[pl.BlockSpec((n, sub, enc), lambda i: (0, 0, 0))] * n_in
        + weight_specs(enc, step),
        out_specs=pl.BlockSpec((n_in, n, sub, step), lambda i: (0, 0, 0, i)),
        compiler_params=params(VMEM_ALL),
        cost_estimate=cost(
            2 * n_in * n * sub * enc * width, 2 * (n_in * n * sub * (enc + width) + enc * width)
        ),
        name="project",
    )(*pieces, wk, wv)


def attend_body(places, n_kv, n_late, near, *refs):
    kvs, late = refs[:n_kv], refs[n_kv : n_kv + n_late]
    wk, wv, q_ref, g_ref, att_ref, dq_ref = refs[n_kv + n_late : n_kv + n_late + 6]
    *grads, near_out, far_out, own_out, late_kv, own_all, core_all = refs[n_kv + n_late + 6 :]
    step = pl.program_id(0)
    width = q_ref.shape[1]
    enc = wk.shape[0]
    scale = 1.0 / math.sqrt(HD)
    heads = width // HD
    group = min(8, heads)
    last = (((1,), (1,)), ((), ()))
    first = (((0,), (0,)), ((), ()))

    def dot(a, b, dims=(((1,), (0,)), ((), ()))):
        return lax.dot_general(a, b, dims, preferred_element_type=F32)

    @pl.when(step == 0)
    def _():
        rows = jnp.concatenate([ref[...].reshape(-1, enc) for ref in late], axis=0)
        shape = late_kv.shape[:3] + (width,)
        late_kv[:, :, :, :width] = dot(rows, wk[...]).astype(BF16).reshape(shape)
        late_kv[:, :, :, width:] = dot(rows, wv[...]).astype(BF16).reshape(shape)

    mine = pl.ds(2 * step, 2)

    def rows_of(col):
        cols = pl.ds(col, HD)
        parts = [ref[:, :, :, cols].reshape(-1, HD) for ref in kvs]
        parts.append(late_kv[:, mine, :, cols].reshape(-1, HD))
        return jnp.concatenate(parts, axis=0)

    def put(col, grad):
        cols = pl.ds(col, HD)
        for at, (kind, i) in enumerate(places):
            block = grad[at * 2 * SUB : (at + 1) * 2 * SUB].reshape(2, SUB, HD)
            grads[kind][i, :, :, cols] = block
            (own_all, core_all)[kind][i, mine, :, cols] = block

    zero = jnp.zeros((SPAN, HD), BF16)
    for h0 in range(0, heads, group):
        hs = range(h0, h0 + group)
        qg, kv = [], []
        for h in hs:
            cols = pl.ds(h * HD, HD)
            top = jnp.concatenate([q_ref[:, cols], zero], axis=1)
            low = jnp.concatenate([zero, g_ref[:, cols]], axis=1)
            qg.append(jnp.concatenate([top, low], axis=0))
            kv.append(jnp.concatenate([rows_of(h * HD), rows_of(width + h * HD)], axis=1))
        both = [dot(a, b, last) for a, b in zip(qg, kv)]
        s = jnp.concatenate([x[:SPAN] for x in both], axis=0) * scale
        dw = jnp.concatenate([x[SPAN:] for x in both], axis=0)
        e = jnp.exp(s - jnp.max(s, axis=1, keepdims=True))
        p = e * (1.0 / jnp.sum(e, axis=1, keepdims=True))
        rs = jnp.sum(dw * p, axis=1, keepdims=True)
        w = p.astype(BF16)
        ds = (p * (dw - rs) * scale).astype(BF16)
        span = [slice(i * SPAN, (i + 1) * SPAN) for i in range(group)]
        dsw = [jnp.concatenate([ds[i], w[i]], axis=0) for i in span]
        out = [dot(a, b).astype(BF16) for a, b in zip(dsw, kv)]
        back = [dot(a, b, first).astype(BF16) for a, b in zip(dsw, qg)]
        for i, h in enumerate(hs):
            dq_ref[:, pl.ds(h * HD, HD)] = out[i][:SPAN, :HD]
            att_ref[:, pl.ds(h * HD, HD)] = out[i][SPAN:, HD:]
            put(h * HD, back[i][:, :HD])
            put(width + h * HD, back[i][:, HD:])

    @pl.when(step == pl.num_programs(0) - 1)
    def _():
        count = own_out.shape[-1]
        for ref, outs in ((core_all, (near_out, far_out)), (own_all, (own_out,))):
            rows = ref[...].reshape(-1, 2 * width)
            res = dot(rows[:, :width], wk[:count, :], last) + dot(rows[:, width:], wv[:count, :], last)
            res = res.reshape(ref.shape[:3] + (count,))
            if len(outs) == 1:
                outs[0][...] = res
            else:
                outs[0][...] = res[:near]
                outs[1][...] = res[near:]


def attend(kvs, late, wk, wv, places, near, count, queries, cotangent):
    tokens, width = queries.shape
    spans = tokens // SPAN
    n = kvs[0].shape[1]
    enc = wk.shape[0]
    pieces = len(places) // 2
    rows = pl.BlockSpec((SPAN, width), lambda i: (i, 0))

    def kv_block(pieces):
        return pl.BlockSpec((pieces, 2, SUB, 2 * width), lambda i: (0, i, 0, 0))

    def whole(shape):
        return pl.BlockSpec(shape, lambda i: (0,) * len(shape))

    keys = len(places) * 2 * SUB
    parts = [(near, n, SUB, count), (pieces - near, n, SUB, count), (pieces, n, SUB, count)]
    every = (pieces, n, SUB, 2 * width)
    return pl.pallas_call(
        functools.partial(attend_body, places, len(kvs), len(late), near),
        out_shape=[jax.ShapeDtypeStruct((tokens, width), BF16)] * 2
        + [jax.ShapeDtypeStruct(every, BF16)] * 2
        + [jax.ShapeDtypeStruct(part, F32) for part in parts],
        grid=(spans,),
        in_specs=[kv_block(kv.shape[0]) for kv in kvs]
        + [whole(x.shape) for x in late]
        + [whole(wk.shape), whole(wv.shape), rows, rows],
        out_specs=[rows, rows] + [kv_block(pieces)] * 2 + [whole(part) for part in parts],
        scratch_shapes=[
            pltpu.VMEM((len(late), n, SUB, 2 * width), BF16),
            pltpu.VMEM(every, BF16),
            pltpu.VMEM(every, BF16),
        ],
        compiler_params=params(VMEM_MORE),
        cost_estimate=cost(
            16 * tokens * width * keys + 4 * n * SUB * width * (len(late) * enc + 2 * pieces * count),
            8 * tokens * width + 8 * spans * keys * 2 * width,
        ),
        name="attend",
    )(*kvs, *late, wk, wv, queries, cotangent)


def encode(x, axes):
    top = jnp.maximum(jnp.max(jnp.abs(x), axis=axes, keepdims=True), 1e-30)
    power = jnp.floor(jnp.log2(top)) + 1.0
    code = jnp.clip(jnp.round(x * jnp.exp2(15.0 - power)), -32767.0, 32767.0)
    return code.astype(jnp.int32).astype(jnp.int16), power


def grads_body(near, first, core_ref, own_ref, wk, wv, near_out, far_out, own_out, core_acc, own_acc):
    i = pl.program_id(0)

    def act(w):
        w = w[first : first + own_acc.shape[1], :]
        for ref, acc in ((core_ref, core_acc), (own_ref, own_acc)):
            rows = ref[...].reshape(acc.shape[0], -1)
            part = lax.dot_general(rows, w, (((1,), (1,)), ((), ())), preferred_element_type=F32)

            @pl.when(i == 0)
            def _():
                acc[...] = part

            @pl.when(i > 0)
            def _():
                acc[...] += part

    with_weight(wk, wv, act)

    @pl.when(i == pl.num_programs(0) - 1)
    def _():
        core = core_acc[...].reshape(core_ref.shape[:3] + core_acc.shape[1:])
        near_out[...] = core[:near]
        far_out[...] = core[near:]
        own_out[...] = own_acc[...].reshape(own_out.shape)


def grads_of(d_core, d_own, wk, wv, near, cols):
    pieces, n, sub, width = d_own.shape
    first, count = cols
    step = width // 4
    shapes = [(near, n, sub, count), (pieces - near, n, sub, count), (pieces, n, sub, count)]
    rows = pieces * n * sub
    return pl.pallas_call(
        functools.partial(grads_body, near, first),
        out_shape=[jax.ShapeDtypeStruct(shape, F32) for shape in shapes],
        grid=(4,),
        in_specs=[pl.BlockSpec((pieces, n, sub, step), lambda i: (0, 0, 0, i))] * 2
        + weight_specs(wk.shape[0], step),
        out_specs=[pl.BlockSpec(shape, lambda i: (0, 0, 0, 0)) for shape in shapes],
        scratch_shapes=[pltpu.VMEM((rows, count), F32)] * 2,
        compiler_params=params(VMEM_ALL),
        cost_estimate=cost(4 * rows * count * width, 2 * (count + 2 * rows) * width + 8 * rows * count),
        name="grads",
    )(d_core, d_own, wk, wv)


def put_codes(far, codes):
    pieces, n, sub, count = far.shape
    near = codes[0].shape[0]
    tiles = count // LANES
    row = lax.broadcasted_iota(jnp.int32, (SUB, LANES), 0)
    for i in range(pieces):
        out, c = codes[i // near], i % near
        code, power = encode(far[i], (1, 2))
        for e in range(tiles):
            out[c, e * n : (e + 1) * n] = code[:, :, e * LANES : (e + 1) * LANES]
        note = jnp.zeros((SUB, LANES), F32)
        for r in range(n):
            note = jnp.where(row == r, power[r], note)
        out[c, tiles * n] = note.astype(jnp.int32).astype(jnp.int16)


def far_codes_body(mine, got, *codes):
    put_codes(mine[...] + got[...], codes)


def far_codes(own, got, near):
    far, n, sub, count = got.shape
    shape = (near, count // LANES * n + 1, sub, LANES)
    return pl.pallas_call(
        far_codes_body,
        out_shape=[jax.ShapeDtypeStruct(shape, jnp.int16)] * (far // near),
        grid=(1,),
        in_specs=[
            pl.BlockSpec((pl.Element(far), pl.Element(n), pl.Element(sub), pl.Element(count)), lambda i: (near, 0, 0, 0)),
            pl.BlockSpec(got.shape, lambda i: (0, 0, 0, 0)),
        ],
        out_specs=[pl.BlockSpec(shape, lambda i: (0, 0, 0, 0))] * (far // near),
        compiler_params=params(),
        cost_estimate=cost(8 * got.size, 10 * got.size),
        name="far_codes",
    )(own, got)


def send_body(n_dp, request, own, got, *rest):
    codes, outs, (stage, powers) = rest[: -n_dp - 2], rest[-n_dp - 2 : -2], rest[-2:]
    n_chunks, n, sub, count = got.shape
    tiles = count // LANES
    cap = request.shape[0] // n_dp
    for c in range(n_chunks):
        for r in range(n):
            total = own[c, r] + got[c, r]
            for code in codes:
                unit = jnp.exp2(code[c, tiles * n].astype(F32)[r : r + 1] - 15.0)
                total = total + jnp.concatenate(
                    [code[c, e * n + r].astype(F32) * unit for e in range(tiles)], axis=1
                )
            coded, power = encode(total, (0, 1))
            for e in range(tiles):
                stage[r, c * tiles + e] = coded[:, e * LANES : (e + 1) * LANES]
            powers[r, c] = jnp.broadcast_to(power, (SUB, LANES))
    row = lax.broadcasted_iota(jnp.int32, (SUB, LANES), 0)
    for d in range(n_dp):
        note = jnp.zeros((SUB, LANES), F32)
        for j in range(cap):
            r = request[d * cap + j]

            @pl.when(r >= 0)
            def _():
                outs[d][pl.ds(j * n_chunks * tiles, n_chunks * tiles)] = stage[r]

            for c in range(n_chunks):
                note = jnp.where(row == j * n_chunks + c, powers[jnp.maximum(r, 0), c], note)
        outs[d][cap * n_chunks * tiles] = note.astype(jnp.int32).astype(jnp.int16)


def send_codes(request, own, got, codes, n_dp):
    n_chunks, n, sub, count = got.shape
    block = pl.BlockSpec(got.shape, lambda i: (0, 0, 0, 0))
    tiles = count // LANES
    cap = request.shape[0] // n_dp
    shape = (cap * n_chunks * tiles + 1, SUB, LANES)
    return pl.pallas_call(
        functools.partial(send_body, n_dp),
        out_shape=[jax.ShapeDtypeStruct(shape, jnp.int16)] * n_dp,
        grid=(1,),
        in_specs=[SMEM, block, block] + [VMEM] * len(codes),
        out_specs=[VMEM] * n_dp,
        scratch_shapes=[
            pltpu.VMEM((n, n_chunks * tiles, SUB, LANES), jnp.int16),
            pltpu.VMEM((n, n_chunks, SUB, LANES), F32),
        ],
        compiler_params=params(),
        cost_estimate=cost(10 * got.size, 6 * got.size + 2 * n_dp * math.prod(shape)),
        name="send_codes",
    )(request, own, got, *codes)


def gather_body(n_dp, n_chunks, first, me, asked, *refs):
    arrived = refs[:n_dp]
    out, total, sem = refs[-3:]
    count = total.shape[2]
    tiles = count // LANES
    cap = asked.shape[1] // n_dp
    total[...] = jnp.zeros_like(total)
    for d in range(n_dp):
        for j in range(cap):
            slab = asked_of(asked, me, d, j)

            @pl.when(slab >= 0)
            def _():
                note = arrived[d][cap * n_chunks * tiles].astype(F32)
                for c in range(n_chunks):
                    at = j * n_chunks + c
                    unit = jnp.exp2(note[at : at + 1] - 15.0)
                    for e in range(tiles):
                        value = arrived[d][at * tiles + e].astype(F32) * unit
                        total[slab, pl.ds(c * SUB, SUB), pl.ds(e * LANES, LANES)] += value

    copy = pltpu.make_async_copy(total, out.at[:, :, pl.ds(first, count)], sem)
    copy.start()
    copy.wait()


def gather_grads(me, asked, arrived, n_slabs, n_chunks, enc, cols, before):
    first, count = cols
    n_dp = asked.shape[0]
    rows = n_chunks * SUB
    return pl.pallas_call(
        functools.partial(gather_body, n_dp, n_chunks, first),
        out_shape=jax.ShapeDtypeStruct((n_slabs, rows, enc), F32),
        in_specs=[SMEM, SMEM] + [VMEM] * n_dp + [ANY] * (before is not None),
        out_specs=ANY,
        scratch_shapes=[pltpu.VMEM((n_slabs, rows, count), F32), pltpu.SemaphoreType.DMA],
        input_output_aliases={} if before is None else {2 + n_dp: 0},
        compiler_params=params(),
        cost_estimate=cost(0, 8 * n_slabs * rows * count),
        name="gather_grads",
    )(me, asked, *arrived, *([] if before is None else [before]))


def on_device(queries, cotangent, table, key_weight, value_weight, owners, slots):
    n_dp = lax.axis_size("dp")
    n_tp = lax.axis_size("tensor")
    n_x = n_tp // 2
    spans = owners.shape[0]
    n_requests = 2 * spans
    n_slabs, n_tokens, enc = table.shape
    cap = max(2, (4 * spans + n_dp - 1) // n_dp)
    share = n_tokens // n_tp
    n_chunks = share // SUB

    def over_core(x):
        return lax.ppermute(x, "tensor", [(t, t ^ 1) for t in range(n_tp)])

    def over_x(x, d):
        return lax.ppermute(x, "tensor", [(t, (t + 2 * d) % n_tp) for t in range(n_tp)])

    def over_dp(x, d):
        return lax.ppermute(x, "dp", [(i, (i + d) % n_dp) for i in range(n_dp)])

    farthest_first = sorted(range(1, n_dp), key=lambda d: -min(d, n_dp - d))

    def to_all(xs, sign, distances=farthest_first):
        got = {d: over_dp(xs[d], sign * d) for d in distances}
        return got

    me, wanted, request = ask(owners, slots, n_dp, cap)
    asked = lax.psum(wanted, "dp")

    def place(c, kind, d):
        return (kind, c if d == 0 else n_chunks * d + c)

    kvs, places = [], []
    early, pieces = {}, []
    sent = pack(me, asked, table, 0, share, cap)
    for c in range(n_chunks):
        rest = [d for d in farthest_first if d not in early]
        arrived = [sent[0]] + [None] * (n_dp - 1)
        for d, x in {**early, **to_all(sent, -1, rest)}.items():
            arrived[d] = x
        if c < n_chunks - 1:
            sent = pack(me, asked, table, c + 1, share, cap)
            early = to_all(sent, -1, farthest_first[:1])
            early, arrived = lax.optimization_barrier((early, arrived))
        mine = compact(request, arrived, n_requests)
        if pieces:
            mine, pieces = lax.optimization_barrier((mine, pieces))
            kvs = kvs + [project(pieces, key_weight, value_weight)]
        near = [mine, over_core(mine)]
        far = [over_x(mine, d) for d in range(1, n_x)]
        near_at = [place(c, kind, 0) for kind in range(2)]
        far_at = [place(c, kind, d) for kind in range(2) for d in range(1, n_x)]
        if c < n_chunks - 1:
            early = {**early, **to_all(sent, -1, farthest_first[1:4])}
            early, far = lax.optimization_barrier((early, far))
            far = far + [over_core(x) for x in far]
            pieces = near + far
        else:
            kvs = kvs + [project(near, key_weight, value_weight)]
            kvs, far = lax.optimization_barrier((kvs, far))
            late = far + [over_core(x) for x in far]
        places += near_at + far_at

    split = 3 * LANES
    parts = ((0, split), (split, enc - split))
    attended, d_query, d_own, d_core, near, far, own = attend(
        kvs, late, key_weight, value_weight, places, n_chunks, split, queries, cotangent
    )
    far_got = over_core(far)
    near_got = over_core(near)
    codes = far_codes(own, far_got, n_chunks)
    near_b, far_b, own_b = grads_of(d_core, d_own, key_weight, value_weight, n_chunks, parts[1])

    codes = [over_x(code, n_x - d) for d, code in enumerate(codes, 1)]
    sent = send_codes(request, own, near_got, codes, n_dp)
    sent, near_b, far_b = lax.optimization_barrier((sent, near_b, far_b))
    came = to_all(sent, 1)
    far_got = over_core(far_b)
    near_got = over_core(near_b)
    codes = far_codes(own_b, far_got, n_chunks)
    codes = [over_x(code, n_x - d) for d, code in enumerate(codes, 1)]
    lead = {d: came[d] for d in farthest_first[:6]}
    codes, lead = lax.optimization_barrier((codes, lead))
    came.update(lead)
    arrived = [sent[0]] + [came[d] for d in range(1, n_dp)]
    d_table = gather_grads(me, asked, arrived, n_slabs, n_chunks, enc, parts[0], None)
    sent = send_codes(request, own_b, near_got, codes, n_dp)
    came = to_all(sent, 1)
    arrived = [sent[0]] + [came[d] for d in range(1, n_dp)]
    d_table = gather_grads(me, asked, arrived, n_slabs, n_chunks, enc, parts[1], d_table)
    return (attended, d_query, d_table)


def solution(mesh):
    in_specs = (
        P("dp", "tensor"),
        P("dp", "tensor"),
        P("dp", None, None),
        P(None, "tensor"),
        P(None, "tensor"),
        P("dp", None),
        P("dp", None),
    )
    out_specs = (P("dp", "tensor"), P("dp", "tensor"), P("dp", "tensor", None))
    return jax.shard_map(
        on_device, mesh=mesh, in_specs=in_specs, out_specs=out_specs, check_vma=False
    )
```

```python
import functools
import math

import jax
import jax.numpy as jnp
from jax import lax
from jax.experimental import pallas as pl
from jax.experimental.pallas import tpu as pltpu
from jax.sharding import PartitionSpec as P

HD = 128
SPAN = 64
LANES = 128
WINDOW = 3
VMEM_LIMIT = 28 * 1024 * 1024
VMEM_MORE = 40 * 1024 * 1024
VMEM_ALL = 60 * 1024 * 1024
F32 = jnp.float32
BF16 = jnp.bfloat16

ANY = pl.BlockSpec(memory_space=pl.ANY)
SMEM = pl.BlockSpec(memory_space=pltpu.SMEM)
VMEM = pl.BlockSpec(memory_space=pltpu.VMEM)


def params(limit=VMEM_LIMIT):
    return pltpu.CompilerParams(vmem_limit_bytes=limit)


def cost(flops, nbytes):
    return pl.CostEstimate(flops=int(flops), bytes_accessed=int(nbytes), transcendentals=0)


def ask_body(cap, owners, slots, me_out, wanted, request, count):
    n_dp = wanted.shape[0]
    me = lax.axis_index("dp")
    me_out[0] = me
    for i in range(n_dp * cap):
        request[i] = -1
        for asker in range(n_dp):
            wanted[asker, i] = 0
    for d in range(n_dp):
        count[d] = 0
    for r in range(owners.size):
        d = owners[r % 2, r // 2] - me
        d = jnp.where(d < 0, d + n_dp, d)
        j = count[d]
        count[d] = j + 1
        wanted[me, d * cap + j] = slots[r % 2, r // 2] + 1
        request[d * cap + j] = r


def ask(owners, slots, n_dp, cap):
    return pl.pallas_call(
        functools.partial(ask_body, cap),
        out_shape=[
            jax.ShapeDtypeStruct((1,), jnp.int32),
            jax.ShapeDtypeStruct((n_dp, n_dp * cap), jnp.int32),
            jax.ShapeDtypeStruct((n_dp * cap,), jnp.int32),
        ],
        in_specs=[SMEM, SMEM],
        out_specs=[SMEM, SMEM, SMEM],
        scratch_shapes=[pltpu.SMEM((n_dp,), jnp.int32)],
        name="ask",
    )(owners.T, slots.T)


def asked_of(asked, me, d, j):
    n_dp = asked.shape[0]
    asker = me[0] - d
    asker = jnp.where(asker < 0, asker + n_dp, asker)
    return asked[asker, d * (asked.shape[1] // n_dp) + j] - 1


def pack_body(n_dp, me, asked, table, *rest):
    outs, sem = rest[:-1], rest[-1]
    cap, share, _ = outs[0].shape
    row = pl.multiple_of(lax.axis_index("tensor") * share, share)

    def each(act):
        for d in range(n_dp):
            for j in range(cap):
                slab = asked_of(asked, me, d, j)

                @pl.when(slab >= 0)
                def _():
                    source = table.at[slab, pl.ds(row, share)]
                    act(pltpu.make_async_copy(source, outs[d].at[j], sem.at[d * cap + j]))

    each(lambda copy: copy.start())
    each(lambda copy: copy.wait())


def pack(me, asked, table, share, cap):
    n_dp = asked.shape[0]
    enc = table.shape[2]
    return pl.pallas_call(
        functools.partial(pack_body, n_dp),
        out_shape=[jax.ShapeDtypeStruct((cap, share, enc), table.dtype)] * n_dp,
        in_specs=[SMEM, SMEM, ANY],
        out_specs=[VMEM] * n_dp,
        scratch_shapes=[pltpu.SemaphoreType.DMA((n_dp * cap,))],
        compiler_params=params(VMEM_ALL),
        cost_estimate=cost(0, 4 * n_dp * cap * share * enc),
        name="pack_rows",
    )(me, asked, table)


def compact_body(n_dp, n_out, request, *refs):
    arrived, outs, sem = refs[: n_dp * n_out], refs[n_dp * n_out : -1], refs[-1]
    cap = arrived[0].shape[0]

    def each(act):
        for d in range(n_dp):
            for j in range(cap):
                r = request[d * cap + j]

                @pl.when(r >= 0)
                def _():
                    for i in range(n_out):
                        source = arrived[i * n_dp + d].at[j]
                        act(pltpu.make_async_copy(source, outs[i].at[r], sem.at[i, d * cap + j]))

    each(lambda copy: copy.start())
    each(lambda copy: copy.wait())


def compact(request, lists, n):
    n_dp, n_out = len(lists[0]), len(lists)
    shape = (n,) + lists[0][0].shape[1:]
    return pl.pallas_call(
        functools.partial(compact_body, n_dp, n_out),
        out_shape=[jax.ShapeDtypeStruct(shape, lists[0][0].dtype)] * n_out,
        in_specs=[SMEM] + [ANY] * (n_dp * n_out),
        out_specs=[VMEM] * n_out,
        scratch_shapes=[pltpu.SemaphoreType.DMA((n_out, request.shape[0]))],
        compiler_params=params(),
        cost_estimate=cost(0, 4 * n_out * math.prod(shape)),
        name="compact_rows",
    )(request, *[block for blocks in lists for block in blocks])


def weight_specs(rows, step):
    return [
        pl.BlockSpec((rows, step), lambda i: (0, jnp.minimum(i, 1))),
        pl.BlockSpec((rows, step), lambda i: (0, jnp.maximum(i - 2, 0))),
    ]


def with_weight(wk, wv, act):
    @pl.when(pl.program_id(0) < 2)
    def _():
        act(wk)

    @pl.when(pl.program_id(0) >= 2)
    def _():
        act(wv)


def project_body(n_in, *refs):
    wk, wv, out = refs[n_in : n_in + 3]
    n, sub, enc = refs[0].shape
    rows = jnp.concatenate([ref[...].reshape(n * sub, enc) for ref in refs[:n_in]], axis=0)

    def act(w):
        res = jnp.dot(rows, w[...], preferred_element_type=F32)
        out[...] = res.astype(BF16).reshape(out.shape)

    with_weight(wk, wv, act)


def project(pieces, wk, wv):
    n_in = len(pieces)
    n, sub, enc = pieces[0].shape
    width = 2 * wk.shape[1]
    step = width // 4
    return pl.pallas_call(
        functools.partial(project_body, n_in),
        out_shape=jax.ShapeDtypeStruct((n_in, n, sub, width), BF16),
        grid=(4,),
        in_specs=[pl.BlockSpec((n, sub, enc), lambda i: (0, 0, 0))] * n_in
        + weight_specs(enc, step),
        out_specs=pl.BlockSpec((n_in, n, sub, step), lambda i: (0, 0, 0, i)),
        compiler_params=params(),
        cost_estimate=cost(
            2 * n_in * n * sub * enc * width, 2 * (n_in * n * sub * (enc + width) + enc * width)
        ),
        name="project",
    )(*pieces, wk, wv)


def attend_body(places, n_kv, n_late, near, *refs):
    kvs, late = refs[:n_kv], refs[n_kv : n_kv + n_late]
    wk, wv, q_ref, g_ref, att_ref, dq_ref = refs[n_kv + n_late : n_kv + n_late + 6]
    *grads, near_out, far_out, own_out, late_kv, own_all, core_all = refs[n_kv + n_late + 6 :]
    step = pl.program_id(0)
    width = q_ref.shape[1]
    enc = wk.shape[0]
    sub = late_kv.shape[2]
    scale = 1.0 / math.sqrt(HD)
    heads = width // HD
    group = min(8, heads)
    last = (((1,), (1,)), ((), ()))
    first = (((0,), (0,)), ((), ()))

    def dot(a, b, dims=(((1,), (0,)), ((), ()))):
        return lax.dot_general(a, b, dims, preferred_element_type=F32)

    @pl.when(step == 0)
    def _():
        rows = jnp.concatenate([ref[...].reshape(-1, enc) for ref in late], axis=0)
        shape = late_kv.shape[:3] + (width,)
        late_kv[:, :, :, :width] = dot(rows, wk[...]).astype(BF16).reshape(shape)
        late_kv[:, :, :, width:] = dot(rows, wv[...]).astype(BF16).reshape(shape)

    mine = pl.ds(2 * step, 2)

    def rows_of(col):
        cols = pl.ds(col, HD)
        parts = [ref[:, :, :, cols].reshape(-1, HD) for ref in kvs]
        parts.append(late_kv[:, mine, :, cols].reshape(-1, HD))
        return jnp.concatenate(parts, axis=0)

    def put(col, grad):
        cols = pl.ds(col, HD)
        for at, (kind, i) in enumerate(places):
            block = grad[at * 2 * sub : (at + 1) * 2 * sub].reshape(2, sub, HD)
            grads[kind][i, :, :, cols] = block
            (own_all, core_all)[kind][i, mine, :, cols] = block

    zero = jnp.zeros((SPAN, HD), BF16)
    for h0 in range(0, heads, group):
        hs = range(h0, h0 + group)
        qg, kv = [], []
        for h in hs:
            cols = pl.ds(h * HD, HD)
            top = jnp.concatenate([q_ref[:, cols], zero], axis=1)
            low = jnp.concatenate([zero, g_ref[:, cols]], axis=1)
            qg.append(jnp.concatenate([top, low], axis=0))
            kv.append(jnp.concatenate([rows_of(h * HD), rows_of(width + h * HD)], axis=1))
        both = [dot(a, b, last) for a, b in zip(qg, kv)]
        s = jnp.concatenate([x[:SPAN] for x in both], axis=0) * scale
        dw = jnp.concatenate([x[SPAN:] for x in both], axis=0)
        e = jnp.exp(s - jnp.max(s, axis=1, keepdims=True))
        p = e * (1.0 / jnp.sum(e, axis=1, keepdims=True))
        rs = jnp.sum(dw * p, axis=1, keepdims=True)
        w = p.astype(BF16)
        ds = (p * (dw - rs) * scale).astype(BF16)
        span = [slice(i * SPAN, (i + 1) * SPAN) for i in range(group)]
        dsw = [jnp.concatenate([ds[i], w[i]], axis=0) for i in span]
        out = [dot(a, b).astype(BF16) for a, b in zip(dsw, kv)]
        back = [dot(a, b, first).astype(BF16) for a, b in zip(dsw, qg)]
        for i, h in enumerate(hs):
            dq_ref[:, pl.ds(h * HD, HD)] = out[i][:SPAN, :HD]
            att_ref[:, pl.ds(h * HD, HD)] = out[i][SPAN:, HD:]
            put(h * HD, back[i][:, :HD])
            put(width + h * HD, back[i][:, HD:])

    @pl.when(step == pl.num_programs(0) - 1)
    def _():
        count = own_out.shape[-1]
        for ref, outs in ((core_all, (near_out, far_out)), (own_all, (own_out,))):
            rows = ref[...].reshape(-1, 2 * width)
            res = dot(rows[:, :width], wk[:count, :], last) + dot(rows[:, width:], wv[:count, :], last)
            res = res.reshape(ref.shape[:3] + (count,))
            if len(outs) == 1:
                outs[0][...] = res
            else:
                outs[0][...] = res[:near]
                outs[1][...] = res[near:]


def attend(kvs, late, wk, wv, places, near, count, queries, cotangent):
    tokens, width = queries.shape
    spans = tokens // SPAN
    n, sub = kvs[0].shape[1:3]
    enc = wk.shape[0]
    pieces = len(places) // 2
    rows = pl.BlockSpec((SPAN, width), lambda i: (i, 0))

    def kv_block(pieces):
        return pl.BlockSpec((pieces, 2, sub, 2 * width), lambda i: (0, i, 0, 0))

    def whole(shape):
        return pl.BlockSpec(shape, lambda i: (0,) * len(shape))

    keys = len(places) * 2 * sub
    parts = [(near, n, sub, count), (pieces - near, n, sub, count), (pieces, n, sub, count)]
    every = (pieces, n, sub, 2 * width)
    return pl.pallas_call(
        functools.partial(attend_body, places, len(kvs), len(late), near),
        out_shape=[jax.ShapeDtypeStruct((tokens, width), BF16)] * 2
        + [jax.ShapeDtypeStruct(every, BF16)] * 2
        + [jax.ShapeDtypeStruct(part, F32) for part in parts],
        grid=(spans,),
        in_specs=[kv_block(kv.shape[0]) for kv in kvs]
        + [whole(x.shape) for x in late]
        + [whole(wk.shape), whole(wv.shape), rows, rows],
        out_specs=[rows, rows] + [kv_block(pieces)] * 2 + [whole(part) for part in parts],
        scratch_shapes=[
            pltpu.VMEM((len(late), n, sub, 2 * width), BF16),
            pltpu.VMEM(every, BF16),
            pltpu.VMEM(every, BF16),
        ],
        compiler_params=params(VMEM_MORE),
        cost_estimate=cost(
            16 * tokens * width * keys + 4 * n * sub * width * (len(late) * enc + 2 * pieces * count),
            8 * tokens * width + 8 * spans * keys * 2 * width,
        ),
        name="attend",
    )(*kvs, *late, wk, wv, queries, cotangent)


def encode(x, axes):
    top = jnp.maximum(jnp.max(jnp.abs(x), axis=axes, keepdims=True), 1e-30)
    power = jnp.floor(jnp.log2(top)) + 1.0
    code = jnp.clip(jnp.round(x * jnp.exp2(15.0 - power)), -32767.0, 32767.0)
    return code.astype(jnp.int32).astype(jnp.int16), power


def grads_body(near, first, core_ref, own_ref, wk, wv, near_out, far_out, own_out, core_acc, own_acc):
    i = pl.program_id(0)

    def act(w):
        w = w[first : first + own_acc.shape[1], :]
        for ref, acc in ((core_ref, core_acc), (own_ref, own_acc)):
            rows = ref[...].reshape(acc.shape[0], -1)
            part = lax.dot_general(rows, w, (((1,), (1,)), ((), ())), preferred_element_type=F32)

            @pl.when(i == 0)
            def _():
                acc[...] = part

            @pl.when(i > 0)
            def _():
                acc[...] += part

    with_weight(wk, wv, act)

    @pl.when(i == pl.num_programs(0) - 1)
    def _():
        core = core_acc[...].reshape(core_ref.shape[:3] + core_acc.shape[1:])
        near_out[...] = core[:near]
        far_out[...] = core[near:]
        own_out[...] = own_acc[...].reshape(own_out.shape)


def grads_of(d_core, d_own, wk, wv, near, cols):
    pieces, n, sub, width = d_own.shape
    first, count = cols
    step = width // 4
    shapes = [(near, n, sub, count), (pieces - near, n, sub, count), (pieces, n, sub, count)]
    rows = pieces * n * sub
    return pl.pallas_call(
        functools.partial(grads_body, near, first),
        out_shape=[jax.ShapeDtypeStruct(shape, F32) for shape in shapes],
        grid=(4,),
        in_specs=[pl.BlockSpec((pieces, n, sub, step), lambda i: (0, 0, 0, i))] * 2
        + weight_specs(wk.shape[0], step),
        out_specs=[pl.BlockSpec(shape, lambda i: (0, 0, 0, 0)) for shape in shapes],
        scratch_shapes=[pltpu.VMEM((rows, count), F32)] * 2,
        compiler_params=params(VMEM_ALL),
        cost_estimate=cost(4 * rows * count * width, 2 * (count + 2 * rows) * width + 8 * rows * count),
        name="grads",
    )(d_core, d_own, wk, wv)


def put_codes(far, codes):
    pieces, n, sub, count = far.shape
    near = codes[0].shape[0]
    tiles = count // LANES
    row = lax.broadcasted_iota(jnp.int32, (sub, LANES), 0)
    for i in range(pieces):
        out, c = codes[i // near], i % near
        code, power = encode(far[i], (1, 2))
        for e in range(tiles):
            out[c, e * n : (e + 1) * n] = code[:, :, e * LANES : (e + 1) * LANES]
        note = jnp.zeros((sub, LANES), F32)
        for r in range(n):
            note = jnp.where(row == r, power[r], note)
        out[c, tiles * n] = note.astype(jnp.int32).astype(jnp.int16)


def far_codes_body(mine, got, *codes):
    put_codes(mine[...] + got[...], codes)


def far_codes(own, got, near):
    far, n, sub, count = got.shape
    shape = (near, count // LANES * n + 1, sub, LANES)
    return pl.pallas_call(
        far_codes_body,
        out_shape=[jax.ShapeDtypeStruct(shape, jnp.int16)] * (far // near),
        grid=(1,),
        in_specs=[
            pl.BlockSpec((pl.Element(far), pl.Element(n), pl.Element(sub), pl.Element(count)), lambda i: (near, 0, 0, 0)),
            pl.BlockSpec(got.shape, lambda i: (0, 0, 0, 0)),
        ],
        out_specs=[pl.BlockSpec(shape, lambda i: (0, 0, 0, 0))] * (far // near),
        compiler_params=params(),
        cost_estimate=cost(8 * got.size, 10 * got.size),
        name="far_codes",
    )(own, got)


def send_body(n_dp, request, own, got, *rest):
    codes, outs, (stage, powers) = rest[: -n_dp - 2], rest[-n_dp - 2 : -2], rest[-2:]
    n_chunks, n, sub, count = got.shape
    tiles = count // LANES
    cap = request.shape[0] // n_dp
    for c in range(n_chunks):
        for r in range(n):
            total = own[c, r] + got[c, r]
            for code in codes:
                unit = jnp.exp2(code[c, tiles * n].astype(F32)[r : r + 1] - 15.0)
                total = total + jnp.concatenate(
                    [code[c, e * n + r].astype(F32) * unit for e in range(tiles)], axis=1
                )
            coded, power = encode(total, (0, 1))
            for e in range(tiles):
                stage[r, c * tiles + e] = coded[:, e * LANES : (e + 1) * LANES]
            powers[r, c] = jnp.broadcast_to(power, (sub, LANES))
    row = lax.broadcasted_iota(jnp.int32, (sub, LANES), 0)
    for d in range(n_dp):
        note = jnp.zeros((sub, LANES), F32)
        for j in range(cap):
            r = request[d * cap + j]

            @pl.when(r >= 0)
            def _():
                outs[d][pl.ds(j * n_chunks * tiles, n_chunks * tiles)] = stage[r]

            for c in range(n_chunks):
                note = jnp.where(row == j * n_chunks + c, powers[jnp.maximum(r, 0), c], note)
        outs[d][cap * n_chunks * tiles] = note.astype(jnp.int32).astype(jnp.int16)


def send_codes(request, own, got, codes, n_dp):
    n_chunks, n, sub, count = got.shape
    block = pl.BlockSpec(got.shape, lambda i: (0, 0, 0, 0))
    tiles = count // LANES
    cap = request.shape[0] // n_dp
    shape = (cap * n_chunks * tiles + 1, sub, LANES)
    return pl.pallas_call(
        functools.partial(send_body, n_dp),
        out_shape=[jax.ShapeDtypeStruct(shape, jnp.int16)] * n_dp,
        grid=(1,),
        in_specs=[SMEM, block, block] + [VMEM] * len(codes),
        out_specs=[VMEM] * n_dp,
        scratch_shapes=[
            pltpu.VMEM((n, n_chunks * tiles, sub, LANES), jnp.int16),
            pltpu.VMEM((n, n_chunks, sub, LANES), F32),
        ],
        compiler_params=params(),
        cost_estimate=cost(10 * got.size, 6 * got.size + 2 * n_dp * math.prod(shape)),
        name="send_codes",
    )(request, own, got, *codes)


def gather_body(n_dp, n_chunks, first, me, asked, *refs):
    arrived = refs[:n_dp]
    out, total, sem = refs[-3:]
    sub, count = total.shape[1] // n_chunks, total.shape[2]
    tiles = count // LANES
    cap = asked.shape[1] // n_dp
    total[...] = jnp.zeros_like(total)
    for d in range(n_dp):
        for j in range(cap):
            slab = asked_of(asked, me, d, j)

            @pl.when(slab >= 0)
            def _():
                note = arrived[d][cap * n_chunks * tiles].astype(F32)
                for c in range(n_chunks):
                    at = j * n_chunks + c
                    unit = jnp.exp2(note[at : at + 1] - 15.0)
                    for e in range(tiles):
                        value = arrived[d][at * tiles + e].astype(F32) * unit
                        total[slab, pl.ds(c * sub, sub), pl.ds(e * LANES, LANES)] += value

    copy = pltpu.make_async_copy(total, out.at[:, :, pl.ds(first, count)], sem)
    copy.start()
    copy.wait()


def gather_grads(me, asked, arrived, n_slabs, rows, enc, cols, before):
    first, count = cols
    n_dp = asked.shape[0]
    return pl.pallas_call(
        functools.partial(gather_body, n_dp, 1, first),
        out_shape=jax.ShapeDtypeStruct((n_slabs, rows, enc), F32),
        in_specs=[SMEM, SMEM] + [VMEM] * n_dp + [ANY] * (before is not None),
        out_specs=ANY,
        scratch_shapes=[pltpu.VMEM((n_slabs, rows, count), F32), pltpu.SemaphoreType.DMA],
        input_output_aliases={} if before is None else {2 + n_dp: 0},
        compiler_params=params(),
        cost_estimate=cost(0, 8 * n_slabs * rows * count),
        name="gather_grads",
    )(me, asked, *arrived, *([] if before is None else [before]))


def on_device(queries, cotangent, table, key_weight, value_weight, owners, slots):
    n_dp = lax.axis_size("dp")
    n_tp = lax.axis_size("tensor")
    n_x = n_tp // 2
    spans = owners.shape[0]
    n_requests = 2 * spans
    n_slabs, n_tokens, enc = table.shape
    cap = max(2, (4 * spans + n_dp - 1) // n_dp)
    share = n_tokens // n_tp

    def over_core(x):
        return lax.ppermute(x, "tensor", [(t, t ^ 1) for t in range(n_tp)])

    def over_x(x, d):
        return lax.ppermute(x, "tensor", [(t, (t + 2 * d) % n_tp) for t in range(n_tp)])

    def over_dp(x, d):
        return lax.ppermute(x, "dp", [(i, (i + d) % n_dp) for i in range(n_dp)])

    farthest_first = sorted(range(1, n_dp), key=lambda d: -min(d, n_dp - d))

    def to_all(xs, sign, distances=farthest_first):
        got = {d: over_dp(xs[d], sign * d) for d in distances}
        return got

    me, wanted, request = ask(owners, slots, n_dp, cap)
    asked = lax.psum(wanted, "dp")

    sent = pack(me, asked, table, share, cap)
    mine = {0: sent[0]}
    far = {0: [over_x(sent[0], k) for k in range(1, n_x)]}
    for i, d in enumerate(farthest_first):
        block = sent[d]
        if i >= WINDOW:
            held = farthest_first[i - WINDOW]
            block, mine[held] = lax.optimization_barrier((block, mine[held]))
            far[held] = [over_x(mine[held], k) for k in range(1, n_x)]
            if i > WINDOW:
                passed = farthest_first[i - WINDOW - 1]
                block, far[passed] = lax.optimization_barrier((block, far[passed]))
            else:
                block, far[0] = lax.optimization_barrier((block, far[0]))
        mine[d] = over_dp(block, -d)
    for d in farthest_first[-WINDOW:]:
        far[d] = [over_x(mine[d], k) for k in range(1, n_x)]
    lists = [[mine[d] for d in range(n_dp)]]
    lists += [[far[d][k] for d in range(n_dp)] for k in range(n_x - 1)]
    mine, *far = compact(request, lists, n_requests)

    early = [mine, *far]
    late = [over_core(x) for x in early]
    kvs = [project(early, key_weight, value_weight)]
    places = [(kind, k) for kind in range(2) for k in range(n_x)]

    split = 3 * LANES
    parts = ((0, split), (split, enc - split))
    attended, d_query, d_own, d_core, near, far, own = attend(
        kvs, late, key_weight, value_weight, places, 1, split, queries, cotangent
    )
    far_got = over_core(far)
    near_got = over_core(near)
    codes = far_codes(own, far_got, 1)
    near_b, far_b, own_b = grads_of(d_core, d_own, key_weight, value_weight, 1, parts[1])

    codes = [over_x(code, n_x - d) for d, code in enumerate(codes, 1)]
    sent = send_codes(request, own, near_got, codes, n_dp)
    sent, near_b, far_b = lax.optimization_barrier((sent, near_b, far_b))
    came = to_all(sent, 1)
    far_got = over_core(far_b)
    near_got = over_core(near_b)
    codes = far_codes(own_b, far_got, 1)
    codes = [over_x(code, n_x - d) for d, code in enumerate(codes, 1)]
    lead = {d: came[d] for d in farthest_first[:6]}
    codes, lead = lax.optimization_barrier((codes, lead))
    came.update(lead)
    arrived = [sent[0]] + [came[d] for d in range(1, n_dp)]
    d_table = gather_grads(me, asked, arrived, n_slabs, share, enc, parts[0], None)
    sent = send_codes(request, own_b, near_got, codes, n_dp)
    came = to_all(sent, 1)
    arrived = [sent[0]] + [came[d] for d in range(1, n_dp)]
    d_table = gather_grads(me, asked, arrived, n_slabs, share, enc, parts[1], d_table)
    return (attended, d_query, d_table)


def solution(mesh):
    in_specs = (
        P("dp", "tensor"),
        P("dp", "tensor"),
        P("dp", None, None),
        P(None, "tensor"),
        P(None, "tensor"),
        P("dp", None),
        P("dp", None),
    )
    out_specs = (P("dp", "tensor"), P("dp", "tensor"), P("dp", "tensor", None))
    return jax.shard_map(
        on_device, mesh=mesh, in_specs=in_specs, out_specs=out_specs, check_vma=False
    )
```

```python
import functools
import math

import jax
import jax.numpy as jnp
from jax import lax
from jax.experimental import pallas as pl
from jax.experimental.pallas import tpu as pltpu
from jax.sharding import PartitionSpec as P

HD = 128
SPAN = 64
LANES = 128
WINDOW = 4
VMEM_LIMIT = 28 * 1024 * 1024
VMEM_MORE = 40 * 1024 * 1024
VMEM_ALL = 60 * 1024 * 1024
F32 = jnp.float32
BF16 = jnp.bfloat16

ANY = pl.BlockSpec(memory_space=pl.ANY)
SMEM = pl.BlockSpec(memory_space=pltpu.SMEM)
VMEM = pl.BlockSpec(memory_space=pltpu.VMEM)


def params(limit=VMEM_LIMIT):
    return pltpu.CompilerParams(vmem_limit_bytes=limit)


def cost(flops, nbytes):
    return pl.CostEstimate(flops=int(flops), bytes_accessed=int(nbytes), transcendentals=0)


def ask_body(cap, owners, slots, me_out, wanted, request, count):
    n_dp = wanted.shape[0]
    me = lax.axis_index("dp")
    me_out[0] = me
    for i in range(n_dp * cap):
        request[i] = -1
        for asker in range(n_dp):
            wanted[asker, i] = 0
    for d in range(n_dp):
        count[d] = 0
    for r in range(owners.size):
        d = owners[r % 2, r // 2] - me
        d = jnp.where(d < 0, d + n_dp, d)
        j = count[d]
        count[d] = j + 1
        wanted[me, d * cap + j] = slots[r % 2, r // 2] + 1
        request[d * cap + j] = r


def ask(owners, slots, n_dp, cap):
    return pl.pallas_call(
        functools.partial(ask_body, cap),
        out_shape=[
            jax.ShapeDtypeStruct((1,), jnp.int32),
            jax.ShapeDtypeStruct((n_dp, n_dp * cap), jnp.int32),
            jax.ShapeDtypeStruct((n_dp * cap,), jnp.int32),
        ],
        in_specs=[SMEM, SMEM],
        out_specs=[SMEM, SMEM, SMEM],
        scratch_shapes=[pltpu.SMEM((n_dp,), jnp.int32)],
        name="ask",
    )(owners.T, slots.T)


def asked_of(asked, me, d, j):
    n_dp = asked.shape[0]
    asker = me[0] - d
    asker = jnp.where(asker < 0, asker + n_dp, asker)
    return asked[asker, d * (asked.shape[1] // n_dp) + j] - 1


def pack_body(n_dp, me, asked, table, *rest):
    outs, sem = rest[:-1], rest[-1]
    cap, share, _ = outs[0].shape
    row = pl.multiple_of(lax.axis_index("tensor") * share, share)

    def each(act):
        for d in range(n_dp):
            for j in range(cap):
                slab = asked_of(asked, me, d, j)

                @pl.when(slab >= 0)
                def _():
                    source = table.at[slab, pl.ds(row, share)]
                    act(pltpu.make_async_copy(source, outs[d].at[j], sem.at[d * cap + j]))

    each(lambda copy: copy.start())
    each(lambda copy: copy.wait())


def pack(me, asked, table, share, cap):
    n_dp = asked.shape[0]
    enc = table.shape[2]
    return pl.pallas_call(
        functools.partial(pack_body, n_dp),
        out_shape=[jax.ShapeDtypeStruct((cap, share, enc), table.dtype)] * n_dp,
        in_specs=[SMEM, SMEM, ANY],
        out_specs=[VMEM] * n_dp,
        scratch_shapes=[pltpu.SemaphoreType.DMA((n_dp * cap,))],
        compiler_params=params(VMEM_ALL),
        cost_estimate=cost(0, 4 * n_dp * cap * share * enc),
        name="pack_rows",
    )(me, asked, table)


def compact_body(n_dp, n_out, request, *refs):
    arrived, outs, sem = refs[: n_dp * n_out], refs[n_dp * n_out : -1], refs[-1]
    cap = arrived[0].shape[0]

    def each(act):
        for d in range(n_dp):
            for j in range(cap):
                r = request[d * cap + j]

                @pl.when(r >= 0)
                def _():
                    for i in range(n_out):
                        source = arrived[i * n_dp + d].at[j]
                        act(pltpu.make_async_copy(source, outs[i].at[r], sem.at[i, d * cap + j]))

    each(lambda copy: copy.start())
    each(lambda copy: copy.wait())


def compact(request, lists, n):
    n_dp, n_out = len(lists[0]), len(lists)
    shape = (n,) + lists[0][0].shape[1:]
    return pl.pallas_call(
        functools.partial(compact_body, n_dp, n_out),
        out_shape=[jax.ShapeDtypeStruct(shape, lists[0][0].dtype)] * n_out,
        in_specs=[SMEM] + [ANY] * (n_dp * n_out),
        out_specs=[VMEM] * n_out,
        scratch_shapes=[pltpu.SemaphoreType.DMA((n_out, request.shape[0]))],
        compiler_params=params(),
        cost_estimate=cost(0, 4 * n_out * math.prod(shape)),
        name="compact_rows",
    )(request, *[block for blocks in lists for block in blocks])


def weight_specs(rows, step):
    return [
        pl.BlockSpec((rows, step), lambda i: (0, jnp.minimum(i, 1))),
        pl.BlockSpec((rows, step), lambda i: (0, jnp.maximum(i - 2, 0))),
    ]


def with_weight(wk, wv, act):
    @pl.when(pl.program_id(0) < 2)
    def _():
        act(wk)

    @pl.when(pl.program_id(0) >= 2)
    def _():
        act(wv)


def project_body(n_in, *refs):
    wk, wv, out = refs[n_in : n_in + 3]
    n, sub, enc = refs[0].shape
    rows = jnp.concatenate([ref[...].reshape(n * sub, enc) for ref in refs[:n_in]], axis=0)

    def act(w):
        res = jnp.dot(rows, w[...], preferred_element_type=F32)
        out[...] = res.astype(BF16).reshape(out.shape)

    with_weight(wk, wv, act)


def project(pieces, wk, wv):
    n_in = len(pieces)
    n, sub, enc = pieces[0].shape
    width = 2 * wk.shape[1]
    step = width // 4
    return pl.pallas_call(
        functools.partial(project_body, n_in),
        out_shape=jax.ShapeDtypeStruct((n_in, n, sub, width), BF16),
        grid=(4,),
        in_specs=[pl.BlockSpec((n, sub, enc), lambda i: (0, 0, 0))] * n_in
        + weight_specs(enc, step),
        out_specs=pl.BlockSpec((n_in, n, sub, step), lambda i: (0, 0, 0, i)),
        compiler_params=params(),
        cost_estimate=cost(
            2 * n_in * n * sub * enc * width, 2 * (n_in * n * sub * (enc + width) + enc * width)
        ),
        name="project",
    )(*pieces, wk, wv)


def attend_body(places, n_kv, n_late, near, *refs):
    kvs, late = refs[:n_kv], refs[n_kv : n_kv + n_late]
    wk, wv, q_ref, g_ref, att_ref, dq_ref = refs[n_kv + n_late : n_kv + n_late + 6]
    *grads, near_out, far_out, own_out, late_kv, own_all, core_all = refs[n_kv + n_late + 6 :]
    step = pl.program_id(0)
    width = q_ref.shape[1]
    enc = wk.shape[0]
    sub = late_kv.shape[2]
    scale = 1.0 / math.sqrt(HD)
    heads = width // HD
    group = min(8, heads)
    last = (((1,), (1,)), ((), ()))
    first = (((0,), (0,)), ((), ()))

    def dot(a, b, dims=(((1,), (0,)), ((), ()))):
        return lax.dot_general(a, b, dims, preferred_element_type=F32)

    @pl.when(step == 0)
    def _():
        rows = jnp.concatenate([ref[...].reshape(-1, enc) for ref in late], axis=0)
        shape = late_kv.shape[:3] + (width,)
        late_kv[:, :, :, :width] = dot(rows, wk[...]).astype(BF16).reshape(shape)
        late_kv[:, :, :, width:] = dot(rows, wv[...]).astype(BF16).reshape(shape)

    mine = pl.ds(2 * step, 2)

    def rows_of(col):
        cols = pl.ds(col, HD)
        parts = [ref[:, :, :, cols].reshape(-1, HD) for ref in kvs]
        parts.append(late_kv[:, mine, :, cols].reshape(-1, HD))
        return jnp.concatenate(parts, axis=0)

    def put(col, grad):
        cols = pl.ds(col, HD)
        for at, (kind, i) in enumerate(places):
            block = grad[at * 2 * sub : (at + 1) * 2 * sub].reshape(2, sub, HD)
            grads[kind][i, :, :, cols] = block
            (own_all, core_all)[kind][i, mine, :, cols] = block

    zero = jnp.zeros((SPAN, HD), BF16)
    for h0 in range(0, heads, group):
        hs = range(h0, h0 + group)
        qg, kv = [], []
        for h in hs:
            cols = pl.ds(h * HD, HD)
            top = jnp.concatenate([q_ref[:, cols], zero], axis=1)
            low = jnp.concatenate([zero, g_ref[:, cols]], axis=1)
            qg.append(jnp.concatenate([top, low], axis=0))
            kv.append(jnp.concatenate([rows_of(h * HD), rows_of(width + h * HD)], axis=1))
        both = [dot(a, b, last) for a, b in zip(qg, kv)]
        s = jnp.concatenate([x[:SPAN] for x in both], axis=0) * scale
        dw = jnp.concatenate([x[SPAN:] for x in both], axis=0)
        e = jnp.exp(s - jnp.max(s, axis=1, keepdims=True))
        p = e * (1.0 / jnp.sum(e, axis=1, keepdims=True))
        rs = jnp.sum(dw * p, axis=1, keepdims=True)
        w = p.astype(BF16)
        ds = (p * (dw - rs) * scale).astype(BF16)
        span = [slice(i * SPAN, (i + 1) * SPAN) for i in range(group)]
        dsw = [jnp.concatenate([ds[i], w[i]], axis=0) for i in span]
        out = [dot(a, b).astype(BF16) for a, b in zip(dsw, kv)]
        back = [dot(a, b, first).astype(BF16) for a, b in zip(dsw, qg)]
        for i, h in enumerate(hs):
            dq_ref[:, pl.ds(h * HD, HD)] = out[i][:SPAN, :HD]
            att_ref[:, pl.ds(h * HD, HD)] = out[i][SPAN:, HD:]
            put(h * HD, back[i][:, :HD])
            put(width + h * HD, back[i][:, HD:])

    @pl.when(step == pl.num_programs(0) - 1)
    def _():
        count = own_out.shape[-1]
        for ref, outs in ((core_all, (near_out, far_out)), (own_all, (own_out,))):
            rows = ref[...].reshape(-1, 2 * width)
            res = dot(rows[:, :width], wk[:count, :], last) + dot(rows[:, width:], wv[:count, :], last)
            res = res.reshape(ref.shape[:3] + (count,))
            if len(outs) == 1:
                outs[0][...] = res
            else:
                outs[0][...] = res[:near]
                outs[1][...] = res[near:]


def attend(kvs, late, wk, wv, places, near, count, queries, cotangent):
    tokens, width = queries.shape
    spans = tokens // SPAN
    n, sub = kvs[0].shape[1:3]
    enc = wk.shape[0]
    pieces = len(places) // 2
    rows = pl.BlockSpec((SPAN, width), lambda i: (i, 0))

    def kv_block(pieces):
        return pl.BlockSpec((pieces, 2, sub, 2 * width), lambda i: (0, i, 0, 0))

    def whole(shape):
        return pl.BlockSpec(shape, lambda i: (0,) * len(shape))

    keys = len(places) * 2 * sub
    parts = [(near, n, sub, count), (pieces - near, n, sub, count), (pieces, n, sub, count)]
    every = (pieces, n, sub, 2 * width)
    return pl.pallas_call(
        functools.partial(attend_body, places, len(kvs), len(late), near),
        out_shape=[jax.ShapeDtypeStruct((tokens, width), BF16)] * 2
        + [jax.ShapeDtypeStruct(every, BF16)] * 2
        + [jax.ShapeDtypeStruct(part, F32) for part in parts],
        grid=(spans,),
        in_specs=[kv_block(kv.shape[0]) for kv in kvs]
        + [whole(x.shape) for x in late]
        + [whole(wk.shape), whole(wv.shape), rows, rows],
        out_specs=[rows, rows] + [kv_block(pieces)] * 2 + [whole(part) for part in parts],
        scratch_shapes=[
            pltpu.VMEM((len(late), n, sub, 2 * width), BF16),
            pltpu.VMEM(every, BF16),
            pltpu.VMEM(every, BF16),
        ],
        compiler_params=params(VMEM_MORE),
        cost_estimate=cost(
            16 * tokens * width * keys + 4 * n * sub * width * (len(late) * enc + 2 * pieces * count),
            8 * tokens * width + 8 * spans * keys * 2 * width,
        ),
        name="attend",
    )(*kvs, *late, wk, wv, queries, cotangent)


def encode(x, axes):
    top = jnp.maximum(jnp.max(jnp.abs(x), axis=axes, keepdims=True), 1e-30)
    power = jnp.floor(jnp.log2(top)) + 1.0
    code = jnp.clip(jnp.round(x * jnp.exp2(15.0 - power)), -32767.0, 32767.0)
    return code.astype(jnp.int32).astype(jnp.int16), power


def grads_body(first, core_ref, own_ref, wk, wv, near_out, far_out, own_out, part, sem):
    i = pl.program_id(0)
    n_x = own_out.shape[0]
    width, count = wk.shape[1], part.shape[-1]
    last = (((1,), (1,)), ((), ()))

    def act(ref):
        rows = ref[...].reshape(-1, 2 * width)
        res = lax.dot_general(
            rows[:, :width], wk[first : first + count, :], last, preferred_element_type=F32
        )
        res += lax.dot_general(
            rows[:, width:], wv[first : first + count, :], last, preferred_element_type=F32
        )
        part[i] = res.reshape(part.shape[1:])

    @pl.when(i < n_x)
    def _():
        act(core_ref)

    @pl.when(i >= n_x)
    def _():
        act(own_ref)

    outs = [near_out.at[0]] + [far_out.at[k] for k in range(n_x - 1)]
    outs += [own_out.at[k] for k in range(n_x)]
    copies = [pltpu.make_async_copy(part.at[k], out, sem.at[k]) for k, out in enumerate(outs)]
    for k, copy in enumerate(copies):

        @pl.when(i == k)
        def _():
            copy.start()

    @pl.when(i == pl.num_programs(0) - 1)
    def _():
        for copy in copies:
            copy.wait()


def grads_of(d_core, d_own, wk, wv, cols):
    n_x, n, sub, width = d_own.shape
    first, count = cols
    shapes = [(1, n, sub, count), (n_x - 1, n, sub, count), (n_x, n, sub, count)]
    rows = n_x * n * sub
    return pl.pallas_call(
        functools.partial(grads_body, first),
        out_shape=[jax.ShapeDtypeStruct(shape, F32) for shape in shapes],
        grid=(2 * n_x,),
        in_specs=[
            pl.BlockSpec((1, n, sub, width), lambda i: (jnp.minimum(i, n_x - 1), 0, 0, 0)),
            pl.BlockSpec((1, n, sub, width), lambda i: (jnp.maximum(i - n_x, 0), 0, 0, 0)),
            pl.BlockSpec(wk.shape, lambda i: (0, 0)),
            pl.BlockSpec(wv.shape, lambda i: (0, 0)),
        ],
        out_specs=[ANY] * 3,
        scratch_shapes=[
            pltpu.VMEM((2 * n_x, n, sub, count), F32),
            pltpu.SemaphoreType.DMA((2 * n_x,)),
        ],
        compiler_params=params(),
        cost_estimate=cost(4 * rows * count * width, 2 * (count + 2 * rows) * width + 8 * rows * count),
        name="grads",
    )(d_core, d_own, wk, wv)


def far_codes_body(cuts, mine, got, *codes):
    far, n, sub, count = got.shape
    row = lax.broadcasted_iota(jnp.int32, (sub, LANES), 0)
    for k in range(far):
        code, power = encode(mine[k] + got[k], (1, 2))
        e = 0
        for cut, out in zip(cuts, codes[k * len(cuts) :]):
            for at in range(cut):
                out[at * n : (at + 1) * n] = code[:, :, e * LANES : (e + 1) * LANES]
                e += 1
        note = jnp.zeros((sub, LANES), F32)
        for r in range(n):
            note = jnp.where(row == r, power[r], note)
        codes[k * len(cuts)][cuts[0] * n] = note.astype(jnp.int32).astype(jnp.int16)


def far_codes(own, got, cuts):
    far, n, sub, count = got.shape
    shapes = [(cut * n + (q == 0), sub, LANES) for q, cut in enumerate(cuts)] * far

    def whole(shape):
        return pl.BlockSpec(shape, lambda i: (0,) * len(shape))

    mine = pl.BlockSpec(tuple(pl.Element(size) for size in got.shape), lambda i: (1, 0, 0, 0))
    out = pl.pallas_call(
        functools.partial(far_codes_body, cuts),
        out_shape=[jax.ShapeDtypeStruct(shape, jnp.int16) for shape in shapes],
        grid=(1,),
        in_specs=[mine, whole(got.shape)],
        out_specs=[whole(shape) for shape in shapes],
        compiler_params=params(),
        cost_estimate=cost(8 * got.size, 10 * got.size),
        name="far_codes",
    )(own, got)
    return [out[k * len(cuts) : (k + 1) * len(cuts)] for k in range(far)]


def send_body(n_dp, cuts, request, own, got, *rest):
    codes, outs, (stage, powers) = rest[: -n_dp - 2], rest[-n_dp - 2 : -2], rest[-2:]
    _, n, sub, count = got.shape
    tiles = count // LANES
    cap = request.shape[0] // n_dp
    notes = [code[cuts[0] * n].astype(F32) for code in codes[:: len(cuts)]]
    for r in range(n):
        total = own[0, r] + got[0, r]
        for k, note in enumerate(notes):
            unit = jnp.exp2(note[r : r + 1] - 15.0)
            blocks = [
                code[at * n + r].astype(F32) * unit
                for cut, code in zip(cuts, codes[k * len(cuts) :])
                for at in range(cut)
            ]
            total = total + jnp.concatenate(blocks, axis=1)
        coded, power = encode(total, (0, 1))
        for e in range(tiles):
            stage[r, e] = coded[:, e * LANES : (e + 1) * LANES]
        powers[r] = jnp.broadcast_to(power, (sub, LANES))
    row = lax.broadcasted_iota(jnp.int32, (sub, LANES), 0)
    for d in range(n_dp):
        note = jnp.zeros((sub, LANES), F32)
        for j in range(cap):
            r = request[d * cap + j]

            @pl.when(r >= 0)
            def _():
                outs[d][pl.ds(j * tiles, tiles)] = stage[r]

            note = jnp.where(row == j, powers[jnp.maximum(r, 0)], note)
        outs[d][cap * tiles] = note.astype(jnp.int32).astype(jnp.int16)


def send_codes(request, own, got, codes, cuts, n_dp):
    _, n, sub, count = got.shape
    block = pl.BlockSpec(got.shape, lambda i: (0, 0, 0, 0))
    tiles = count // LANES
    cap = request.shape[0] // n_dp
    shape = (cap * tiles + 1, sub, LANES)
    codes = [x for piece in codes for x in piece]
    return pl.pallas_call(
        functools.partial(send_body, n_dp, cuts),
        out_shape=[jax.ShapeDtypeStruct(shape, jnp.int16)] * n_dp,
        grid=(1,),
        in_specs=[SMEM, block, block] + [VMEM] * len(codes),
        out_specs=[VMEM] * n_dp,
        scratch_shapes=[
            pltpu.VMEM((n, tiles, sub, LANES), jnp.int16),
            pltpu.VMEM((n, sub, LANES), F32),
        ],
        compiler_params=params(),
        cost_estimate=cost(10 * got.size, 6 * got.size + 2 * n_dp * math.prod(shape)),
        name="send_codes",
    )(request, own, got, *codes)


def gather_body(n_dp, first, me, asked, *refs):
    arrived = refs[:n_dp]
    out, total, sem = refs[-3:]
    tiles = total.shape[2] // LANES
    cap = asked.shape[1] // n_dp
    total[...] = jnp.zeros_like(total)
    for d in range(n_dp):
        for j in range(cap):
            slab = asked_of(asked, me, d, j)

            @pl.when(slab >= 0)
            def _():
                note = arrived[d][cap * tiles].astype(F32)
                unit = jnp.exp2(note[j : j + 1] - 15.0)
                for e in range(tiles):
                    value = arrived[d][j * tiles + e].astype(F32) * unit
                    total[slab, :, pl.ds(e * LANES, LANES)] += value

    copy = pltpu.make_async_copy(total, out.at[:, :, pl.ds(first, total.shape[2])], sem)
    copy.start()
    copy.wait()


def gather_grads(me, asked, arrived, n_slabs, rows, enc, cols, before):
    first, count = cols
    n_dp = asked.shape[0]
    return pl.pallas_call(
        functools.partial(gather_body, n_dp, first),
        out_shape=jax.ShapeDtypeStruct((n_slabs, rows, enc), F32),
        in_specs=[SMEM, SMEM] + [VMEM] * n_dp + [ANY] * (before is not None),
        out_specs=ANY,
        scratch_shapes=[pltpu.VMEM((n_slabs, rows, count), F32), pltpu.SemaphoreType.DMA],
        input_output_aliases={} if before is None else {2 + n_dp: 0},
        compiler_params=params(),
        cost_estimate=cost(0, 8 * n_slabs * rows * count),
        name="gather_grads",
    )(me, asked, *arrived, *([] if before is None else [before]))


def on_device(queries, cotangent, table, key_weight, value_weight, owners, slots):
    n_dp = lax.axis_size("dp")
    n_tp = lax.axis_size("tensor")
    n_x = n_tp // 2
    spans = owners.shape[0]
    n_requests = 2 * spans
    n_slabs, n_tokens, enc = table.shape
    cap = max(2, (4 * spans + n_dp - 1) // n_dp)
    share = n_tokens // n_tp

    def over_core(x):
        return lax.ppermute(x, "tensor", [(t, t ^ 1) for t in range(n_tp)])

    def over_x(x, d):
        return lax.ppermute(x, "tensor", [(t, (t + 2 * d) % n_tp) for t in range(n_tp)])

    def over_dp(x, d):
        return lax.ppermute(x, "dp", [(i, (i + d) % n_dp) for i in range(n_dp)])

    nearest_first = sorted(range(1, n_dp), key=lambda d: min(d, n_dp - d))
    farthest_first = sorted(range(1, n_dp), key=lambda d: -min(d, n_dp - d))

    def to_all(xs, sign, distances=farthest_first):
        got = {d: over_dp(xs[d], sign * d) for d in distances}
        return got

    me, wanted, request = ask(owners, slots, n_dp, cap)
    asked = lax.psum(wanted, "dp")

    sent = pack(me, asked, table, share, cap)
    mine = {0: sent[0]}
    for i, d in enumerate(nearest_first):
        block = sent[d]
        if i >= WINDOW:
            held = nearest_first[i - WINDOW]
            block, mine[held] = lax.optimization_barrier((block, mine[held]))
        mine[d] = over_dp(block, -d)
    far = [[over_x(mine[d], k) for k in range(1, n_x)] for d in range(n_dp)]
    lists = [[mine[d] for d in range(n_dp)]]
    lists += [[far[d][k] for d in range(n_dp)] for k in range(n_x - 1)]
    mine, *far = compact(request, lists, n_requests)

    early = [mine, *far]
    late = [over_core(x) for x in early]
    kvs = [project(early, key_weight, value_weight)]
    places = [(kind, k) for kind in range(2) for k in range(n_x)]

    split = 3 * LANES
    parts = ((0, split), (split, enc - split))
    attended, d_query, d_own, d_core, near, far, own = attend(
        kvs, late, key_weight, value_weight, places, 1, split, queries, cotangent
    )
    far_got = over_core(far)
    near_got = over_core(near)
    cuts = (2, 1)
    codes = far_codes(own, far_got, cuts)
    near_b, far_b, own_b = grads_of(d_core, d_own, key_weight, value_weight, parts[1])

    codes = [[over_x(x, n_x - k) for x in piece] for k, piece in enumerate(codes, 1)]
    lead, near_b, far_b = lax.optimization_barrier(([piece[0] for piece in codes], near_b, far_b))
    codes = [[x, *piece[1:]] for x, piece in zip(lead, codes)]
    far_got_b = over_core(far_b)
    near_got_b = over_core(near_b)
    sent = send_codes(request, own, near_got, codes, cuts, n_dp)
    came = to_all(sent, 1)
    arrived = [sent[0]] + [came[d] for d in range(1, n_dp)]
    d_table = gather_grads(me, asked, arrived, n_slabs, share, enc, parts[0], None)

    cuts = (parts[1][1] // LANES,)
    codes = far_codes(own_b, far_got_b, cuts)
    codes, before = lax.optimization_barrier((codes, sent[0]))
    codes = [[over_x(x, n_x - k) for x in piece] for k, piece in enumerate(codes, 1)]
    sent = send_codes(request, own_b, near_got_b, codes, cuts, n_dp)
    came = to_all(sent, 1)
    arrived = [sent[0]] + [came[d] for d in range(1, n_dp)]
    d_table = gather_grads(me, asked, arrived, n_slabs, share, enc, parts[1], d_table)
    return (attended, d_query, d_table)


def solution(mesh):
    in_specs = (
        P("dp", "tensor"),
        P("dp", "tensor"),
        P("dp", None, None),
        P(None, "tensor"),
        P(None, "tensor"),
        P("dp", None),
        P("dp", None),
    )
    out_specs = (P("dp", "tensor"), P("dp", "tensor"), P("dp", "tensor", None))
    return jax.shard_map(
        on_device, mesh=mesh, in_specs=in_specs, out_specs=out_specs, check_vma=False
    )
```

```python
import functools
import math

import jax
import jax.numpy as jnp
from jax import lax
from jax.experimental import pallas as pl
from jax.experimental.pallas import tpu as pltpu
from jax.sharding import PartitionSpec as P

HD = 128
SPAN = 64
LANES = 128
TILE = 16
WINDOW = 4
VMEM_LIMIT = 28 * 1024 * 1024
VMEM_MORE = 46 * 1024 * 1024
VMEM_ALL = 60 * 1024 * 1024
F32 = jnp.float32
BF16 = jnp.bfloat16

ANY = pl.BlockSpec(memory_space=pl.ANY)
SMEM = pl.BlockSpec(memory_space=pltpu.SMEM)
VMEM = pl.BlockSpec(memory_space=pltpu.VMEM)


def params(limit=VMEM_LIMIT):
    return pltpu.CompilerParams(vmem_limit_bytes=limit)


def cost(flops, nbytes):
    return pl.CostEstimate(flops=int(flops), bytes_accessed=int(nbytes), transcendentals=0)


def ask_body(cap, owners, slots, me_out, wanted, request, count):
    n_dp = wanted.shape[0]
    me = lax.axis_index("dp")
    me_out[0] = me
    for i in range(n_dp * cap):
        request[i] = -1
        for asker in range(n_dp):
            wanted[asker, i] = 0
    for d in range(n_dp):
        count[d] = 0
    for r in range(owners.size):
        d = owners[r % 2, r // 2] - me
        d = jnp.where(d < 0, d + n_dp, d)
        j = count[d]
        count[d] = j + 1
        wanted[me, d * cap + j] = slots[r % 2, r // 2] + 1
        request[d * cap + j] = r


def ask(owners, slots, n_dp, cap):
    return pl.pallas_call(
        functools.partial(ask_body, cap),
        out_shape=[
            jax.ShapeDtypeStruct((1,), jnp.int32),
            jax.ShapeDtypeStruct((n_dp, n_dp * cap), jnp.int32),
            jax.ShapeDtypeStruct((n_dp * cap,), jnp.int32),
        ],
        in_specs=[SMEM, SMEM],
        out_specs=[SMEM, SMEM, SMEM],
        scratch_shapes=[pltpu.SMEM((n_dp,), jnp.int32)],
        name="ask",
    )(owners.T, slots.T)


def asked_of(asked, me, d, j):
    n_dp = asked.shape[0]
    asker = me[0] - d
    asker = jnp.where(asker < 0, asker + n_dp, asker)
    return asked[asker, d * (asked.shape[1] // n_dp) + j] - 1


def pack_body(n_dp, me, asked, table, *rest):
    outs, sem = rest[:-1], rest[-1]
    cap, share, _ = outs[0].shape
    row = pl.multiple_of(lax.axis_index("tensor") * share, share)

    def each(act):
        for d in range(n_dp):
            for j in range(cap):
                slab = asked_of(asked, me, d, j)

                @pl.when(slab >= 0)
                def _():
                    source = table.at[slab, pl.ds(row, share)]
                    act(pltpu.make_async_copy(source, outs[d].at[j], sem.at[d * cap + j]))

    each(lambda copy: copy.start())
    each(lambda copy: copy.wait())


def pack(me, asked, table, share, cap):
    n_dp = asked.shape[0]
    enc = table.shape[2]
    return pl.pallas_call(
        functools.partial(pack_body, n_dp),
        out_shape=[jax.ShapeDtypeStruct((cap, share, enc), table.dtype)] * n_dp,
        in_specs=[SMEM, SMEM, ANY],
        out_specs=[VMEM] * n_dp,
        scratch_shapes=[pltpu.SemaphoreType.DMA((n_dp * cap,))],
        compiler_params=params(VMEM_ALL),
        cost_estimate=cost(0, 4 * n_dp * cap * share * enc),
        name="pack_rows",
    )(me, asked, table)


def compact_body(n_dp, n_out, request, *refs):
    arrived, outs, sem = refs[: n_dp * n_out], refs[n_dp * n_out : -1], refs[-1]
    cap = arrived[0].shape[0]

    def each(act):
        for d in range(n_dp):
            for j in range(cap):
                r = request[d * cap + j]

                @pl.when(r >= 0)
                def _():
                    for i in range(n_out):
                        source = arrived[i * n_dp + d].at[j]
                        act(pltpu.make_async_copy(source, outs[i].at[r], sem.at[i, d * cap + j]))

    each(lambda copy: copy.start())
    each(lambda copy: copy.wait())


def compact(request, lists, n):
    n_dp, n_out = len(lists[0]), len(lists)
    shape = (n,) + lists[0][0].shape[1:]
    return pl.pallas_call(
        functools.partial(compact_body, n_dp, n_out),
        out_shape=[jax.ShapeDtypeStruct(shape, lists[0][0].dtype)] * n_out,
        in_specs=[SMEM] + [ANY] * (n_dp * n_out),
        out_specs=[VMEM] * n_out,
        scratch_shapes=[pltpu.SemaphoreType.DMA((n_out, request.shape[0]))],
        compiler_params=params(),
        cost_estimate=cost(0, 4 * n_out * math.prod(shape)),
        name="compact_rows",
    )(request, *[block for blocks in lists for block in blocks])


def attend_body(places, near, *refs):
    n_in = len(places)
    pieces = refs[:n_in]
    wk, wv, q_ref, g_ref, att_ref, dq_ref = refs[n_in : n_in + 6]
    *grads, near_out, far_out, own_out, key_value, own_all, core_all = refs[n_in + 6 :]
    step = pl.program_id(0)
    width = q_ref.shape[1]
    enc = wk.shape[0]
    sub = key_value.shape[2]
    scale = 1.0 / math.sqrt(HD)
    heads = width // HD
    group = min(8, heads)
    last = (((1,), (1,)), ((), ()))
    first = (((0,), (0,)), ((), ()))

    def dot(a, b, dims=(((1,), (0,)), ((), ()))):
        return lax.dot_general(a, b, dims, preferred_element_type=F32)

    @pl.when(step == 0)
    def _():
        for i, ref in enumerate(pieces):
            rows = ref[...].reshape(-1, enc)
            shape = ref.shape[:2] + (width,)
            key_value[i, :, :, :width] = dot(rows, wk[...]).astype(BF16).reshape(shape)
            key_value[i, :, :, width:] = dot(rows, wv[...]).astype(BF16).reshape(shape)

    mine = pl.ds(2 * step, 2)

    def rows_of(col):
        return key_value[:, mine, :, pl.ds(col, HD)].reshape(-1, HD)

    def put(col, grad):
        cols = pl.ds(col, HD)
        for at, (kind, i) in enumerate(places):
            block = grad[at * 2 * sub : (at + 1) * 2 * sub].reshape(2, sub, HD)
            grads[kind][i, :, :, cols] = block
            (own_all, core_all)[kind][i, mine, :, cols] = block

    zero = jnp.zeros((SPAN, HD), BF16)
    for h0 in range(0, heads, group):
        hs = range(h0, h0 + group)
        qg, kv = [], []
        for h in hs:
            cols = pl.ds(h * HD, HD)
            top = jnp.concatenate([q_ref[:, cols], zero], axis=1)
            low = jnp.concatenate([zero, g_ref[:, cols]], axis=1)
            qg.append(jnp.concatenate([top, low], axis=0))
            kv.append(jnp.concatenate([rows_of(h * HD), rows_of(width + h * HD)], axis=1))
        both = [dot(a, b, last) for a, b in zip(qg, kv)]
        s = jnp.concatenate([x[:SPAN] for x in both], axis=0) * scale
        dw = jnp.concatenate([x[SPAN:] for x in both], axis=0)
        e = jnp.exp(s - jnp.max(s, axis=1, keepdims=True))
        p = e * (1.0 / jnp.sum(e, axis=1, keepdims=True))
        rs = jnp.sum(dw * p, axis=1, keepdims=True)
        w = p.astype(BF16)
        ds = (p * (dw - rs) * scale).astype(BF16)
        span = [slice(i * SPAN, (i + 1) * SPAN) for i in range(group)]
        dsw = [jnp.concatenate([ds[i], w[i]], axis=0) for i in span]
        out = [dot(a, b).astype(BF16) for a, b in zip(dsw, kv)]
        back = [dot(a, b, first).astype(BF16) for a, b in zip(dsw, qg)]
        for i, h in enumerate(hs):
            dq_ref[:, pl.ds(h * HD, HD)] = out[i][:SPAN, :HD]
            att_ref[:, pl.ds(h * HD, HD)] = out[i][SPAN:, HD:]
            put(h * HD, back[i][:, :HD])
            put(width + h * HD, back[i][:, HD:])

    @pl.when(step == pl.num_programs(0) - 1)
    def _():
        count = own_out.shape[-1]
        for ref, outs in ((core_all, (near_out, far_out)), (own_all, (own_out,))):
            rows = ref[...].reshape(-1, 2 * width)
            res = dot(rows[:, :width], wk[:count, :], last) + dot(rows[:, width:], wv[:count, :], last)
            res = res.reshape(ref.shape[:3] + (count,))
            if len(outs) == 1:
                outs[0][...] = res
            else:
                outs[0][...] = res[:near]
                outs[1][...] = res[near:]


def attend(pieces, wk, wv, places, near, count, queries, cotangent):
    tokens, width = queries.shape
    n, sub, enc = pieces[0].shape
    total = len(places)
    half = total // 2
    rows = pl.BlockSpec((SPAN, width), lambda i: (i, 0))
    grads = pl.BlockSpec((half, 2, sub, 2 * width), lambda i: (0, i, 0, 0))

    def once(shape):
        return pl.BlockSpec(shape, lambda i: (0,) * len(shape), pipeline_mode=pl.Buffered(1))

    def whole(shape):
        return pl.BlockSpec(shape, lambda i: (0,) * len(shape))

    parts = [(near, n, sub, count), (half - near, n, sub, count), (half, n, sub, count)]
    every = (half, n, sub, 2 * width)
    return pl.pallas_call(
        functools.partial(attend_body, places, near),
        out_shape=[jax.ShapeDtypeStruct((tokens, width), BF16)] * 2
        + [jax.ShapeDtypeStruct(every, BF16)] * 2
        + [jax.ShapeDtypeStruct(part, F32) for part in parts],
        grid=(tokens // SPAN,),
        in_specs=[once(x.shape) for x in pieces] + [once(wk.shape), once(wv.shape), rows, rows],
        out_specs=[rows, rows, grads, grads] + [whole(part) for part in parts],
        scratch_shapes=[
            pltpu.VMEM((total, n, sub, 2 * width), BF16),
            pltpu.VMEM(every, BF16),
            pltpu.VMEM(every, BF16),
        ],
        compiler_params=params(VMEM_MORE),
        cost_estimate=cost(
            16 * tokens * width * total * 2 * sub + 4 * n * sub * width * total * (enc + count),
            8 * tokens * width + 8 * total * n * sub * width,
        ),
        name="attend",
    )(*pieces, wk, wv, queries, cotangent)


def encode(x, axes):
    top = jnp.maximum(jnp.max(jnp.abs(x), axis=axes, keepdims=True), 1e-30)
    power = jnp.floor(jnp.log2(top)) + 1.0
    code = jnp.clip(jnp.round(x * jnp.exp2(15.0 - power)), -32767.0, 32767.0)
    return code.astype(jnp.int32).astype(jnp.int16), power


def grads_body(first, core_ref, own_ref, wk, wv, near_out, far_out, own_out, part, sem):
    i = pl.program_id(0)
    n_x = own_out.shape[0]
    width, count = wk.shape[1], part.shape[-1]
    last = (((1,), (1,)), ((), ()))

    def act(ref):
        rows = ref[...].reshape(-1, 2 * width)
        res = lax.dot_general(
            rows[:, :width], wk[first : first + count, :], last, preferred_element_type=F32
        )
        res += lax.dot_general(
            rows[:, width:], wv[first : first + count, :], last, preferred_element_type=F32
        )
        part[i] = res.reshape(part.shape[1:])

    @pl.when(i < n_x)
    def _():
        act(core_ref)

    @pl.when(i >= n_x)
    def _():
        act(own_ref)

    outs = [near_out.at[0]] + [far_out.at[k] for k in range(n_x - 1)]
    outs += [own_out.at[k] for k in range(n_x)]
    copies = [pltpu.make_async_copy(part.at[k], out, sem.at[k]) for k, out in enumerate(outs)]
    for k, copy in enumerate(copies):

        @pl.when(i == k)
        def _():
            copy.start()

    @pl.when(i == pl.num_programs(0) - 1)
    def _():
        for copy in copies:
            copy.wait()


def grads_of(d_core, d_own, wk, wv, cols):
    n_x, n, sub, width = d_own.shape
    first, count = cols
    shapes = [(1, n, sub, count), (n_x - 1, n, sub, count), (n_x, n, sub, count)]
    rows = n_x * n * sub
    return pl.pallas_call(
        functools.partial(grads_body, first),
        out_shape=[jax.ShapeDtypeStruct(shape, F32) for shape in shapes],
        grid=(2 * n_x,),
        in_specs=[
            pl.BlockSpec((1, n, sub, width), lambda i: (jnp.minimum(i, n_x - 1), 0, 0, 0)),
            pl.BlockSpec((1, n, sub, width), lambda i: (jnp.maximum(i - n_x, 0), 0, 0, 0)),
            pl.BlockSpec(wk.shape, lambda i: (0, 0)),
            pl.BlockSpec(wv.shape, lambda i: (0, 0)),
        ],
        out_specs=[ANY] * 3,
        scratch_shapes=[
            pltpu.VMEM((2 * n_x, n, sub, count), F32),
            pltpu.SemaphoreType.DMA((2 * n_x,)),
        ],
        compiler_params=params(VMEM_ALL),
        cost_estimate=cost(4 * rows * count * width, 2 * (count + 2 * rows) * width + 8 * rows * count),
        name="grads",
    )(d_core, d_own, wk, wv)


def far_codes_body(cuts, mine, got, *codes):
    far, n, sub, count = got.shape
    row = lax.broadcasted_iota(jnp.int32, (sub, LANES), 0)
    for k in range(far):
        code, power = encode(mine[k] + got[k], (1, 2))
        e = 0
        for cut, out in zip(cuts, codes[k * len(cuts) :]):
            for at in range(cut):
                out[at * n : (at + 1) * n] = code[:, :, e * LANES : (e + 1) * LANES]
                e += 1
        note = jnp.zeros((sub, LANES), F32)
        for r in range(n):
            note = jnp.where(row == r, power[r], note)
        codes[k * len(cuts)][cuts[0] * n] = note.astype(jnp.int32).astype(jnp.int16)


def far_codes(own, got, cuts):
    far, n, sub, count = got.shape
    shapes = [(cut * n + (q == 0), sub, LANES) for q, cut in enumerate(cuts)] * far

    def whole(shape):
        return pl.BlockSpec(shape, lambda i: (0,) * len(shape))

    mine = pl.BlockSpec(tuple(pl.Element(size) for size in got.shape), lambda i: (1, 0, 0, 0))
    out = pl.pallas_call(
        functools.partial(far_codes_body, cuts),
        out_shape=[jax.ShapeDtypeStruct(shape, jnp.int16) for shape in shapes],
        grid=(1,),
        in_specs=[mine, whole(got.shape)],
        out_specs=[whole(shape) for shape in shapes],
        compiler_params=params(),
        cost_estimate=cost(8 * got.size, 10 * got.size),
        name="far_codes",
    )(own, got)
    return [out[k * len(cuts) : (k + 1) * len(cuts)] for k in range(far)]


def send_body(n_dp, cuts, request, own, got, *rest):
    codes, outs, (stage, powers) = rest[: -n_dp - 2], rest[-n_dp - 2 : -2], rest[-2:]
    _, n, sub, count = got.shape
    tiles = count // LANES
    cap = request.shape[0] // n_dp
    notes = [code[cuts[0] * n].astype(F32) for code in codes[:: len(cuts)]]
    for r in range(n):
        total = own[0, r] + got[0, r]
        for k, note in enumerate(notes):
            unit = jnp.exp2(note[r : r + 1] - 15.0)
            blocks = [
                code[at * n + r].astype(F32) * unit
                for cut, code in zip(cuts, codes[k * len(cuts) :])
                for at in range(cut)
            ]
            total = total + jnp.concatenate(blocks, axis=1)
        coded, power = encode(total, (0, 1))
        for e in range(tiles):
            for h in range(sub // TILE):
                block = coded[h * TILE : (h + 1) * TILE, e * LANES : (e + 1) * LANES]
                stage[r, e * (sub // TILE) + h] = block
        powers[r] = jnp.broadcast_to(power, (TILE, LANES))
    row = lax.broadcasted_iota(jnp.int32, (TILE, LANES), 0)
    size = stage.shape[1]
    for d in range(n_dp):
        note = jnp.zeros((TILE, LANES), F32)
        for j in range(cap):
            r = request[d * cap + j]

            @pl.when(r >= 0)
            def _():
                outs[d][pl.ds(j * size, size)] = stage[r]

            note = jnp.where(row == j, powers[jnp.maximum(r, 0)], note)
        outs[d][cap * size] = note.astype(jnp.int32).astype(jnp.int16)


def send_codes(request, own, got, codes, cuts, n_dp):
    _, n, sub, count = got.shape
    block = pl.BlockSpec(got.shape, lambda i: (0, 0, 0, 0))
    size = count // LANES * (sub // TILE)
    cap = request.shape[0] // n_dp
    shape = (cap * size + 1, TILE, LANES)
    codes = [x for piece in codes for x in piece]
    return pl.pallas_call(
        functools.partial(send_body, n_dp, cuts),
        out_shape=[jax.ShapeDtypeStruct(shape, jnp.int16)] * n_dp,
        grid=(1,),
        in_specs=[SMEM, block, block] + [VMEM] * len(codes),
        out_specs=[VMEM] * n_dp,
        scratch_shapes=[
            pltpu.VMEM((n, size, TILE, LANES), jnp.int16),
            pltpu.VMEM((n, TILE, LANES), F32),
        ],
        compiler_params=params(),
        cost_estimate=cost(10 * got.size, 6 * got.size + 2 * n_dp * math.prod(shape)),
        name="send_codes",
    )(request, own, got, *codes)


def gather_body(n_dp, first, me, asked, *refs):
    arrived = refs[:n_dp]
    out, total, sem = refs[-3:]
    tiles, halves = total.shape[2] // LANES, total.shape[1] // TILE
    size = tiles * halves
    cap = asked.shape[1] // n_dp
    total[...] = jnp.zeros_like(total)
    for d in range(n_dp):
        for j in range(cap):
            slab = asked_of(asked, me, d, j)

            @pl.when(slab >= 0)
            def _():
                note = arrived[d][cap * size].astype(F32)
                unit = jnp.exp2(note[j : j + 1] - 15.0)
                for e in range(tiles):
                    for h in range(halves):
                        value = arrived[d][j * size + e * halves + h].astype(F32) * unit
                        total[slab, pl.ds(h * TILE, TILE), pl.ds(e * LANES, LANES)] += value

    copy = pltpu.make_async_copy(total, out.at[:, :, pl.ds(first, total.shape[2])], sem)
    copy.start()
    copy.wait()


def gather_grads(me, asked, arrived, n_slabs, rows, enc, cols, before):
    first, count = cols
    n_dp = asked.shape[0]
    return pl.pallas_call(
        functools.partial(gather_body, n_dp, first),
        out_shape=jax.ShapeDtypeStruct((n_slabs, rows, enc), F32),
        in_specs=[SMEM, SMEM] + [VMEM] * n_dp + [ANY] * (before is not None),
        out_specs=ANY,
        scratch_shapes=[pltpu.VMEM((n_slabs, rows, count), F32), pltpu.SemaphoreType.DMA],
        input_output_aliases={} if before is None else {2 + n_dp: 0},
        compiler_params=params(),
        cost_estimate=cost(0, 8 * n_slabs * rows * count),
        name="gather_grads",
    )(me, asked, *arrived, *([] if before is None else [before]))


def on_device(queries, cotangent, table, key_weight, value_weight, owners, slots):
    n_dp = lax.axis_size("dp")
    n_tp = lax.axis_size("tensor")
    n_x = n_tp // 2
    spans = owners.shape[0]
    n_requests = 2 * spans
    n_slabs, n_tokens, enc = table.shape
    cap = max(2, (4 * spans + n_dp - 1) // n_dp)
    share = n_tokens // n_tp

    def over_core(x):
        return lax.ppermute(x, "tensor", [(t, t ^ 1) for t in range(n_tp)])

    def over_x(x, d):
        return lax.ppermute(x, "tensor", [(t, (t + 2 * d) % n_tp) for t in range(n_tp)])

    def over_dp(x, d):
        return lax.ppermute(x, "dp", [(i, (i + d) % n_dp) for i in range(n_dp)])

    nearest_first = sorted(range(1, n_dp), key=lambda d: min(d, n_dp - d))
    farthest_first = sorted(range(1, n_dp), key=lambda d: -min(d, n_dp - d))

    def to_all(xs, sign, distances=farthest_first):
        got = {d: over_dp(xs[d], sign * d) for d in distances}
        return got

    me, wanted, request = ask(owners, slots, n_dp, cap)
    asked = lax.psum(wanted, "dp")

    sent = pack(me, asked, table, share, cap)
    mine = {0: sent[0]}
    for i, d in enumerate(nearest_first):
        block = sent[d]
        if i >= WINDOW:
            held = nearest_first[i - WINDOW]
            block, mine[held] = lax.optimization_barrier((block, mine[held]))
        mine[d] = over_dp(block, -d)
    far = [[over_x(mine[d], k) for k in range(1, n_x)] for d in range(n_dp)]
    lists = [[mine[d] for d in range(n_dp)]]
    lists += [[far[d][k] for d in range(n_dp)] for k in range(n_x - 1)]
    mine, *far = compact(request, lists, n_requests)

    pieces = [mine, *far]
    pieces += [over_core(x) for x in pieces]
    places = [(kind, k) for kind in range(2) for k in range(n_x)]

    split = 3 * LANES
    parts = ((0, split), (split, enc - split))
    attended, d_query, d_own, d_core, near, far, own = attend(
        pieces, key_weight, value_weight, places, 1, split, queries, cotangent
    )
    far_got = over_core(far)
    near_got = over_core(near)
    cuts = (2, 1)
    codes = far_codes(own, far_got, cuts)
    near_b, far_b, own_b = grads_of(d_core, d_own, key_weight, value_weight, parts[1])

    codes = [[over_x(x, n_x - k) for x in piece] for k, piece in enumerate(codes, 1)]
    lead, near_b, far_b = lax.optimization_barrier(([piece[0] for piece in codes], near_b, far_b))
    codes = [[x, *piece[1:]] for x, piece in zip(lead, codes)]
    far_got_b = over_core(far_b)
    near_got_b = over_core(near_b)
    sent = send_codes(request, own, near_got, codes, cuts, n_dp)
    came = to_all(sent, 1)
    arrived = [sent[0]] + [came[d] for d in range(1, n_dp)]
    d_table = gather_grads(me, asked, arrived, n_slabs, share, enc, parts[0], None)

    cuts = (parts[1][1] // LANES,)
    codes = far_codes(own_b, far_got_b, cuts)
    codes, before = lax.optimization_barrier((codes, sent[0]))
    codes = [[over_x(x, n_x - k) for x in piece] for k, piece in enumerate(codes, 1)]
    sent = send_codes(request, own_b, near_got_b, codes, cuts, n_dp)
    came = to_all(sent, 1)
    arrived = [sent[0]] + [came[d] for d in range(1, n_dp)]
    d_table = gather_grads(me, asked, arrived, n_slabs, share, enc, parts[1], d_table)
    return (attended, d_query, d_table)


def solution(mesh):
    in_specs = (
        P("dp", "tensor"),
        P("dp", "tensor"),
        P("dp", None, None),
        P(None, "tensor"),
        P(None, "tensor"),
        P("dp", None),
        P("dp", None),
    )
    out_specs = (P("dp", "tensor"), P("dp", "tensor"), P("dp", "tensor", None))
    return jax.shard_map(
        on_device, mesh=mesh, in_specs=in_specs, out_specs=out_specs, check_vma=False
    )
```

```python
import functools
import math

import jax
import jax.numpy as jnp
from jax import lax
from jax.experimental import pallas as pl
from jax.experimental.pallas import tpu as pltpu
from jax.sharding import PartitionSpec as P

HD = 128
SPAN = 64
LANES = 128
TILE = 16
WINDOW = 4
VMEM_LIMIT = 28 * 1024 * 1024
VMEM_MORE = 50 * 1024 * 1024
VMEM_ALL = 60 * 1024 * 1024
VMEM_GRADS = 56 * 1024 * 1024
F32 = jnp.float32
BF16 = jnp.bfloat16

ANY = pl.BlockSpec(memory_space=pl.ANY)
SMEM = pl.BlockSpec(memory_space=pltpu.SMEM)
VMEM = pl.BlockSpec(memory_space=pltpu.VMEM)


def params(limit=VMEM_LIMIT):
    return pltpu.CompilerParams(vmem_limit_bytes=limit)


def cost(flops, nbytes):
    return pl.CostEstimate(flops=int(flops), bytes_accessed=int(nbytes), transcendentals=0)


def ask_body(cap, owners, slots, me_out, wanted, request, count):
    n_dp = wanted.shape[0]
    me = lax.axis_index("dp")
    me_out[0] = me
    for i in range(n_dp * cap):
        request[i] = -1
        for asker in range(n_dp):
            wanted[asker, i] = 0
    for d in range(n_dp):
        count[d] = 0
    for r in range(owners.size):
        d = owners[r % 2, r // 2] - me
        d = jnp.where(d < 0, d + n_dp, d)
        j = count[d]
        count[d] = j + 1
        wanted[me, d * cap + j] = slots[r % 2, r // 2] + 1
        request[d * cap + j] = r


def ask(owners, slots, n_dp, cap):
    return pl.pallas_call(
        functools.partial(ask_body, cap),
        out_shape=[
            jax.ShapeDtypeStruct((1,), jnp.int32),
            jax.ShapeDtypeStruct((n_dp, n_dp * cap), jnp.int32),
            jax.ShapeDtypeStruct((n_dp * cap,), jnp.int32),
        ],
        in_specs=[SMEM, SMEM],
        out_specs=[SMEM, SMEM, SMEM],
        scratch_shapes=[pltpu.SMEM((n_dp,), jnp.int32)],
        name="ask",
    )(owners.T, slots.T)


def asked_of(asked, me, d, j):
    n_dp = asked.shape[0]
    asker = me[0] - d
    asker = jnp.where(asker < 0, asker + n_dp, asker)
    return asked[asker, d * (asked.shape[1] // n_dp) + j] - 1


def pack_body(n_dp, me, asked, table, *rest):
    outs, sem = rest[:-1], rest[-1]
    cap, share, _ = outs[0].shape
    row = pl.multiple_of(lax.axis_index("tensor") * share, share)

    def each(act):
        for d in range(n_dp):
            for j in range(cap):
                slab = asked_of(asked, me, d, j)

                @pl.when(slab >= 0)
                def _():
                    source = table.at[slab, pl.ds(row, share)]
                    act(pltpu.make_async_copy(source, outs[d].at[j], sem.at[d * cap + j]))

    each(lambda copy: copy.start())
    each(lambda copy: copy.wait())


def pack(me, asked, table, share, cap):
    n_dp = asked.shape[0]
    enc = table.shape[2]
    return pl.pallas_call(
        functools.partial(pack_body, n_dp),
        out_shape=[jax.ShapeDtypeStruct((cap, share, enc), table.dtype)] * n_dp,
        in_specs=[SMEM, SMEM, ANY],
        out_specs=[VMEM] * n_dp,
        scratch_shapes=[pltpu.SemaphoreType.DMA((n_dp * cap,))],
        compiler_params=params(VMEM_ALL),
        cost_estimate=cost(0, 4 * n_dp * cap * share * enc),
        name="pack_rows",
    )(me, asked, table)


def compact_body(n_dp, n_out, request, *refs):
    arrived, outs, sem = refs[: n_dp * n_out], refs[n_dp * n_out : -1], refs[-1]
    cap = arrived[0].shape[0]

    def each(act):
        for d in range(n_dp):
            for j in range(cap):
                r = request[d * cap + j]

                @pl.when(r >= 0)
                def _():
                    for i in range(n_out):
                        source = arrived[i * n_dp + d].at[j]
                        act(pltpu.make_async_copy(source, outs[i].at[r], sem.at[i, d * cap + j]))

    each(lambda copy: copy.start())
    each(lambda copy: copy.wait())


def compact(request, lists, n):
    n_dp, n_out = len(lists[0]), len(lists)
    shape = (n,) + lists[0][0].shape[1:]
    return pl.pallas_call(
        functools.partial(compact_body, n_dp, n_out),
        out_shape=[jax.ShapeDtypeStruct(shape, lists[0][0].dtype)] * n_out,
        in_specs=[SMEM] + [ANY] * (n_dp * n_out),
        out_specs=[VMEM] * n_out,
        scratch_shapes=[pltpu.SemaphoreType.DMA((n_out, request.shape[0]))],
        compiler_params=params(),
        cost_estimate=cost(0, 4 * n_out * math.prod(shape)),
        name="compact_rows",
    )(request, *[block for blocks in lists for block in blocks])


def attend_body(places, near, *refs):
    n_in = len(places)
    pieces = refs[:n_in]
    wk, wv, q_ref, g_ref, att_ref, dq_ref = refs[n_in : n_in + 6]
    *grads, near_out, far_out, own_out, rest_out, key_value, own_all, core_all = refs[n_in + 6 :]
    step = pl.program_id(0)
    width = q_ref.shape[1]
    enc = wk.shape[0]
    sub = key_value.shape[2]
    scale = 1.0 / math.sqrt(HD)
    heads = width // HD
    group = min(8, heads)
    last = (((1,), (1,)), ((), ()))
    first = (((0,), (0,)), ((), ()))

    def dot(a, b, dims=(((1,), (0,)), ((), ()))):
        return lax.dot_general(a, b, dims, preferred_element_type=F32)

    @pl.when(step == 0)
    def _():
        for i, ref in enumerate(pieces):
            rows = ref[...].reshape(-1, enc)
            shape = ref.shape[:2] + (width,)
            key_value[i, :, :, :width] = dot(rows, wk[...]).astype(BF16).reshape(shape)
            key_value[i, :, :, width:] = dot(rows, wv[...]).astype(BF16).reshape(shape)

    mine = pl.ds(2 * step, 2)

    def rows_of(col):
        return key_value[:, mine, :, pl.ds(col, HD)].reshape(-1, HD)

    def put(col, grad):
        cols = pl.ds(col, HD)
        for at, (kind, i) in enumerate(places):
            block = grad[at * 2 * sub : (at + 1) * 2 * sub].reshape(2, sub, HD)
            grads[kind][i, :, :, cols] = block
            (own_all, core_all)[kind][i, mine, :, cols] = block

    zero = jnp.zeros((SPAN, HD), BF16)
    for h0 in range(0, heads, group):
        hs = range(h0, h0 + group)
        qg, kv = [], []
        for h in hs:
            cols = pl.ds(h * HD, HD)
            top = jnp.concatenate([q_ref[:, cols], zero], axis=1)
            low = jnp.concatenate([zero, g_ref[:, cols]], axis=1)
            qg.append(jnp.concatenate([top, low], axis=0))
            kv.append(jnp.concatenate([rows_of(h * HD), rows_of(width + h * HD)], axis=1))
        both = [dot(a, b, last) for a, b in zip(qg, kv)]
        s = jnp.concatenate([x[:SPAN] for x in both], axis=0) * scale
        dw = jnp.concatenate([x[SPAN:] for x in both], axis=0)
        e = jnp.exp(s - jnp.max(s, axis=1, keepdims=True))
        p = e * (1.0 / jnp.sum(e, axis=1, keepdims=True))
        rs = jnp.sum(dw * p, axis=1, keepdims=True)
        w = p.astype(BF16)
        ds = (p * (dw - rs) * scale).astype(BF16)
        span = [slice(i * SPAN, (i + 1) * SPAN) for i in range(group)]
        dsw = [jnp.concatenate([ds[i], w[i]], axis=0) for i in span]
        out = [dot(a, b).astype(BF16) for a, b in zip(dsw, kv)]
        back = [dot(a, b, first).astype(BF16) for a, b in zip(dsw, qg)]
        for i, h in enumerate(hs):
            dq_ref[:, pl.ds(h * HD, HD)] = out[i][:SPAN, :HD]
            att_ref[:, pl.ds(h * HD, HD)] = out[i][SPAN:, HD:]
            put(h * HD, back[i][:, :HD])
            put(width + h * HD, back[i][:, HD:])

    @pl.when(step == pl.num_programs(0) - 1)
    def _():
        count = own_out.shape[-1]

        def part(ref, cols, out):
            rows = ref[...].reshape(-1, 2 * width)
            res = dot(rows[:, :width], wk[cols, :], last) + dot(rows[:, width:], wv[cols, :], last)
            out[...] = res.reshape(out.shape)

        part(core_all.at[near:], slice(0, count), far_out)
        part(core_all.at[:near], slice(0, count), near_out)
        part(own_all, slice(0, count), own_out)
        part(core_all.at[near:], slice(count, enc), rest_out)


def attend(pieces, wk, wv, places, near, count, queries, cotangent):
    tokens, width = queries.shape
    n, sub, enc = pieces[0].shape
    total = len(places)
    half = total // 2
    rows = pl.BlockSpec((SPAN, width), lambda i: (i, 0))
    grads = pl.BlockSpec((half, 2, sub, 2 * width), lambda i: (0, i, 0, 0))

    def once(shape):
        return pl.BlockSpec(shape, lambda i: (0,) * len(shape), pipeline_mode=pl.Buffered(1))

    def whole(shape):
        return pl.BlockSpec(shape, lambda i: (0,) * len(shape))

    parts = [(near, n, sub, count), (half - near, n, sub, count), (half, n, sub, count)]
    parts.append((half - near, n, sub, enc - count))
    every = (half, n, sub, 2 * width)
    return pl.pallas_call(
        functools.partial(attend_body, places, near),
        out_shape=[jax.ShapeDtypeStruct((tokens, width), BF16)] * 2
        + [jax.ShapeDtypeStruct(every, BF16)] * 2
        + [jax.ShapeDtypeStruct(part, F32) for part in parts],
        grid=(tokens // SPAN,),
        in_specs=[once(x.shape) for x in pieces] + [once(wk.shape), once(wv.shape), rows, rows],
        out_specs=[rows, rows, grads, grads] + [whole(part) for part in parts],
        scratch_shapes=[
            pltpu.VMEM((total, n, sub, 2 * width), BF16),
            pltpu.VMEM(every, BF16),
            pltpu.VMEM(every, BF16),
        ],
        compiler_params=params(VMEM_MORE),
        cost_estimate=cost(
            16 * tokens * width * total * 2 * sub + 4 * n * sub * width * total * (enc + count),
            8 * tokens * width + 8 * total * n * sub * width,
        ),
        name="attend",
    )(*pieces, wk, wv, queries, cotangent)


def encode(x, axes):
    top = jnp.maximum(jnp.max(jnp.abs(x), axis=axes, keepdims=True), 1e-30)
    power = jnp.floor(jnp.log2(top)) + 1.0
    code = jnp.clip(jnp.round(x * jnp.exp2(15.0 - power)), -32767.0, 32767.0)
    return code.astype(jnp.int32).astype(jnp.int16), power


def grads_body(first, core_ref, own_ref, wk, wv, near_out, own_out, part, sem):
    i = pl.program_id(0)
    n_x = own_out.shape[0]
    width, count = wk.shape[1], part.shape[-1]
    last = (((1,), (1,)), ((), ()))

    def act(ref):
        rows = ref[...].reshape(-1, 2 * width)
        res = lax.dot_general(
            rows[:, :width], wk[first : first + count, :], last, preferred_element_type=F32
        )
        res += lax.dot_general(
            rows[:, width:], wv[first : first + count, :], last, preferred_element_type=F32
        )
        part[i] = res.reshape(part.shape[1:])

    @pl.when(i == n_x)
    def _():
        act(core_ref)

    @pl.when(i < n_x)
    def _():
        act(own_ref)

    outs = [own_out.at[k] for k in range(n_x)] + [near_out.at[0]]
    copies = [pltpu.make_async_copy(part.at[k], out, sem.at[k]) for k, out in enumerate(outs)]
    for k, copy in enumerate(copies):

        @pl.when(i == k)
        def _():
            copy.start()

    @pl.when(i == pl.num_programs(0) - 1)
    def _():
        for copy in copies:
            copy.wait()


def grads_of(d_core, d_own, wk, wv, cols):
    n_x, n, sub, width = d_own.shape
    first, count = cols
    rows = n_x * n * sub
    return pl.pallas_call(
        functools.partial(grads_body, first),
        out_shape=[
            jax.ShapeDtypeStruct((1, n, sub, count), F32),
            jax.ShapeDtypeStruct((n_x, n, sub, count), F32),
        ],
        grid=(n_x + 1,),
        in_specs=[
            pl.BlockSpec((1, n, sub, width), lambda i: (0, 0, 0, 0)),
            pl.BlockSpec((1, n, sub, width), lambda i: (jnp.minimum(i, n_x - 1), 0, 0, 0)),
            pl.BlockSpec(wk.shape, lambda i: (0, 0)),
            pl.BlockSpec(wv.shape, lambda i: (0, 0)),
        ],
        out_specs=[ANY] * 2,
        scratch_shapes=[
            pltpu.VMEM((n_x + 1, n, sub, count), F32),
            pltpu.SemaphoreType.DMA((n_x + 1,)),
        ],
        compiler_params=params(VMEM_GRADS),
        cost_estimate=cost(4 * rows * count * width, 2 * (count + 2 * rows) * width + 8 * rows * count),
        name="grads",
    )(d_core, d_own, wk, wv)


def far_codes_body(cuts, mine, got, *codes):
    far, n, sub, count = got.shape
    row = lax.broadcasted_iota(jnp.int32, (sub, LANES), 0)
    for k in range(far):
        code, power = encode(mine[k] + got[k], (1, 2))
        e = 0
        for cut, out in zip(cuts, codes[k * len(cuts) :]):
            for at in range(cut):
                out[at * n : (at + 1) * n] = code[:, :, e * LANES : (e + 1) * LANES]
                e += 1
        note = jnp.zeros((sub, LANES), F32)
        for r in range(n):
            note = jnp.where(row == r, power[r], note)
        codes[k * len(cuts)][cuts[0] * n] = note.astype(jnp.int32).astype(jnp.int16)


def far_codes(own, got, cuts):
    far, n, sub, count = got.shape
    shapes = [(cut * n + (q == 0), sub, LANES) for q, cut in enumerate(cuts)] * far

    def whole(shape):
        return pl.BlockSpec(shape, lambda i: (0,) * len(shape))

    mine = pl.BlockSpec(tuple(pl.Element(size) for size in got.shape), lambda i: (1, 0, 0, 0))
    out = pl.pallas_call(
        functools.partial(far_codes_body, cuts),
        out_shape=[jax.ShapeDtypeStruct(shape, jnp.int16) for shape in shapes],
        grid=(1,),
        in_specs=[mine, whole(got.shape)],
        out_specs=[whole(shape) for shape in shapes],
        compiler_params=params(),
        cost_estimate=cost(8 * got.size, 10 * got.size),
        name="far_codes",
    )(own, got)
    return [out[k * len(cuts) : (k + 1) * len(cuts)] for k in range(far)]


def send_body(n_dp, cuts, request, own, got, *rest):
    codes, outs, (stage, powers) = rest[: -n_dp - 2], rest[-n_dp - 2 : -2], rest[-2:]
    _, n, sub, count = got.shape
    tiles = count // LANES
    cap = request.shape[0] // n_dp
    notes = [code[cuts[0] * n].astype(F32) for code in codes[:: len(cuts)]]
    for r in range(n):
        total = own[0, r] + got[0, r]
        for k, note in enumerate(notes):
            unit = jnp.exp2(note[r : r + 1] - 15.0)
            blocks = [
                code[at * n + r].astype(F32) * unit
                for cut, code in zip(cuts, codes[k * len(cuts) :])
                for at in range(cut)
            ]
            total = total + jnp.concatenate(blocks, axis=1)
        coded, power = encode(total, (0, 1))
        for e in range(tiles):
            for h in range(sub // TILE):
                block = coded[h * TILE : (h + 1) * TILE, e * LANES : (e + 1) * LANES]
                stage[r, e * (sub // TILE) + h] = block
        powers[r] = jnp.broadcast_to(power, (TILE, LANES))
    row = lax.broadcasted_iota(jnp.int32, (TILE, LANES), 0)
    size = stage.shape[1]
    for d in range(n_dp):
        note = jnp.zeros((TILE, LANES), F32)
        for j in range(cap):
            r = request[d * cap + j]

            @pl.when(r >= 0)
            def _():
                outs[d][pl.ds(j * size, size)] = stage[r]

            note = jnp.where(row == j, powers[jnp.maximum(r, 0)], note)
        outs[d][cap * size] = note.astype(jnp.int32).astype(jnp.int16)


def send_codes(request, own, got, codes, cuts, n_dp):
    _, n, sub, count = got.shape
    block = pl.BlockSpec(got.shape, lambda i: (0, 0, 0, 0))
    size = count // LANES * (sub // TILE)
    cap = request.shape[0] // n_dp
    shape = (cap * size + 1, TILE, LANES)
    codes = [x for piece in codes for x in piece]
    return pl.pallas_call(
        functools.partial(send_body, n_dp, cuts),
        out_shape=[jax.ShapeDtypeStruct(shape, jnp.int16)] * n_dp,
        grid=(1,),
        in_specs=[SMEM, block, block] + [VMEM] * len(codes),
        out_specs=[VMEM] * n_dp,
        scratch_shapes=[
            pltpu.VMEM((n, size, TILE, LANES), jnp.int16),
            pltpu.VMEM((n, TILE, LANES), F32),
        ],
        compiler_params=params(),
        cost_estimate=cost(10 * got.size, 6 * got.size + 2 * n_dp * math.prod(shape)),
        name="send_codes",
    )(request, own, got, *codes)


def gather_body(n_dp, first, me, asked, *refs):
    arrived = refs[:n_dp]
    out, total, sem = refs[-3:]
    tiles, halves = total.shape[2] // LANES, total.shape[1] // TILE
    size = tiles * halves
    cap = asked.shape[1] // n_dp
    total[...] = jnp.zeros_like(total)
    for d in range(n_dp):
        for j in range(cap):
            slab = asked_of(asked, me, d, j)

            @pl.when(slab >= 0)
            def _():
                note = arrived[d][cap * size].astype(F32)
                unit = jnp.exp2(note[j : j + 1] - 15.0)
                for e in range(tiles):
                    for h in range(halves):
                        value = arrived[d][j * size + e * halves + h].astype(F32) * unit
                        total[slab, pl.ds(h * TILE, TILE), pl.ds(e * LANES, LANES)] += value

    copy = pltpu.make_async_copy(total, out.at[:, :, pl.ds(first, total.shape[2])], sem)
    copy.start()
    copy.wait()


def gather_grads(me, asked, arrived, n_slabs, rows, enc, cols, before):
    first, count = cols
    n_dp = asked.shape[0]
    return pl.pallas_call(
        functools.partial(gather_body, n_dp, first),
        out_shape=jax.ShapeDtypeStruct((n_slabs, rows, enc), F32),
        in_specs=[SMEM, SMEM] + [VMEM] * n_dp + [ANY] * (before is not None),
        out_specs=ANY,
        scratch_shapes=[pltpu.VMEM((n_slabs, rows, count), F32), pltpu.SemaphoreType.DMA],
        input_output_aliases={} if before is None else {2 + n_dp: 0},
        compiler_params=params(),
        cost_estimate=cost(0, 8 * n_slabs * rows * count),
        name="gather_grads",
    )(me, asked, *arrived, *([] if before is None else [before]))


def on_device(queries, cotangent, table, key_weight, value_weight, owners, slots):
    n_dp = lax.axis_size("dp")
    n_tp = lax.axis_size("tensor")
    n_x = n_tp // 2
    spans = owners.shape[0]
    n_requests = 2 * spans
    n_slabs, n_tokens, enc = table.shape
    cap = max(2, (4 * spans + n_dp - 1) // n_dp)
    share = n_tokens // n_tp

    def over_core(x):
        return lax.ppermute(x, "tensor", [(t, t ^ 1) for t in range(n_tp)])

    def over_x(x, d):
        return lax.ppermute(x, "tensor", [(t, (t + 2 * d) % n_tp) for t in range(n_tp)])

    def over_dp(x, d):
        return lax.ppermute(x, "dp", [(i, (i + d) % n_dp) for i in range(n_dp)])

    nearest_first = sorted(range(1, n_dp), key=lambda d: min(d, n_dp - d))
    farthest_first = sorted(range(1, n_dp), key=lambda d: -min(d, n_dp - d))

    def to_all(xs, sign, distances=farthest_first):
        got = {d: over_dp(xs[d], sign * d) for d in distances}
        return got

    me, wanted, request = ask(owners, slots, n_dp, cap)
    asked = lax.psum(wanted, "dp")

    sent = pack(me, asked, table, share, cap)
    mine = {0: sent[0]}
    for i, d in enumerate(nearest_first):
        block = sent[d]
        if i >= WINDOW:
            held = nearest_first[i - WINDOW]
            block, mine[held] = lax.optimization_barrier((block, mine[held]))
        mine[d] = over_dp(block, -d)
    far = [[over_x(mine[d], k) for k in range(1, n_x)] for d in range(n_dp)]
    lists = [[mine[d] for d in range(n_dp)]]
    lists += [[far[d][k] for d in range(n_dp)] for k in range(n_x - 1)]
    mine, *far = compact(request, lists, n_requests)

    pieces = [mine, *far]
    pieces += [over_core(x) for x in pieces]
    places = [(kind, k) for kind in range(2) for k in range(n_x)]

    split = 3 * LANES
    parts = ((0, split), (split, enc - split))
    attended, d_query, d_own, d_core, near, far, own, far_b = attend(
        pieces, key_weight, value_weight, places, 1, split, queries, cotangent
    )
    far_got = over_core(far)
    near_got = over_core(near)
    far_got_b = over_core(far_b)
    cuts = (parts[0][1] // LANES,)
    codes = far_codes(own, far_got, cuts)
    near_got, d_own = lax.optimization_barrier((near_got, d_own))
    near_b, own_b = grads_of(d_core, d_own, key_weight, value_weight, parts[1])

    codes = [[over_x(x, n_x - k) for x in piece] for k, piece in enumerate(codes, 1)]
    codes, near_b = lax.optimization_barrier((codes, near_b))
    near_got_b = over_core(near_b)
    sent = send_codes(request, own, near_got, codes, cuts, n_dp)
    sent, near_got_b = lax.optimization_barrier((sent, near_got_b))
    came = to_all(sent, 1)
    arrived = [sent[0]] + [came[d] for d in range(1, n_dp)]
    d_table = gather_grads(me, asked, arrived, n_slabs, share, enc, parts[0], None)

    cuts = (parts[1][1] // LANES,)
    far_got_b, _ = lax.optimization_barrier((far_got_b, codes))
    codes = far_codes(own_b, far_got_b, cuts)
    codes = [[over_x(x, n_x - k) for x in piece] for k, piece in enumerate(codes, 1)]
    sent = send_codes(request, own_b, near_got_b, codes, cuts, n_dp)
    came = to_all(sent, 1)
    arrived = [sent[0]] + [came[d] for d in range(1, n_dp)]
    d_table = gather_grads(me, asked, arrived, n_slabs, share, enc, parts[1], d_table)
    return (attended, d_query, d_table)


def solution(mesh):
    in_specs = (
        P("dp", "tensor"),
        P("dp", "tensor"),
        P("dp", None, None),
        P(None, "tensor"),
        P(None, "tensor"),
        P("dp", None),
        P("dp", None),
    )
    out_specs = (P("dp", "tensor"), P("dp", "tensor"), P("dp", "tensor", None))
    return jax.shard_map(
        on_device, mesh=mesh, in_specs=in_specs, out_specs=out_specs, check_vma=False
    )
```

```python
import functools
import math

import jax
import jax.numpy as jnp
from jax import lax
from jax.experimental import pallas as pl
from jax.experimental.pallas import tpu as pltpu
from jax.sharding import PartitionSpec as P

HD = 128
SPAN = 64
LANES = 128
TILE = 16
VMEM_LIMIT = 28 * 1024 * 1024
VMEM_MORE = 44 * 1024 * 1024
VMEM_ALL = 60 * 1024 * 1024
F32 = jnp.float32
BF16 = jnp.bfloat16

ANY = pl.BlockSpec(memory_space=pl.ANY)
SMEM = pl.BlockSpec(memory_space=pltpu.SMEM)
VMEM = pl.BlockSpec(memory_space=pltpu.VMEM)


def params(limit=VMEM_LIMIT):
    return pltpu.CompilerParams(vmem_limit_bytes=limit)


def cost(flops, nbytes):
    return pl.CostEstimate(flops=int(flops), bytes_accessed=int(nbytes), transcendentals=0)


def ask_body(cap, owners, slots, me_out, wanted, request, count):
    n_dp = wanted.shape[0]
    me = lax.axis_index("dp")
    me_out[0] = me
    for i in range(n_dp * cap):
        request[i] = -1
        for asker in range(n_dp):
            wanted[asker, i] = 0
    for d in range(n_dp):
        count[d] = 0
    for r in range(owners.size):
        d = owners[r % 2, r // 2] - me
        d = jnp.where(d < 0, d + n_dp, d)
        j = count[d]
        count[d] = j + 1
        wanted[me, d * cap + j] = slots[r % 2, r // 2] + 1
        request[d * cap + j] = r


def ask(owners, slots, n_dp, cap):
    return pl.pallas_call(
        functools.partial(ask_body, cap),
        out_shape=[
            jax.ShapeDtypeStruct((1,), jnp.int32),
            jax.ShapeDtypeStruct((n_dp, n_dp * cap), jnp.int32),
            jax.ShapeDtypeStruct((n_dp * cap,), jnp.int32),
        ],
        in_specs=[SMEM, SMEM],
        out_specs=[SMEM, SMEM, SMEM],
        scratch_shapes=[pltpu.SMEM((n_dp,), jnp.int32)],
        name="ask",
    )(owners.T, slots.T)


def asked_of(asked, me, d, j):
    n_dp = asked.shape[0]
    asker = me[0] - d
    asker = jnp.where(asker < 0, asker + n_dp, asker)
    return asked[asker, d * (asked.shape[1] // n_dp) + j] - 1


def pack_body(n_dp, chunk, share, me, asked, table, *rest):
    outs, sem = rest[:-1], rest[-1]
    cap = outs[0].shape[0]
    row = pl.multiple_of(lax.axis_index("tensor") * share + chunk * TILE, TILE)

    def each(act):
        for d in range(n_dp):
            for j in range(cap):
                slab = asked_of(asked, me, d, j)

                @pl.when(slab >= 0)
                def _():
                    source = table.at[slab, pl.ds(row, TILE)]
                    act(pltpu.make_async_copy(source, outs[d].at[j], sem.at[d * cap + j]))

    each(lambda copy: copy.start())
    each(lambda copy: copy.wait())


def pack(me, asked, table, chunk, share, cap):
    n_dp = asked.shape[0]
    enc = table.shape[2]
    return pl.pallas_call(
        functools.partial(pack_body, n_dp, chunk, share),
        out_shape=[jax.ShapeDtypeStruct((cap, TILE, enc), table.dtype)] * n_dp,
        in_specs=[SMEM, SMEM, ANY],
        out_specs=[VMEM] * n_dp,
        scratch_shapes=[pltpu.SemaphoreType.DMA((n_dp * cap,))],
        compiler_params=params(VMEM_ALL),
        cost_estimate=cost(0, 4 * n_dp * cap * TILE * enc),
        name="pack_rows",
    )(me, asked, table)


def compact_body(n_dp, request, *refs):
    arrived, out, sem = refs[:n_dp], refs[n_dp], refs[n_dp + 1]
    cap = arrived[0].shape[0]

    def each(act):
        for d in range(n_dp):
            for j in range(cap):
                r = request[d * cap + j]

                @pl.when(r >= 0)
                def _():
                    act(pltpu.make_async_copy(arrived[d].at[j], out.at[r], sem.at[d * cap + j]))

    each(lambda copy: copy.start())
    each(lambda copy: copy.wait())


def compact(request, arrived, n):
    shape = (n,) + arrived[0].shape[1:]
    return pl.pallas_call(
        functools.partial(compact_body, len(arrived)),
        out_shape=jax.ShapeDtypeStruct(shape, arrived[0].dtype),
        in_specs=[SMEM] + [ANY] * len(arrived),
        out_specs=VMEM,
        scratch_shapes=[pltpu.SemaphoreType.DMA((request.shape[0],))],
        compiler_params=params(),
        cost_estimate=cost(0, 4 * math.prod(shape)),
        name="compact_rows",
    )(request, *arrived)


def weight_specs(rows, step):
    return [
        pl.BlockSpec((rows, step), lambda i: (0, jnp.minimum(i, 1))),
        pl.BlockSpec((rows, step), lambda i: (0, jnp.maximum(i - 2, 0))),
    ]


def with_weight(wk, wv, act):
    @pl.when(pl.program_id(0) < 2)
    def _():
        act(wk)

    @pl.when(pl.program_id(0) >= 2)
    def _():
        act(wv)


def project_body(n_in, *refs):
    wk, wv, out = refs[n_in : n_in + 3]
    n, sub, enc = refs[0].shape
    rows = jnp.concatenate([ref[...].reshape(n * sub, enc) for ref in refs[:n_in]], axis=0)

    def act(w):
        res = jnp.dot(rows, w[...], preferred_element_type=F32)
        out[...] = res.astype(BF16).reshape(out.shape)

    with_weight(wk, wv, act)


def project(pieces, wk, wv):
    n_in = len(pieces)
    n, sub, enc = pieces[0].shape
    width = 2 * wk.shape[1]
    step = width // 4
    return pl.pallas_call(
        functools.partial(project_body, n_in),
        out_shape=jax.ShapeDtypeStruct((n_in, n, sub, width), BF16),
        grid=(4,),
        in_specs=[pl.BlockSpec((n, sub, enc), lambda i: (0, 0, 0))] * n_in
        + weight_specs(enc, step),
        out_specs=pl.BlockSpec((n_in, n, sub, step), lambda i: (0, 0, 0, i)),
        compiler_params=params(),
        cost_estimate=cost(
            2 * n_in * n * sub * enc * width, 2 * (n_in * n * sub * (enc + width) + enc * width)
        ),
        name="project",
    )(*pieces, wk, wv)


def attend_body(places, n_kv, n_late, near, *refs):
    kvs, late = refs[:n_kv], refs[n_kv : n_kv + n_late]
    wk, wv, q_ref, g_ref, att_ref, dq_ref = refs[n_kv + n_late : n_kv + n_late + 6]
    *grads, near_out, far_out, own_out, rest_out, late_kv, own_all, core_all = refs[n_kv + n_late + 6 :]
    step = pl.program_id(0)
    width = q_ref.shape[1]
    enc = wk.shape[0]
    scale = 1.0 / math.sqrt(HD)
    heads = width // HD
    group = min(8, heads)
    last = (((1,), (1,)), ((), ()))
    first = (((0,), (0,)), ((), ()))

    def dot(a, b, dims=(((1,), (0,)), ((), ()))):
        return lax.dot_general(a, b, dims, preferred_element_type=F32)

    @pl.when(step == 0)
    def _():
        for i, ref in enumerate(late):
            rows = ref[...].reshape(-1, enc)
            shape = ref.shape[:2] + (width,)
            late_kv[i, :, :, :width] = dot(rows, wk[...]).astype(BF16).reshape(shape)
            late_kv[i, :, :, width:] = dot(rows, wv[...]).astype(BF16).reshape(shape)

    mine = pl.ds(2 * step, 2)

    def rows_of(col):
        cols = pl.ds(col, HD)
        parts = [ref[:, :, :, cols].reshape(-1, HD) for ref in kvs]
        parts.append(late_kv[:, mine, :, cols].reshape(-1, HD))
        return jnp.concatenate(parts, axis=0)

    def put(col, grad):
        cols = pl.ds(col, HD)
        for at, (kind, k, c) in enumerate(places):
            block = grad[at * 2 * TILE : (at + 1) * 2 * TILE].reshape(2, TILE, HD)
            tokens = pl.ds(c * TILE, TILE)
            grads[kind][k, :, tokens, cols] = block
            (own_all, core_all)[kind][k, mine, tokens, cols] = block

    zero = jnp.zeros((SPAN, HD), BF16)
    for h0 in range(0, heads, group):
        hs = range(h0, h0 + group)
        qg, kv = [], []
        for h in hs:
            cols = pl.ds(h * HD, HD)
            top = jnp.concatenate([q_ref[:, cols], zero], axis=1)
            low = jnp.concatenate([zero, g_ref[:, cols]], axis=1)
            qg.append(jnp.concatenate([top, low], axis=0))
            kv.append(jnp.concatenate([rows_of(h * HD), rows_of(width + h * HD)], axis=1))
        both = [dot(a, b, last) for a, b in zip(qg, kv)]
        s = jnp.concatenate([x[:SPAN] for x in both], axis=0) * scale
        dw = jnp.concatenate([x[SPAN:] for x in both], axis=0)
        e = jnp.exp(s - jnp.max(s, axis=1, keepdims=True))
        p = e * (1.0 / jnp.sum(e, axis=1, keepdims=True))
        rs = jnp.sum(dw * p, axis=1, keepdims=True)
        w = p.astype(BF16)
        ds = (p * (dw - rs) * scale).astype(BF16)
        span = [slice(i * SPAN, (i + 1) * SPAN) for i in range(group)]
        dsw = [jnp.concatenate([ds[i], w[i]], axis=0) for i in span]
        out = [dot(a, b).astype(BF16) for a, b in zip(dsw, kv)]
        back = [dot(a, b, first).astype(BF16) for a, b in zip(dsw, qg)]
        for i, h in enumerate(hs):
            dq_ref[:, pl.ds(h * HD, HD)] = out[i][:SPAN, :HD]
            att_ref[:, pl.ds(h * HD, HD)] = out[i][SPAN:, HD:]
            put(h * HD, back[i][:, :HD])
            put(width + h * HD, back[i][:, HD:])

    @pl.when(step == pl.num_programs(0) - 1)
    def _():
        count = own_out.shape[-1]

        def part(ref, cols, out):
            rows = ref[...].reshape(-1, 2 * width)
            res = dot(rows[:, :width], wk[cols, :], last) + dot(rows[:, width:], wv[cols, :], last)
            out[...] = res.reshape(out.shape)

        part(core_all.at[near:], slice(0, count), far_out)
        part(core_all.at[:near], slice(0, count), near_out)
        part(own_all, slice(0, count), own_out)
        part(core_all.at[near:], slice(count, enc), rest_out)


def attend(kvs, late, wk, wv, places, near, share, count, queries, cotangent):
    tokens, width = queries.shape
    n, enc = late[0].shape[0], wk.shape[0]
    sub = share
    half = len(places) // (2 * (share // TILE))
    total = 2 * half
    rows = pl.BlockSpec((SPAN, width), lambda i: (i, 0))
    grads = pl.BlockSpec((half, 2, sub, 2 * width), lambda i: (0, i, 0, 0))

    def kv_block(kv):
        return pl.BlockSpec((kv.shape[0], 2, TILE, 2 * width), lambda i: (0, i, 0, 0))

    def once(shape):
        return pl.BlockSpec(shape, lambda i: (0,) * len(shape), pipeline_mode=pl.Buffered(1))

    def whole(shape):
        return pl.BlockSpec(shape, lambda i: (0,) * len(shape))

    parts = [(near, n, sub, count), (half - near, n, sub, count), (half, n, sub, count)]
    parts.append((half - near, n, sub, enc - count))
    every = (half, n, sub, 2 * width)
    return pl.pallas_call(
        functools.partial(attend_body, places, len(kvs), len(late), near),
        out_shape=[jax.ShapeDtypeStruct((tokens, width), BF16)] * 2
        + [jax.ShapeDtypeStruct(every, BF16)] * 2
        + [jax.ShapeDtypeStruct(part, F32) for part in parts],
        grid=(tokens // SPAN,),
        in_specs=[kv_block(kv) for kv in kvs]
        + [once(x.shape) for x in late]
        + [once(wk.shape), once(wv.shape), rows, rows],
        out_specs=[rows, rows, grads, grads] + [whole(part) for part in parts],
        scratch_shapes=[
            pltpu.VMEM((len(late), n, TILE, 2 * width), BF16),
            pltpu.VMEM(every, BF16),
            pltpu.VMEM(every, BF16),
        ],
        compiler_params=params(VMEM_MORE),
        cost_estimate=cost(
            16 * tokens * width * total * 2 * sub + 4 * n * width * (len(late) * TILE * enc + total * sub * count),
            8 * tokens * width + 8 * total * n * sub * width,
        ),
        name="attend",
    )(*kvs, *late, wk, wv, queries, cotangent)


def encode(x, axes):
    top = jnp.maximum(jnp.max(jnp.abs(x), axis=axes, keepdims=True), 1e-30)
    power = jnp.floor(jnp.log2(top)) + 1.0
    code = jnp.clip(jnp.round(x * jnp.exp2(15.0 - power)), -32767.0, 32767.0)
    return code.astype(jnp.int32).astype(jnp.int16), power


def grads_body(first, core_ref, own_ref, wk, wv, near_out, own_out, part, sem):
    i = pl.program_id(0)
    n_x = own_out.shape[0]
    width, count = wk.shape[1], part.shape[-1]
    last = (((1,), (1,)), ((), ()))

    def act(ref):
        rows = ref[...].reshape(-1, 2 * width)
        res = lax.dot_general(
            rows[:, :width], wk[first : first + count, :], last, preferred_element_type=F32
        )
        res += lax.dot_general(
            rows[:, width:], wv[first : first + count, :], last, preferred_element_type=F32
        )
        part[i] = res.reshape(part.shape[1:])

    @pl.when(i == n_x)
    def _():
        act(core_ref)

    @pl.when(i < n_x)
    def _():
        act(own_ref)

    outs = [own_out.at[k] for k in range(n_x)] + [near_out.at[0]]
    copies = [pltpu.make_async_copy(part.at[k], out, sem.at[k]) for k, out in enumerate(outs)]
    for k, copy in enumerate(copies):

        @pl.when(i == k)
        def _():
            copy.start()

    @pl.when(i == pl.num_programs(0) - 1)
    def _():
        for copy in copies:
            copy.wait()


def grads_of(d_core, d_own, wk, wv, cols):
    n_x, n, sub, width = d_own.shape
    first, count = cols
    rows = n_x * n * sub
    return pl.pallas_call(
        functools.partial(grads_body, first),
        out_shape=[
            jax.ShapeDtypeStruct((1, n, sub, count), F32),
            jax.ShapeDtypeStruct((n_x, n, sub, count), F32),
        ],
        grid=(n_x + 1,),
        in_specs=[
            pl.BlockSpec((1, n, sub, width), lambda i: (0, 0, 0, 0)),
            pl.BlockSpec((1, n, sub, width), lambda i: (jnp.minimum(i, n_x - 1), 0, 0, 0)),
            pl.BlockSpec(wk.shape, lambda i: (0, 0)),
            pl.BlockSpec(wv.shape, lambda i: (0, 0)),
        ],
        out_specs=[ANY] * 2,
        scratch_shapes=[
            pltpu.VMEM((n_x + 1, n, sub, count), F32),
            pltpu.SemaphoreType.DMA((n_x + 1,)),
        ],
        compiler_params=params(),
        cost_estimate=cost(4 * rows * count * width, 2 * (count + 2 * rows) * width + 8 * rows * count),
        name="grads",
    )(d_core, d_own, wk, wv)


def far_codes_body(cuts, mine, got, *codes):
    far, n, sub, count = got.shape
    row = lax.broadcasted_iota(jnp.int32, (sub, LANES), 0)
    for k in range(far):
        code, power = encode(mine[k] + got[k], (1, 2))
        e = 0
        for cut, out in zip(cuts, codes[k * len(cuts) :]):
            for at in range(cut):
                out[at * n : (at + 1) * n] = code[:, :, e * LANES : (e + 1) * LANES]
                e += 1
        note = jnp.zeros((sub, LANES), F32)
        for r in range(n):
            note = jnp.where(row == r, power[r], note)
        codes[k * len(cuts)][cuts[0] * n] = note.astype(jnp.int32).astype(jnp.int16)


def far_codes(own, got, cuts):
    far, n, sub, count = got.shape
    shapes = [(cut * n + (q == 0), sub, LANES) for q, cut in enumerate(cuts)] * far

    def whole(shape):
        return pl.BlockSpec(shape, lambda i: (0,) * len(shape))

    mine = pl.BlockSpec(tuple(pl.Element(size) for size in got.shape), lambda i: (1, 0, 0, 0))
    out = pl.pallas_call(
        functools.partial(far_codes_body, cuts),
        out_shape=[jax.ShapeDtypeStruct(shape, jnp.int16) for shape in shapes],
        grid=(1,),
        in_specs=[mine, whole(got.shape)],
        out_specs=[whole(shape) for shape in shapes],
        compiler_params=params(),
        cost_estimate=cost(8 * got.size, 10 * got.size),
        name="far_codes",
    )(own, got)
    return [out[k * len(cuts) : (k + 1) * len(cuts)] for k in range(far)]


def send_body(n_dp, cuts, request, own, got, *rest):
    codes, outs, (stage, powers) = rest[: -n_dp - 2], rest[-n_dp - 2 : -2], rest[-2:]
    _, n, sub, count = got.shape
    tiles = count // LANES
    cap = request.shape[0] // n_dp
    notes = [code[cuts[0] * n].astype(F32) for code in codes[:: len(cuts)]]
    for r in range(n):
        total = own[0, r] + got[0, r]
        for k, note in enumerate(notes):
            unit = jnp.exp2(note[r : r + 1] - 15.0)
            blocks = [
                code[at * n + r].astype(F32) * unit
                for cut, code in zip(cuts, codes[k * len(cuts) :])
                for at in range(cut)
            ]
            total = total + jnp.concatenate(blocks, axis=1)
        coded, power = encode(total, (0, 1))
        for e in range(tiles):
            for h in range(sub // TILE):
                block = coded[h * TILE : (h + 1) * TILE, e * LANES : (e + 1) * LANES]
                stage[r, e * (sub // TILE) + h] = block
        powers[r] = jnp.broadcast_to(power, (TILE, LANES))
    row = lax.broadcasted_iota(jnp.int32, (TILE, LANES), 0)
    size = stage.shape[1]
    for d in range(n_dp):
        note = jnp.zeros((TILE, LANES), F32)
        for j in range(cap):
            r = request[d * cap + j]

            @pl.when(r >= 0)
            def _():
                outs[d][pl.ds(j * size, size)] = stage[r]

            note = jnp.where(row == j, powers[jnp.maximum(r, 0)], note)
        outs[d][cap * size] = note.astype(jnp.int32).astype(jnp.int16)


def send_codes(request, own, got, codes, cuts, n_dp):
    _, n, sub, count = got.shape
    block = pl.BlockSpec(got.shape, lambda i: (0, 0, 0, 0))
    size = count // LANES * (sub // TILE)
    cap = request.shape[0] // n_dp
    shape = (cap * size + 1, TILE, LANES)
    codes = [x for piece in codes for x in piece]
    return pl.pallas_call(
        functools.partial(send_body, n_dp, cuts),
        out_shape=[jax.ShapeDtypeStruct(shape, jnp.int16)] * n_dp,
        grid=(1,),
        in_specs=[SMEM, block, block] + [VMEM] * len(codes),
        out_specs=[VMEM] * n_dp,
        scratch_shapes=[
            pltpu.VMEM((n, size, TILE, LANES), jnp.int16),
            pltpu.VMEM((n, TILE, LANES), F32),
        ],
        compiler_params=params(),
        cost_estimate=cost(10 * got.size, 6 * got.size + 2 * n_dp * math.prod(shape)),
        name="send_codes",
    )(request, own, got, *codes)


def gather_body(n_dp, first, me, asked, *refs):
    arrived = refs[:n_dp]
    out, total, sem = refs[-3:]
    tiles, halves = total.shape[2] // LANES, total.shape[1] // TILE
    size = tiles * halves
    cap = asked.shape[1] // n_dp
    total[...] = jnp.zeros_like(total)
    for d in range(n_dp):
        for j in range(cap):
            slab = asked_of(asked, me, d, j)

            @pl.when(slab >= 0)
            def _():
                note = arrived[d][cap * size].astype(F32)
                unit = jnp.exp2(note[j : j + 1] - 15.0)
                for e in range(tiles):
                    for h in range(halves):
                        value = arrived[d][j * size + e * halves + h].astype(F32) * unit
                        total[slab, pl.ds(h * TILE, TILE), pl.ds(e * LANES, LANES)] += value

    copy = pltpu.make_async_copy(total, out.at[:, :, pl.ds(first, total.shape[2])], sem)
    copy.start()
    copy.wait()


def gather_grads(me, asked, arrived, n_slabs, rows, enc, cols, before):
    first, count = cols
    n_dp = asked.shape[0]
    return pl.pallas_call(
        functools.partial(gather_body, n_dp, first),
        out_shape=jax.ShapeDtypeStruct((n_slabs, rows, enc), F32),
        in_specs=[SMEM, SMEM] + [VMEM] * n_dp + [ANY] * (before is not None),
        out_specs=ANY,
        scratch_shapes=[pltpu.VMEM((n_slabs, rows, count), F32), pltpu.SemaphoreType.DMA],
        input_output_aliases={} if before is None else {2 + n_dp: 0},
        compiler_params=params(),
        cost_estimate=cost(0, 8 * n_slabs * rows * count),
        name="gather_grads",
    )(me, asked, *arrived, *([] if before is None else [before]))


def on_device(queries, cotangent, table, key_weight, value_weight, owners, slots):
    n_dp = lax.axis_size("dp")
    n_tp = lax.axis_size("tensor")
    n_x = n_tp // 2
    spans = owners.shape[0]
    n_requests = 2 * spans
    n_slabs, n_tokens, enc = table.shape
    cap = max(2, (4 * spans + n_dp - 1) // n_dp)
    share = n_tokens // n_tp
    n_chunks = share // TILE

    def over_core(x):
        return lax.ppermute(x, "tensor", [(t, t ^ 1) for t in range(n_tp)])

    def over_x(x, d):
        return lax.ppermute(x, "tensor", [(t, (t + 2 * d) % n_tp) for t in range(n_tp)])

    def over_dp(x, d):
        return lax.ppermute(x, "dp", [(i, (i + d) % n_dp) for i in range(n_dp)])

    farthest_first = sorted(range(1, n_dp), key=lambda d: -min(d, n_dp - d))

    def to_all(xs, sign, distances=farthest_first):
        got = {d: over_dp(xs[d], sign * d) for d in distances}
        return got

    me, wanted, request = ask(owners, slots, n_dp, cap)
    asked = lax.psum(wanted, "dp")

    kvs, places = [], []
    early = {}
    sent = pack(me, asked, table, 0, share, cap)
    for c in range(n_chunks):
        rest = [d for d in farthest_first if d not in early]
        arrived = [sent[0]] + [None] * (n_dp - 1)
        for d, x in {**early, **to_all(sent, -1, rest)}.items():
            arrived[d] = x
        if c < n_chunks - 1:
            sent = pack(me, asked, table, c + 1, share, cap)
            early = to_all(sent, -1, farthest_first[:1])
            early, arrived = lax.optimization_barrier((early, arrived))
        if kvs:
            arrived, kvs = lax.optimization_barrier((arrived, kvs))
        mine = compact(request, arrived, n_requests)
        near = [mine, over_core(mine)]
        far = [over_x(mine, k) for k in range(1, n_x)]
        if c < n_chunks - 1:
            early = {**early, **to_all(sent, -1, farthest_first[1:4])}
            early, far = lax.optimization_barrier((early, far))
            far = far + [over_core(x) for x in far]
            kvs = kvs + [project(near + far, key_weight, value_weight)]
        else:
            near = project(near, key_weight, value_weight)
            near, far = lax.optimization_barrier((near, far))
            late = far + [over_core(x) for x in far]
            kvs = kvs + [near]
        places += [(kind, 0, c) for kind in range(2)]
        places += [(kind, k, c) for kind in range(2) for k in range(1, n_x)]

    split = 3 * LANES
    parts = ((0, split), (split, enc - split))
    attended, d_query, d_own, d_core, near, far, own, far_b = attend(
        kvs, late, key_weight, value_weight, places, 1, share, split, queries, cotangent
    )
    far_got = over_core(far)
    near_got = over_core(near)
    far_got_b = over_core(far_b)
    cuts = (parts[0][1] // LANES,)
    codes = far_codes(own, far_got, cuts)
    near_b, own_b = grads_of(d_core, d_own, key_weight, value_weight, parts[1])

    codes = [[over_x(x, n_x - k) for x in piece] for k, piece in enumerate(codes, 1)]
    codes, near_b = lax.optimization_barrier((codes, near_b))
    near_got_b = over_core(near_b)
    sent = send_codes(request, own, near_got, codes, cuts, n_dp)
    sent, near_got_b = lax.optimization_barrier((sent, near_got_b))
    came = to_all(sent, 1)
    arrived = [sent[0]] + [came[d] for d in range(1, n_dp)]
    d_table = gather_grads(me, asked, arrived, n_slabs, share, enc, parts[0], None)

    cuts = (parts[1][1] // LANES,)
    far_got_b, _ = lax.optimization_barrier((far_got_b, codes))
    codes = far_codes(own_b, far_got_b, cuts)
    codes = [[over_x(x, n_x - k) for x in piece] for k, piece in enumerate(codes, 1)]
    sent = send_codes(request, own_b, near_got_b, codes, cuts, n_dp)
    came = to_all(sent, 1)
    arrived = [sent[0]] + [came[d] for d in range(1, n_dp)]
    d_table = gather_grads(me, asked, arrived, n_slabs, share, enc, parts[1], d_table)
    return (attended, d_query, d_table)


def solution(mesh):
    in_specs = (
        P("dp", "tensor"),
        P("dp", "tensor"),
        P("dp", None, None),
        P(None, "tensor"),
        P(None, "tensor"),
        P("dp", None),
        P("dp", None),
    )
    out_specs = (P("dp", "tensor"), P("dp", "tensor"), P("dp", "tensor", None))
    return jax.shard_map(
        on_device, mesh=mesh, in_specs=in_specs, out_specs=out_specs, check_vma=False
    )
```

```python
import functools
import math

import jax
import jax.numpy as jnp
from jax import lax
from jax.experimental import pallas as pl
from jax.experimental.pallas import tpu as pltpu
from jax.sharding import PartitionSpec as P

HD = 128
SPAN = 64
LANES = 128
TILE = 16
VMEM_LIMIT = 28 * 1024 * 1024
VMEM_MORE = 44 * 1024 * 1024
VMEM_ALL = 60 * 1024 * 1024
F32 = jnp.float32
BF16 = jnp.bfloat16

ANY = pl.BlockSpec(memory_space=pl.ANY)
SMEM = pl.BlockSpec(memory_space=pltpu.SMEM)
VMEM = pl.BlockSpec(memory_space=pltpu.VMEM)


def params(limit=VMEM_LIMIT):
    return pltpu.CompilerParams(vmem_limit_bytes=limit)


def cost(flops, nbytes):
    return pl.CostEstimate(flops=int(flops), bytes_accessed=int(nbytes), transcendentals=0)


def ask_body(cap, owners, slots, me_out, wanted, request, count):
    n_dp = wanted.shape[0]
    me = lax.axis_index("dp")
    me_out[0] = me
    for i in range(n_dp * cap):
        request[i] = -1
        for asker in range(n_dp):
            wanted[asker, i] = 0
    for d in range(n_dp):
        count[d] = 0
    for r in range(owners.size):
        d = owners[r % 2, r // 2] - me
        d = jnp.where(d < 0, d + n_dp, d)
        j = count[d]
        count[d] = j + 1
        wanted[me, d * cap + j] = slots[r % 2, r // 2] + 1
        request[d * cap + j] = r


def ask(owners, slots, n_dp, cap):
    return pl.pallas_call(
        functools.partial(ask_body, cap),
        out_shape=[
            jax.ShapeDtypeStruct((1,), jnp.int32),
            jax.ShapeDtypeStruct((n_dp, n_dp * cap), jnp.int32),
            jax.ShapeDtypeStruct((n_dp * cap,), jnp.int32),
        ],
        in_specs=[SMEM, SMEM],
        out_specs=[SMEM, SMEM, SMEM],
        scratch_shapes=[pltpu.SMEM((n_dp,), jnp.int32)],
        name="ask",
    )(owners.T, slots.T)


def asked_of(asked, me, d, j):
    n_dp = asked.shape[0]
    asker = me[0] - d
    asker = jnp.where(asker < 0, asker + n_dp, asker)
    return asked[asker, d * (asked.shape[1] // n_dp) + j] - 1


def pack_body(n_dp, chunk, share, me, asked, table, *rest):
    outs, sem = rest[:-1], rest[-1]
    cap = outs[0].shape[0]
    row = pl.multiple_of(lax.axis_index("tensor") * share + chunk * TILE, TILE)

    def each(act):
        for d in range(n_dp):
            for j in range(cap):
                slab = asked_of(asked, me, d, j)

                @pl.when(slab >= 0)
                def _():
                    source = table.at[slab, pl.ds(row, TILE)]
                    act(pltpu.make_async_copy(source, outs[d].at[j], sem.at[d * cap + j]))

    each(lambda copy: copy.start())
    each(lambda copy: copy.wait())


def pack(me, asked, table, chunk, share, cap):
    n_dp = asked.shape[0]
    enc = table.shape[2]
    return pl.pallas_call(
        functools.partial(pack_body, n_dp, chunk, share),
        out_shape=[jax.ShapeDtypeStruct((cap, TILE, enc), table.dtype)] * n_dp,
        in_specs=[SMEM, SMEM, ANY],
        out_specs=[VMEM] * n_dp,
        scratch_shapes=[pltpu.SemaphoreType.DMA((n_dp * cap,))],
        compiler_params=params(VMEM_ALL),
        cost_estimate=cost(0, 4 * n_dp * cap * TILE * enc),
        name="pack_rows",
    )(me, asked, table)


def compact_body(n_dp, request, *refs):
    arrived, out, sem = refs[:n_dp], refs[n_dp], refs[n_dp + 1]
    cap = arrived[0].shape[0]

    def each(act):
        for d in range(n_dp):
            for j in range(cap):
                r = request[d * cap + j]

                @pl.when(r >= 0)
                def _():
                    act(pltpu.make_async_copy(arrived[d].at[j], out.at[r], sem.at[d * cap + j]))

    each(lambda copy: copy.start())
    each(lambda copy: copy.wait())


def compact(request, arrived, n):
    shape = (n,) + arrived[0].shape[1:]
    return pl.pallas_call(
        functools.partial(compact_body, len(arrived)),
        out_shape=jax.ShapeDtypeStruct(shape, arrived[0].dtype),
        in_specs=[SMEM] + [ANY] * len(arrived),
        out_specs=VMEM,
        scratch_shapes=[pltpu.SemaphoreType.DMA((request.shape[0],))],
        compiler_params=params(),
        cost_estimate=cost(0, 4 * math.prod(shape)),
        name="compact_rows",
    )(request, *arrived)


def weight_specs(rows, step):
    return [
        pl.BlockSpec((rows, step), lambda i: (0, jnp.minimum(i, 1))),
        pl.BlockSpec((rows, step), lambda i: (0, jnp.maximum(i - 2, 0))),
    ]


def with_weight(wk, wv, act):
    @pl.when(pl.program_id(0) < 2)
    def _():
        act(wk)

    @pl.when(pl.program_id(0) >= 2)
    def _():
        act(wv)


def project_body(n_in, *refs):
    wk, wv, out = refs[n_in : n_in + 3]
    n, sub, enc = refs[0].shape
    rows = jnp.concatenate([ref[...].reshape(n * sub, enc) for ref in refs[:n_in]], axis=0)

    def act(w):
        res = jnp.dot(rows, w[...], preferred_element_type=F32)
        out[...] = res.astype(BF16).reshape(out.shape)

    with_weight(wk, wv, act)


def project(pieces, wk, wv):
    n_in = len(pieces)
    n, sub, enc = pieces[0].shape
    width = 2 * wk.shape[1]
    step = width // 4
    return pl.pallas_call(
        functools.partial(project_body, n_in),
        out_shape=jax.ShapeDtypeStruct((n_in, n, sub, width), BF16),
        grid=(4,),
        in_specs=[pl.BlockSpec((n, sub, enc), lambda i: (0, 0, 0))] * n_in
        + weight_specs(enc, step),
        out_specs=pl.BlockSpec((n_in, n, sub, step), lambda i: (0, 0, 0, i)),
        compiler_params=params(),
        cost_estimate=cost(
            2 * n_in * n * sub * enc * width, 2 * (n_in * n * sub * (enc + width) + enc * width)
        ),
        name="project",
    )(*pieces, wk, wv)


def attend_body(places, n_kv, n_late, near, *refs):
    kvs, late = refs[:n_kv], refs[n_kv : n_kv + n_late]
    wk, wv, q_ref, g_ref, att_ref, dq_ref = refs[n_kv + n_late : n_kv + n_late + 6]
    *grads, near_out, far_out, own_out, rest_out, late_kv, own_all, core_all = refs[n_kv + n_late + 6 :]
    step = pl.program_id(0)
    width = q_ref.shape[1]
    enc = wk.shape[0]
    scale = 1.0 / math.sqrt(HD)
    heads = width // HD
    group = min(8, heads)
    last = (((1,), (1,)), ((), ()))
    first = (((0,), (0,)), ((), ()))

    def dot(a, b, dims=(((1,), (0,)), ((), ()))):
        return lax.dot_general(a, b, dims, preferred_element_type=F32)

    @pl.when(step == 0)
    def _():
        for i, ref in enumerate(late):
            rows = ref[...].reshape(-1, enc)
            shape = ref.shape[:2] + (width,)
            late_kv[i, :, :, :width] = dot(rows, wk[...]).astype(BF16).reshape(shape)
            late_kv[i, :, :, width:] = dot(rows, wv[...]).astype(BF16).reshape(shape)

    mine = pl.ds(2 * step, 2)

    def rows_of(col):
        cols = pl.ds(col, HD)
        parts = [ref[:, :, :, cols].reshape(-1, HD) for ref in kvs]
        parts.append(late_kv[:, mine, :, cols].reshape(-1, HD))
        return jnp.concatenate(parts, axis=0)

    def put(col, grad):
        cols = pl.ds(col, HD)
        for at, (kind, k, c) in enumerate(places):
            block = grad[at * 2 * TILE : (at + 1) * 2 * TILE].reshape(2, TILE, HD)
            tokens = pl.ds(c * TILE, TILE)
            grads[kind][k, :, tokens, cols] = block
            (own_all, core_all)[kind][k, mine, tokens, cols] = block

    zero = jnp.zeros((SPAN, HD), BF16)
    for h0 in range(0, heads, group):
        hs = range(h0, h0 + group)
        qg, kv = [], []
        for h in hs:
            cols = pl.ds(h * HD, HD)
            top = jnp.concatenate([q_ref[:, cols], zero], axis=1)
            low = jnp.concatenate([zero, g_ref[:, cols]], axis=1)
            qg.append(jnp.concatenate([top, low], axis=0))
            kv.append(jnp.concatenate([rows_of(h * HD), rows_of(width + h * HD)], axis=1))
        both = [dot(a, b, last) for a, b in zip(qg, kv)]
        s = jnp.concatenate([x[:SPAN] for x in both], axis=0) * scale
        dw = jnp.concatenate([x[SPAN:] for x in both], axis=0)
        e = jnp.exp(s - jnp.max(s, axis=1, keepdims=True))
        p = e * (1.0 / jnp.sum(e, axis=1, keepdims=True))
        rs = jnp.sum(dw * p, axis=1, keepdims=True)
        w = p.astype(BF16)
        ds = (p * (dw - rs) * scale).astype(BF16)
        span = [slice(i * SPAN, (i + 1) * SPAN) for i in range(group)]
        dsw = [jnp.concatenate([ds[i], w[i]], axis=0) for i in span]
        out = [dot(a, b).astype(BF16) for a, b in zip(dsw, kv)]
        back = [dot(a, b, first).astype(BF16) for a, b in zip(dsw, qg)]
        for i, h in enumerate(hs):
            dq_ref[:, pl.ds(h * HD, HD)] = out[i][:SPAN, :HD]
            att_ref[:, pl.ds(h * HD, HD)] = out[i][SPAN:, HD:]
            put(h * HD, back[i][:, :HD])
            put(width + h * HD, back[i][:, HD:])

    @pl.when(step == pl.num_programs(0) - 1)
    def _():
        count = own_out.shape[-1]

        def part(ref, cols, out):
            rows = ref[...].reshape(-1, 2 * width)
            res = dot(rows[:, :width], wk[cols, :], last) + dot(rows[:, width:], wv[cols, :], last)
            out[...] = res.reshape(out.shape)

        part(core_all.at[near:], slice(0, count), far_out)
        part(core_all.at[:near], slice(0, count), near_out)
        part(own_all, slice(0, count), own_out)
        part(core_all.at[near:], slice(count, enc), rest_out)


def attend(kvs, late, wk, wv, places, near, share, count, queries, cotangent):
    tokens, width = queries.shape
    n, enc = late[0].shape[0], wk.shape[0]
    sub = share
    half = len(places) // (2 * (share // TILE))
    total = 2 * half
    rows = pl.BlockSpec((SPAN, width), lambda i: (i, 0))
    grads = pl.BlockSpec((half, 2, sub, 2 * width), lambda i: (0, i, 0, 0))

    def kv_block(kv):
        return pl.BlockSpec((kv.shape[0], 2, TILE, 2 * width), lambda i: (0, i, 0, 0))

    def once(shape):
        return pl.BlockSpec(shape, lambda i: (0,) * len(shape), pipeline_mode=pl.Buffered(1))

    def whole(shape):
        return pl.BlockSpec(shape, lambda i: (0,) * len(shape))

    parts = [(near, n, sub, count), (half - near, n, sub, count), (half, n, sub, count)]
    parts.append((half - near, n, sub, enc - count))
    every = (half, n, sub, 2 * width)
    return pl.pallas_call(
        functools.partial(attend_body, places, len(kvs), len(late), near),
        out_shape=[jax.ShapeDtypeStruct((tokens, width), BF16)] * 2
        + [jax.ShapeDtypeStruct(every, BF16)] * 2
        + [jax.ShapeDtypeStruct(part, F32) for part in parts],
        grid=(tokens // SPAN,),
        in_specs=[kv_block(kv) for kv in kvs]
        + [once(x.shape) for x in late]
        + [once(wk.shape), once(wv.shape), rows, rows],
        out_specs=[rows, rows, grads, grads] + [whole(part) for part in parts],
        scratch_shapes=[
            pltpu.VMEM((len(late), n, TILE, 2 * width), BF16),
            pltpu.VMEM(every, BF16),
            pltpu.VMEM(every, BF16),
        ],
        compiler_params=params(VMEM_MORE),
        cost_estimate=cost(
            16 * tokens * width * total * 2 * sub + 4 * n * width * (len(late) * TILE * enc + total * sub * count),
            8 * tokens * width + 8 * total * n * sub * width,
        ),
        name="attend",
    )(*kvs, *late, wk, wv, queries, cotangent)


def encode(x, axes):
    top = jnp.maximum(jnp.max(jnp.abs(x), axis=axes, keepdims=True), 1e-30)
    power = jnp.floor(jnp.log2(top)) + 1.0
    code = jnp.clip(jnp.round(x * jnp.exp2(15.0 - power)), -32767.0, 32767.0)
    return code.astype(jnp.int32).astype(jnp.int16), power


def grads_body(first, core_ref, own_ref, wk, wv, near_out, own_out, part, sem):
    i = pl.program_id(0)
    n_x = own_out.shape[0]
    width, count = wk.shape[1], part.shape[-1]
    last = (((1,), (1,)), ((), ()))

    def act(ref):
        rows = ref[...].reshape(-1, 2 * width)
        res = lax.dot_general(
            rows[:, :width], wk[first : first + count, :], last, preferred_element_type=F32
        )
        res += lax.dot_general(
            rows[:, width:], wv[first : first + count, :], last, preferred_element_type=F32
        )
        part[i] = res.reshape(part.shape[1:])

    @pl.when(i == n_x)
    def _():
        act(core_ref)

    @pl.when(i < n_x)
    def _():
        act(own_ref)

    outs = [own_out.at[k] for k in range(n_x)] + [near_out.at[0]]
    copies = [pltpu.make_async_copy(part.at[k], out, sem.at[k]) for k, out in enumerate(outs)]
    for k, copy in enumerate(copies):

        @pl.when(i == k)
        def _():
            copy.start()

    @pl.when(i == pl.num_programs(0) - 1)
    def _():
        for copy in copies:
            copy.wait()


def grads_of(d_core, d_own, wk, wv, cols):
    n_x, n, sub, width = d_own.shape
    first, count = cols
    rows = n_x * n * sub
    return pl.pallas_call(
        functools.partial(grads_body, first),
        out_shape=[
            jax.ShapeDtypeStruct((1, n, sub, count), F32),
            jax.ShapeDtypeStruct((n_x, n, sub, count), F32),
        ],
        grid=(n_x + 1,),
        in_specs=[
            pl.BlockSpec((1, n, sub, width), lambda i: (0, 0, 0, 0)),
            pl.BlockSpec((1, n, sub, width), lambda i: (jnp.minimum(i, n_x - 1), 0, 0, 0)),
            pl.BlockSpec(wk.shape, lambda i: (0, 0)),
            pl.BlockSpec(wv.shape, lambda i: (0, 0)),
        ],
        out_specs=[ANY] * 2,
        scratch_shapes=[
            pltpu.VMEM((n_x + 1, n, sub, count), F32),
            pltpu.SemaphoreType.DMA((n_x + 1,)),
        ],
        compiler_params=params(),
        cost_estimate=cost(4 * rows * count * width, 2 * (count + 2 * rows) * width + 8 * rows * count),
        name="grads",
    )(d_core, d_own, wk, wv)


def far_codes_body(cuts, mine, got, *codes):
    far, n, sub, count = got.shape
    row = lax.broadcasted_iota(jnp.int32, (sub, LANES), 0)
    for k in range(far):
        code, power = encode(mine[k] + got[k], (1, 2))
        e = 0
        for cut, out in zip(cuts, codes[k * len(cuts) :]):
            for at in range(cut):
                out[at * n : (at + 1) * n] = code[:, :, e * LANES : (e + 1) * LANES]
                e += 1
        note = jnp.zeros((sub, LANES), F32)
        for r in range(n):
            note = jnp.where(row == r, power[r], note)
        codes[k * len(cuts)][cuts[0] * n] = note.astype(jnp.int32).astype(jnp.int16)


def far_codes(own, got, cuts):
    far, n, sub, count = got.shape
    shapes = [(cut * n + (q == 0), sub, LANES) for q, cut in enumerate(cuts)] * far

    def whole(shape):
        return pl.BlockSpec(shape, lambda i: (0,) * len(shape))

    mine = pl.BlockSpec(tuple(pl.Element(size) for size in got.shape), lambda i: (1, 0, 0, 0))
    out = pl.pallas_call(
        functools.partial(far_codes_body, cuts),
        out_shape=[jax.ShapeDtypeStruct(shape, jnp.int16) for shape in shapes],
        grid=(1,),
        in_specs=[mine, whole(got.shape)],
        out_specs=[whole(shape) for shape in shapes],
        compiler_params=params(),
        cost_estimate=cost(8 * got.size, 10 * got.size),
        name="far_codes",
    )(own, got)
    return [out[k * len(cuts) : (k + 1) * len(cuts)] for k in range(far)]


def send_body(n_dp, cuts, request, own, got, *rest):
    codes, outs, (stage, powers) = rest[: -n_dp - 2], rest[-n_dp - 2 : -2], rest[-2:]
    _, n, sub, count = got.shape
    tiles = count // LANES
    cap = request.shape[0] // n_dp
    notes = [code[cuts[0] * n].astype(F32) for code in codes[:: len(cuts)]]
    for r in range(n):
        total = own[0, r] + got[0, r]
        for k, note in enumerate(notes):
            unit = jnp.exp2(note[r : r + 1] - 15.0)
            blocks = [
                code[at * n + r].astype(F32) * unit
                for cut, code in zip(cuts, codes[k * len(cuts) :])
                for at in range(cut)
            ]
            total = total + jnp.concatenate(blocks, axis=1)
        coded, power = encode(total, (0, 1))
        for e in range(tiles):
            for h in range(sub // TILE):
                block = coded[h * TILE : (h + 1) * TILE, e * LANES : (e + 1) * LANES]
                stage[r, e * (sub // TILE) + h] = block
        powers[r] = jnp.broadcast_to(power, (TILE, LANES))
    row = lax.broadcasted_iota(jnp.int32, (TILE, LANES), 0)
    size = stage.shape[1]
    for d in range(n_dp):
        note = jnp.zeros((TILE, LANES), F32)
        for j in range(cap):
            r = request[d * cap + j]

            @pl.when(r >= 0)
            def _():
                outs[d][pl.ds(j * size, size)] = stage[r]

            note = jnp.where(row == j, powers[jnp.maximum(r, 0)], note)
        outs[d][cap * size] = note.astype(jnp.int32).astype(jnp.int16)


def send_codes(request, own, got, codes, cuts, n_dp):
    _, n, sub, count = got.shape
    block = pl.BlockSpec(got.shape, lambda i: (0, 0, 0, 0))
    size = count // LANES * (sub // TILE)
    cap = request.shape[0] // n_dp
    shape = (cap * size + 1, TILE, LANES)
    codes = [x for piece in codes for x in piece]
    return pl.pallas_call(
        functools.partial(send_body, n_dp, cuts),
        out_shape=[jax.ShapeDtypeStruct(shape, jnp.int16)] * n_dp,
        grid=(1,),
        in_specs=[SMEM, block, block] + [VMEM] * len(codes),
        out_specs=[VMEM] * n_dp,
        scratch_shapes=[
            pltpu.VMEM((n, size, TILE, LANES), jnp.int16),
            pltpu.VMEM((n, TILE, LANES), F32),
        ],
        compiler_params=params(),
        cost_estimate=cost(10 * got.size, 6 * got.size + 2 * n_dp * math.prod(shape)),
        name="send_codes",
    )(request, own, got, *codes)


def gather_body(n_dp, first, me, asked, *refs):
    arrived = refs[:n_dp]
    out, total, sem = refs[-3:]
    tiles, halves = total.shape[2] // LANES, total.shape[1] // TILE
    size = tiles * halves
    cap = asked.shape[1] // n_dp
    total[...] = jnp.zeros_like(total)
    for d in range(n_dp):
        for j in range(cap):
            slab = asked_of(asked, me, d, j)

            @pl.when(slab >= 0)
            def _():
                note = arrived[d][cap * size].astype(F32)
                unit = jnp.exp2(note[j : j + 1] - 15.0)
                for e in range(tiles):
                    for h in range(halves):
                        value = arrived[d][j * size + e * halves + h].astype(F32) * unit
                        total[slab, pl.ds(h * TILE, TILE), pl.ds(e * LANES, LANES)] += value

    copy = pltpu.make_async_copy(total, out.at[:, :, pl.ds(first, total.shape[2])], sem)
    copy.start()
    copy.wait()


def gather_grads(me, asked, arrived, n_slabs, rows, enc, cols, before):
    first, count = cols
    n_dp = asked.shape[0]
    return pl.pallas_call(
        functools.partial(gather_body, n_dp, first),
        out_shape=jax.ShapeDtypeStruct((n_slabs, rows, enc), F32),
        in_specs=[SMEM, SMEM] + [VMEM] * n_dp + [ANY] * (before is not None),
        out_specs=ANY,
        scratch_shapes=[pltpu.VMEM((n_slabs, rows, count), F32), pltpu.SemaphoreType.DMA],
        input_output_aliases={} if before is None else {2 + n_dp: 0},
        compiler_params=params(),
        cost_estimate=cost(0, 8 * n_slabs * rows * count),
        name="gather_grads",
    )(me, asked, *arrived, *([] if before is None else [before]))


def on_device(queries, cotangent, table, key_weight, value_weight, owners, slots):
    n_dp = lax.axis_size("dp")
    n_tp = lax.axis_size("tensor")
    n_x = n_tp // 2
    spans = owners.shape[0]
    n_requests = 2 * spans
    n_slabs, n_tokens, enc = table.shape
    cap = max(2, (4 * spans + n_dp - 1) // n_dp)
    share = n_tokens // n_tp
    n_chunks = share // TILE

    def over_core(x):
        return lax.ppermute(x, "tensor", [(t, t ^ 1) for t in range(n_tp)])

    def over_x(x, d):
        return lax.ppermute(x, "tensor", [(t, (t + 2 * d) % n_tp) for t in range(n_tp)])

    def over_dp(x, d):
        return lax.ppermute(x, "dp", [(i, (i + d) % n_dp) for i in range(n_dp)])

    farthest_first = sorted(range(1, n_dp), key=lambda d: -min(d, n_dp - d))

    def to_all(xs, sign, distances=farthest_first):
        got = {d: over_dp(xs[d], sign * d) for d in distances}
        return got

    me, wanted, request = ask(owners, slots, n_dp, cap)
    asked = lax.psum(wanted, "dp")

    kvs, places = [], []
    early, pieces = {}, []
    sent = pack(me, asked, table, 0, share, cap)
    for c in range(n_chunks):
        rest = [d for d in farthest_first if d not in early]
        arrived = [sent[0]] + [None] * (n_dp - 1)
        for d, x in {**early, **to_all(sent, -1, rest)}.items():
            arrived[d] = x
        if c < n_chunks - 1:
            sent = pack(me, asked, table, c + 1, share, cap)
            early = to_all(sent, -1, farthest_first[:1])
            early, arrived = lax.optimization_barrier((early, arrived))
        mine = compact(request, arrived, n_requests)
        if pieces:
            mine, pieces = lax.optimization_barrier((mine, pieces))
            kvs = [project(pieces, key_weight, value_weight)]
        far = [over_x(mine, k) for k in range(1, n_x)]
        if c < n_chunks - 1:
            early = {**early, **to_all(sent, -1, farthest_first[1:5])}
            early, far, mine = lax.optimization_barrier((early, far, mine))
            pieces = [mine, over_core(mine)] + far + [over_core(x) for x in far]
        else:
            near = project([mine, over_core(mine)], key_weight, value_weight)
            kvs, near, far = lax.optimization_barrier((kvs, near, far))
            late = far + [over_core(x) for x in far]
            kvs = kvs + [near]
        places += [(kind, 0, c) for kind in range(2)]
        places += [(kind, k, c) for kind in range(2) for k in range(1, n_x)]

    split = 2 * LANES
    parts = ((0, split), (split, enc - split))
    attended, d_query, d_own, d_core, near, far, own, far_b = attend(
        kvs, late, key_weight, value_weight, places, 1, share, split, queries, cotangent
    )
    far_got = over_core(far)
    near_got = over_core(near)
    far_got_b = over_core(far_b)
    cuts = (parts[0][1] // LANES,)
    codes = far_codes(own, far_got, cuts)
    near_b, own_b = grads_of(d_core, d_own, key_weight, value_weight, parts[1])

    codes = [[over_x(x, n_x - k) for x in piece] for k, piece in enumerate(codes, 1)]
    codes, near_b = lax.optimization_barrier((codes, near_b))
    near_got_b = over_core(near_b)
    sent = send_codes(request, own, near_got, codes, cuts, n_dp)
    sent, near_got_b = lax.optimization_barrier((sent, near_got_b))
    came = to_all(sent, 1)

    cuts = (parts[1][1] // LANES,)
    far_got_b, _ = lax.optimization_barrier((far_got_b, codes))
    codes = far_codes(own_b, far_got_b, cuts)
    codes = [[over_x(x, n_x - k) for x in piece] for k, piece in enumerate(codes, 1)]
    lead = {d: came[d] for d in range(1, n_dp - 1)}
    codes, lead = lax.optimization_barrier((codes, lead))
    came.update(lead)
    arrived = [sent[0]] + [came[d] for d in range(1, n_dp)]
    d_table = gather_grads(me, asked, arrived, n_slabs, share, enc, parts[0], None)
    sent = send_codes(request, own_b, near_got_b, codes, cuts, n_dp)
    came = to_all(sent, 1)
    arrived = [sent[0]] + [came[d] for d in range(1, n_dp)]
    d_table = gather_grads(me, asked, arrived, n_slabs, share, enc, parts[1], d_table)
    return (attended, d_query, d_table)


def solution(mesh):
    in_specs = (
        P("dp", "tensor"),
        P("dp", "tensor"),
        P("dp", None, None),
        P(None, "tensor"),
        P(None, "tensor"),
        P("dp", None),
        P("dp", None),
    )
    out_specs = (P("dp", "tensor"), P("dp", "tensor"), P("dp", "tensor", None))
    return jax.shard_map(
        on_device, mesh=mesh, in_specs=in_specs, out_specs=out_specs, check_vma=False
    )
```

```python
import functools
import math

import jax
import jax.numpy as jnp
from jax import lax
from jax.experimental import pallas as pl
from jax.experimental.pallas import tpu as pltpu
from jax.sharding import PartitionSpec as P

HD = 128
SPAN = 64
LANES = 128
TILE = 16
VMEM_LIMIT = 28 * 1024 * 1024
VMEM_MORE = 48 * 1024 * 1024
VMEM_ALL = 60 * 1024 * 1024
F32 = jnp.float32
BF16 = jnp.bfloat16

ANY = pl.BlockSpec(memory_space=pl.ANY)
SMEM = pl.BlockSpec(memory_space=pltpu.SMEM)
VMEM = pl.BlockSpec(memory_space=pltpu.VMEM)


def params(limit=VMEM_LIMIT):
    return pltpu.CompilerParams(vmem_limit_bytes=limit)


def cost(flops, nbytes):
    return pl.CostEstimate(flops=int(flops), bytes_accessed=int(nbytes), transcendentals=0)


def ask_body(cap, owners, slots, me_out, wanted, request, count):
    n_dp = wanted.shape[0]
    me = lax.axis_index("dp")
    me_out[0] = me
    for i in range(n_dp * cap):
        request[i] = -1
        for asker in range(n_dp):
            wanted[asker, i] = 0
    for d in range(n_dp):
        count[d] = 0
    for r in range(owners.size):
        d = owners[r % 2, r // 2] - me
        d = jnp.where(d < 0, d + n_dp, d)
        j = count[d]
        count[d] = j + 1
        wanted[me, d * cap + j] = slots[r % 2, r // 2] + 1
        request[d * cap + j] = r


def ask(owners, slots, n_dp, cap):
    return pl.pallas_call(
        functools.partial(ask_body, cap),
        out_shape=[
            jax.ShapeDtypeStruct((1,), jnp.int32),
            jax.ShapeDtypeStruct((n_dp, n_dp * cap), jnp.int32),
            jax.ShapeDtypeStruct((n_dp * cap,), jnp.int32),
        ],
        in_specs=[SMEM, SMEM],
        out_specs=[SMEM, SMEM, SMEM],
        scratch_shapes=[pltpu.SMEM((n_dp,), jnp.int32)],
        name="ask",
    )(owners.T, slots.T)


def asked_of(asked, me, d, j):
    n_dp = asked.shape[0]
    asker = me[0] - d
    asker = jnp.where(asker < 0, asker + n_dp, asker)
    return asked[asker, d * (asked.shape[1] // n_dp) + j] - 1


def pack_body(n_dp, chunk, share, me, asked, table, *rest):
    outs, sem = rest[:-1], rest[-1]
    cap = outs[0].shape[0]
    row = pl.multiple_of(lax.axis_index("tensor") * share + chunk * TILE, TILE)

    def each(act):
        for d in range(n_dp):
            for j in range(cap):
                slab = asked_of(asked, me, d, j)

                @pl.when(slab >= 0)
                def _():
                    source = table.at[slab, pl.ds(row, TILE)]
                    act(pltpu.make_async_copy(source, outs[d].at[j], sem.at[d * cap + j]))

    each(lambda copy: copy.start())
    each(lambda copy: copy.wait())


def pack(me, asked, table, chunk, share, cap):
    n_dp = asked.shape[0]
    enc = table.shape[2]
    return pl.pallas_call(
        functools.partial(pack_body, n_dp, chunk, share),
        out_shape=[jax.ShapeDtypeStruct((cap, TILE, enc), table.dtype)] * n_dp,
        in_specs=[SMEM, SMEM, ANY],
        out_specs=[VMEM] * n_dp,
        scratch_shapes=[pltpu.SemaphoreType.DMA((n_dp * cap,))],
        compiler_params=params(VMEM_ALL),
        cost_estimate=cost(0, 4 * n_dp * cap * TILE * enc),
        name="pack_rows",
    )(me, asked, table)


def compact_body(n_dp, request, *refs):
    arrived, out, sem = refs[:n_dp], refs[n_dp], refs[n_dp + 1]
    cap = arrived[0].shape[0]

    def each(act):
        for d in range(n_dp):
            for j in range(cap):
                r = request[d * cap + j]

                @pl.when(r >= 0)
                def _():
                    act(pltpu.make_async_copy(arrived[d].at[j], out.at[r], sem.at[d * cap + j]))

    each(lambda copy: copy.start())
    each(lambda copy: copy.wait())


def compact(request, arrived, n):
    shape = (n,) + arrived[0].shape[1:]
    return pl.pallas_call(
        functools.partial(compact_body, len(arrived)),
        out_shape=jax.ShapeDtypeStruct(shape, arrived[0].dtype),
        in_specs=[SMEM] + [ANY] * len(arrived),
        out_specs=VMEM,
        scratch_shapes=[pltpu.SemaphoreType.DMA((request.shape[0],))],
        compiler_params=params(),
        cost_estimate=cost(0, 4 * math.prod(shape)),
        name="compact_rows",
    )(request, *arrived)


def weight_specs(rows, step):
    return [
        pl.BlockSpec((rows, step), lambda i: (0, jnp.minimum(i, 1))),
        pl.BlockSpec((rows, step), lambda i: (0, jnp.maximum(i - 2, 0))),
    ]


def with_weight(wk, wv, act):
    @pl.when(pl.program_id(0) < 2)
    def _():
        act(wk)

    @pl.when(pl.program_id(0) >= 2)
    def _():
        act(wv)


def project_body(n_in, *refs):
    wk, wv, out = refs[n_in : n_in + 3]
    n, sub, enc = refs[0].shape
    rows = jnp.concatenate([ref[...].reshape(n * sub, enc) for ref in refs[:n_in]], axis=0)

    def act(w):
        res = jnp.dot(rows, w[...], preferred_element_type=F32)
        out[...] = res.astype(BF16).reshape(out.shape)

    with_weight(wk, wv, act)


def project(pieces, wk, wv):
    n_in = len(pieces)
    n, sub, enc = pieces[0].shape
    width = 2 * wk.shape[1]
    step = width // 4
    return pl.pallas_call(
        functools.partial(project_body, n_in),
        out_shape=jax.ShapeDtypeStruct((n_in, n, sub, width), BF16),
        grid=(4,),
        in_specs=[pl.BlockSpec((n, sub, enc), lambda i: (0, 0, 0))] * n_in
        + weight_specs(enc, step),
        out_specs=pl.BlockSpec((n_in, n, sub, step), lambda i: (0, 0, 0, i)),
        compiler_params=params(),
        cost_estimate=cost(
            2 * n_in * n * sub * enc * width, 2 * (n_in * n * sub * (enc + width) + enc * width)
        ),
        name="project",
    )(*pieces, wk, wv)


def attend_body(places, n_kv, n_late, near, *refs):
    kvs, late = refs[:n_kv], refs[n_kv : n_kv + n_late]
    wk, wv, q_ref, g_ref, att_ref, dq_ref = refs[n_kv + n_late : n_kv + n_late + 6]
    *grads, near_out, far_out, own_out, rest_out, late_kv, own_all, core_all = refs[n_kv + n_late + 6 :]
    step = pl.program_id(0)
    width = q_ref.shape[1]
    enc = wk.shape[0]
    scale = 1.0 / math.sqrt(HD)
    heads = width // HD
    group = min(8, heads)
    per = q_ref.shape[0] // SPAN
    last = (((1,), (1,)), ((), ()))
    first = (((0,), (0,)), ((), ()))

    def dot(a, b, dims=(((1,), (0,)), ((), ()))):
        return lax.dot_general(a, b, dims, preferred_element_type=F32)

    @pl.when(step == 0)
    def _():
        for i, ref in enumerate(late):
            rows = ref[...].reshape(-1, enc)
            shape = ref.shape[:2] + (width,)
            late_kv[i, :, :, :width] = dot(rows, wk[...]).astype(BF16).reshape(shape)
            late_kv[i, :, :, width:] = dot(rows, wv[...]).astype(BF16).reshape(shape)

    def rows_of(u, col):
        cols = pl.ds(col, HD)
        parts = [ref[:, 2 * u : 2 * u + 2, :, cols].reshape(-1, HD) for ref in kvs]
        parts.append(late_kv[:, pl.ds(2 * (per * step + u), 2), :, cols].reshape(-1, HD))
        return jnp.concatenate(parts, axis=0)

    def put(u, col, grad):
        cols = pl.ds(col, HD)
        for at, (kind, k, c) in enumerate(places):
            block = grad[at * 2 * TILE : (at + 1) * 2 * TILE].reshape(2, TILE, HD)
            tokens = pl.ds(c * TILE, TILE)
            if k < grads[kind].shape[0]:
                grads[kind][k, 2 * u : 2 * u + 2, tokens, cols] = block
            (own_all, core_all)[kind][k, pl.ds(2 * (per * step + u), 2), tokens, cols] = block

    zero = jnp.zeros((SPAN, HD), BF16)
    for u, h0 in [(u, h0) for u in range(per) for h0 in range(0, heads, group)]:
        hs = range(h0, h0 + group)
        at = slice(u * SPAN, (u + 1) * SPAN)
        qg, kv = [], []
        for h in hs:
            cols = pl.ds(h * HD, HD)
            top = jnp.concatenate([q_ref[at, cols], zero], axis=1)
            low = jnp.concatenate([zero, g_ref[at, cols]], axis=1)
            qg.append(jnp.concatenate([top, low], axis=0))
            kv.append(jnp.concatenate([rows_of(u, h * HD), rows_of(u, width + h * HD)], axis=1))
        both = [dot(a, b, last) for a, b in zip(qg, kv)]
        s = jnp.concatenate([x[:SPAN] for x in both], axis=0) * scale
        dw = jnp.concatenate([x[SPAN:] for x in both], axis=0)
        e = jnp.exp(s - jnp.max(s, axis=1, keepdims=True))
        p = e * (1.0 / jnp.sum(e, axis=1, keepdims=True))
        rs = jnp.sum(dw * p, axis=1, keepdims=True)
        w = p.astype(BF16)
        ds = (p * (dw - rs) * scale).astype(BF16)
        span = [slice(i * SPAN, (i + 1) * SPAN) for i in range(group)]
        dsw = [jnp.concatenate([ds[i], w[i]], axis=0) for i in span]
        out = [dot(a, b).astype(BF16) for a, b in zip(dsw, kv)]
        back = [dot(a, b, first).astype(BF16) for a, b in zip(dsw, qg)]
        for i, h in enumerate(hs):
            dq_ref[at, pl.ds(h * HD, HD)] = out[i][:SPAN, :HD]
            att_ref[at, pl.ds(h * HD, HD)] = out[i][SPAN:, HD:]
            put(u, h * HD, back[i][:, :HD])
            put(u, width + h * HD, back[i][:, HD:])

    @pl.when(step == pl.num_programs(0) - 1)
    def _():
        count = own_out.shape[-1]

        def part(ref, cols, out):
            rows = ref[...].reshape(-1, 2 * width)
            res = dot(rows[:, :width], wk[cols, :], last) + dot(rows[:, width:], wv[cols, :], last)
            out[...] = res.reshape(out.shape)

        part(core_all.at[near:], slice(0, count), far_out)
        part(core_all.at[:near], slice(0, count), near_out)
        part(own_all, slice(0, count), own_out)
        part(core_all.at[near:], slice(count, enc), rest_out)


def attend(kvs, late, wk, wv, places, near, share, count, queries, cotangent):
    tokens, width = queries.shape
    n, enc = late[0].shape[0], wk.shape[0]
    sub = share
    half = len(places) // (2 * (share // TILE))
    total = 2 * half
    per = 2 if tokens % (2 * SPAN) == 0 else 1
    rows = pl.BlockSpec((per * SPAN, width), lambda i: (i, 0))

    def grads(pieces):
        return pl.BlockSpec((pieces, 2 * per, sub, 2 * width), lambda i: (0, i, 0, 0))

    def kv_block(kv):
        return pl.BlockSpec((kv.shape[0], 2 * per, TILE, 2 * width), lambda i: (0, i, 0, 0))

    def once(shape):
        return pl.BlockSpec(shape, lambda i: (0,) * len(shape), pipeline_mode=pl.Buffered(1))

    def whole(shape):
        return pl.BlockSpec(shape, lambda i: (0,) * len(shape))

    parts = [(near, n, sub, count), (half - near, n, sub, count), (half, n, sub, count)]
    parts.append((half - near, n, sub, enc - count))
    every = (half, n, sub, 2 * width)
    return pl.pallas_call(
        functools.partial(attend_body, places, len(kvs), len(late), near),
        out_shape=[jax.ShapeDtypeStruct((tokens, width), BF16)] * 2
        + [jax.ShapeDtypeStruct(every, BF16), jax.ShapeDtypeStruct((near, *every[1:]), BF16)]
        + [jax.ShapeDtypeStruct(part, F32) for part in parts],
        grid=(tokens // (per * SPAN),),
        in_specs=[kv_block(kv) for kv in kvs]
        + [once(x.shape) for x in late]
        + [once(wk.shape), once(wv.shape), rows, rows],
        out_specs=[rows, rows, grads(half), grads(near)] + [whole(part) for part in parts],
        scratch_shapes=[
            pltpu.VMEM((len(late), n, TILE, 2 * width), BF16),
            pltpu.VMEM(every, BF16),
            pltpu.VMEM(every, BF16),
        ],
        compiler_params=params(VMEM_MORE),
        cost_estimate=cost(
            16 * tokens * width * total * 2 * sub + 4 * n * width * (len(late) * TILE * enc + total * sub * count),
            8 * tokens * width + 8 * total * n * sub * width,
        ),
        name="attend",
    )(*kvs, *late, wk, wv, queries, cotangent)


def encode(x, axes):
    top = jnp.maximum(jnp.max(jnp.abs(x), axis=axes, keepdims=True), 1e-30)
    power = jnp.floor(jnp.log2(top)) + 1.0
    code = jnp.clip(jnp.round(x * jnp.exp2(15.0 - power)), -32767.0, 32767.0)
    return code.astype(jnp.int32).astype(jnp.int16), power


def grads_body(first, core_ref, own_ref, wk, wv, near_out, own_out, part, sem):
    i = pl.program_id(0)
    n_x = own_out.shape[0]
    width, count = wk.shape[1], part.shape[-1]
    last = (((1,), (1,)), ((), ()))

    def act(ref):
        rows = ref[...].reshape(-1, 2 * width)
        res = lax.dot_general(
            rows[:, :width], wk[first : first + count, :], last, preferred_element_type=F32
        )
        res += lax.dot_general(
            rows[:, width:], wv[first : first + count, :], last, preferred_element_type=F32
        )
        part[i] = res.reshape(part.shape[1:])

    @pl.when(i == n_x)
    def _():
        act(core_ref)

    @pl.when(i < n_x)
    def _():
        act(own_ref)

    outs = [own_out.at[k] for k in range(n_x)] + [near_out.at[0]]
    copies = [pltpu.make_async_copy(part.at[k], out, sem.at[k]) for k, out in enumerate(outs)]
    for k, copy in enumerate(copies):

        @pl.when(i == k)
        def _():
            copy.start()

    @pl.when(i == pl.num_programs(0) - 1)
    def _():
        for copy in copies:
            copy.wait()


def grads_of(d_core, d_own, wk, wv, cols):
    n_x, n, sub, width = d_own.shape
    first, count = cols
    rows = n_x * n * sub
    return pl.pallas_call(
        functools.partial(grads_body, first),
        out_shape=[
            jax.ShapeDtypeStruct((1, n, sub, count), F32),
            jax.ShapeDtypeStruct((n_x, n, sub, count), F32),
        ],
        grid=(n_x + 1,),
        in_specs=[
            pl.BlockSpec((1, n, sub, width), lambda i: (0, 0, 0, 0)),
            pl.BlockSpec((1, n, sub, width), lambda i: (jnp.minimum(i, n_x - 1), 0, 0, 0)),
            pl.BlockSpec(wk.shape, lambda i: (0, 0)),
            pl.BlockSpec(wv.shape, lambda i: (0, 0)),
        ],
        out_specs=[ANY] * 2,
        scratch_shapes=[
            pltpu.VMEM((n_x + 1, n, sub, count), F32),
            pltpu.SemaphoreType.DMA((n_x + 1,)),
        ],
        compiler_params=params(),
        cost_estimate=cost(4 * rows * count * width, 2 * (count + 2 * rows) * width + 8 * rows * count),
        name="grads",
    )(d_core, d_own, wk, wv)


def far_codes_body(cuts, mine, got, *codes):
    far, n, sub, count = got.shape
    row = lax.broadcasted_iota(jnp.int32, (sub, LANES), 0)
    for k in range(far):
        code, power = encode(mine[k] + got[k], (1, 2))
        e = 0
        for cut, out in zip(cuts, codes[k * len(cuts) :]):
            for at in range(cut):
                out[at * n : (at + 1) * n] = code[:, :, e * LANES : (e + 1) * LANES]
                e += 1
        note = jnp.zeros((sub, LANES), F32)
        for r in range(n):
            note = jnp.where(row == r, power[r], note)
        codes[k * len(cuts)][cuts[0] * n] = note.astype(jnp.int32).astype(jnp.int16)


def far_codes(own, got, cuts):
    far, n, sub, count = got.shape
    shapes = [(cut * n + (q == 0), sub, LANES) for q, cut in enumerate(cuts)] * far

    def whole(shape):
        return pl.BlockSpec(shape, lambda i: (0,) * len(shape))

    mine = pl.BlockSpec(tuple(pl.Element(size) for size in got.shape), lambda i: (1, 0, 0, 0))
    out = pl.pallas_call(
        functools.partial(far_codes_body, cuts),
        out_shape=[jax.ShapeDtypeStruct(shape, jnp.int16) for shape in shapes],
        grid=(1,),
        in_specs=[mine, whole(got.shape)],
        out_specs=[whole(shape) for shape in shapes],
        compiler_params=params(),
        cost_estimate=cost(8 * got.size, 10 * got.size),
        name="far_codes",
    )(own, got)
    return [out[k * len(cuts) : (k + 1) * len(cuts)] for k in range(far)]


def send_body(n_dp, cuts, request, own, got, *rest):
    codes, outs, (stage, powers) = rest[: -n_dp - 2], rest[-n_dp - 2 : -2], rest[-2:]
    _, n, sub, count = got.shape
    tiles = count // LANES
    cap = request.shape[0] // n_dp
    notes = [code[cuts[0] * n].astype(F32) for code in codes[:: len(cuts)]]
    for r in range(n):
        total = own[0, r] + got[0, r]
        for k, note in enumerate(notes):
            unit = jnp.exp2(note[r : r + 1] - 15.0)
            blocks = [
                code[at * n + r].astype(F32) * unit
                for cut, code in zip(cuts, codes[k * len(cuts) :])
                for at in range(cut)
            ]
            total = total + jnp.concatenate(blocks, axis=1)
        coded, power = encode(total, (0, 1))
        for e in range(tiles):
            for h in range(sub // TILE):
                block = coded[h * TILE : (h + 1) * TILE, e * LANES : (e + 1) * LANES]
                stage[r, e * (sub // TILE) + h] = block
        powers[r] = jnp.broadcast_to(power, (TILE, LANES))
    row = lax.broadcasted_iota(jnp.int32, (TILE, LANES), 0)
    size = stage.shape[1]
    for d in range(n_dp):
        note = jnp.zeros((TILE, LANES), F32)
        for j in range(cap):
            r = request[d * cap + j]

            @pl.when(r >= 0)
            def _():
                outs[d][pl.ds(j * size, size)] = stage[r]

            note = jnp.where(row == j, powers[jnp.maximum(r, 0)], note)
        outs[d][cap * size] = note.astype(jnp.int32).astype(jnp.int16)


def send_codes(request, own, got, codes, cuts, n_dp):
    _, n, sub, count = got.shape
    block = pl.BlockSpec(got.shape, lambda i: (0, 0, 0, 0))
    size = count // LANES * (sub // TILE)
    cap = request.shape[0] // n_dp
    shape = (cap * size + 1, TILE, LANES)
    codes = [x for piece in codes for x in piece]
    return pl.pallas_call(
        functools.partial(send_body, n_dp, cuts),
        out_shape=[jax.ShapeDtypeStruct(shape, jnp.int16)] * n_dp,
        grid=(1,),
        in_specs=[SMEM, block, block] + [VMEM] * len(codes),
        out_specs=[VMEM] * n_dp,
        scratch_shapes=[
            pltpu.VMEM((n, size, TILE, LANES), jnp.int16),
            pltpu.VMEM((n, TILE, LANES), F32),
        ],
        compiler_params=params(),
        cost_estimate=cost(10 * got.size, 6 * got.size + 2 * n_dp * math.prod(shape)),
        name="send_codes",
    )(request, own, got, *codes)


def gather_body(n_dp, first, me, asked, *refs):
    arrived = refs[:n_dp]
    out, total, sem = refs[-3:]
    tiles, halves = total.shape[2] // LANES, total.shape[1] // TILE
    size = tiles * halves
    cap = asked.shape[1] // n_dp
    total[...] = jnp.zeros_like(total)
    for d in range(n_dp):
        for j in range(cap):
            slab = asked_of(asked, me, d, j)

            @pl.when(slab >= 0)
            def _():
                note = arrived[d][cap * size].astype(F32)
                unit = jnp.exp2(note[j : j + 1] - 15.0)
                for e in range(tiles):
                    for h in range(halves):
                        value = arrived[d][j * size + e * halves + h].astype(F32) * unit
                        total[slab, pl.ds(h * TILE, TILE), pl.ds(e * LANES, LANES)] += value

    copy = pltpu.make_async_copy(total, out.at[:, :, pl.ds(first, total.shape[2])], sem)
    copy.start()
    copy.wait()


def gather_grads(me, asked, arrived, n_slabs, rows, enc, cols, before):
    first, count = cols
    n_dp = asked.shape[0]
    return pl.pallas_call(
        functools.partial(gather_body, n_dp, first),
        out_shape=jax.ShapeDtypeStruct((n_slabs, rows, enc), F32),
        in_specs=[SMEM, SMEM] + [VMEM] * n_dp + [ANY] * (before is not None),
        out_specs=ANY,
        scratch_shapes=[pltpu.VMEM((n_slabs, rows, count), F32), pltpu.SemaphoreType.DMA],
        input_output_aliases={} if before is None else {2 + n_dp: 0},
        compiler_params=params(),
        cost_estimate=cost(0, 8 * n_slabs * rows * count),
        name="gather_grads",
    )(me, asked, *arrived, *([] if before is None else [before]))


def on_device(queries, cotangent, table, key_weight, value_weight, owners, slots):
    n_dp = lax.axis_size("dp")
    n_tp = lax.axis_size("tensor")
    n_x = n_tp // 2
    spans = owners.shape[0]
    n_requests = 2 * spans
    n_slabs, n_tokens, enc = table.shape
    cap = max(2, (4 * spans + n_dp - 1) // n_dp)
    share = n_tokens // n_tp
    n_chunks = share // TILE

    def over_core(x):
        return lax.ppermute(x, "tensor", [(t, t ^ 1) for t in range(n_tp)])

    def over_x(x, d):
        return lax.ppermute(x, "tensor", [(t, (t + 2 * d) % n_tp) for t in range(n_tp)])

    def over_dp(x, d):
        return lax.ppermute(x, "dp", [(i, (i + d) % n_dp) for i in range(n_dp)])

    farthest_first = sorted(range(1, n_dp), key=lambda d: -min(d, n_dp - d))

    def to_all(xs, sign, distances=farthest_first):
        got = {d: over_dp(xs[d], sign * d) for d in distances}
        return got

    me, wanted, request = ask(owners, slots, n_dp, cap)
    asked = lax.psum(wanted, "dp")

    kvs, places = [], []
    early = {}
    sent = pack(me, asked, table, 0, share, cap)
    for c in range(n_chunks):
        rest = [d for d in farthest_first if d not in early]
        arrived = [sent[0]] + [None] * (n_dp - 1)
        for d, x in {**early, **to_all(sent, -1, rest)}.items():
            arrived[d] = x
        if c < n_chunks - 1:
            sent = pack(me, asked, table, c + 1, share, cap)
            early = to_all(sent, -1, farthest_first[:1])
            early, arrived = lax.optimization_barrier((early, arrived))
        if kvs:
            arrived, kvs = lax.optimization_barrier((arrived, kvs))
        mine = compact(request, arrived, n_requests)
        near = [mine, over_core(mine)]
        far = [over_x(mine, k) for k in range(1, n_x)]
        if c < n_chunks - 1:
            early = {**early, **to_all(sent, -1, farthest_first[1:4])}
            early, far = lax.optimization_barrier((early, far))
            far = far + [over_core(x) for x in far]
            kvs = kvs + [project(near + far, key_weight, value_weight)]
        else:
            near = project(near, key_weight, value_weight)
            near, far = lax.optimization_barrier((near, far))
            late = far + [over_core(x) for x in far]
            kvs = kvs + [near]
        places += [(kind, 0, c) for kind in range(2)]
        places += [(kind, k, c) for kind in range(2) for k in range(1, n_x)]

    split = 3 * LANES
    parts = ((0, split), (split, enc - split))
    attended, d_query, d_own, d_core, near, far, own, far_b = attend(
        kvs, late, key_weight, value_weight, places, 1, share, split, queries, cotangent
    )
    far_got = over_core(far)
    near_got = over_core(near)
    far_got_b = over_core(far_b)
    cuts = (parts[0][1] // LANES,)
    codes = far_codes(own, far_got, cuts)
    near_b, own_b = grads_of(d_core, d_own, key_weight, value_weight, parts[1])

    codes = [[over_x(x, n_x - k) for x in piece] for k, piece in enumerate(codes, 1)]
    codes, near_b = lax.optimization_barrier((codes, near_b))
    near_got_b = over_core(near_b)
    sent = send_codes(request, own, near_got, codes, cuts, n_dp)
    sent, near_got_b = lax.optimization_barrier((sent, near_got_b))
    came = to_all(sent, 1)
    arrived = [sent[0]] + [came[d] for d in range(1, n_dp)]
    d_table = gather_grads(me, asked, arrived, n_slabs, share, enc, parts[0], None)

    cuts = (parts[1][1] // LANES,)
    far_got_b, _ = lax.optimization_barrier((far_got_b, codes))
    codes = far_codes(own_b, far_got_b, cuts)
    codes = [[over_x(x, n_x - k) for x in piece] for k, piece in enumerate(codes, 1)]
    sent = send_codes(request, own_b, near_got_b, codes, cuts, n_dp)
    came = to_all(sent, 1)
    arrived = [sent[0]] + [came[d] for d in range(1, n_dp)]
    d_table = gather_grads(me, asked, arrived, n_slabs, share, enc, parts[1], d_table)
    return (attended, d_query, d_table)


def solution(mesh):
    in_specs = (
        P("dp", "tensor"),
        P("dp", "tensor"),
        P("dp", None, None),
        P(None, "tensor"),
        P(None, "tensor"),
        P("dp", None),
        P("dp", None),
    )
    out_specs = (P("dp", "tensor"), P("dp", "tensor"), P("dp", "tensor", None))
    return jax.shard_map(
        on_device, mesh=mesh, in_specs=in_specs, out_specs=out_specs, check_vma=False
    )
```

```python
import functools
import math

import jax
import jax.numpy as jnp
from jax import lax
from jax.experimental import pallas as pl
from jax.experimental.pallas import tpu as pltpu
from jax.sharding import PartitionSpec as P

HD = 128
SPAN = 64
LANES = 128
TILE = 16
VMEM_LIMIT = 28 * 1024 * 1024
VMEM_MORE = 44 * 1024 * 1024
VMEM_ALL = 60 * 1024 * 1024
F32 = jnp.float32
BF16 = jnp.bfloat16

ANY = pl.BlockSpec(memory_space=pl.ANY)
SMEM = pl.BlockSpec(memory_space=pltpu.SMEM)
VMEM = pl.BlockSpec(memory_space=pltpu.VMEM)


def params(limit=VMEM_LIMIT):
    return pltpu.CompilerParams(vmem_limit_bytes=limit)


def cost(flops, nbytes):
    return pl.CostEstimate(flops=int(flops), bytes_accessed=int(nbytes), transcendentals=0)


def ask_body(cap, owners, slots, me_out, wanted, request, count):
    n_dp = wanted.shape[0]
    me = lax.axis_index("dp")
    me_out[0] = me
    for i in range(n_dp * cap):
        request[i] = -1
        for asker in range(n_dp):
            wanted[asker, i] = 0
    for d in range(n_dp):
        count[d] = 0
    for r in range(owners.size):
        d = owners[r % 2, r // 2] - me
        d = jnp.where(d < 0, d + n_dp, d)
        j = count[d]
        count[d] = j + 1
        wanted[me, d * cap + j] = slots[r % 2, r // 2] + 1
        request[d * cap + j] = r


def ask(owners, slots, n_dp, cap):
    return pl.pallas_call(
        functools.partial(ask_body, cap),
        out_shape=[
            jax.ShapeDtypeStruct((1,), jnp.int32),
            jax.ShapeDtypeStruct((n_dp, n_dp * cap), jnp.int32),
            jax.ShapeDtypeStruct((n_dp * cap,), jnp.int32),
        ],
        in_specs=[SMEM, SMEM],
        out_specs=[SMEM, SMEM, SMEM],
        scratch_shapes=[pltpu.SMEM((n_dp,), jnp.int32)],
        name="ask",
    )(owners.T, slots.T)


def asked_of(asked, me, d, j):
    n_dp = asked.shape[0]
    asker = me[0] - d
    asker = jnp.where(asker < 0, asker + n_dp, asker)
    return asked[asker, d * (asked.shape[1] // n_dp) + j] - 1


def pack_body(n_dp, chunk, share, me, asked, table, *rest):
    outs, sem = rest[:-1], rest[-1]
    cap = outs[0].shape[0]
    row = pl.multiple_of(lax.axis_index("tensor") * share + chunk * TILE, TILE)

    def each(act):
        for d in range(n_dp):
            for j in range(cap):
                slab = asked_of(asked, me, d, j)

                @pl.when(slab >= 0)
                def _():
                    source = table.at[slab, pl.ds(row, TILE)]
                    act(pltpu.make_async_copy(source, outs[d].at[j], sem.at[d * cap + j]))

    each(lambda copy: copy.start())
    each(lambda copy: copy.wait())


def pack(me, asked, table, chunk, share, cap):
    n_dp = asked.shape[0]
    enc = table.shape[2]
    return pl.pallas_call(
        functools.partial(pack_body, n_dp, chunk, share),
        out_shape=[jax.ShapeDtypeStruct((cap, TILE, enc), table.dtype)] * n_dp,
        in_specs=[SMEM, SMEM, ANY],
        out_specs=[VMEM] * n_dp,
        scratch_shapes=[pltpu.SemaphoreType.DMA((n_dp * cap,))],
        compiler_params=params(VMEM_ALL),
        cost_estimate=cost(0, 4 * n_dp * cap * TILE * enc),
        name="pack_rows",
    )(me, asked, table)


def compact_body(n_dp, request, *refs):
    arrived, out, sem = refs[:n_dp], refs[n_dp], refs[n_dp + 1]
    cap = arrived[0].shape[0]

    def each(act):
        for d in range(n_dp):
            for j in range(cap):
                r = request[d * cap + j]

                @pl.when(r >= 0)
                def _():
                    act(pltpu.make_async_copy(arrived[d].at[j], out.at[r], sem.at[d * cap + j]))

    each(lambda copy: copy.start())
    each(lambda copy: copy.wait())


def compact(request, arrived, n):
    shape = (n,) + arrived[0].shape[1:]
    return pl.pallas_call(
        functools.partial(compact_body, len(arrived)),
        out_shape=jax.ShapeDtypeStruct(shape, arrived[0].dtype),
        in_specs=[SMEM] + [ANY] * len(arrived),
        out_specs=VMEM,
        scratch_shapes=[pltpu.SemaphoreType.DMA((request.shape[0],))],
        compiler_params=params(),
        cost_estimate=cost(0, 4 * math.prod(shape)),
        name="compact_rows",
    )(request, *arrived)


def weight_specs(rows, step):
    return [
        pl.BlockSpec((rows, step), lambda i: (0, jnp.minimum(i, 1))),
        pl.BlockSpec((rows, step), lambda i: (0, jnp.maximum(i - 2, 0))),
    ]


def with_weight(wk, wv, act):
    @pl.when(pl.program_id(0) < 2)
    def _():
        act(wk)

    @pl.when(pl.program_id(0) >= 2)
    def _():
        act(wv)


def project_body(n_in, *refs):
    wk, wv, out = refs[n_in : n_in + 3]
    n, sub, enc = refs[0].shape
    rows = jnp.concatenate([ref[...].reshape(n * sub, enc) for ref in refs[:n_in]], axis=0)

    def act(w):
        res = jnp.dot(rows, w[...], preferred_element_type=F32)
        out[...] = res.astype(BF16).reshape(out.shape)

    with_weight(wk, wv, act)


def project(pieces, wk, wv):
    n_in = len(pieces)
    n, sub, enc = pieces[0].shape
    width = 2 * wk.shape[1]
    step = width // 4
    return pl.pallas_call(
        functools.partial(project_body, n_in),
        out_shape=jax.ShapeDtypeStruct((n_in, n, sub, width), BF16),
        grid=(4,),
        in_specs=[pl.BlockSpec((n, sub, enc), lambda i: (0, 0, 0))] * n_in
        + weight_specs(enc, step),
        out_specs=pl.BlockSpec((n_in, n, sub, step), lambda i: (0, 0, 0, i)),
        compiler_params=params(),
        cost_estimate=cost(
            2 * n_in * n * sub * enc * width, 2 * (n_in * n * sub * (enc + width) + enc * width)
        ),
        name="project",
    )(*pieces, wk, wv)


def attend_body(places, n_kv, n_late, near, *refs):
    kvs, late = refs[:n_kv], refs[n_kv : n_kv + n_late]
    wk, wv, q_ref, g_ref, att_ref, dq_ref = refs[n_kv + n_late : n_kv + n_late + 6]
    *grads, far_out, own_out, rest_out, late_kv, own_all, core_all = refs[n_kv + n_late + 6 :]
    step = pl.program_id(0)
    width = q_ref.shape[1]
    enc = wk.shape[0]
    scale = 1.0 / math.sqrt(HD)
    heads = width // HD
    group = min(8, heads)
    per = q_ref.shape[0] // SPAN
    last = (((1,), (1,)), ((), ()))
    first = (((0,), (0,)), ((), ()))

    def dot(a, b, dims=(((1,), (0,)), ((), ()))):
        return lax.dot_general(a, b, dims, preferred_element_type=F32)

    @pl.when(step == 0)
    def _():
        for i, ref in enumerate(late):
            rows = ref[...].reshape(-1, enc)
            shape = ref.shape[:2] + (width,)
            late_kv[i, :, :, :width] = dot(rows, wk[...]).astype(BF16).reshape(shape)
            late_kv[i, :, :, width:] = dot(rows, wv[...]).astype(BF16).reshape(shape)

    def rows_of(u, col):
        cols = pl.ds(col, HD)
        parts = [ref[:, 2 * u : 2 * u + 2, :, cols].reshape(-1, HD) for ref in kvs]
        parts.append(late_kv[:, pl.ds(2 * (per * step + u), 2), :, cols].reshape(-1, HD))
        return jnp.concatenate(parts, axis=0)

    def put(u, col, grad):
        cols = pl.ds(col, HD)
        for at, (kind, k, c) in enumerate(places):
            block = grad[at * 2 * TILE : (at + 1) * 2 * TILE].reshape(2, TILE, HD)
            tokens = pl.ds(c * TILE, TILE)
            if k < grads[kind].shape[0]:
                grads[kind][k, 2 * u : 2 * u + 2, tokens, cols] = block
            (own_all, core_all)[kind][k, pl.ds(2 * (per * step + u), 2), tokens, cols] = block

    zero = jnp.zeros((SPAN, HD), BF16)
    for u, h0 in [(u, h0) for u in range(per) for h0 in range(0, heads, group)]:
        hs = range(h0, h0 + group)
        at = slice(u * SPAN, (u + 1) * SPAN)
        qg, kv = [], []
        for h in hs:
            cols = pl.ds(h * HD, HD)
            top = jnp.concatenate([q_ref[at, cols], zero], axis=1)
            low = jnp.concatenate([zero, g_ref[at, cols]], axis=1)
            qg.append(jnp.concatenate([top, low], axis=0))
            kv.append(jnp.concatenate([rows_of(u, h * HD), rows_of(u, width + h * HD)], axis=1))
        both = [dot(a, b, last) for a, b in zip(qg, kv)]
        s = jnp.concatenate([x[:SPAN] for x in both], axis=0) * scale
        dw = jnp.concatenate([x[SPAN:] for x in both], axis=0)
        e = jnp.exp(s - jnp.max(s, axis=1, keepdims=True))
        p = e * (1.0 / jnp.sum(e, axis=1, keepdims=True))
        rs = jnp.sum(dw * p, axis=1, keepdims=True)
        w = p.astype(BF16)
        ds = (p * (dw - rs) * scale).astype(BF16)
        span = [slice(i * SPAN, (i + 1) * SPAN) for i in range(group)]
        dsw = [jnp.concatenate([ds[i], w[i]], axis=0) for i in span]
        out = [dot(a, b).astype(BF16) for a, b in zip(dsw, kv)]
        back = [dot(a, b, first).astype(BF16) for a, b in zip(dsw, qg)]
        for i, h in enumerate(hs):
            dq_ref[at, pl.ds(h * HD, HD)] = out[i][:SPAN, :HD]
            att_ref[at, pl.ds(h * HD, HD)] = out[i][SPAN:, HD:]
            put(u, h * HD, back[i][:, :HD])
            put(u, width + h * HD, back[i][:, HD:])

    @pl.when(step == pl.num_programs(0) - 1)
    def _():
        count = own_out.shape[-1]

        def part(ref, cols):
            rows = ref[...].reshape(-1, 2 * width)
            res = dot(rows[:, :width], wk[cols, :], last) + dot(rows[:, width:], wv[cols, :], last)
            return res.reshape(ref.shape[:3] + (-1,))

        far_out[...] = part(core_all.at[near:], slice(0, count))
        own_out[...] = part(own_all, slice(0, count))
        rest_out[:near] = jnp.zeros_like(rest_out[:near])
        rest_out[:near, :, :, :count] = part(core_all.at[:near], slice(0, count))
        rest_out[near:] = part(core_all.at[near:], slice(count, enc))


def attend(kvs, late, wk, wv, places, near, share, count, queries, cotangent):
    tokens, width = queries.shape
    n, enc = late[0].shape[0], wk.shape[0]
    sub = share
    half = len(places) // (2 * (share // TILE))
    total = 2 * half
    per = 2 if tokens % (2 * SPAN) == 0 else 1
    rows = pl.BlockSpec((per * SPAN, width), lambda i: (i, 0))

    def grads(pieces):
        return pl.BlockSpec((pieces, 2 * per, sub, 2 * width), lambda i: (0, i, 0, 0))

    def kv_block(kv):
        return pl.BlockSpec((kv.shape[0], 2 * per, TILE, 2 * width), lambda i: (0, i, 0, 0))

    def once(shape):
        return pl.BlockSpec(shape, lambda i: (0,) * len(shape), pipeline_mode=pl.Buffered(1))

    def whole(shape):
        return pl.BlockSpec(shape, lambda i: (0,) * len(shape))

    parts = [(half - near, n, sub, count), (half, n, sub, count), (half, n, sub, enc - count)]
    every = (half, n, sub, 2 * width)
    return pl.pallas_call(
        functools.partial(attend_body, places, len(kvs), len(late), near),
        out_shape=[jax.ShapeDtypeStruct((tokens, width), BF16)] * 2
        + [jax.ShapeDtypeStruct(every, BF16), jax.ShapeDtypeStruct((near, *every[1:]), BF16)]
        + [jax.ShapeDtypeStruct(part, F32) for part in parts],
        grid=(tokens // (per * SPAN),),
        in_specs=[kv_block(kv) for kv in kvs]
        + [once(x.shape) for x in late]
        + [once(wk.shape), once(wv.shape), rows, rows],
        out_specs=[rows, rows, grads(half), grads(near)] + [whole(part) for part in parts],
        scratch_shapes=[
            pltpu.VMEM((len(late), n, TILE, 2 * width), BF16),
            pltpu.VMEM(every, BF16),
            pltpu.VMEM(every, BF16),
        ],
        compiler_params=params(VMEM_MORE),
        cost_estimate=cost(
            16 * tokens * width * total * 2 * sub + 4 * n * width * (len(late) * TILE * enc + total * sub * count),
            8 * tokens * width + 8 * total * n * sub * width,
        ),
        name="attend",
    )(*kvs, *late, wk, wv, queries, cotangent)


def encode(x, axes):
    top = jnp.maximum(jnp.max(jnp.abs(x), axis=axes, keepdims=True), 1e-30)
    power = jnp.floor(jnp.log2(top)) + 1.0
    code = jnp.clip(jnp.round(x * jnp.exp2(15.0 - power)), -32767.0, 32767.0)
    return code.astype(jnp.int32).astype(jnp.int16), power


def grads_body(first, core_ref, own_ref, wk, wv, near_out, own_out, part, sem):
    i = pl.program_id(0)
    n_x = own_out.shape[0]
    width, count = wk.shape[1], part.shape[-1]
    last = (((1,), (1,)), ((), ()))

    def act(ref):
        rows = ref[...].reshape(-1, 2 * width)
        res = lax.dot_general(
            rows[:, :width], wk[first : first + count, :], last, preferred_element_type=F32
        )
        res += lax.dot_general(
            rows[:, width:], wv[first : first + count, :], last, preferred_element_type=F32
        )
        part[i] = res.reshape(part.shape[1:])

    @pl.when(i == n_x)
    def _():
        act(core_ref)

    @pl.when(i < n_x)
    def _():
        act(own_ref)

    outs = [own_out.at[k] for k in range(n_x)] + [near_out.at[0]]
    copies = [pltpu.make_async_copy(part.at[k], out, sem.at[k]) for k, out in enumerate(outs)]
    for k, copy in enumerate(copies):

        @pl.when(i == k)
        def _():
            copy.start()

    @pl.when(i == pl.num_programs(0) - 1)
    def _():
        for copy in copies:
            copy.wait()


def grads_of(d_core, d_own, wk, wv, cols):
    n_x, n, sub, width = d_own.shape
    first, count = cols
    rows = n_x * n * sub
    return pl.pallas_call(
        functools.partial(grads_body, first),
        out_shape=[
            jax.ShapeDtypeStruct((1, n, sub, count), F32),
            jax.ShapeDtypeStruct((n_x, n, sub, count), F32),
        ],
        grid=(n_x + 1,),
        in_specs=[
            pl.BlockSpec((1, n, sub, width), lambda i: (0, 0, 0, 0)),
            pl.BlockSpec((1, n, sub, width), lambda i: (jnp.minimum(i, n_x - 1), 0, 0, 0)),
            pl.BlockSpec(wk.shape, lambda i: (0, 0)),
            pl.BlockSpec(wv.shape, lambda i: (0, 0)),
        ],
        out_specs=[ANY] * 2,
        scratch_shapes=[
            pltpu.VMEM((n_x + 1, n, sub, count), F32),
            pltpu.SemaphoreType.DMA((n_x + 1,)),
        ],
        compiler_params=params(),
        cost_estimate=cost(4 * rows * count * width, 2 * (count + 2 * rows) * width + 8 * rows * count),
        name="grads",
    )(d_core, d_own, wk, wv)


def far_codes_body(cuts, mine, got, *codes):
    far, n, sub, count = mine.shape
    row = lax.broadcasted_iota(jnp.int32, (sub, LANES), 0)
    for k in range(far):
        code, power = encode(mine[k] + got[k], (1, 2))
        e = 0
        for cut, out in zip(cuts, codes[k * len(cuts) :]):
            for at in range(cut):
                out[at * n : (at + 1) * n] = code[:, :, e * LANES : (e + 1) * LANES]
                e += 1
        note = jnp.zeros((sub, LANES), F32)
        for r in range(n):
            note = jnp.where(row == r, power[r], note)
        codes[k * len(cuts)][cuts[0] * n] = note.astype(jnp.int32).astype(jnp.int16)


def far_codes(own, got, cuts):
    n_x, n, sub, count = own.shape
    far = n_x - 1
    shapes = [(cut * n + (q == 0), sub, LANES) for q, cut in enumerate(cuts)] * far
    block = tuple(pl.Element(size) for size in (far, n, sub, count))

    def whole(shape):
        return pl.BlockSpec(shape, lambda i: (0,) * len(shape))

    behind = got.shape[0] - far
    mine = pl.BlockSpec(block, lambda i: (1, 0, 0, 0))
    theirs = pl.BlockSpec(block, lambda i: (behind, 0, 0, 0))
    out = pl.pallas_call(
        functools.partial(far_codes_body, cuts),
        out_shape=[jax.ShapeDtypeStruct(shape, jnp.int16) for shape in shapes],
        grid=(1,),
        in_specs=[mine, theirs],
        out_specs=[whole(shape) for shape in shapes],
        compiler_params=params(),
        cost_estimate=cost(8 * got.size, 10 * got.size),
        name="far_codes",
    )(own, got)
    return [out[k * len(cuts) : (k + 1) * len(cuts)] for k in range(far)]


def send_body(n_dp, cuts, request, own, got, *rest):
    codes, outs, (stage, powers) = rest[: -n_dp - 2], rest[-n_dp - 2 : -2], rest[-2:]
    _, n, sub, count = got.shape
    tiles = count // LANES
    cap = request.shape[0] // n_dp
    notes = [code[cuts[0] * n].astype(F32) for code in codes[:: len(cuts)]]
    for r in range(n):
        total = own[0, r] + got[0, r]
        for k, note in enumerate(notes):
            unit = jnp.exp2(note[r : r + 1] - 15.0)
            blocks = [
                code[at * n + r].astype(F32) * unit
                for cut, code in zip(cuts, codes[k * len(cuts) :])
                for at in range(cut)
            ]
            total = total + jnp.concatenate(blocks, axis=1)
        coded, power = encode(total, (0, 1))
        for e in range(tiles):
            for h in range(sub // TILE):
                block = coded[h * TILE : (h + 1) * TILE, e * LANES : (e + 1) * LANES]
                stage[r, e * (sub // TILE) + h] = block
        powers[r] = jnp.broadcast_to(power, (TILE, LANES))
    row = lax.broadcasted_iota(jnp.int32, (TILE, LANES), 0)
    size = stage.shape[1]
    for d in range(n_dp):
        note = jnp.zeros((TILE, LANES), F32)
        for j in range(cap):
            r = request[d * cap + j]

            @pl.when(r >= 0)
            def _():
                outs[d][pl.ds(j * size, size)] = stage[r]

            note = jnp.where(row == j, powers[jnp.maximum(r, 0)], note)
        outs[d][cap * size] = note.astype(jnp.int32).astype(jnp.int16)


def send_codes(request, own, got, codes, cuts, n_dp):
    _, n, sub, count = own.shape
    block = pl.BlockSpec((1, n, sub, count), lambda i: (0, 0, 0, 0))
    size = count // LANES * (sub // TILE)
    cap = request.shape[0] // n_dp
    shape = (cap * size + 1, TILE, LANES)
    codes = [x for piece in codes for x in piece]
    return pl.pallas_call(
        functools.partial(send_body, n_dp, cuts),
        out_shape=[jax.ShapeDtypeStruct(shape, jnp.int16)] * n_dp,
        grid=(1,),
        in_specs=[SMEM, block, block] + [VMEM] * len(codes),
        out_specs=[VMEM] * n_dp,
        scratch_shapes=[
            pltpu.VMEM((n, size, TILE, LANES), jnp.int16),
            pltpu.VMEM((n, TILE, LANES), F32),
        ],
        compiler_params=params(),
        cost_estimate=cost(10 * got.size, 6 * got.size + 2 * n_dp * math.prod(shape)),
        name="send_codes",
    )(request, own, got, *codes)


def gather_body(n_dp, first, me, asked, *refs):
    arrived = refs[:n_dp]
    out, total, sem = refs[-3:]
    tiles, halves = total.shape[2] // LANES, total.shape[1] // TILE
    size = tiles * halves
    cap = asked.shape[1] // n_dp
    total[...] = jnp.zeros_like(total)
    for d in range(n_dp):
        for j in range(cap):
            slab = asked_of(asked, me, d, j)

            @pl.when(slab >= 0)
            def _():
                note = arrived[d][cap * size].astype(F32)
                unit = jnp.exp2(note[j : j + 1] - 15.0)
                for e in range(tiles):
                    for h in range(halves):
                        value = arrived[d][j * size + e * halves + h].astype(F32) * unit
                        total[slab, pl.ds(h * TILE, TILE), pl.ds(e * LANES, LANES)] += value

    copy = pltpu.make_async_copy(total, out.at[:, :, pl.ds(first, total.shape[2])], sem)
    copy.start()
    copy.wait()


def gather_grads(me, asked, arrived, n_slabs, rows, enc, cols, before):
    first, count = cols
    n_dp = asked.shape[0]
    return pl.pallas_call(
        functools.partial(gather_body, n_dp, first),
        out_shape=jax.ShapeDtypeStruct((n_slabs, rows, enc), F32),
        in_specs=[SMEM, SMEM] + [VMEM] * n_dp + [ANY] * (before is not None),
        out_specs=ANY,
        scratch_shapes=[pltpu.VMEM((n_slabs, rows, count), F32), pltpu.SemaphoreType.DMA],
        input_output_aliases={} if before is None else {2 + n_dp: 0},
        compiler_params=params(),
        cost_estimate=cost(0, 8 * n_slabs * rows * count),
        name="gather_grads",
    )(me, asked, *arrived, *([] if before is None else [before]))


def on_device(queries, cotangent, table, key_weight, value_weight, owners, slots):
    n_dp = lax.axis_size("dp")
    n_tp = lax.axis_size("tensor")
    n_x = n_tp // 2
    spans = owners.shape[0]
    n_requests = 2 * spans
    n_slabs, n_tokens, enc = table.shape
    cap = max(2, (4 * spans + n_dp - 1) // n_dp)
    share = n_tokens // n_tp
    n_chunks = share // TILE

    def over_core(x):
        return lax.ppermute(x, "tensor", [(t, t ^ 1) for t in range(n_tp)])

    def over_x(x, d):
        return lax.ppermute(x, "tensor", [(t, (t + 2 * d) % n_tp) for t in range(n_tp)])

    def over_dp(x, d):
        return lax.ppermute(x, "dp", [(i, (i + d) % n_dp) for i in range(n_dp)])

    farthest_first = sorted(range(1, n_dp), key=lambda d: -min(d, n_dp - d))

    def to_all(xs, sign, distances=farthest_first):
        got = {d: over_dp(xs[d], sign * d) for d in distances}
        return got

    me, wanted, request = ask(owners, slots, n_dp, cap)
    asked = lax.psum(wanted, "dp")

    kvs, places = [], []
    early = {}
    sent = pack(me, asked, table, 0, share, cap)
    for c in range(n_chunks):
        rest = [d for d in farthest_first if d not in early]
        arrived = [sent[0]] + [None] * (n_dp - 1)
        for d, x in {**early, **to_all(sent, -1, rest)}.items():
            arrived[d] = x
        if c < n_chunks - 1:
            sent = pack(me, asked, table, c + 1, share, cap)
            early = to_all(sent, -1, farthest_first[:1])
            early, arrived = lax.optimization_barrier((early, arrived))
        if kvs:
            arrived, kvs = lax.optimization_barrier((arrived, kvs))
        mine = compact(request, arrived, n_requests)
        near = [mine, over_core(mine)]
        far = [over_x(mine, k) for k in range(1, n_x)]
        if c < n_chunks - 1:
            early = {**early, **to_all(sent, -1, farthest_first[1:4])}
            early, far = lax.optimization_barrier((early, far))
            far = far + [over_core(x) for x in far]
            kvs = kvs + [project(near + far, key_weight, value_weight)]
        else:
            near = project(near, key_weight, value_weight)
            near, far = lax.optimization_barrier((near, far))
            late = far + [over_core(x) for x in far]
            kvs = kvs + [near]
        places += [(kind, 0, c) for kind in range(2)]
        places += [(kind, k, c) for kind in range(2) for k in range(1, n_x)]

    split = 3 * LANES
    parts = ((0, split), (split, enc - split))
    attended, d_query, d_own, d_core, far, own, rest = attend(
        kvs, late, key_weight, value_weight, places, 1, share, split, queries, cotangent
    )
    far_got = over_core(far)
    near_got = far_got_b = over_core(rest)
    cuts = (parts[0][1] // LANES,)
    codes = far_codes(own, far_got, cuts)
    near_b, own_b = grads_of(d_core, d_own, key_weight, value_weight, parts[1])

    codes = [[over_x(x, n_x - k) for x in piece] for k, piece in enumerate(codes, 1)]
    codes, near_b = lax.optimization_barrier((codes, near_b))
    near_got_b = over_core(near_b)
    sent = send_codes(request, own, near_got, codes, cuts, n_dp)
    sent, near_got_b = lax.optimization_barrier((sent, near_got_b))
    came = to_all(sent, 1)
    arrived = [sent[0]] + [came[d] for d in range(1, n_dp)]
    d_table = gather_grads(me, asked, arrived, n_slabs, share, enc, parts[0], None)

    cuts = (parts[1][1] // LANES,)
    far_got_b, _ = lax.optimization_barrier((far_got_b, codes))
    codes = far_codes(own_b, far_got_b, cuts)
    codes = [[over_x(x, n_x - k) for x in piece] for k, piece in enumerate(codes, 1)]
    sent = send_codes(request, own_b, near_got_b, codes, cuts, n_dp)
    came = to_all(sent, 1)
    arrived = [sent[0]] + [came[d] for d in range(1, n_dp)]
    d_table = gather_grads(me, asked, arrived, n_slabs, share, enc, parts[1], d_table)
    return (attended, d_query, d_table)


def solution(mesh):
    in_specs = (
        P("dp", "tensor"),
        P("dp", "tensor"),
        P("dp", None, None),
        P(None, "tensor"),
        P(None, "tensor"),
        P("dp", None),
        P("dp", None),
    )
    out_specs = (P("dp", "tensor"), P("dp", "tensor"), P("dp", "tensor", None))
    return jax.shard_map(
        on_device, mesh=mesh, in_specs=in_specs, out_specs=out_specs, check_vma=False
    )
```

```python
import functools
import math

import jax
import jax.numpy as jnp
from jax import lax
from jax.experimental import pallas as pl
from jax.experimental.pallas import tpu as pltpu
from jax.sharding import PartitionSpec as P

HD = 128
SPAN = 64
LANES = 128
TILE = 16
VMEM_LIMIT = 28 * 1024 * 1024
VMEM_MORE = 44 * 1024 * 1024
VMEM_ALL = 60 * 1024 * 1024
F32 = jnp.float32
BF16 = jnp.bfloat16

ANY = pl.BlockSpec(memory_space=pl.ANY)
SMEM = pl.BlockSpec(memory_space=pltpu.SMEM)
VMEM = pl.BlockSpec(memory_space=pltpu.VMEM)


def params(limit=VMEM_LIMIT):
    return pltpu.CompilerParams(vmem_limit_bytes=limit)


def cost(flops, nbytes):
    return pl.CostEstimate(flops=int(flops), bytes_accessed=int(nbytes), transcendentals=0)


def ask_body(cap, owners, slots, me_out, wanted, request, count):
    n_dp = wanted.shape[0]
    me = lax.axis_index("dp")
    me_out[0] = me
    for i in range(n_dp * cap):
        request[i] = -1
        for asker in range(n_dp):
            wanted[asker, i] = 0
    for d in range(n_dp):
        count[d] = 0
    for r in range(owners.size):
        d = owners[r % 2, r // 2] - me
        d = jnp.where(d < 0, d + n_dp, d)
        j = count[d]
        count[d] = j + 1
        wanted[me, d * cap + j] = slots[r % 2, r // 2] + 1
        request[d * cap + j] = r


def ask(owners, slots, n_dp, cap):
    return pl.pallas_call(
        functools.partial(ask_body, cap),
        out_shape=[
            jax.ShapeDtypeStruct((1,), jnp.int32),
            jax.ShapeDtypeStruct((n_dp, n_dp * cap), jnp.int32),
            jax.ShapeDtypeStruct((n_dp * cap,), jnp.int32),
        ],
        in_specs=[SMEM, SMEM],
        out_specs=[SMEM, SMEM, SMEM],
        scratch_shapes=[pltpu.SMEM((n_dp,), jnp.int32)],
        name="ask",
    )(owners.T, slots.T)


def asked_of(asked, me, d, j):
    n_dp = asked.shape[0]
    asker = me[0] - d
    asker = jnp.where(asker < 0, asker + n_dp, asker)
    return asked[asker, d * (asked.shape[1] // n_dp) + j] - 1


def pack_body(n_dp, chunk, share, me, asked, table, *rest):
    outs, sem = rest[:-1], rest[-1]
    cap = outs[0].shape[0]
    row = pl.multiple_of(lax.axis_index("tensor") * share + chunk * TILE, TILE)

    def each(act):
        for d in range(n_dp):
            for j in range(cap):
                slab = asked_of(asked, me, d, j)

                @pl.when(slab >= 0)
                def _():
                    source = table.at[slab, pl.ds(row, TILE)]
                    act(pltpu.make_async_copy(source, outs[d].at[j], sem.at[d * cap + j]))

    each(lambda copy: copy.start())
    each(lambda copy: copy.wait())


def pack(me, asked, table, chunk, share, cap):
    n_dp = asked.shape[0]
    enc = table.shape[2]
    return pl.pallas_call(
        functools.partial(pack_body, n_dp, chunk, share),
        out_shape=[jax.ShapeDtypeStruct((cap, TILE, enc), table.dtype)] * n_dp,
        in_specs=[SMEM, SMEM, ANY],
        out_specs=[VMEM] * n_dp,
        scratch_shapes=[pltpu.SemaphoreType.DMA((n_dp * cap,))],
        compiler_params=params(VMEM_ALL),
        cost_estimate=cost(0, 4 * n_dp * cap * TILE * enc),
        name="pack_rows",
    )(me, asked, table)


def compact_body(n_dp, request, *refs):
    arrived, out, sem = refs[:n_dp], refs[n_dp], refs[n_dp + 1]
    cap = arrived[0].shape[0]

    def each(act):
        for d in range(n_dp):
            for j in range(cap):
                r = request[d * cap + j]

                @pl.when(r >= 0)
                def _():
                    act(pltpu.make_async_copy(arrived[d].at[j], out.at[r], sem.at[d * cap + j]))

    each(lambda copy: copy.start())
    each(lambda copy: copy.wait())


def compact(request, arrived, n):
    shape = (n,) + arrived[0].shape[1:]
    return pl.pallas_call(
        functools.partial(compact_body, len(arrived)),
        out_shape=jax.ShapeDtypeStruct(shape, arrived[0].dtype),
        in_specs=[SMEM] + [ANY] * len(arrived),
        out_specs=VMEM,
        scratch_shapes=[pltpu.SemaphoreType.DMA((request.shape[0],))],
        compiler_params=params(),
        cost_estimate=cost(0, 4 * math.prod(shape)),
        name="compact_rows",
    )(request, *arrived)


def weight_specs(rows, step):
    return [
        pl.BlockSpec((rows, step), lambda i: (0, jnp.minimum(i, 1))),
        pl.BlockSpec((rows, step), lambda i: (0, jnp.maximum(i - 2, 0))),
    ]


def with_weight(wk, wv, act):
    @pl.when(pl.program_id(0) < 2)
    def _():
        act(wk)

    @pl.when(pl.program_id(0) >= 2)
    def _():
        act(wv)


def project_body(n_in, *refs):
    wk, wv, out = refs[n_in : n_in + 3]
    n, sub, enc = refs[0].shape
    rows = jnp.concatenate([ref[...].reshape(n * sub, enc) for ref in refs[:n_in]], axis=0)

    def act(w):
        res = jnp.dot(rows, w[...], preferred_element_type=F32)
        out[...] = res.astype(BF16).reshape(out.shape)

    with_weight(wk, wv, act)


def project(pieces, wk, wv):
    n_in = len(pieces)
    n, sub, enc = pieces[0].shape
    width = 2 * wk.shape[1]
    step = width // 4
    return pl.pallas_call(
        functools.partial(project_body, n_in),
        out_shape=jax.ShapeDtypeStruct((n_in, n, sub, width), BF16),
        grid=(4,),
        in_specs=[pl.BlockSpec((n, sub, enc), lambda i: (0, 0, 0))] * n_in
        + weight_specs(enc, step),
        out_specs=pl.BlockSpec((n_in, n, sub, step), lambda i: (0, 0, 0, i)),
        compiler_params=params(),
        cost_estimate=cost(
            2 * n_in * n * sub * enc * width, 2 * (n_in * n * sub * (enc + width) + enc * width)
        ),
        name="project",
    )(*pieces, wk, wv)


def attend_body(places, n_kv, n_late, near, *refs):
    kvs, late = refs[:n_kv], refs[n_kv : n_kv + n_late]
    wk, wv, q_ref, g_ref, att_ref, dq_ref = refs[n_kv + n_late : n_kv + n_late + 6]
    *grads, near_out, far_out, own_out, rest_out, late_kv, own_all, core_all = refs[n_kv + n_late + 6 :]
    step = pl.program_id(0)
    width = q_ref.shape[1]
    enc = wk.shape[0]
    scale = 1.0 / math.sqrt(HD)
    heads = width // HD
    group = min(8, heads)
    per = q_ref.shape[0] // SPAN
    last = (((1,), (1,)), ((), ()))
    first = (((0,), (0,)), ((), ()))

    def dot(a, b, dims=(((1,), (0,)), ((), ()))):
        return lax.dot_general(a, b, dims, preferred_element_type=F32)

    @pl.when(step == 0)
    def _():
        for i, ref in enumerate(late):
            rows = ref[...].reshape(-1, enc)
            shape = ref.shape[:2] + (width,)
            late_kv[i, :, :, :width] = dot(rows, wk[...]).astype(BF16).reshape(shape)
            late_kv[i, :, :, width:] = dot(rows, wv[...]).astype(BF16).reshape(shape)

    def rows_of(u, col):
        cols = pl.ds(col, HD)
        parts = [ref[:, 2 * u : 2 * u + 2, :, cols].reshape(-1, HD) for ref in kvs]
        parts.append(late_kv[:, pl.ds(2 * (per * step + u), 2), :, cols].reshape(-1, HD))
        return jnp.concatenate(parts, axis=0)

    def put(u, col, grad):
        cols = pl.ds(col, HD)
        for at, (kind, k, c) in enumerate(places):
            block = grad[at * 2 * TILE : (at + 1) * 2 * TILE].reshape(2, TILE, HD)
            tokens = pl.ds(c * TILE, TILE)
            if k < grads[kind].shape[0]:
                grads[kind][k, 2 * u : 2 * u + 2, tokens, cols] = block
            (own_all, core_all)[kind][k, pl.ds(2 * (per * step + u), 2), tokens, cols] = block

    zero = jnp.zeros((SPAN, HD), BF16)
    for u, h0 in [(u, h0) for u in range(per) for h0 in range(0, heads, group)]:
        hs = range(h0, h0 + group)
        at = slice(u * SPAN, (u + 1) * SPAN)
        qg, kv = [], []
        for h in hs:
            cols = pl.ds(h * HD, HD)
            top = jnp.concatenate([q_ref[at, cols], zero], axis=1)
            low = jnp.concatenate([zero, g_ref[at, cols]], axis=1)
            qg.append(jnp.concatenate([top, low], axis=0))
            kv.append(jnp.concatenate([rows_of(u, h * HD), rows_of(u, width + h * HD)], axis=1))
        both = [dot(a, b, last) for a, b in zip(qg, kv)]
        s = jnp.concatenate([x[:SPAN] for x in both], axis=0) * scale
        dw = jnp.concatenate([x[SPAN:] for x in both], axis=0)
        e = jnp.exp(s - jnp.max(s, axis=1, keepdims=True))
        p = e * (1.0 / jnp.sum(e, axis=1, keepdims=True))
        rs = jnp.sum(dw * p, axis=1, keepdims=True)
        w = p.astype(BF16)
        ds = (p * (dw - rs) * scale).astype(BF16)
        span = [slice(i * SPAN, (i + 1) * SPAN) for i in range(group)]
        dsw = [jnp.concatenate([ds[i], w[i]], axis=0) for i in span]
        out = [dot(a, b).astype(BF16) for a, b in zip(dsw, kv)]
        back = [dot(a, b, first).astype(BF16) for a, b in zip(dsw, qg)]
        for i, h in enumerate(hs):
            dq_ref[at, pl.ds(h * HD, HD)] = out[i][:SPAN, :HD]
            att_ref[at, pl.ds(h * HD, HD)] = out[i][SPAN:, HD:]
            put(u, h * HD, back[i][:, :HD])
            put(u, width + h * HD, back[i][:, HD:])

    @pl.when(step == pl.num_programs(0) - 1)
    def _():
        count = own_out.shape[-1]

        def part(ref, cols, out):
            rows = ref[...].reshape(-1, 2 * width)
            res = dot(rows[:, :width], wk[cols, :], last) + dot(rows[:, width:], wv[cols, :], last)
            out[...] = res.reshape(out.shape)

        part(core_all.at[near:], slice(0, count), far_out)
        part(core_all.at[:near], slice(0, count), near_out)
        part(own_all, slice(0, count), own_out)
        part(core_all.at[near:], slice(count, enc), rest_out)


def attend(kvs, late, wk, wv, places, near, share, count, queries, cotangent):
    tokens, width = queries.shape
    n, enc = late[0].shape[0], wk.shape[0]
    sub = share
    half = len(places) // (2 * (share // TILE))
    total = 2 * half
    per = 2 if tokens % (2 * SPAN) == 0 else 1
    rows = pl.BlockSpec((per * SPAN, width), lambda i: (i, 0))

    def grads(pieces):
        return pl.BlockSpec((pieces, 2 * per, sub, 2 * width), lambda i: (0, i, 0, 0))

    def kv_block(kv):
        return pl.BlockSpec((kv.shape[0], 2 * per, TILE, 2 * width), lambda i: (0, i, 0, 0))

    def once(shape):
        return pl.BlockSpec(shape, lambda i: (0,) * len(shape), pipeline_mode=pl.Buffered(1))

    def whole(shape):
        return pl.BlockSpec(shape, lambda i: (0,) * len(shape))

    parts = [(near, n, sub, count), (half - near, n, sub, count), (half, n, sub, count)]
    parts.append((half - near, n, sub, enc - count))
    every = (half, n, sub, 2 * width)
    return pl.pallas_call(
        functools.partial(attend_body, places, len(kvs), len(late), near),
        out_shape=[jax.ShapeDtypeStruct((tokens, width), BF16)] * 2
        + [jax.ShapeDtypeStruct(every, BF16), jax.ShapeDtypeStruct((near, *every[1:]), BF16)]
        + [jax.ShapeDtypeStruct(part, F32) for part in parts],
        grid=(tokens // (per * SPAN),),
        in_specs=[kv_block(kv) for kv in kvs]
        + [once(x.shape) for x in late]
        + [once(wk.shape), once(wv.shape), rows, rows],
        out_specs=[rows, rows, grads(half), grads(near)] + [whole(part) for part in parts],
        scratch_shapes=[
            pltpu.VMEM((len(late), n, TILE, 2 * width), BF16),
            pltpu.VMEM(every, BF16),
            pltpu.VMEM(every, BF16),
        ],
        compiler_params=params(VMEM_MORE),
        cost_estimate=cost(
            16 * tokens * width * total * 2 * sub + 4 * n * width * (len(late) * TILE * enc + total * sub * count),
            8 * tokens * width + 8 * total * n * sub * width,
        ),
        name="attend",
    )(*kvs, *late, wk, wv, queries, cotangent)


def encode(x, axes):
    top = jnp.maximum(jnp.max(jnp.abs(x), axis=axes, keepdims=True), 1e-30)
    power = jnp.floor(jnp.log2(top)) + 1.0
    code = jnp.clip(jnp.round(x * jnp.exp2(15.0 - power)), -32767.0, 32767.0)
    return code.astype(jnp.int32).astype(jnp.int16), power


def grads_body(first, core_ref, own_ref, wk, wv, near_out, own_out, part, sem):
    i = pl.program_id(0)
    n_x = own_out.shape[0]
    width, count = wk.shape[1], part.shape[-1]
    last = (((1,), (1,)), ((), ()))

    def act(ref):
        rows = ref[...].reshape(-1, 2 * width)
        res = lax.dot_general(
            rows[:, :width], wk[first : first + count, :], last, preferred_element_type=F32
        )
        res += lax.dot_general(
            rows[:, width:], wv[first : first + count, :], last, preferred_element_type=F32
        )
        part[i] = res.reshape(part.shape[1:])

    @pl.when(i == n_x)
    def _():
        act(core_ref)

    @pl.when(i < n_x)
    def _():
        act(own_ref)

    outs = [own_out.at[k] for k in range(n_x)] + [near_out.at[0]]
    copies = [pltpu.make_async_copy(part.at[k], out, sem.at[k]) for k, out in enumerate(outs)]
    for k, copy in enumerate(copies):

        @pl.when(i == k)
        def _():
            copy.start()

    @pl.when(i == pl.num_programs(0) - 1)
    def _():
        for copy in copies:
            copy.wait()


def grads_of(d_core, d_own, wk, wv, cols):
    n_x, n, sub, width = d_own.shape
    first, count = cols
    rows = n_x * n * sub
    return pl.pallas_call(
        functools.partial(grads_body, first),
        out_shape=[
            jax.ShapeDtypeStruct((1, n, sub, count), F32),
            jax.ShapeDtypeStruct((n_x, n, sub, count), F32),
        ],
        grid=(n_x + 1,),
        in_specs=[
            pl.BlockSpec((1, n, sub, width), lambda i: (0, 0, 0, 0)),
            pl.BlockSpec((1, n, sub, width), lambda i: (jnp.minimum(i, n_x - 1), 0, 0, 0)),
            pl.BlockSpec(wk.shape, lambda i: (0, 0)),
            pl.BlockSpec(wv.shape, lambda i: (0, 0)),
        ],
        out_specs=[ANY] * 2,
        scratch_shapes=[
            pltpu.VMEM((n_x + 1, n, sub, count), F32),
            pltpu.SemaphoreType.DMA((n_x + 1,)),
        ],
        compiler_params=params(),
        cost_estimate=cost(4 * rows * count * width, 2 * (count + 2 * rows) * width + 8 * rows * count),
        name="grads",
    )(d_core, d_own, wk, wv)


def far_codes_body(cuts, mine, got, *codes):
    far, n, sub, count = got.shape
    row = lax.broadcasted_iota(jnp.int32, (sub, LANES), 0)
    for k in range(far):
        code, power = encode(mine[k] + got[k], (1, 2))
        e = 0
        for cut, out in zip(cuts, codes[k * len(cuts) :]):
            for at in range(cut):
                out[at * n : (at + 1) * n] = code[:, :, e * LANES : (e + 1) * LANES]
                e += 1
        note = jnp.zeros((sub, LANES), F32)
        for r in range(n):
            note = jnp.where(row == r, power[r], note)
        codes[k * len(cuts)][cuts[0] * n] = note.astype(jnp.int32).astype(jnp.int16)


def far_codes(own, got, cuts):
    far, n, sub, count = got.shape
    shapes = [(cut * n + (q == 0), sub, LANES) for q, cut in enumerate(cuts)] * far

    def whole(shape):
        return pl.BlockSpec(shape, lambda i: (0,) * len(shape))

    mine = pl.BlockSpec(tuple(pl.Element(size) for size in got.shape), lambda i: (1, 0, 0, 0))
    out = pl.pallas_call(
        functools.partial(far_codes_body, cuts),
        out_shape=[jax.ShapeDtypeStruct(shape, jnp.int16) for shape in shapes],
        grid=(1,),
        in_specs=[mine, whole(got.shape)],
        out_specs=[whole(shape) for shape in shapes],
        compiler_params=params(),
        cost_estimate=cost(8 * got.size, 10 * got.size),
        name="far_codes",
    )(own, got)
    return [out[k * len(cuts) : (k + 1) * len(cuts)] for k in range(far)]


def send_body(n_dp, cuts, request, own, got, *rest):
    codes, outs, (stage, powers) = rest[: -n_dp - 2], rest[-n_dp - 2 : -2], rest[-2:]
    _, n, sub, count = got.shape
    tiles = count // LANES
    cap = request.shape[0] // n_dp
    notes = [code[cuts[0] * n].astype(F32) for code in codes[:: len(cuts)]]
    for r in range(n):
        total = own[0, r] + got[0, r]
        for k, note in enumerate(notes):
            unit = jnp.exp2(note[r : r + 1] - 15.0)
            blocks = [
                code[at * n + r].astype(F32) * unit
                for cut, code in zip(cuts, codes[k * len(cuts) :])
                for at in range(cut)
            ]
            total = total + jnp.concatenate(blocks, axis=1)
        coded, power = encode(total, (0, 1))
        for e in range(tiles):
            for h in range(sub // TILE):
                block = coded[h * TILE : (h + 1) * TILE, e * LANES : (e + 1) * LANES]
                stage[r, e * (sub // TILE) + h] = block
        powers[r] = jnp.broadcast_to(power, (TILE, LANES))
    row = lax.broadcasted_iota(jnp.int32, (TILE, LANES), 0)
    size = stage.shape[1]
    for d in range(n_dp):
        note = jnp.zeros((TILE, LANES), F32)
        for j in range(cap):
            r = request[d * cap + j]

            @pl.when(r >= 0)
            def _():
                outs[d][pl.ds(j * size, size)] = stage[r]

            note = jnp.where(row == j, powers[jnp.maximum(r, 0)], note)
        outs[d][cap * size] = note.astype(jnp.int32).astype(jnp.int16)


def send_codes(request, own, got, codes, cuts, n_dp):
    _, n, sub, count = got.shape
    block = pl.BlockSpec(got.shape, lambda i: (0, 0, 0, 0))
    size = count // LANES * (sub // TILE)
    cap = request.shape[0] // n_dp
    shape = (cap * size + 1, TILE, LANES)
    codes = [x for piece in codes for x in piece]
    return pl.pallas_call(
        functools.partial(send_body, n_dp, cuts),
        out_shape=[jax.ShapeDtypeStruct(shape, jnp.int16)] * n_dp,
        grid=(1,),
        in_specs=[SMEM, block, block] + [VMEM] * len(codes),
        out_specs=[VMEM] * n_dp,
        scratch_shapes=[
            pltpu.VMEM((n, size, TILE, LANES), jnp.int16),
            pltpu.VMEM((n, TILE, LANES), F32),
        ],
        compiler_params=params(),
        cost_estimate=cost(10 * got.size, 6 * got.size + 2 * n_dp * math.prod(shape)),
        name="send_codes",
    )(request, own, got, *codes)


def gather_body(n_dp, first, me, asked, *refs):
    arrived = refs[:n_dp]
    out, total, sem = refs[-3:]
    tiles, halves = total.shape[2] // LANES, total.shape[1] // TILE
    size = tiles * halves
    cap = asked.shape[1] // n_dp
    total[...] = jnp.zeros_like(total)
    for d in range(n_dp):
        for j in range(cap):
            slab = asked_of(asked, me, d, j)

            @pl.when(slab >= 0)
            def _():
                note = arrived[d][cap * size].astype(F32)
                unit = jnp.exp2(note[j : j + 1] - 15.0)
                for e in range(tiles):
                    for h in range(halves):
                        value = arrived[d][j * size + e * halves + h].astype(F32) * unit
                        total[slab, pl.ds(h * TILE, TILE), pl.ds(e * LANES, LANES)] += value

    copy = pltpu.make_async_copy(total, out.at[:, :, pl.ds(first, total.shape[2])], sem)
    copy.start()
    copy.wait()


def gather_grads(me, asked, arrived, n_slabs, rows, enc, cols, before):
    first, count = cols
    n_dp = asked.shape[0]
    return pl.pallas_call(
        functools.partial(gather_body, n_dp, first),
        out_shape=jax.ShapeDtypeStruct((n_slabs, rows, enc), F32),
        in_specs=[SMEM, SMEM] + [VMEM] * n_dp + [ANY] * (before is not None),
        out_specs=ANY,
        scratch_shapes=[pltpu.VMEM((n_slabs, rows, count), F32), pltpu.SemaphoreType.DMA],
        input_output_aliases={} if before is None else {2 + n_dp: 0},
        compiler_params=params(),
        cost_estimate=cost(0, 8 * n_slabs * rows * count),
        name="gather_grads",
    )(me, asked, *arrived, *([] if before is None else [before]))


def on_device(queries, cotangent, table, key_weight, value_weight, owners, slots):
    n_dp = lax.axis_size("dp")
    n_tp = lax.axis_size("tensor")
    n_x = n_tp // 2
    spans = owners.shape[0]
    n_requests = 2 * spans
    n_slabs, n_tokens, enc = table.shape
    cap = max(2, (4 * spans + n_dp - 1) // n_dp)
    share = n_tokens // n_tp
    n_chunks = share // TILE

    def over_core(x):
        return lax.ppermute(x, "tensor", [(t, t ^ 1) for t in range(n_tp)])

    def over_x(x, d):
        return lax.ppermute(x, "tensor", [(t, (t + 2 * d) % n_tp) for t in range(n_tp)])

    def over_dp(x, d):
        return lax.ppermute(x, "dp", [(i, (i + d) % n_dp) for i in range(n_dp)])

    farthest_first = sorted(range(1, n_dp), key=lambda d: -min(d, n_dp - d))

    def to_all(xs, sign, distances=farthest_first):
        got = {d: over_dp(xs[d], sign * d) for d in distances}
        return got

    me, wanted, request = ask(owners, slots, n_dp, cap)
    asked = lax.psum(wanted, "dp")

    kvs, places = [], []
    early = {}
    sent = pack(me, asked, table, 0, share, cap)
    for c in range(n_chunks):
        rest = [d for d in farthest_first if d not in early]
        arrived = [sent[0]] + [None] * (n_dp - 1)
        for d, x in {**early, **to_all(sent, -1, rest)}.items():
            arrived[d] = x
        if c < n_chunks - 1:
            sent = pack(me, asked, table, c + 1, share, cap)
            early = to_all(sent, -1, farthest_first[:1])
            early, arrived = lax.optimization_barrier((early, arrived))
        if kvs:
            arrived, kvs = lax.optimization_barrier((arrived, kvs))
        mine = compact(request, arrived, n_requests)
        near = [mine, over_core(mine)]
        far = [over_x(mine, k) for k in range(1, n_x)]
        if c < n_chunks - 1:
            early = {**early, **to_all(sent, -1, farthest_first[1:4])}
            early, far = lax.optimization_barrier((early, far))
            far = far + [over_core(x) for x in far]
            kvs = kvs + [project(near + far, key_weight, value_weight)]
        else:
            near = project(near, key_weight, value_weight)
            near, far = lax.optimization_barrier((near, far))
            late = far + [over_core(x) for x in far]
            kvs = kvs + [near]
        places += [(kind, 0, c) for kind in range(2)]
        places += [(kind, k, c) for kind in range(2) for k in range(1, n_x)]

    split = 3 * LANES
    parts = ((0, split), (split, enc - split))
    attended, d_query, d_own, d_core, near, far, own, far_b = attend(
        kvs, late, key_weight, value_weight, places, 1, share, split, queries, cotangent
    )
    far_got = over_core(far)
    near_got = over_core(near)
    far_got_b = over_core(far_b)
    cuts = (parts[0][1] // LANES,)
    codes = far_codes(own, far_got, cuts)
    near_b, own_b = grads_of(d_core, d_own, key_weight, value_weight, parts[1])

    codes = [[over_x(x, n_x - k) for x in piece] for k, piece in enumerate(codes, 1)]
    codes, near_b = lax.optimization_barrier((codes, near_b))
    near_got_b = over_core(near_b)
    sent = send_codes(request, own, near_got, codes, cuts, n_dp)
    sent, near_got_b = lax.optimization_barrier((sent, near_got_b))
    came = to_all(sent, 1)
    arrived = [sent[0]] + [came[d] for d in range(1, n_dp)]
    d_table = gather_grads(me, asked, arrived, n_slabs, share, enc, parts[0], None)

    cuts = (parts[1][1] // LANES,)
    far_got_b, _ = lax.optimization_barrier((far_got_b, codes))
    codes = far_codes(own_b, far_got_b, cuts)
    codes = [[over_x(x, n_x - k) for x in piece] for k, piece in enumerate(codes, 1)]
    sent = send_codes(request, own_b, near_got_b, codes, cuts, n_dp)
    came = to_all(sent, 1)
    arrived = [sent[0]] + [came[d] for d in range(1, n_dp)]
    d_table = gather_grads(me, asked, arrived, n_slabs, share, enc, parts[1], d_table)
    return (attended, d_query, d_table)


def solution(mesh):
    in_specs = (
        P("dp", "tensor"),
        P("dp", "tensor"),
        P("dp", None, None),
        P(None, "tensor"),
        P(None, "tensor"),
        P("dp", None),
        P("dp", None),
    )
    out_specs = (P("dp", "tensor"), P("dp", "tensor"), P("dp", "tensor", None))
    return jax.shard_map(
        on_device, mesh=mesh, in_specs=in_specs, out_specs=out_specs, check_vma=False
    )
```
